32 devices in a mesh: dp: 16 (over z, y, x), tensor: 2 (over core).
Axes of the slice: x: 2, y: 2, z: 4, core: 2. Of those that a mesh axis runs over, the one named last changes fastest.
Arguments:
- tokens: bfloat16 [65536, 384], P(('dp', 'tensor')), may hold values from -6 to 6
- query_weight: bfloat16 [384, 384], replicated, may hold values from -0.3125 to 0.3125
- query_bias: bfloat16 [384], replicated, may hold values from -3 to 3
- key_weight: bfloat16 [384, 384], replicated, may hold values from -0.3125 to 0.3125
- value_weight: bfloat16 [384, 384], replicated, may hold values from -0.3125 to 0.3125
- value_bias: bfloat16 [384], replicated, may hold values from -3 to 3
- proj_weight: bfloat16 [384, 384], replicated, may hold values from -1.75 to 1.75
- proj_bias: bfloat16 [384], replicated, may hold values from -3 to 3
- first_gain: bfloat16 [384], replicated, may hold values from 0.5 to 1.5
- first_shift: bfloat16 [384], replicated, may hold values from -3 to 3
- up_weight: bfloat16 [384, 1536], P(None, 'tensor'), may hold values from -0.3125 to 0.3125
- up_bias: bfloat16 [1536], P('tensor'), may hold values from -3 to 3
- down_weight: bfloat16 [1536, 384], P('tensor'), may hold values from -0.15625 to 0.15625
- down_bias: bfloat16 [384], replicated, may hold values from -3 to 3
- second_gain: bfloat16 [384], replicated, may hold values from 0.5 to 1.5
- second_shift: bfloat16 [384], replicated, may hold values from -3 to 3
- teach_query: bfloat16 [65536, 768], P(('dp', 'tensor')), may hold values from -6 to 6
- teach_key: bfloat16 [65536, 768], P(('dp', 'tensor')), may hold values from -6 to 6
- teach_value: bfloat16 [65536, 768], P(('dp', 'tensor')), may hold values from -4.5 to 4.5
- short_lengths: int32 [256], P(('dp', 'tensor')), may hold values from 32 to 128, as said below
- long_lengths: int32 [64], P(('dp', 'tensor')), may hold values from 128 to 512, as said below
- cotangent: bfloat16 [65536, 384], P(('dp', 'tensor')), may hold values from -6 to 6
Outputs:
- block_out: bfloat16 [65536, 384], P(('dp', 'tensor'))
- tokens_grad: bfloat16 [65536, 384], P(('dp', 'tensor'))
- query_weight_grad: float32 [384, 384], replicated
- query_bias_grad: float32 [384], replicated
- key_weight_grad: float32 [384, 384], replicated
- value_weight_grad: float32 [384, 384], replicated
- value_bias_grad: float32 [384], replicated
- proj_weight_grad: float32 [384, 384], replicated
- proj_bias_grad: float32 [384], replicated
- first_gain_grad: float32 [384], replicated
- first_shift_grad: float32 [384], replicated
- up_weight_grad: float32 [384, 1536], P(None, 'tensor')
- up_bias_grad: float32 [1536], P('tensor')
- down_weight_grad: float32 [1536, 384], P('tensor')
- down_bias_grad: float32 [384], replicated
- second_gain_grad: float32 [384], replicated
- second_shift_grad: float32 [384], replicated
The draws below stay inside these ranges and needn't reach their ends.
Inputs may be any that keep to these rules, and one draw needn't show every extreme that they name: `short_lengths`: each short item has between 32 and 128 valid tokens; both ends are taken by some item in every draw. `long_lengths`: each long item has between 128 and 512 valid tokens; both ends are taken by some item in every draw.
All inputs are finite; a program needn't handle non-finite values.
Results may differ from the reference program's by a relative error of at most 0.015.
Values may be sent and summed in bfloat16 or wider, within the bound.
No kernel may reach another device: no remote copies, remote signals or barrier semaphores. Data moves between devices by JAX's collectives and lax.ppermute only.
A program may use at most 384 MiB of HBM per device.

```python
import jax
import jax.numpy as jnp
from jax import lax

D = 384
HEADS = 12
HEAD_DIM = 32
FF = 1536
TD = 768
TEACH_HD = 64
SHORT_LEN = 128
LONG_LEN = 512
SHORT_DEV = 8
TOK_DEV = 2048
SHORT_ALL = 256
LONG_ALL = 64
TOKENS = 65536
DEVICES = 32


def ragged_lengths(key, item_total, longest):
    first_key, second_key = jax.random.split(key)
    values = jax.random.randint(first_key, (item_total,), longest // 4, longest + 1)
    where_full = jax.random.randint(second_key, (), 0, item_total)
    values = values.at[where_full].set(longest)
    values = values.at[(where_full + 1) % item_total].set(longest // 4)
    return values.astype(jnp.int32)


def draw_short_lengths(key, part):
    key = jax.random.fold_in(key, 11)
    return ragged_lengths(key, SHORT_ALL, SHORT_LEN)


def draw_long_lengths(key, part):
    key = jax.random.fold_in(key, 23)
    return ragged_lengths(key, LONG_ALL, LONG_LEN)


def level_of(own_key, dims, shards, low, top_value):
    def one(position, shards_of):
        heights = jax.random.uniform(jax.random.fold_in(jax.random.fold_in(own_key, 6), position), (shards_of,), jnp.float32, low / len(shards), top_value / len(shards))
        return jnp.repeat(jnp.exp(heights), dims[position] // shards_of).reshape((-1,) + (1,) * (len(dims) - position - 1))

    loudness = one(*shards[0])
    for cut in shards[1:]:
        loudness = loudness * one(*cut)
    return loudness


def noise(rng, dims, scale, limit, cuts=(), kind=jnp.bfloat16):
    values = scale * jax.random.normal(rng, dims, jnp.float32)
    if cuts:
        values = values * level_of(rng, dims, cuts, -0.22, 0.18)
    return jnp.clip(values, -limit, limit).astype(kind)


def setup_inputs(seed: int = 0) -> dict:
    splits = jax.random.split(jax.random.key(seed), 23)
    tokens = noise(splits[0], (TOKENS, D), 1.0, 6.0, ((0, 32),))
    query_weight = noise(splits[1], (D, D), D ** -0.5, 0.3125)
    query_bias = noise(splits[2], (D,), 0.5, 3.0)
    key_weight = noise(splits[3], (D, D), D ** -0.5, 0.3125)
    value_weight = noise(splits[4], (D, D), D ** -0.5, 0.3125)
    value_bias = noise(splits[5], (D,), 0.5, 3.0)
    proj_weight = noise(splits[6], (D, D), (D // 32) ** -0.5, 1.75)
    proj_bias = noise(splits[7], (D,), 0.5, 3.0)
    first_gain = jnp.clip(1.0 + 0.1 * jax.random.normal(splits[8], (D,), jnp.float32), 0.5, 1.5).astype(jnp.bfloat16)
    first_shift = noise(splits[9], (D,), 0.5, 3.0)
    up_weight = noise(splits[10], (D, FF), D ** -0.5, 0.3125, ((1, 2),))
    up_bias = noise(splits[11], (FF,), 0.5, 3.0, ((0, 2),))
    down_weight = noise(splits[12], (FF, D), FF ** -0.5, 0.15625, ((0, 2),))
    down_bias = noise(splits[13], (D,), 0.5, 3.0)
    second_gain = jnp.clip(1.0 + 0.1 * jax.random.normal(splits[14], (D,), jnp.float32), 0.5, 1.5).astype(jnp.bfloat16)
    second_shift = noise(splits[15], (D,), 0.5, 3.0)
    teach_query = noise(splits[16], (TOKENS, TD), 1.0, 6.0, ((0, 32),))
    teach_key = noise(splits[17], (TOKENS, TD), 1.0, 6.0, ((0, 32),))
    teach_value = noise(splits[18], (TOKENS, TD), 0.75, 4.5, ((0, 32),))
    short_lengths = draw_short_lengths(jax.random.fold_in(splits[22], 71), 0)
    long_lengths = draw_long_lengths(jax.random.fold_in(splits[22], 71), 0)
    cotangent = noise(splits[21], (TOKENS, D), 1.0, 6.0, ((0, 32),))
    return {"tokens": tokens, "query_weight": query_weight, "query_bias": query_bias, "key_weight": key_weight, "value_weight": value_weight, "value_bias": value_bias, "proj_weight": proj_weight, "proj_bias": proj_bias, "first_gain": first_gain, "first_shift": first_shift, "up_weight": up_weight, "up_bias": up_bias, "down_weight": down_weight, "down_bias": down_bias, "second_gain": second_gain, "second_shift": second_shift, "teach_query": teach_query, "teach_key": teach_key, "teach_value": teach_value, "short_lengths": short_lengths, "long_lengths": long_lengths, "cotangent": cotangent}


@jax.custom_vjp
def low(v):
    return lax.optimization_barrier(v.astype(jnp.bfloat16)).astype(jnp.float32)

@jax.custom_vjp
def low_back(v):
    return v

def low_keep(v):
    return (low(v), None)

def low_pass(kept, grad):
    return (grad,)

def back_keep(v):
    return (v, None)

def back_low(kept, grad):
    return (low(grad),)
low.defvjp(low_keep, low_pass)
low_back.defvjp(back_keep, back_low)
PRECISE = lax.Precision.HIGHEST
MASKED = -1000000000.0
EPSILON = 1e-06

def matmul_hi(left, right):
    return jnp.dot(left, right, precision=PRECISE, preferred_element_type=jnp.float32)

def pair_scores(left, right):
    return jnp.einsum('bqhd,bkhd->bhqk', left, right, precision=PRECISE)

def layer_norm(resid, gain, shift):
    centred = resid - lax.optimization_barrier(jnp.mean(resid, axis=-1, keepdims=True))
    spread = lax.optimization_barrier(jnp.mean(centred * centred, axis=-1, keepdims=True))
    return centred * lax.rsqrt(spread + EPSILON) * gain + shift

def key_allowed(lengths, seq_len):
    return jnp.arange(seq_len, dtype=jnp.int32)[None, :] < lengths[:, None]

def group_terms(queries, key_rows, value_rows, teach_q, teach_k, teach_v, lengths):
    item_count = lengths.shape[0]
    seq_len = queries.shape[0] // item_count
    key_ok = key_allowed(lengths, seq_len)
    mask_keys = key_ok[:, None, None, :]
    rows_on = key_ok[:, None, :, None].astype(jnp.float32)

    def split_heads(block):
        return block.reshape(item_count, seq_len, HEADS, -1)

    def teacher_log(left, right):
        logits = jnp.where(mask_keys, pair_scores(split_heads(left), split_heads(right)) * TEACH_HD ** (-0.5), MASKED)
        return logits - jax.nn.logsumexp(logits, axis=-1, keepdims=True)
    head_scale = HEAD_DIM ** (-0.5)
    query_heads = split_heads(queries)
    key_heads = split_heads(key_rows)
    value_heads = split_heads(value_rows)
    scores = low_back(jnp.where(mask_keys, pair_scores(query_heads, key_heads) * head_scale, MASKED))
    log_probs = scores - jax.nn.logsumexp(scores, axis=-1, keepdims=True)
    attn_probs = low(jnp.exp(log_probs))
    context = jnp.einsum('bhqk,bkhd->bqhd', attn_probs, value_heads, precision=PRECISE)
    relation = low_back(jnp.where(mask_keys, pair_scores(value_heads, value_heads) * head_scale, MASKED))
    relation_log = relation - jax.nn.logsumexp(relation, axis=-1, keepdims=True)
    teach_att = teacher_log(teach_q, teach_k)
    teach_rel = teacher_log(teach_v, teach_v)
    losses = jnp.sum(rows_on * jnp.exp(teach_att) * (teach_att - log_probs))
    losses = losses + jnp.sum(rows_on * jnp.exp(teach_rel) * (teach_rel - relation_log))
    return (context.reshape(item_count * seq_len, -1), losses)

def reference(tokens, query_weight, query_bias, key_weight, value_weight, value_bias, proj_weight, proj_bias, first_gain, first_shift, up_weight, up_bias, down_weight, down_bias, second_gain, second_shift, teach_query, teach_key, teach_value, short_lengths, long_lengths, cotangent):
    params = tuple((item.astype(jnp.float32) for item in (tokens, query_weight, query_bias, key_weight, value_weight, value_bias, proj_weight, proj_bias, first_gain, first_shift, up_weight, up_bias, down_weight, down_bias, second_gain, second_shift)))
    teach_blocks = tuple((item.astype(jnp.float32).reshape(DEVICES, TOK_DEV, TD) for item in (teach_query, teach_key, teach_value)))
    short_split = short_lengths.reshape(DEVICES, -1)
    long_split = long_lengths.reshape(DEVICES, -1)
    short_rows = SHORT_DEV * SHORT_LEN

    def device_terms(block):
        queries, key_rows, value_rows, teach_q, teach_k, teach_v, short_len, long_len = block
        head_ctx, head_loss = group_terms(queries[:short_rows], key_rows[:short_rows], value_rows[:short_rows], teach_q[:short_rows], teach_k[:short_rows], teach_v[:short_rows], short_len)
        tail_ctx, tail_loss = group_terms(queries[short_rows:], key_rows[short_rows:], value_rows[short_rows:], teach_q[short_rows:], teach_k[short_rows:], teach_v[short_rows:], long_len)
        return (jnp.concatenate([head_ctx, tail_ctx], 0), head_loss + tail_loss)

    def forward(inputs, wq_mat, bq_vec, wk_mat, wv_mat, bv_vec, wo_mat, bo_vec, gain_one, shift_one, wu_mat, bu_vec, wd_mat, bd_vec, gain_two, shift_two):
        queries = low(low_back(matmul_hi(inputs, wq_mat) + bq_vec))
        key_rows = low(low_back(matmul_hi(inputs, wk_mat)))
        value_rows = low(low_back(matmul_hi(inputs, wv_mat) + bv_vec))
        contexts, losses = lax.map(jax.checkpoint(device_terms), (queries.reshape(DEVICES, TOK_DEV, D), key_rows.reshape(DEVICES, TOK_DEV, D), value_rows.reshape(DEVICES, TOK_DEV, D), teach_blocks[0], teach_blocks[1], teach_blocks[2], short_split, long_split))
        context = low(low_back(contexts.reshape(TOKENS, D)))
        attn_out = low_back(matmul_hi(context, wo_mat) + bo_vec)
        normed = layer_norm(inputs + attn_out, gain_one, shift_one)
        normed_low = low(normed)
        hidden_pre = low_back(matmul_hi(normed_low, wu_mat) + bu_vec)
        active = low(jax.nn.gelu(hidden_pre, approximate=False))
        branch = low_back(matmul_hi(active, wd_mat) + bd_vec)
        output = layer_norm(normed + branch, gain_two, shift_two)
        return (output, jnp.sum(losses))
    (output, loss_total), back = jax.vjp(forward, *params)
    grads = back((cotangent.astype(jnp.float32), jnp.ones_like(loss_total)))
    return (output.astype(jnp.bfloat16), grads[0].astype(jnp.bfloat16), grads[1], grads[2], grads[3], grads[4], grads[5], grads[6], grads[7], grads[8], grads[9], grads[10], grads[11], grads[12], grads[13], grads[14], grads[15])
```

```python
import functools

import jax
import jax.numpy as jnp
from jax import lax
from jax.experimental import pallas as pl
from jax.experimental.pallas import tpu as pltpu
from jax.sharding import PartitionSpec as P

HEADS = 12
HEAD_DIM = 32
TEACH_HD = 64
SHORT_LEN = 128
GROUP = 4
LANES = GROUP * HEAD_DIM
GROUPS = HEADS // GROUP
BLOCK = 512

MASKED = -1e30
EPSILON = 1e-06
LOG2E = 1.4426950408889634
SCALE = HEAD_DIM**-0.5
EXP_SCALE = LOG2E * SCALE
TEACH_SCALE = LOG2E * TEACH_HD**-0.5
VMEM_BYTES = 56 * 2**20

F32 = jnp.float32
BF16 = jnp.bfloat16


def dot_nn(left, right):
    return lax.dot_general(left, right, (((1,), (0,)), ((), ())), preferred_element_type=F32)


def dot_nt(left, right):
    return lax.dot_general(left, right, (((1,), (1,)), ((), ())), preferred_element_type=F32)


def dot_tn(left, right):
    return lax.dot_general(left, right, (((0,), (0,)), ((), ())), preferred_element_type=F32)


def dot_tt(left, right):
    return lax.dot_general(left, right, (((0,), (1,)), ((), ())), preferred_element_type=F32)


def head_mask(block, head, width):
    lane = lax.broadcasted_iota(jnp.int32, block.shape, 1)
    return jnp.where(lane // width == head, block, jnp.zeros_like(block))


def key_bias(length, size):
    return jnp.where(lax.broadcasted_iota(jnp.int32, (1, size), 1) < length, 0.0, MASKED)


def query_flag(length, size):
    return (lax.broadcasted_iota(jnp.int32, (size, 1), 0) < length).astype(F32)


def exp_rows(scores, bias, scale):
    scores = scores + bias
    heights = jnp.exp2((scores - jnp.max(scores, axis=1, keepdims=True)) * scale)
    return heights, jnp.sum(heights, axis=1, keepdims=True)


def params():
    return pltpu.CompilerParams(vmem_limit_bytes=VMEM_BYTES)


def whole(shape):
    return pl.BlockSpec(shape, lambda i: (0,) * len(shape))


def smem():
    return pl.BlockSpec(memory_space=pltpu.SMEM)


def forward_kernel(
    short_blocks,
    short_len,
    long_len,
    tokens,
    wq,
    bq,
    wk,
    wv,
    bv,
    q_out,
    k_out,
    v_out,
    ctx_out,
    ps_out,
    pl_out,
):
    step = pl.program_id(0)
    x = tokens[...]
    q_out[...] = (dot_nn(x, wq[...]) + bq[...].astype(F32)).astype(BF16)
    k_out[...] = dot_nn(x, wk[...]).astype(BF16)
    v_out[...] = (dot_nn(x, wv[...]) + bv[...].astype(F32)).astype(BF16)

    @pl.when(step < short_blocks)
    def _():
        items = BLOCK // SHORT_LEN

        @pl.loop(0, items)
        def _(item):
            rows = pl.ds(pl.multiple_of(item * SHORT_LEN, SHORT_LEN), SHORT_LEN)
            bias = key_bias(short_len[step * items + item], SHORT_LEN)
            for g in range(GROUPS):
                cols = slice(g * LANES, (g + 1) * LANES)
                q, k, v = q_out[rows, cols], k_out[rows, cols], v_out[rows, cols]
                k_all = jnp.concatenate([head_mask(k, h, HEAD_DIM) for h in range(GROUP)], 0)
                v_all = jnp.concatenate([head_mask(v, h, HEAD_DIM) for h in range(GROUP)], 0)
                scores = dot_nt(q, k_all)
                parts = []
                for h in range(GROUP):
                    e, total = exp_rows(
                        scores[:, h * SHORT_LEN : (h + 1) * SHORT_LEN], bias, EXP_SCALE
                    )
                    parts.append((e * (1.0 / total)).astype(BF16))
                probs = jnp.concatenate(parts, 1)
                ps_out[g, rows, :] = probs
                ctx_out[rows, cols] = dot_nn(probs, v_all).astype(BF16)

    @pl.when(step >= short_blocks)
    def _():
        bias = key_bias(long_len[step - short_blocks], BLOCK)

        @pl.loop(0, GROUPS)
        def _(g):
            cols = pl.ds(pl.multiple_of(g * LANES, LANES), LANES)
            q, k, v = q_out[:, cols], k_out[:, cols], v_out[:, cols]
            ctx = jnp.zeros((BLOCK, LANES), F32)
            for h in range(GROUP):
                e, total = exp_rows(dot_nt(head_mask(q, h, HEAD_DIM), k), bias, EXP_SCALE)
                probs = (e * (1.0 / total)).astype(BF16)
                pl_out[g * GROUP + h] = probs
                ctx = ctx + dot_nn(probs, head_mask(v, h, HEAD_DIM))
            ctx_out[:, cols] = ctx.astype(BF16)


def attention_forward(tokens, wq, bq, wk, wv, bv, short_len, long_len):
    rows, width = tokens.shape
    blocks = rows // BLOCK
    short_blocks = short_len.shape[0] * SHORT_LEN // BLOCK
    long_blocks = blocks - short_blocks
    row_spec = pl.BlockSpec((BLOCK, width), lambda i: (i, 0))
    act = jax.ShapeDtypeStruct((rows, width), BF16)
    return pl.pallas_call(
        functools.partial(forward_kernel, short_blocks),
        grid=(blocks,),
        in_specs=[smem(), smem(), row_spec]
        + [whole(a.shape) for a in (wq, bq, wk, wv, bv)],
        out_specs=[
            row_spec,
            row_spec,
            row_spec,
            row_spec,
            pl.BlockSpec((GROUPS, BLOCK, BLOCK), lambda i: (0, jnp.minimum(i, short_blocks - 1), 0)),
            pl.BlockSpec((HEADS, BLOCK, BLOCK), lambda i: (0, jnp.maximum(i - short_blocks, 0), 0)),
        ],
        out_shape=[
            act,
            act,
            act,
            act,
            jax.ShapeDtypeStruct((GROUPS, short_blocks * BLOCK, BLOCK), BF16),
            jax.ShapeDtypeStruct((HEADS, long_blocks * BLOCK, BLOCK), BF16),
        ],
        compiler_params=params(),
        cost_estimate=pl.CostEstimate(
            flops=12_000_000_000, bytes_accessed=24_000_000, transcendentals=8_000_000
        ),
        name="attention_forward",
    )(short_len, long_len, tokens, wq, bq, wk, wv, bv)


def norm_parts(resid):
    centred = resid - jnp.mean(resid, axis=-1, keepdims=True)
    spread = jnp.mean(centred * centred, axis=-1, keepdims=True)
    root = lax.rsqrt(spread + EPSILON)
    return centred * root, root


def norm_back(grad, y, root):
    return root * (
        grad
        - jnp.mean(grad, axis=-1, keepdims=True)
        - y * jnp.mean(grad * y, axis=-1, keepdims=True)
    )


def column_sum(block):
    return jnp.sum(block.astype(F32), axis=0, keepdims=True)


def middle_kernel(
    tokens,
    ctx,
    cot,
    wo,
    bo,
    g1,
    s1,
    up0,
    up1,
    ub0,
    ub1,
    dn0,
    dn1,
    db,
    g2,
    s2,
    block_out,
    dres_out,
    dctx_out,
    ffn0_out,
    ffn1_out,
    attn_out,
    acc_up,
    acc_dn,
    acc_wo,
    acc_ub,
    acc_vec,
    slope,
    active,
):
    step = pl.program_id(0)
    half = up0.shape[1]
    width = up0.shape[0]

    @pl.when(step == 0)
    def _():
        for ref in (acc_up, acc_dn, acc_wo, acc_ub, acc_vec):
            ref[...] = jnp.zeros_like(ref)

    ctx_low = ctx[...]
    resid = tokens[...].astype(F32) + dot_nn(ctx_low, wo[...]) + bo[...].astype(F32)
    y1, root1 = norm_parts(resid)
    gain1 = g1[...].astype(F32)
    normed = y1 * gain1 + s1[...].astype(F32)
    normed_low = normed.astype(BF16)
    mid = normed + db[...].astype(F32)
    for j, (up, ub, dn) in enumerate(((up0, ub0, dn0), (up1, ub1, dn1))):
        pre = dot_nn(normed_low, up[...]) + ub[...].astype(F32)
        phi = 0.5 + 0.5 * lax.erf(pre * (0.5**0.5))
        act = (pre * phi).astype(BF16)
        slope[j] = phi + pre * (jnp.exp2(pre * pre * (-0.5 * LOG2E)) * 0.3989422804014327)
        active[j] = act
        mid = mid + dot_nn(act, dn[...])
    y2, root2 = norm_parts(mid)
    gain2 = g2[...].astype(F32)
    block_out[...] = (y2 * gain2 + s2[...].astype(F32)).astype(BF16)
    cotangent = cot[...].astype(F32)
    dmid = norm_back(cotangent * gain2, y2, root2)
    dbranch = dmid.astype(BF16)
    acc_vec[3:4, :] += column_sum(dbranch)
    acc_vec[4:5, :] += column_sum(cotangent * y2)
    acc_vec[5:6, :] += column_sum(cotangent)
    dnormed = dmid
    for j, (up, dn) in enumerate(((up0, dn0), (up1, dn1))):
        acc_dn[j] += dot_tn(active[j], dbranch)
        dpre = (dot_nt(dbranch, dn[...]) * slope[j]).astype(BF16)
        acc_up[j] += dot_tn(normed_low, dpre)
        acc_ub[j : j + 1, :] += column_sum(dpre)
        dnormed = dnormed + dot_nt(dpre, up[...])
    acc_vec[1:2, :] += column_sum(dnormed * y1)
    acc_vec[2:3, :] += column_sum(dnormed)
    dres = norm_back(dnormed * gain1, y1, root1)
    dres_out[...] = dres
    dattn = dres.astype(BF16)
    acc_vec[0:1, :] += column_sum(dattn)
    acc_wo[...] += dot_tn(ctx_low, dattn)
    dctx_out[...] = dot_nt(dattn, wo[...]).astype(BF16)

    @pl.when(step == pl.num_programs(0) - 1)
    def _():
        for j, out in enumerate((ffn0_out, ffn1_out)):
            for part in range(half // width):
                cols = slice(part * width, (part + 1) * width)
                out[part * width : (part + 1) * width, :] = acc_up[j, :, cols].astype(BF16)
            out[half : 2 * half, :] = acc_dn[j].astype(BF16)
            pads = [
                acc_ub[j : j + 1, part * width : (part + 1) * width]
                for part in range(half // width)
            ]
            pads.append(jnp.zeros((16 - len(pads), width), F32))
            out[2 * half :, :] = jnp.concatenate(pads, 0).astype(BF16)
        attn_out[:width, :] = acc_wo[...].astype(BF16)
        tail = jnp.concatenate([acc_vec[...], jnp.zeros((88, width), F32)], 0)
        attn_out[width:, :] = tail.astype(BF16)


def middle(tokens, ctx, cot, wo, bo, g1, s1, ups, ubs, dns, db, g2, s2):
    rows, width = tokens.shape
    half = ups[0].shape[1]
    row_spec = pl.BlockSpec((BLOCK, width), lambda i: (i, 0))
    weights = (wo, bo, g1, s1, *ups, *ubs, *dns, db, g2, s2)
    act = jax.ShapeDtypeStruct((rows, width), BF16)
    ffn = jax.ShapeDtypeStruct((2 * half + 16, width), BF16)
    attn = jax.ShapeDtypeStruct((width + 96, width), BF16)
    return pl.pallas_call(
        middle_kernel,
        grid=(rows // BLOCK,),
        in_specs=[row_spec] * 3 + [whole(w.shape) for w in weights],
        out_specs=[row_spec] * 3 + [whole(ffn.shape), whole(ffn.shape), whole(attn.shape)],
        out_shape=[act, jax.ShapeDtypeStruct((rows, width), F32), act, ffn, ffn, attn],
        scratch_shapes=[
            pltpu.VMEM((2, width, half), F32),
            pltpu.VMEM((2, half, width), F32),
            pltpu.VMEM((width, width), F32),
            pltpu.VMEM((8, half), F32),
            pltpu.VMEM((8, width), F32),
            pltpu.VMEM((2, BLOCK, half), F32),
            pltpu.VMEM((2, BLOCK, half), BF16),
        ],
        compiler_params=params(),
        cost_estimate=pl.CostEstimate(
            flops=34_000_000_000, bytes_accessed=20_000_000, transcendentals=6_000_000
        ),
        name="middle",
    )(tokens, ctx, cot, *weights)


def finish_block(x, dq, dkt, dvt, dq_out, dkt_out, dvt_out, acc, bias_acc):
    dq_low = dq.astype(BF16)
    dkt_low = dkt.astype(BF16)
    dvt_low = dvt.astype(BF16)
    dq_out[...] = dq_low
    dkt_out[...] = dkt_low
    dvt_out[...] = dvt_low
    both = jnp.concatenate([dq_low.T, dkt_low, dvt_low], 0)
    acc[...] += dot_nn(both, x)
    bias_acc[0:1, :] += column_sum(dq_low)
    bias_acc[1:2, :] += column_sum(dvt_low.T)


def short_backward_kernel(
    lengths,
    tokens,
    q_in,
    k_in,
    v_in,
    ctx_in,
    dctx_in,
    tq_in,
    tk_in,
    tv_in,
    p_in,
    dq_out,
    dkt_out,
    dvt_out,
    acc,
    bias_acc,
    dq_buf,
    dkt_buf,
    dvt_buf,
):
    step = pl.program_id(0)
    items = BLOCK // SHORT_LEN

    @pl.when(step == 0)
    def _():
        acc[...] = jnp.zeros_like(acc)
        bias_acc[...] = jnp.zeros_like(bias_acc)

    def spans(block):
        return [block[:, h * SHORT_LEN : (h + 1) * SHORT_LEN] for h in range(GROUP)]

    def stack(block, width):
        return jnp.concatenate([head_mask(block, h, width) for h in range(GROUP)], 0)

    def softmax_heads(scores, bias, scale, flag):
        parts = []
        for part in spans(scores):
            e, total = exp_rows(part, bias, scale)
            parts.append(e * (flag / total))
        return jnp.concatenate(parts, 1)

    def diagonal(block):
        return jnp.concatenate(
            [
                block[h * HEAD_DIM : (h + 1) * HEAD_DIM, h * SHORT_LEN : (h + 1) * SHORT_LEN]
                for h in range(GROUP)
            ],
            0,
        )

    for item in range(items):
        rows = slice(item * SHORT_LEN, (item + 1) * SHORT_LEN)
        length = lengths[step * items + item]
        bias = key_bias(length, SHORT_LEN)
        flag = query_flag(length, SHORT_LEN)
        q, k, v = q_in[rows, :], k_in[rows, :], v_in[rows, :]
        dctx, ctx = dctx_in[rows, :], ctx_in[rows, :]
        tq, tk, tv = tq_in[rows, :], tk_in[rows, :], tv_in[rows, :]
        k_all, v_all = stack(k, HEAD_DIM), stack(v, HEAD_DIM)
        p_low = p_in[0, rows, :]
        p = p_low.astype(F32)
        teach = softmax_heads(dot_nt(tq, stack(tk, TEACH_HD)), bias, TEACH_SCALE, flag)
        weighed = -(dctx.astype(F32) * ctx.astype(F32)).astype(BF16)
        ones = stack(jnp.ones_like(v), HEAD_DIM)
        dp = dot_nt(jnp.concatenate([dctx, weighed], 1), jnp.concatenate([v_all, ones], 1))
        ds = (p * (dp + flag) - teach).astype(BF16)
        relation = softmax_heads(dot_nt(v, v_all), bias, EXP_SCALE, flag)
        teach_rel = softmax_heads(dot_nt(tv, stack(tv, TEACH_HD)), bias, TEACH_SCALE, flag)
        drel = (relation - teach_rel).astype(BF16)
        dq_buf[rows, :] = dot_nn(ds, k_all) * SCALE
        dkt_buf[:, rows] = diagonal(dot_tn(q, ds)) * SCALE
        dvt = diagonal(dot_tn(dctx, p_low))
        dvt_buf[:, rows] = dvt + SCALE * (diagonal(dot_tn(v, drel)) + dot_nn(drel, v_all).T)
    finish_block(
        tokens[...], dq_buf[...], dkt_buf[...], dvt_buf[...], dq_out, dkt_out, dvt_out, acc, bias_acc
    )


def long_backward_kernel(
    lengths,
    tokens,
    q_in,
    k_in,
    v_in,
    ctx_in,
    dctx_in,
    tq_in,
    tk_in,
    tv_in,
    p_in,
    acc_in,
    bias_in,
    _dq,
    _dkt,
    _dvt,
    dq_out,
    dkt_out,
    dvt_out,
    sum_out,
    acc,
    bias_acc,
    dq_buf,
    dkt_buf,
    dvt_buf,
    rel_buf,
):
    step = pl.program_id(0)

    @pl.when(step == 0)
    def _():
        acc[...] = acc_in[...]
        bias_acc[...] = bias_in[...]

    length = lengths[step]
    bias = key_bias(length, BLOCK)
    flag = query_flag(length, BLOCK)
    q, k, v = q_in[...], k_in[...], v_in[...]
    dctx, ctx = dctx_in[...], ctx_in[...]
    qt, vt, dctxt = q.T, v.T, dctx.T
    weighed = -(dctx.astype(F32) * ctx.astype(F32)).astype(BF16)
    right = jnp.concatenate([v, jnp.ones_like(v)], 1)

    def soft(scores, scale):
        e, total = exp_rows(scores, bias, scale)
        return e * (flag / total)

    for h in range(GROUP):
        dims = slice(h * HEAD_DIM, (h + 1) * HEAD_DIM)
        pair = slice(h // 2 * 2 * TEACH_HD, (h // 2 + 1) * 2 * TEACH_HD)
        tq, tk, tv = tq_in[:, pair], tk_in[:, pair], tv_in[:, pair]
        k_h, v_h = head_mask(k, h, HEAD_DIM), head_mask(v, h, HEAD_DIM)
        p_low = p_in[h]
        teach = soft(dot_nt(head_mask(tq, h % 2, TEACH_HD), tk), TEACH_SCALE)
        left = jnp.concatenate(
            [head_mask(dctx, h, HEAD_DIM), head_mask(weighed, h, HEAD_DIM)], 1
        )
        dp = dot_nt(left, right)
        ds = (p_low.astype(F32) * (dp + flag) - teach).astype(BF16)
        dq = dot_nn(ds, k_h)
        dkt_buf[dims, :] = dot_nn(qt[dims, :], ds) * SCALE
        dvt = dot_nn(dctxt[dims, :], p_low)
        relation = soft(dot_nt(v_h, v), EXP_SCALE)
        teach_rel = soft(dot_nt(head_mask(tv, h % 2, TEACH_HD), tv), TEACH_SCALE)
        drel = (relation - teach_rel).astype(BF16)
        dvt_buf[dims, :] = dvt + SCALE * dot_nn(vt[dims, :], drel)
        rel = dot_nn(drel, v_h)
        if h == 0:
            dq_buf[...] = dq
            rel_buf[...] = rel
        else:
            dq_buf[...] += dq
            rel_buf[...] += rel
    finish_block(
        tokens[...],
        dq_buf[...] * SCALE,
        dkt_buf[...],
        dvt_buf[...] + SCALE * rel_buf[...].T,
        dq_out,
        dkt_out,
        dvt_out,
        acc,
        bias_acc,
    )

    @pl.when(step == pl.num_programs(0) - 1)
    def _():
        width = tokens.shape[1]
        for w in range(3):
            part = acc[w * LANES : (w + 1) * LANES, :].T
            sum_out[w * width : (w + 1) * width, :] = part.astype(BF16)
        tail = jnp.concatenate([bias_acc[...], jnp.zeros((120, LANES), F32)], 0)
        sum_out[3 * width :, :] = tail.astype(BF16)


def attention_backward(g, tokens, q, k, v, ctx, dctx, teach, p_short, p_long, short_len, long_len):
    rows, width = tokens.shape
    short_blocks = short_len.shape[0] * SHORT_LEN // BLOCK
    long_blocks = rows // BLOCK - short_blocks
    wide = GROUP * TEACH_HD

    def specs(first):
        group_spec = pl.BlockSpec((BLOCK, LANES), lambda i: (i + first, g))
        teach_spec = pl.BlockSpec((BLOCK, wide), lambda i: (i + first, g))
        row_spec = pl.BlockSpec((BLOCK, width), lambda i: (i + first, 0))
        outs = [
            pl.BlockSpec((BLOCK, LANES), lambda i: (i + first, 0)),
            pl.BlockSpec((LANES, BLOCK), lambda i: (0, i + first)),
            pl.BlockSpec((LANES, BLOCK), lambda i: (0, i + first)),
        ]
        return [smem(), row_spec] + [group_spec] * 5 + [teach_spec] * 3, outs

    grads = [
        jax.ShapeDtypeStruct((rows, LANES), BF16),
        jax.ShapeDtypeStruct((LANES, rows), BF16),
        jax.ShapeDtypeStruct((LANES, rows), BF16),
    ]
    acc = jax.ShapeDtypeStruct((3 * LANES, width), F32)
    bias_acc = jax.ShapeDtypeStruct((8, LANES), F32)
    buffers = [
        pltpu.VMEM((BLOCK, LANES), F32),
        pltpu.VMEM((LANES, BLOCK), F32),
        pltpu.VMEM((LANES, BLOCK), F32),
    ]
    ins, outs = specs(0)
    dq, dkt, dvt, acc_v, bias_v = pl.pallas_call(
        short_backward_kernel,
        grid=(short_blocks,),
        in_specs=ins + [pl.BlockSpec((1, BLOCK, BLOCK), lambda i: (g, i, 0))],
        out_specs=outs + [whole(acc.shape), whole(bias_acc.shape)],
        out_shape=grads + [acc, bias_acc],
        scratch_shapes=buffers,
        compiler_params=params(),
        cost_estimate=pl.CostEstimate(
            flops=9_000_000_000, bytes_accessed=8_000_000, transcendentals=2_000_000
        ),
        name=f"short_backward_{g}",
    )(short_len, tokens, q, k, v, ctx, dctx, *teach, p_short)
    ins, outs = specs(short_blocks)
    sums = jax.ShapeDtypeStruct((3 * width + 128, LANES), BF16)
    dq, dkt, dvt, summed = pl.pallas_call(
        long_backward_kernel,
        grid=(long_blocks,),
        in_specs=ins
        + [pl.BlockSpec((GROUP, BLOCK, BLOCK), lambda i: (g, i, 0))]
        + [whole(acc.shape), whole(bias_acc.shape)]
        + [pl.BlockSpec(memory_space=pl.ANY)] * 3,
        out_specs=outs + [whole(sums.shape)],
        out_shape=grads + [sums],
        scratch_shapes=[pltpu.VMEM(acc.shape, F32), pltpu.VMEM(bias_acc.shape, F32)]
        + buffers
        + [pltpu.VMEM((BLOCK, LANES), F32)],
        input_output_aliases={13: 0, 14: 1, 15: 2},
        compiler_params=params(),
        cost_estimate=pl.CostEstimate(
            flops=18_000_000_000, bytes_accessed=10_000_000, transcendentals=6_000_000
        ),
        name=f"long_backward_{g}",
    )(long_len, tokens, q, k, v, ctx, dctx, *teach, p_long, acc_v, bias_v, dq, dkt, dvt)
    return (dq, dkt, dvt), summed


def tokens_grad_kernel(dres, wq, wk, wv, *refs):
    out = refs[-1]
    total = dres[...]
    for g in range(GROUPS):
        dq, dkt, dvt = refs[3 * g : 3 * g + 3]
        cols = slice(g * LANES, (g + 1) * LANES)
        total = total + dot_nt(dq[...], wq[:, cols])
        total = total + dot_tt(dkt[...], wk[:, cols])
        total = total + dot_tt(dvt[...], wv[:, cols])
    out[...] = total.astype(BF16)


def tokens_gradient(dres, wq, wk, wv, parts):
    rows, width = dres.shape
    row_spec = pl.BlockSpec((BLOCK, width), lambda i: (i, 0))
    side = pl.BlockSpec((LANES, BLOCK), lambda i: (0, i))
    return pl.pallas_call(
        tokens_grad_kernel,
        grid=(rows // BLOCK,),
        in_specs=[row_spec]
        + [whole(wq.shape)] * 3
        + [pl.BlockSpec((BLOCK, LANES), lambda i: (i, 0)), side, side] * GROUPS,
        out_specs=row_spec,
        out_shape=jax.ShapeDtypeStruct((rows, width), BF16),
        compiler_params=params(),
        cost_estimate=pl.CostEstimate(
            flops=2_000_000_000, bytes_accessed=10_000_000, transcendentals=0
        ),
        name="tokens_gradient",
    )(dres, wq, wk, wv, *[part for trio in parts for part in trio])


def tensor_swap(block):
    return lax.ppermute(block, "tensor", [(0, 1), (1, 0)])


def add_low(first, *others):
    total = first.astype(F32)
    for other in others:
        total = total + other.astype(F32)
    return total.astype(BF16)


def stages_of(count):
    stages = []
    shift = 0
    while (1 << shift) < count:
        size = 4 if (4 << shift) <= count else 2
        stages.append((shift, size))
        shift += size.bit_length() - 1
    return stages


def sum_over_dp(block, count):
    rows, width = block.shape
    me = lax.axis_index("dp")
    chunk = rows // count
    chunks = block.reshape(count, chunk, width)
    order = jnp.arange(count, dtype=jnp.int32) ^ me
    rel = jnp.take(chunks, order, axis=0)
    stages = stages_of(count)

    def send(value, offset):
        return lax.ppermute(value, "dp", [(i, i ^ offset) for i in range(count)])

    for shift, size in stages:
        rel = rel.reshape(-1, size, chunk, width)
        got = [send(rel[:, j], j << shift) for j in range(1, size)]
        rel = add_low(rel[:, 0], *got)
    rel = rel.reshape(1, chunk, width)
    for shift, size in stages[::-1]:
        got = [rel] + [send(rel, j << shift) for j in range(1, size)]
        rel = jnp.stack(got, 1).reshape(-1, chunk, width)
    return jnp.take(rel, order, axis=0).reshape(rows, width)


def halves(block):
    size = block.shape[0] // 2
    mine = lax.axis_index("tensor")
    keep = lax.dynamic_slice_in_dim(block, mine * size, size, 0)
    give = lax.dynamic_slice_in_dim(block, (1 - mine) * size, size, 0)
    return keep, give


def join(first, second):
    mine = lax.axis_index("tensor")
    low = jnp.where(mine == 0, first, second)
    high = jnp.where(mine == 0, second, first)
    return jnp.concatenate([low, high], 0)


def per_device(
    dp_count,
    tokens,
    query_weight,
    query_bias,
    key_weight,
    value_weight,
    value_bias,
    proj_weight,
    proj_bias,
    first_gain,
    first_shift,
    up_weight,
    up_bias,
    down_weight,
    down_bias,
    second_gain,
    second_shift,
    teach_query,
    teach_key,
    teach_value,
    short_lengths,
    long_lengths,
    cotangent,
):
    width = tokens.shape[1]
    half = up_weight.shape[1]

    def row(vector):
        return vector.reshape(1, -1)

    up_other = tensor_swap(up_weight)
    ub_other = tensor_swap(row(up_bias))
    down_other = tensor_swap(down_weight)
    q, k, v, ctx, p_short, p_long = attention_forward(
        tokens,
        query_weight,
        row(query_bias),
        key_weight,
        value_weight,
        row(value_bias),
        short_lengths,
        long_lengths,
    )
    block_out, dres, dctx, ffn_mine, ffn_other, attn_sum = middle(
        tokens,
        ctx,
        cotangent,
        proj_weight,
        row(proj_bias),
        row(first_gain),
        row(first_shift),
        (up_weight, up_other),
        (row(up_bias), ub_other),
        (down_weight, down_other),
        row(down_bias),
        row(second_gain),
        row(second_shift),
    )
    keep, give = halves(attn_sum)
    got_ffn = tensor_swap(ffn_other)
    got_attn = tensor_swap(give)
    first = jnp.concatenate([add_low(ffn_mine, got_ffn), add_low(keep, got_attn)], 0)
    first = sum_over_dp(first, dp_count)

    teach = (teach_query, teach_key, teach_value)
    parts = []
    sums = []
    for g in range(GROUPS):
        trio, summed = attention_backward(
            g, tokens, q, k, v, ctx, dctx, teach, p_short, p_long, short_lengths, long_lengths
        )
        parts.append(trio)
        keep, give = halves(summed)
        total = sum_over_dp(add_low(keep, tensor_swap(give)), dp_count)
        sums.append(join(total, tensor_swap(total)))
    tokens_grad = tokens_gradient(dres, query_weight, key_weight, value_weight, parts)

    ffn = first[: 2 * half + 16].astype(F32)
    count = half // width
    up_grad = jnp.concatenate([ffn[i * width : (i + 1) * width] for i in range(count)], 1)
    down_grad = ffn[half : 2 * half]
    up_bias_grad = ffn[2 * half : 2 * half + count].reshape(half)
    attn = first[2 * half + 16 :]
    attn = join(attn, tensor_swap(attn)).astype(F32)
    vectors = attn[width : width + 6]
    qkv = jnp.concatenate(sums, 1).astype(F32)
    return (
        block_out,
        tokens_grad,
        qkv[:width],
        qkv[3 * width],
        qkv[width : 2 * width],
        qkv[2 * width : 3 * width],
        qkv[3 * width + 1],
        attn[:width],
        vectors[0],
        vectors[1],
        vectors[2],
        up_grad,
        up_bias_grad,
        down_grad,
        vectors[3],
        vectors[4],
        vectors[5],
    )


def solution(mesh):
    in_specs = (
        P(("dp", "tensor"), None),
        P(),
        P(),
        P(),
        P(),
        P(),
        P(),
        P(),
        P(),
        P(),
        P(None, "tensor"),
        P("tensor"),
        P("tensor", None),
        P(),
        P(),
        P(),
        P(("dp", "tensor"), None),
        P(("dp", "tensor"), None),
        P(("dp", "tensor"), None),
        P(("dp", "tensor")),
        P(("dp", "tensor")),
        P(("dp", "tensor"), None),
    )
    out_specs = (
        P(("dp", "tensor"), None),
        P(("dp", "tensor"), None),
        P(),
        P(),
        P(),
        P(),
        P(),
        P(),
        P(),
        P(),
        P(),
        P(None, "tensor"),
        P("tensor"),
        P("tensor", None),
        P(),
        P(),
        P(),
    )
    return jax.shard_map(
        functools.partial(per_device, mesh.shape["dp"]),
        mesh=mesh,
        in_specs=in_specs,
        out_specs=out_specs,
        check_vma=False,
    )
```

```python
import functools

import jax
import jax.numpy as jnp
from jax import lax
from jax.experimental import pallas as pl
from jax.experimental.pallas import tpu as pltpu
from jax.sharding import PartitionSpec as P

HEADS = 12
HEAD_DIM = 32
TEACH_HD = 64
SHORT_LEN = 128
GROUP = 4
LANES = GROUP * HEAD_DIM
GROUPS = HEADS // GROUP
BLOCK = 512

MASKED = -1e30
EPSILON = 1e-06
LOG2E = 1.4426950408889634
SCALE = HEAD_DIM**-0.5
EXP_SCALE = LOG2E * SCALE
TEACH_SCALE = LOG2E * TEACH_HD**-0.5
VMEM_BYTES = 56 * 2**20

F32 = jnp.float32
BF16 = jnp.bfloat16


def dot_nn(left, right):
    return lax.dot_general(left, right, (((1,), (0,)), ((), ())), preferred_element_type=F32)


def dot_nt(left, right):
    return lax.dot_general(left, right, (((1,), (1,)), ((), ())), preferred_element_type=F32)


def dot_tn(left, right):
    return lax.dot_general(left, right, (((0,), (0,)), ((), ())), preferred_element_type=F32)


def dot_tt(left, right):
    return lax.dot_general(left, right, (((0,), (1,)), ((), ())), preferred_element_type=F32)


def head_mask(block, head, width):
    lane = lax.broadcasted_iota(jnp.int32, block.shape, 1)
    return jnp.where(lane // width == head, block, jnp.zeros_like(block))


def key_bias(length, size):
    return jnp.where(lax.broadcasted_iota(jnp.int32, (1, size), 1) < length, 0.0, MASKED)


def query_flag(length, size):
    return (lax.broadcasted_iota(jnp.int32, (size, 1), 0) < length).astype(F32)


def exp_rows(scores, bias, scale):
    scores = scores + bias
    heights = jnp.exp2((scores - jnp.max(scores, axis=1, keepdims=True)) * scale)
    return heights, jnp.sum(heights, axis=1, keepdims=True)


def params():
    return pltpu.CompilerParams(vmem_limit_bytes=VMEM_BYTES)


def whole(shape):
    return pl.BlockSpec(shape, lambda i: (0,) * len(shape))


def smem():
    return pl.BlockSpec(memory_space=pltpu.SMEM)


def forward_kernel(
    short_blocks,
    short_len,
    long_len,
    tokens,
    wq,
    wk,
    wv,
    vectors,
    q_out,
    k_out,
    v_out,
    ctx_out,
    ps_out,
    pl_out,
):
    step = pl.program_id(0)
    x = tokens[...]
    q_out[...] = (dot_nn(x, wq[...]) + vectors[0:1, :]).astype(BF16)
    k_out[...] = dot_nn(x, wk[...]).astype(BF16)
    v_out[...] = (dot_nn(x, wv[...]) + vectors[1:2, :]).astype(BF16)

    @pl.when(step < short_blocks)
    def _():
        items = BLOCK // SHORT_LEN

        @pl.loop(0, items)
        def _(item):
            rows = pl.ds(pl.multiple_of(item * SHORT_LEN, SHORT_LEN), SHORT_LEN)
            bias = key_bias(short_len[step * items + item], SHORT_LEN)
            for g in range(GROUPS):
                cols = slice(g * LANES, (g + 1) * LANES)
                q, k, v = q_out[rows, cols], k_out[rows, cols], v_out[rows, cols]
                k_all = jnp.concatenate([head_mask(k, h, HEAD_DIM) for h in range(GROUP)], 0)
                v_all = jnp.concatenate([head_mask(v, h, HEAD_DIM) for h in range(GROUP)], 0)
                scores = dot_nt(q, k_all)
                parts = []
                for h in range(GROUP):
                    e, total = exp_rows(
                        scores[:, h * SHORT_LEN : (h + 1) * SHORT_LEN], bias, EXP_SCALE
                    )
                    parts.append((e * (1.0 / total)).astype(BF16))
                probs = jnp.concatenate(parts, 1)
                ps_out[g, rows, :] = probs
                ctx_out[rows, cols] = dot_nn(probs, v_all).astype(BF16)

    @pl.when(step >= short_blocks)
    def _():
        bias = key_bias(long_len[step - short_blocks], BLOCK)

        @pl.loop(0, GROUPS)
        def _(g):
            cols = pl.ds(pl.multiple_of(g * LANES, LANES), LANES)
            q, k, v = q_out[:, cols], k_out[:, cols], v_out[:, cols]
            ctx = jnp.zeros((BLOCK, LANES), F32)
            for h in range(GROUP):
                e, total = exp_rows(dot_nt(head_mask(q, h, HEAD_DIM), k), bias, EXP_SCALE)
                probs = (e * (1.0 / total)).astype(BF16)
                pl_out[g * GROUP + h] = probs
                ctx = ctx + dot_nn(probs, head_mask(v, h, HEAD_DIM))
            ctx_out[:, cols] = ctx.astype(BF16)


def attention_forward(tokens, wq, wk, wv, vectors, short_len, long_len):
    rows, width = tokens.shape
    blocks = rows // BLOCK
    short_blocks = short_len.shape[0] * SHORT_LEN // BLOCK
    long_blocks = blocks - short_blocks
    row_spec = pl.BlockSpec((BLOCK, width), lambda i: (i, 0))
    act = jax.ShapeDtypeStruct((rows, width), BF16)
    return pl.pallas_call(
        functools.partial(forward_kernel, short_blocks),
        grid=(blocks,),
        in_specs=[smem(), smem(), row_spec]
        + [whole(a.shape) for a in (wq, wk, wv, vectors)],
        out_specs=[
            row_spec,
            row_spec,
            row_spec,
            row_spec,
            pl.BlockSpec((GROUPS, BLOCK, BLOCK), lambda i: (0, jnp.minimum(i, short_blocks - 1), 0)),
            pl.BlockSpec((HEADS, BLOCK, BLOCK), lambda i: (0, jnp.maximum(i - short_blocks, 0), 0)),
        ],
        out_shape=[
            act,
            act,
            act,
            act,
            jax.ShapeDtypeStruct((GROUPS, short_blocks * BLOCK, BLOCK), BF16),
            jax.ShapeDtypeStruct((HEADS, long_blocks * BLOCK, BLOCK), BF16),
        ],
        compiler_params=params(),
        cost_estimate=pl.CostEstimate(
            flops=12_000_000_000, bytes_accessed=24_000_000, transcendentals=8_000_000
        ),
        name="attention_forward",
    )(short_len, long_len, tokens, wq, wk, wv, vectors)


def norm_parts(resid):
    centred = resid - jnp.mean(resid, axis=-1, keepdims=True)
    spread = jnp.mean(centred * centred, axis=-1, keepdims=True)
    root = lax.rsqrt(spread + EPSILON)
    return centred * root, root


def norm_back(grad, y, root):
    return root * (
        grad
        - jnp.mean(grad, axis=-1, keepdims=True)
        - y * jnp.mean(grad * y, axis=-1, keepdims=True)
    )


def column_sum(block):
    return jnp.sum(block.astype(F32), axis=0, keepdims=True)


def middle_kernel(
    tokens,
    ctx,
    cot,
    vectors,
    wo,
    up0,
    up1,
    ub0,
    ub1,
    dn0,
    dn1,
    block_out,
    dres_out,
    dctx_out,
    ffn0_out,
    ffn1_out,
    attn_out,
    acc_up,
    acc_dn,
    acc_wo,
    acc_ub,
    acc_vec,
    slope,
    active,
):
    step = pl.program_id(0)
    half = up0.shape[1]
    width = up0.shape[0]

    @pl.when(step == 0)
    def _():
        for ref in (acc_up, acc_dn, acc_wo, acc_ub, acc_vec):
            ref[...] = jnp.zeros_like(ref)

    bo, gain1, shift1, db, gain2, shift2 = (vectors[i : i + 1, :] for i in range(2, 8))
    ctx_low = ctx[...]
    resid = tokens[...].astype(F32) + dot_nn(ctx_low, wo[...]) + bo
    y1, root1 = norm_parts(resid)
    normed = y1 * gain1 + shift1
    normed_low = normed.astype(BF16)
    mid = normed + db
    for j, (up, ub, dn) in enumerate(((up0, ub0, dn0), (up1, ub1, dn1))):
        pre = dot_nn(normed_low, up[...]) + ub[...].astype(F32)
        phi = 0.5 + 0.5 * lax.erf(pre * (0.5**0.5))
        act = (pre * phi).astype(BF16)
        slope[j] = phi + pre * (jnp.exp2(pre * pre * (-0.5 * LOG2E)) * 0.3989422804014327)
        active[j] = act
        mid = mid + dot_nn(act, dn[...])
    y2, root2 = norm_parts(mid)
    block_out[...] = (y2 * gain2 + shift2).astype(BF16)
    cotangent = cot[...].astype(F32)
    dmid = norm_back(cotangent * gain2, y2, root2)
    dbranch = dmid.astype(BF16)
    acc_vec[3:4, :] += column_sum(dbranch)
    acc_vec[4:5, :] += column_sum(cotangent * y2)
    acc_vec[5:6, :] += column_sum(cotangent)
    dnormed = dmid
    for j, (up, dn) in enumerate(((up0, dn0), (up1, dn1))):
        acc_dn[j] += dot_tn(active[j], dbranch)
        dpre = (dot_nt(dbranch, dn[...]) * slope[j]).astype(BF16)
        acc_up[j] += dot_tn(normed_low, dpre)
        acc_ub[j : j + 1, :] += column_sum(dpre)
        dnormed = dnormed + dot_nt(dpre, up[...])
    acc_vec[1:2, :] += column_sum(dnormed * y1)
    acc_vec[2:3, :] += column_sum(dnormed)
    dres = norm_back(dnormed * gain1, y1, root1)
    dres_out[...] = dres
    dattn = dres.astype(BF16)
    acc_vec[0:1, :] += column_sum(dattn)
    acc_wo[...] += dot_tn(ctx_low, dattn)
    dctx_out[...] = dot_nt(dattn, wo[...]).astype(BF16)

    @pl.when(step == pl.num_programs(0) - 1)
    def _():
        for j, out in enumerate((ffn0_out, ffn1_out)):
            for part in range(half // width):
                cols = slice(part * width, (part + 1) * width)
                out[part * width : (part + 1) * width, :] = acc_up[j, :, cols].astype(BF16)
            out[half : 2 * half, :] = acc_dn[j].astype(BF16)
            pads = [
                acc_ub[j : j + 1, part * width : (part + 1) * width]
                for part in range(half // width)
            ]
            pads.append(jnp.zeros((16 - len(pads), width), F32))
            out[2 * half :, :] = jnp.concatenate(pads, 0).astype(BF16)
        attn_out[:width, :] = acc_wo[...].astype(BF16)
        tail = jnp.concatenate([acc_vec[...], jnp.zeros((88, width), F32)], 0)
        attn_out[width:, :] = tail.astype(BF16)


def middle(tokens, ctx, cot, vectors, wo, ups, ubs, dns):
    rows, width = tokens.shape
    half = ups[0].shape[1]
    row_spec = pl.BlockSpec((BLOCK, width), lambda i: (i, 0))
    weights = (vectors, wo, *ups, *ubs, *dns)
    act = jax.ShapeDtypeStruct((rows, width), BF16)
    ffn = jax.ShapeDtypeStruct((2 * half + 16, width), BF16)
    attn = jax.ShapeDtypeStruct((width + 96, width), BF16)
    return pl.pallas_call(
        middle_kernel,
        grid=(rows // BLOCK,),
        in_specs=[row_spec] * 3 + [whole(w.shape) for w in weights],
        out_specs=[row_spec] * 3 + [whole(ffn.shape), whole(ffn.shape), whole(attn.shape)],
        out_shape=[act, jax.ShapeDtypeStruct((rows, width), F32), act, ffn, ffn, attn],
        scratch_shapes=[
            pltpu.VMEM((2, width, half), F32),
            pltpu.VMEM((2, half, width), F32),
            pltpu.VMEM((width, width), F32),
            pltpu.VMEM((8, half), F32),
            pltpu.VMEM((8, width), F32),
            pltpu.VMEM((2, BLOCK, half), F32),
            pltpu.VMEM((2, BLOCK, half), BF16),
        ],
        compiler_params=params(),
        cost_estimate=pl.CostEstimate(
            flops=34_000_000_000, bytes_accessed=20_000_000, transcendentals=6_000_000
        ),
        name="middle",
    )(tokens, ctx, cot, *weights)


def finish_block(x, dq, dkt, dvt, dq_out, dkt_out, dvt_out, acc, bias_acc):
    dq_low = dq.astype(BF16)
    dkt_low = dkt.astype(BF16)
    dvt_low = dvt.astype(BF16)
    dq_out[...] = dq_low
    dkt_out[...] = dkt_low
    dvt_out[...] = dvt_low
    both = jnp.concatenate([dq_low.T, dkt_low, dvt_low], 0)
    acc[...] += dot_nn(both, x)
    bias_acc[0:1, :] += column_sum(dq_low)
    bias_acc[1:2, :] += column_sum(dvt_low.T)


def short_backward_kernel(
    lengths,
    tokens,
    q_in,
    k_in,
    v_in,
    ctx_in,
    dctx_in,
    tq_in,
    tk_in,
    tv_in,
    p_in,
    dq_out,
    dkt_out,
    dvt_out,
    acc,
    bias_acc,
    dq_buf,
    dkt_buf,
    dvt_buf,
):
    step = pl.program_id(0)
    items = BLOCK // SHORT_LEN

    @pl.when(step == 0)
    def _():
        acc[...] = jnp.zeros_like(acc)
        bias_acc[...] = jnp.zeros_like(bias_acc)

    def spans(block):
        return [block[:, h * SHORT_LEN : (h + 1) * SHORT_LEN] for h in range(GROUP)]

    def stack(block, width):
        return jnp.concatenate([head_mask(block, h, width) for h in range(GROUP)], 0)

    def softmax_heads(scores, bias, scale, flag):
        parts = []
        for part in spans(scores):
            e, total = exp_rows(part, bias, scale)
            parts.append(e * (flag / total))
        return jnp.concatenate(parts, 1)

    def diagonal(block):
        return jnp.concatenate(
            [
                block[h * HEAD_DIM : (h + 1) * HEAD_DIM, h * SHORT_LEN : (h + 1) * SHORT_LEN]
                for h in range(GROUP)
            ],
            0,
        )

    for item in range(items):
        rows = slice(item * SHORT_LEN, (item + 1) * SHORT_LEN)
        length = lengths[step * items + item]
        bias = key_bias(length, SHORT_LEN)
        flag = query_flag(length, SHORT_LEN)
        q, k, v = q_in[rows, :], k_in[rows, :], v_in[rows, :]
        dctx, ctx = dctx_in[rows, :], ctx_in[rows, :]
        tq, tk, tv = tq_in[rows, :], tk_in[rows, :], tv_in[rows, :]
        k_all, v_all = stack(k, HEAD_DIM), stack(v, HEAD_DIM)
        p_low = p_in[0, rows, :]
        p = p_low.astype(F32)
        teach = softmax_heads(dot_nt(tq, stack(tk, TEACH_HD)), bias, TEACH_SCALE, flag)
        weighed = -(dctx.astype(F32) * ctx.astype(F32)).astype(BF16)
        ones = stack(jnp.ones_like(v), HEAD_DIM)
        dp = dot_nt(jnp.concatenate([dctx, weighed], 1), jnp.concatenate([v_all, ones], 1))
        ds = (p * (dp + flag) - teach).astype(BF16)
        relation = softmax_heads(dot_nt(v, v_all), bias, EXP_SCALE, flag)
        teach_rel = softmax_heads(dot_nt(tv, stack(tv, TEACH_HD)), bias, TEACH_SCALE, flag)
        drel = (relation - teach_rel).astype(BF16)
        dq_buf[rows, :] = dot_nn(ds, k_all) * SCALE
        dkt_buf[:, rows] = diagonal(dot_tn(q, ds)) * SCALE
        dvt = diagonal(dot_tn(dctx, p_low))
        dvt_buf[:, rows] = dvt + SCALE * (diagonal(dot_tn(v, drel)) + dot_nn(drel, v_all).T)
    finish_block(
        tokens[...], dq_buf[...], dkt_buf[...], dvt_buf[...], dq_out, dkt_out, dvt_out, acc, bias_acc
    )


def long_backward_kernel(
    lengths,
    tokens,
    q_in,
    k_in,
    v_in,
    ctx_in,
    dctx_in,
    tq_in,
    tk_in,
    tv_in,
    p_in,
    acc_in,
    bias_in,
    _dq,
    _dkt,
    _dvt,
    _sums,
    dq_out,
    dkt_out,
    dvt_out,
    sum_out,
    dq_buf,
    dkt_buf,
    dvt_buf,
    rel_buf,
    acc,
    bias_acc,
):
    step = pl.program_id(0)

    @pl.when(step == 0)
    def _():
        acc[...] = acc_in[...]
        bias_acc[...] = bias_in[...]

    length = lengths[step]
    bias = key_bias(length, BLOCK)
    flag = query_flag(length, BLOCK)
    q, k, v = q_in[...], k_in[...], v_in[...]
    dctx, ctx = dctx_in[...], ctx_in[...]
    qt, vt, dctxt = q.T, v.T, dctx.T
    weighed = -(dctx.astype(F32) * ctx.astype(F32)).astype(BF16)
    right = jnp.concatenate([v, jnp.ones_like(v)], 1)

    def soft(scores, scale):
        e, total = exp_rows(scores, bias, scale)
        return e * (flag / total)

    for h in range(GROUP):
        dims = slice(h * HEAD_DIM, (h + 1) * HEAD_DIM)
        pair = slice(h // 2 * 2 * TEACH_HD, (h // 2 + 1) * 2 * TEACH_HD)
        tq, tk, tv = tq_in[:, pair], tk_in[:, pair], tv_in[:, pair]
        k_h, v_h = head_mask(k, h, HEAD_DIM), head_mask(v, h, HEAD_DIM)
        p_low = p_in[h]
        teach = soft(dot_nt(head_mask(tq, h % 2, TEACH_HD), tk), TEACH_SCALE)
        left = jnp.concatenate(
            [head_mask(dctx, h, HEAD_DIM), head_mask(weighed, h, HEAD_DIM)], 1
        )
        dp = dot_nt(left, right)
        ds = (p_low.astype(F32) * (dp + flag) - teach).astype(BF16)
        dq = dot_nn(ds, k_h)
        dkt_buf[dims, :] = dot_nn(qt[dims, :], ds) * SCALE
        dvt = dot_nn(dctxt[dims, :], p_low)
        relation = soft(dot_nt(v_h, v), EXP_SCALE)
        teach_rel = soft(dot_nt(head_mask(tv, h % 2, TEACH_HD), tv), TEACH_SCALE)
        drel = (relation - teach_rel).astype(BF16)
        dvt_buf[dims, :] = dvt + SCALE * dot_nn(vt[dims, :], drel)
        rel = dot_nn(drel, v_h)
        if h == 0:
            dq_buf[...] = dq
            rel_buf[...] = rel
        else:
            dq_buf[...] += dq
            rel_buf[...] += rel
    finish_block(
        tokens[...],
        dq_buf[...] * SCALE,
        dkt_buf[...],
        dvt_buf[...] + SCALE * rel_buf[...].T,
        dq_out,
        dkt_out,
        dvt_out,
        acc,
        bias_acc,
    )

    @pl.when(step == pl.num_programs(0) - 1)
    def _():
        width = tokens.shape[1]
        for w in range(3):
            part = acc[w * LANES : (w + 1) * LANES, :].T
            sum_out[w * width : (w + 1) * width, :] = part.astype(BF16)
        tail = jnp.concatenate([bias_acc[...], jnp.zeros((120, LANES), F32)], 0)
        sum_out[3 * width :, :] = tail.astype(BF16)


def backward_specs(g, width, first):
    wide = GROUP * TEACH_HD
    group_spec = pl.BlockSpec((BLOCK, LANES), lambda i: (i + first, g))
    teach_spec = pl.BlockSpec((BLOCK, wide), lambda i: (i + first, g))
    row_spec = pl.BlockSpec((BLOCK, width), lambda i: (i + first, 0))
    outs = [
        pl.BlockSpec((BLOCK, LANES), lambda i: (i + first, 0)),
        pl.BlockSpec((LANES, BLOCK), lambda i: (0, i + first)),
        pl.BlockSpec((LANES, BLOCK), lambda i: (0, i + first)),
    ]
    return [smem(), row_spec] + [group_spec] * 5 + [teach_spec] * 3, outs


def backward_shapes(rows, width):
    grads = [
        jax.ShapeDtypeStruct((rows, LANES), BF16),
        jax.ShapeDtypeStruct((LANES, rows), BF16),
        jax.ShapeDtypeStruct((LANES, rows), BF16),
    ]
    acc = jax.ShapeDtypeStruct((3 * LANES, width), F32)
    bias_acc = jax.ShapeDtypeStruct((8, LANES), F32)
    buffers = [
        pltpu.VMEM((BLOCK, LANES), F32),
        pltpu.VMEM((LANES, BLOCK), F32),
        pltpu.VMEM((LANES, BLOCK), F32),
    ]
    return grads, acc, bias_acc, buffers


def short_backward(g, blocks, lengths, tokens, acts, p_short):
    rows, width = tokens.shape
    grads, acc, bias_acc, buffers = backward_shapes(rows, width)
    ins, outs = backward_specs(g, width, 0)
    return pl.pallas_call(
        short_backward_kernel,
        grid=(blocks,),
        in_specs=ins + [pl.BlockSpec((1, BLOCK, BLOCK), lambda i: (g, i, 0))],
        out_specs=outs + [whole(acc.shape), whole(bias_acc.shape)],
        out_shape=grads + [acc, bias_acc],
        scratch_shapes=buffers,
        compiler_params=params(),
        cost_estimate=pl.CostEstimate(
            flops=9_000_000_000, bytes_accessed=8_000_000, transcendentals=2_000_000
        ),
        name=f"short_backward_{g}",
    )(lengths, tokens, *acts, p_short)


def long_backward(g, first, lengths, tokens, acts, p_long, state, sums):
    rows, width = tokens.shape
    grads, acc, bias_acc, buffers = backward_shapes(rows, width)
    ins, outs = backward_specs(g, width, first)
    dq, dkt, dvt, acc_v, bias_v = state
    *grads, sums = pl.pallas_call(
        long_backward_kernel,
        grid=(lengths.shape[0],),
        in_specs=ins
        + [pl.BlockSpec((GROUP, BLOCK, BLOCK), lambda i: (g, i, 0))]
        + [whole(acc.shape), whole(bias_acc.shape)]
        + [pl.BlockSpec(memory_space=pl.ANY)] * 4,
        out_specs=outs + [pl.BlockSpec((sums.shape[0] // GROUPS, LANES), lambda i: (g, 0))],
        out_shape=grads + [jax.ShapeDtypeStruct(sums.shape, sums.dtype)],
        scratch_shapes=buffers
        + [
            pltpu.VMEM((BLOCK, LANES), F32),
            pltpu.VMEM(acc.shape, F32),
            pltpu.VMEM(bias_acc.shape, F32),
        ],
        input_output_aliases={13: 0, 14: 1, 15: 2, 16: 3},
        compiler_params=params(),
        cost_estimate=pl.CostEstimate(
            flops=18_000_000_000, bytes_accessed=10_000_000, transcendentals=6_000_000
        ),
        name=f"long_backward_{g}",
    )(lengths, tokens, *acts, p_long, acc_v, bias_v, dq, dkt, dvt, sums)
    return grads, sums


def tokens_grad_kernel(dres, wq, wk, wv, *refs):
    out = refs[-1]
    total = dres[...]
    for g in range(GROUPS):
        dq, dkt, dvt = refs[3 * g : 3 * g + 3]
        cols = slice(g * LANES, (g + 1) * LANES)
        total = total + dot_nt(dq[...], wq[:, cols])
        total = total + dot_tt(dkt[...], wk[:, cols])
        total = total + dot_tt(dvt[...], wv[:, cols])
    out[...] = total.astype(BF16)


def tokens_gradient(dres, wq, wk, wv, parts):
    rows, width = dres.shape
    row_spec = pl.BlockSpec((BLOCK, width), lambda i: (i, 0))
    side = pl.BlockSpec((LANES, BLOCK), lambda i: (0, i))
    return pl.pallas_call(
        tokens_grad_kernel,
        grid=(rows // BLOCK,),
        in_specs=[row_spec]
        + [whole(wq.shape)] * 3
        + [pl.BlockSpec((BLOCK, LANES), lambda i: (i, 0)), side, side] * GROUPS,
        out_specs=row_spec,
        out_shape=jax.ShapeDtypeStruct((rows, width), BF16),
        compiler_params=params(),
        cost_estimate=pl.CostEstimate(
            flops=2_000_000_000, bytes_accessed=10_000_000, transcendentals=0
        ),
        name="tokens_gradient",
    )(dres, wq, wk, wv, *[part for trio in parts for part in trio])


def swap(value):
    return lax.ppermute(value, "tensor", [(0, 1), (1, 0)])


def spread(value):
    return lax.all_to_all(value, "dp", 0, 0, tiled=True)


def gather(value):
    return lax.all_gather(value, "dp", axis=0, tiled=True)


def add_low(first, *others):
    total = first.astype(F32)
    for other in others:
        total = total + other.astype(F32)
    return total.astype(BF16)


def halves(block):
    size = block.shape[0] // 2
    mine = lax.axis_index("tensor")
    keep = lax.dynamic_slice_in_dim(block, mine * size, size, 0)
    give = lax.dynamic_slice_in_dim(block, (1 - mine) * size, size, 0)
    return keep, give


def join(first, second):
    mine = lax.axis_index("tensor")
    low = jnp.where(mine == 0, first, second)
    high = jnp.where(mine == 0, second, first)
    return jnp.concatenate([low, high], 0)


def scatter_sum(block, count, span):
    rows, width = block.shape
    (got,) = yield span, [(spread, block.reshape(count, rows // count, width))]
    return jnp.sum(got.astype(F32), axis=0).astype(BF16)


def qkv_chain(summed, count):
    keep, give = halves(summed)
    (got,) = yield 1, [(swap, give)]
    part = yield from scatter_sum(add_low(keep, got), count, 1)
    every = jnp.broadcast_to(part[None], (count, *part.shape))
    (got,) = yield 1, [(spread, every)]
    total = got.reshape(keep.shape)
    (got,) = yield 1, [(swap, total)]
    return join(total, got)


def first_chain(ffn_mine, ffn_other, attn_sum, count, steps):
    keep, give = halves(attn_sum)
    got_ffn, got_attn = yield 1, [(swap, ffn_other), (swap, give)]
    ffn_rows = ffn_mine.shape[0]
    both = jnp.concatenate([add_low(ffn_mine, got_ffn), add_low(keep, got_attn)], 0)
    part = yield from scatter_sum(both, count, 2)
    (total,) = yield steps - 3, [(gather, part)]
    attn = total[ffn_rows:]
    (got,) = yield 1, [(swap, attn)]
    return total[:ffn_rows], join(attn, got)


class Flights:
    def __init__(self):
        self.asked = {}
        self.flying = {}
        self.done = {}

    def advance(self, name, generator, got=None):
        try:
            span, wants = next(generator) if got is None else generator.send(got)
            self.asked[name] = (generator, span, wants)
        except StopIteration as end:
            self.done[name] = end.value

    def busy(self):
        return bool(self.asked or self.flying)

    def step(self, token, work=None):
        asked, self.asked = self.asked, {}
        sends = [value for _, _, wants in asked.values() for _, value in wants]
        token, *sends = lax.optimization_barrier((token, *sends))
        sent = iter(sends)
        for name, (generator, span, wants) in asked.items():
            self.flying[name] = [generator, span, [move(next(sent)) for move, _ in wants]]
        result = None
        if work is not None:
            result, token = work(token)
        landed = []
        for name, flight in self.flying.items():
            flight[1] -= 1
            if flight[1] <= 0 or work is None:
                landed.append(name)
        for name in landed:
            generator, _, got = self.flying.pop(name)
            if work is not None:
                token, *got = lax.optimization_barrier((token, *got))
            self.advance(name, generator, got)
        return result, token


def per_device(
    dp_count,
    tokens,
    query_weight,
    query_bias,
    key_weight,
    value_weight,
    value_bias,
    proj_weight,
    proj_bias,
    first_gain,
    first_shift,
    up_weight,
    up_bias,
    down_weight,
    down_bias,
    second_gain,
    second_shift,
    teach_query,
    teach_key,
    teach_value,
    short_lengths,
    long_lengths,
    cotangent,
):
    width = tokens.shape[1]
    half = up_weight.shape[1]

    up_other, down_other, ub_other = (
        swap(value) for value in (up_weight, down_weight, up_bias.reshape(1, -1))
    )
    vectors = jnp.stack(
        [
            query_bias,
            value_bias,
            proj_bias,
            first_gain,
            first_shift,
            down_bias,
            second_gain,
            second_shift,
        ]
    ).astype(F32)
    q, k, v, ctx, p_short, p_long = attention_forward(
        tokens, query_weight, key_weight, value_weight, vectors, short_lengths, long_lengths
    )
    block_out, dres, dctx, ffn_mine, ffn_other, attn_sum = middle(
        tokens,
        ctx,
        cotangent,
        vectors,
        proj_weight,
        (up_weight, up_other),
        (up_bias.reshape(1, -1), ub_other),
        (down_weight, down_other),
    )
    flights = Flights()
    flights.advance("first", first_chain(ffn_mine, ffn_other, attn_sum, dp_count, 2 * GROUPS))
    acts = (q, k, v, ctx, dctx, teach_query, teach_key, teach_value)
    short_blocks = short_lengths.shape[0] * SHORT_LEN // BLOCK
    parts = []
    token = short_lengths
    sums = jnp.zeros((GROUPS * (3 * width + 128), LANES), BF16)
    for g in range(GROUPS):

        def short_work(lens):
            out = short_backward(g, short_blocks, lens, tokens, acts, p_short)
            return out[:4], out[4]

        state, bias_sum = flights.step(token, short_work)

        def long_work(bias_in):
            return long_backward(
                g, short_blocks, long_lengths, tokens, acts, p_long, [*state, bias_in], sums
            )

        grads, sums = flights.step(bias_sum, long_work)
        parts.append(grads)
        if g < GROUPS - 1:
            token, sums = lax.optimization_barrier((short_lengths, sums))
    flights.advance("qkv", qkv_chain(sums, dp_count))
    tokens_grad = tokens_gradient(dres, query_weight, key_weight, value_weight, parts)
    while flights.busy():
        flights.step(short_lengths)

    ffn, attn = flights.done["first"]
    ffn = ffn.astype(F32)
    attn = attn.astype(F32)
    count = half // width
    up_grad = jnp.concatenate([ffn[i * width : (i + 1) * width] for i in range(count)], 1)
    down_grad = ffn[half : 2 * half]
    up_bias_grad = ffn[2 * half : 2 * half + count].reshape(half)
    vectors = attn[width : width + 6]
    qkv = flights.done["qkv"].reshape(GROUPS, -1, LANES).astype(F32)

    def columns(start, stop):
        return jnp.concatenate([qkv[g, start:stop] for g in range(GROUPS)], 1)

    biases = columns(3 * width, 3 * width + 2)
    return (
        block_out,
        tokens_grad,
        columns(0, width),
        biases[0],
        columns(width, 2 * width),
        columns(2 * width, 3 * width),
        biases[1],
        attn[:width],
        vectors[0],
        vectors[1],
        vectors[2],
        up_grad,
        up_bias_grad,
        down_grad,
        vectors[3],
        vectors[4],
        vectors[5],
    )


def solution(mesh):
    in_specs = (
        P(("dp", "tensor"), None),
        P(),
        P(),
        P(),
        P(),
        P(),
        P(),
        P(),
        P(),
        P(),
        P(None, "tensor"),
        P("tensor"),
        P("tensor", None),
        P(),
        P(),
        P(),
        P(("dp", "tensor"), None),
        P(("dp", "tensor"), None),
        P(("dp", "tensor"), None),
        P(("dp", "tensor")),
        P(("dp", "tensor")),
        P(("dp", "tensor"), None),
    )
    out_specs = (
        P(("dp", "tensor"), None),
        P(("dp", "tensor"), None),
        P(),
        P(),
        P(),
        P(),
        P(),
        P(),
        P(),
        P(),
        P(),
        P(None, "tensor"),
        P("tensor"),
        P("tensor", None),
        P(),
        P(),
        P(),
    )
    return jax.shard_map(
        functools.partial(per_device, mesh.shape["dp"]),
        mesh=mesh,
        in_specs=in_specs,
        out_specs=out_specs,
        check_vma=False,
    )
```

```python
import functools

import jax
import jax.numpy as jnp
from jax import lax
from jax.experimental import pallas as pl
from jax.experimental.pallas import tpu as pltpu
from jax.sharding import PartitionSpec as P

HEADS = 12
HEAD_DIM = 32
TEACH_HD = 64
SHORT_LEN = 128
GROUP = 4
LANES = GROUP * HEAD_DIM
GROUPS = HEADS // GROUP
BLOCK = 512

MASKED = -1e30
LIMIT = 110.0
EPSILON = 1e-06
LOG2E = 1.4426950408889634
SCALE = HEAD_DIM**-0.5
EXP_SCALE = LOG2E * SCALE
TEACH_SCALE = LOG2E * TEACH_HD**-0.5
VMEM_BYTES = 56 * 2**20

F32 = jnp.float32
BF16 = jnp.bfloat16


def dot_nn(left, right):
    return lax.dot_general(left, right, (((1,), (0,)), ((), ())), preferred_element_type=F32)


def dot_nt(left, right):
    return lax.dot_general(left, right, (((1,), (1,)), ((), ())), preferred_element_type=F32)


def dot_tn(left, right):
    return lax.dot_general(left, right, (((0,), (0,)), ((), ())), preferred_element_type=F32)


def dot_tt(left, right):
    return lax.dot_general(left, right, (((0,), (1,)), ((), ())), preferred_element_type=F32)


def lane_row(condition, width=LANES):
    lane = lax.broadcasted_iota(jnp.int32, (1, width), 1)
    return condition(lane).astype(F32).astype(BF16)


def head_mask(block, head, width):
    return block * lane_row(lambda lane: lane // width == head, block.shape[1])


def scaled(block, factor):
    return (block.astype(F32) * factor).astype(BF16)


def peaks(block, width):
    size = block.shape[1]
    head = lax.broadcasted_iota(jnp.int32, (size, LANES), 0) // width
    own = (head == lax.broadcasted_iota(jnp.int32, (size, LANES), 1)).astype(F32).astype(BF16)
    return jnp.max(dot_nn(block * block, own), axis=0, keepdims=True)


def spare_lane(head, width):
    return LANES - width if head * width < LANES // 2 else 0


def with_bias(keys, lane, length):
    row = lax.broadcasted_iota(jnp.int32, keys.shape, 0)
    column = lax.broadcasted_iota(jnp.int32, keys.shape, 1)
    bias = jnp.where(row < length, 0.0, MASKED).astype(BF16)
    return jnp.where(column == lane, bias, keys)


def masked_sides(queries, keys, head, width):
    lane = spare_lane(head, width)
    one = lane_row(lambda index: index == lane)
    return head_mask(queries, head, width) + one, keys[lane]


def biased(keys, width, length):
    return {lane: with_bias(keys, lane, length) for lane in (LANES - width, 0)}


def query_flag(length, size):
    return (lax.broadcasted_iota(jnp.int32, (size, 1), 0) < length).astype(F32)


def weave(works):
    ticks = max(count for _, count in works)
    for tick in range(ticks):
        for work, count in works:
            if (tick + 1) * count // ticks > tick * count // ticks:
                next(work)
    for work, _ in works:
        for _ in work:
            pass


def exps(scores, axis, careful):
    if careful:
        scores = scores - jnp.max(scores, axis=axis, keepdims=True)
    heights = jnp.exp2(scores)
    return heights, jnp.sum(heights, axis=axis, keepdims=True)


def low_rows(column, size):
    block = jnp.broadcast_to(column, (column.shape[0], LANES)).astype(BF16)
    return jnp.concatenate([block] * (size // LANES), 1)


def short_bias(length):
    shape = (SHORT_LEN, GROUP * SHORT_LEN)
    return jnp.where(lax.broadcasted_iota(jnp.int32, shape, 0) < length, 0.0, MASKED)


def stack(block, width):
    return jnp.concatenate([head_mask(block, h, width) for h in range(GROUP)], 0)


def diagonal(block):
    return jnp.concatenate(
        [
            block[h * HEAD_DIM : (h + 1) * HEAD_DIM, h * SHORT_LEN : (h + 1) * SHORT_LEN]
            for h in range(GROUP)
        ],
        0,
    )


def params():
    return pltpu.CompilerParams(vmem_limit_bytes=VMEM_BYTES)


def whole(shape):
    return pl.BlockSpec(shape, lambda i: (0,) * len(shape))


def smem():
    return pl.BlockSpec(memory_space=pltpu.SMEM)


def forward_kernel(
    short_blocks,
    short_len,
    long_len,
    tokens,
    wq,
    wk,
    wv,
    vectors,
    q_out,
    k_out,
    v_out,
    ctx_out,
    ps_out,
    pl_out,
):
    step = pl.program_id(0)
    x = tokens[...]
    q_out[...] = (dot_nn(x, wq[...]) + vectors[0:1, :]).astype(BF16)
    k_out[...] = dot_nn(x, wk[...]).astype(BF16)
    v_out[...] = (dot_nn(x, wv[...]) + vectors[1:2, :]).astype(BF16)

    shift = EXP_SCALE * EXP_SCALE
    bound = jnp.max(peaks(q_out[...], HEAD_DIM) * peaks(k_out[...], HEAD_DIM)) * shift
    tame = bound < LIMIT * LIMIT

    def short_items(careful):
        items = BLOCK // SHORT_LEN

        @pl.loop(0, items)
        def _(item):
            rows = pl.ds(pl.multiple_of(item * SHORT_LEN, SHORT_LEN), SHORT_LEN)
            bias = short_bias(short_len[step * items + item])
            for g in range(GROUPS):
                cols = slice(g * LANES, (g + 1) * LANES)
                q, k, v = q_out[rows, cols], k_out[rows, cols], v_out[rows, cols]
                queries = stack(scaled(q, EXP_SCALE), HEAD_DIM)
                e, total = exps(dot_nt(k, queries) + bias, 0, careful)
                probs = e.astype(BF16) * (1.0 / total).astype(BF16)
                ps_out[g, rows, :] = probs
                ctx_out[rows, cols] = diagonal(dot_tn(v, probs)).T.astype(BF16)

    def long_item(careful):
        length = long_len[step - short_blocks]

        @pl.loop(0, GROUPS)
        def _(g):
            cols = pl.ds(pl.multiple_of(g * LANES, LANES), LANES)
            q = scaled(q_out[:, cols], EXP_SCALE)
            k = biased(k_out[:, cols], HEAD_DIM, length)
            v = v_out[:, cols]
            for h in range(GROUP):
                e, total = exps(dot_nt(*masked_sides(q, k, h, HEAD_DIM)), 1, careful)
                pl_out[g * GROUP + h] = e.astype(BF16) * low_rows(1.0 / total, BLOCK)
            probs = jnp.concatenate([pl_out[g * GROUP + h] for h in range(GROUP)], 1)
            ctx_out[:, cols] = dot_nn(probs, stack(v, HEAD_DIM)).astype(BF16)

    short = step < short_blocks
    for careful, chosen in ((False, tame), (True, jnp.logical_not(tame))):
        pl.when(jnp.logical_and(short, chosen))(functools.partial(short_items, careful))
        pl.when(jnp.logical_and(jnp.logical_not(short), chosen))(
            functools.partial(long_item, careful)
        )


def attention_forward(tokens, wq, wk, wv, vectors, short_len, long_len):
    rows, width = tokens.shape
    blocks = rows // BLOCK
    short_blocks = short_len.shape[0] * SHORT_LEN // BLOCK
    long_blocks = blocks - short_blocks
    row_spec = pl.BlockSpec((BLOCK, width), lambda i: (i, 0))
    act = jax.ShapeDtypeStruct((rows, width), BF16)
    return pl.pallas_call(
        functools.partial(forward_kernel, short_blocks),
        grid=(blocks,),
        in_specs=[smem(), smem(), row_spec]
        + [whole(a.shape) for a in (wq, wk, wv, vectors)],
        out_specs=[
            row_spec,
            row_spec,
            row_spec,
            row_spec,
            pl.BlockSpec((GROUPS, BLOCK, BLOCK), lambda i: (0, jnp.minimum(i, short_blocks - 1), 0)),
            pl.BlockSpec((HEADS, BLOCK, BLOCK), lambda i: (0, jnp.maximum(i - short_blocks, 0), 0)),
        ],
        out_shape=[
            act,
            act,
            act,
            act,
            jax.ShapeDtypeStruct((GROUPS, short_blocks * BLOCK, BLOCK), BF16),
            jax.ShapeDtypeStruct((HEADS, long_blocks * BLOCK, BLOCK), BF16),
        ],
        compiler_params=params(),
        cost_estimate=pl.CostEstimate(
            flops=12_000_000_000, bytes_accessed=24_000_000, transcendentals=8_000_000
        ),
        name="attention_forward",
    )(short_len, long_len, tokens, wq, wk, wv, vectors)


def norm_parts(resid):
    centred = resid - jnp.mean(resid, axis=-1, keepdims=True)
    spread = jnp.mean(centred * centred, axis=-1, keepdims=True)
    root = lax.rsqrt(spread + EPSILON)
    return centred * root, root


def norm_back(grad, y, root):
    return root * (
        grad
        - jnp.mean(grad, axis=-1, keepdims=True)
        - y * jnp.mean(grad * y, axis=-1, keepdims=True)
    )


def column_sum(block):
    return jnp.sum(block.astype(F32), axis=0, keepdims=True)


def middle_kernel(
    tokens,
    ctx,
    cot,
    vectors,
    wo,
    up0,
    up1,
    ub0,
    ub1,
    dn0,
    dn1,
    block_out,
    dres_out,
    dctx_out,
    ffn0_out,
    ffn1_out,
    attn_out,
    acc_up,
    acc_dn,
    acc_wo,
    acc_ub,
    acc_vec,
    slope,
    active,
):
    step = pl.program_id(0)
    half = up0.shape[1]
    width = up0.shape[0]

    @pl.when(step == 0)
    def _():
        for ref in (acc_up, acc_dn, acc_wo, acc_ub, acc_vec):
            ref[...] = jnp.zeros_like(ref)

    bo, gain1, shift1, db, gain2, shift2 = (vectors[i : i + 1, :] for i in range(2, 8))
    ctx_low = ctx[...]
    resid = tokens[...].astype(F32) + dot_nn(ctx_low, wo[...]) + bo
    y1, root1 = norm_parts(resid)
    normed = y1 * gain1 + shift1
    normed_low = normed.astype(BF16)
    mid = normed + db
    for j, (up, ub, dn) in enumerate(((up0, ub0, dn0), (up1, ub1, dn1))):
        pre = dot_nn(normed_low, up[...]) + ub[...].astype(F32)
        phi = 0.5 + 0.5 * lax.erf(pre * (0.5**0.5))
        act = (pre * phi).astype(BF16)
        slope[j] = phi + pre * (jnp.exp2(pre * pre * (-0.5 * LOG2E)) * 0.3989422804014327)
        active[j] = act
        mid = mid + dot_nn(act, dn[...])
    y2, root2 = norm_parts(mid)
    block_out[...] = (y2 * gain2 + shift2).astype(BF16)
    cotangent = cot[...].astype(F32)
    dmid = norm_back(cotangent * gain2, y2, root2)
    dbranch = dmid.astype(BF16)
    acc_vec[3:4, :] += column_sum(dbranch)
    acc_vec[4:5, :] += column_sum(cotangent * y2)
    acc_vec[5:6, :] += column_sum(cotangent)
    dnormed = dmid
    for j, (up, dn) in enumerate(((up0, dn0), (up1, dn1))):
        acc_dn[j] += dot_tn(active[j], dbranch)
        dpre = (dot_nt(dbranch, dn[...]) * slope[j]).astype(BF16)
        acc_up[j] += dot_tn(normed_low, dpre)
        acc_ub[j : j + 1, :] += column_sum(dpre)
        dnormed = dnormed + dot_nt(dpre, up[...])
    acc_vec[1:2, :] += column_sum(dnormed * y1)
    acc_vec[2:3, :] += column_sum(dnormed)
    dres = norm_back(dnormed * gain1, y1, root1)
    dres_out[...] = dres
    dattn = dres.astype(BF16)
    acc_vec[0:1, :] += column_sum(dattn)
    acc_wo[...] += dot_tn(ctx_low, dattn)
    dctx_out[...] = dot_nt(dattn, wo[...]).astype(BF16)

    @pl.when(step == pl.num_programs(0) - 1)
    def _():
        for j, out in enumerate((ffn0_out, ffn1_out)):
            for part in range(half // width):
                cols = slice(part * width, (part + 1) * width)
                out[part * width : (part + 1) * width, :] = acc_up[j, :, cols].astype(BF16)
            out[half : 2 * half, :] = acc_dn[j].astype(BF16)
            pads = [
                acc_ub[j : j + 1, part * width : (part + 1) * width]
                for part in range(half // width)
            ]
            pads.append(jnp.zeros((16 - len(pads), width), F32))
            out[2 * half :, :] = jnp.concatenate(pads, 0).astype(BF16)
        attn_out[:width, :] = acc_wo[...].astype(BF16)
        tail = jnp.concatenate([acc_vec[...], jnp.zeros((88, width), F32)], 0)
        attn_out[width:, :] = tail.astype(BF16)


def middle(tokens, ctx, cot, vectors, wo, ups, ubs, dns):
    rows, width = tokens.shape
    half = ups[0].shape[1]
    row_spec = pl.BlockSpec((BLOCK, width), lambda i: (i, 0))
    weights = (vectors, wo, *ups, *ubs, *dns)
    act = jax.ShapeDtypeStruct((rows, width), BF16)
    ffn = jax.ShapeDtypeStruct((2 * half + 16, width), BF16)
    attn = jax.ShapeDtypeStruct((width + 96, width), BF16)
    return pl.pallas_call(
        middle_kernel,
        grid=(rows // BLOCK,),
        in_specs=[row_spec] * 3 + [whole(w.shape) for w in weights],
        out_specs=[row_spec] * 3 + [whole(ffn.shape), whole(ffn.shape), whole(attn.shape)],
        out_shape=[act, jax.ShapeDtypeStruct((rows, width), F32), act, ffn, ffn, attn],
        scratch_shapes=[
            pltpu.VMEM((2, width, half), F32),
            pltpu.VMEM((2, half, width), F32),
            pltpu.VMEM((width, width), F32),
            pltpu.VMEM((8, half), F32),
            pltpu.VMEM((8, width), F32),
            pltpu.VMEM((2, BLOCK, half), F32),
            pltpu.VMEM((2, BLOCK, half), BF16),
        ],
        compiler_params=params(),
        cost_estimate=pl.CostEstimate(
            flops=34_000_000_000, bytes_accessed=20_000_000, transcendentals=6_000_000
        ),
        name="middle",
    )(tokens, ctx, cot, *weights)


def backward_kernel(
    first,
    blocks,
    short_blocks,
    short_len,
    long_len,
    tokens,
    q_in,
    k_in,
    v_in,
    ctx_in,
    dctx_in,
    tq_in,
    tk_in,
    tv_in,
    ps_in,
    pl_in,
    grad_out,
    sum_out,
    acc,
    bias_acc,
    dq_buf,
    dk_buf,
    dv_buf,
    dkt_buf,
    dvt_buf,
    dp_buf,
    exp_buf,
    total_buf,
    ds_buf,
    drel_buf,
):
    block = lax.rem(first + pl.program_id(0), blocks)

    @pl.when(block == 0)
    def _():
        acc[...] = jnp.zeros_like(acc)
        bias_acc[...] = jnp.zeros_like(bias_acc)

    teach_peak = peaks(tq_in[...], TEACH_HD) * peaks(tk_in[...], TEACH_HD)
    rel_peak = peaks(tv_in[...], TEACH_HD)
    own_peak = peaks(v_in[...], HEAD_DIM) * EXP_SCALE
    bound = jnp.maximum(teach_peak, rel_peak * rel_peak) * (TEACH_SCALE * TEACH_SCALE)
    tame = jnp.max(jnp.maximum(bound, own_peak * own_peak)) < LIMIT * LIMIT


    def teach_scores(keys, queries):
        queries = scaled(queries, TEACH_SCALE)
        parts = []
        for pair in range(GROUP // 2):
            cols = slice(pair * LANES, (pair + 1) * LANES)
            both = jnp.concatenate([head_mask(queries[:, cols], h, TEACH_HD) for h in range(2)], 0)
            parts.append(dot_nt(keys[:, cols], both))
        return jnp.concatenate(parts, 1)

    def short_item(careful, item):
        start = item * SHORT_LEN
        if careful:
            start = pl.multiple_of(start, SHORT_LEN)
        rows = pl.ds(start, SHORT_LEN)
        length = short_len[block * (BLOCK // SHORT_LEN) + item]
        bias = short_bias(length)
        lane = lax.broadcasted_iota(jnp.int32, (1, GROUP * SHORT_LEN), 1)
        flag = (lane % SHORT_LEN < length).astype(F32)
        q, k, v = q_in[rows, :], k_in[rows, :], v_in[rows, :]
        dctx, ctx = dctx_in[rows, :], ctx_in[rows, :]
        tq, tk, tv = tq_in[rows, :], tk_in[rows, :], tv_in[rows, :]
        q_all, v_all, dctx_all = (stack(part, HEAD_DIM) for part in (q, v, dctx))
        p = ps_in[0, rows, :]

        def soft(scores):
            e, total = exps(scores + bias, 0, careful)
            return e.astype(BF16) * (flag / total).astype(BF16)

        weighed = (dctx.astype(F32) * ctx.astype(F32)).T
        delta = jnp.concatenate(
            [
                jnp.sum(weighed[h * HEAD_DIM : (h + 1) * HEAD_DIM], axis=0, keepdims=True)
                for h in range(GROUP)
            ],
            1,
        )
        dp = (dot_nt(v, dctx_all) + (flag - delta)).astype(BF16)
        ds = p * dp - soft(teach_scores(tk, tq))
        dq_buf[rows, :] = diagonal(dot_tn(k, ds)).T * SCALE
        dk_buf[rows, :] = dot_nn(ds, q_all) * SCALE
        own = soft(dot_nt(v, stack(scaled(v, EXP_SCALE), HEAD_DIM)))
        drel = own - soft(teach_scores(tv, tv))
        rel = dot_nn(drel, v_all) + diagonal(dot_tn(v, drel)).T
        dv_buf[rows, :] = dot_nn(p, dctx_all) + SCALE * rel

    def short_items(careful):
        if careful:
            pl.loop(0, BLOCK // SHORT_LEN)(functools.partial(short_item, True))
        else:
            for item in range(BLOCK // SHORT_LEN):
                short_item(False, item)


    def long_item():
        length = long_len[block - short_blocks]
        q, k, v = q_in[...], k_in[...], v_in[...]
        dctx, ctx = dctx_in[...], ctx_in[...]
        qt, vt, dctxt = q.T, v.T, dctx.T
        weighed = -(dctx.astype(F32) * ctx.astype(F32)).astype(BF16)
        right = jnp.concatenate([v, jnp.ones_like(v)], 1)
        v_scaled = scaled(v, EXP_SCALE)
        v_keys = biased(v, HEAD_DIM, length)
        flag = query_flag(length, BLOCK)
        flags = jnp.broadcast_to(flag, v.shape).astype(BF16)
        teach = {}

        def teach_pair(source, pair):
            if (source, pair) not in teach:
                part = (tq_in, tk_in, tv_in)[source][:, pair * LANES : (pair + 1) * LANES]
                teach[source, pair] = (
                    biased(part, TEACH_HD, length) if source else None,
                    None if source == 1 else scaled(part, TEACH_SCALE),
                )
            return teach[source, pair]

        def sides(kind, h):
            if kind == 0:
                left, keys = teach_pair(0, h // 2)[1], teach_pair(1, h // 2)[0]
                return masked_sides(left, keys, h % 2, TEACH_HD)
            if kind == 1:
                return masked_sides(v_scaled, v_keys, h, HEAD_DIM)
            if kind == 2:
                keys, left = teach_pair(2, h // 2)
                return masked_sides(left, keys, h % 2, TEACH_HD)
            lane = spare_lane(h, HEAD_DIM)
            extra = head_mask(weighed, h, HEAD_DIM) + flags * lane_row(lambda i: i == lane)
            return jnp.concatenate([head_mask(dctx, h, HEAD_DIM), extra], 1), right

        halves = [slice(i * (BLOCK // 2), (i + 1) * (BLOCK // 2)) for i in range(2)]

        def score_items(h):
            for kind in range(4):
                left, keys = sides(kind, h)
                for j, cols in enumerate(halves):
                    scores = dot_nt(left, keys[cols])
                    if kind == 3:
                        dp_buf[h % 2, :, cols] = scores.astype(BF16)
                    else:
                        e = jnp.exp2(scores)
                        exp_buf[h % 2, kind, :, cols] = e.astype(BF16)
                        part = e[:, :LANES] + e[:, LANES:]
                        if j == 0:
                            total_buf[h % 2, kind] = part
                        else:
                            total_buf[h % 2, kind] += part
                    yield

        def product_items(h):
            dims = slice(h * HEAD_DIM, (h + 1) * HEAD_DIM)
            ds, drel = ds_buf.at[h % 2], drel_buf.at[h % 2]
            for cols in halves:
                dvt_buf[dims, cols] = dot_nn(dctxt[dims, :], pl_in[h, :, cols])
                yield
                dkt_buf[dims, cols] = dot_nn(qt[dims, :], ds[:, cols]) * SCALE
                yield
                dvt_buf[dims, cols] += SCALE * dot_nn(vt[dims, :], drel[:, cols])
                yield
            for buf, grads, keys in ((dq_buf, ds, k), (dv_buf, drel, v)):
                part = dot_nn(grads[...], head_mask(keys, h, HEAD_DIM))
                if h == 0:
                    buf[...] = part
                else:
                    buf[...] += part
                yield

        def row_items(h):
            count = BLOCK // 8
            for i in range(8):
                rows = slice(i * count, (i + 1) * count)

                def soft(kind):
                    total = jnp.sum(total_buf[h % 2, kind, rows, :], axis=1, keepdims=True)
                    return exp_buf[h % 2, kind, rows, :] * low_rows(flag[rows] / total, BLOCK)

                ds_buf[h % 2, rows, :] = pl_in[h, rows, :] * dp_buf[h % 2, rows, :] - soft(0)
                drel_buf[h % 2, rows, :] = soft(1) - soft(2)
                yield

        for h in range(-1, GROUP + 1):
            works = []
            if h + 1 < GROUP:
                works.append((score_items(h + 1), 8))
            if 0 <= h < GROUP:
                works.append((row_items(h), 8))
            if h >= 1:
                works.append((product_items(h - 1), 8))
            weave(works)
        dq_buf[...] *= SCALE
        dk_buf[...] = dkt_buf[...].T
        dv_buf[...] = dvt_buf[...].T + SCALE * dv_buf[...]

    def long_item_careful():
        length = long_len[block - short_blocks]
        flag = query_flag(length, BLOCK)
        bias = jnp.where(
            lax.broadcasted_iota(jnp.int32, (1, BLOCK), 1) < length, 0.0, MASKED
        )
        for buf in (dq_buf, dk_buf, dv_buf):
            buf[...] = jnp.zeros_like(buf)

        def soft(queries, keys, h, width, scale):
            scores = dot_nt(head_mask(scaled(queries, scale), h, width), keys)
            e, total = exps(scores + bias, 1, True)
            return e * (flag / total)

        @pl.loop(0, GROUP)
        def _(h):
            q, k, v, dctx = (
                head_mask(ref[...], h, HEAD_DIM) for ref in (q_in, k_in, v_in, dctx_in)
            )
            p = pl_in[h]
            delta = jnp.sum(dctx.astype(F32) * ctx_in[...].astype(F32), axis=1, keepdims=True)
            dp = dot_nt(dctx, v) + (flag - delta)
            teach = soft(tq_in[...], tk_in[...], h, TEACH_HD, TEACH_SCALE)
            ds = (p.astype(F32) * dp - teach).astype(BF16)
            own = soft(v, v, h, HEAD_DIM, EXP_SCALE)
            drel = (own - soft(tv_in[...], tv_in[...], h, TEACH_HD, TEACH_SCALE)).astype(BF16)
            dq_buf[...] += dot_nn(ds, k) * SCALE
            dk_buf[...] += dot_tn(ds, q) * SCALE
            dv_buf[...] += dot_tn(p, dctx) + SCALE * (dot_nn(drel, v) + dot_tn(drel, v))

    short = block < short_blocks
    long = jnp.logical_not(short)
    wild = jnp.logical_not(tame)
    pl.when(jnp.logical_and(short, tame))(functools.partial(short_items, False))
    pl.when(jnp.logical_and(short, wild))(functools.partial(short_items, True))
    pl.when(jnp.logical_and(long, tame))(long_item)
    pl.when(jnp.logical_and(long, wild))(long_item_careful)

    grads = jnp.concatenate([buf[...].astype(BF16) for buf in (dq_buf, dk_buf, dv_buf)], 1)
    grad_out[...] = grads
    acc[...] += dot_tn(tokens[...], grads)
    bias_acc[0:1, :] += column_sum(grads)

    @pl.when(block == blocks - 1)
    def _():
        width = tokens.shape[1]
        for w in range(3):
            cols = slice(w * LANES, (w + 1) * LANES)
            sum_out[w * width : (w + 1) * width, :] = acc[:, cols].astype(BF16)
        sides = [bias_acc[0:1, w * LANES : (w + 1) * LANES] for w in range(3)]
        tail = jnp.concatenate([*sides, jnp.zeros((125, LANES), F32)], 0)
        sum_out[3 * width :, :] = tail.astype(BF16)


def attention_backward(start, stop, short_len, long_len, tokens, acts, p_short, p_long):
    rows, width = tokens.shape
    blocks = rows // BLOCK
    short_blocks = short_len.shape[0] * SHORT_LEN // BLOCK
    count = stop - start

    def place(pick):
        return lambda i: pick(start + i // blocks, i % blocks)

    def group_spec(size):
        return pl.BlockSpec((BLOCK, size), place(lambda g, b: (b, g)))

    p_specs = [
        pl.BlockSpec(
            (1, BLOCK, BLOCK), place(lambda g, b: (g, jnp.minimum(b, short_blocks - 1), 0))
        ),
        pl.BlockSpec(
            (GROUP, BLOCK, BLOCK), place(lambda g, b: (g, jnp.maximum(b - short_blocks, 0), 0))
        ),
    ]
    square = (BLOCK, LANES)
    return pl.pallas_call(
        functools.partial(backward_kernel, start * blocks, blocks, short_blocks),
        grid=(count * blocks,),
        in_specs=[smem(), smem(), pl.BlockSpec((BLOCK, width), place(lambda g, b: (b, 0)))]
        + [group_spec(LANES)] * 5
        + [group_spec(GROUP * TEACH_HD)] * 3
        + p_specs,
        out_specs=[
            pl.BlockSpec((BLOCK, 3 * LANES), place(lambda g, b: (b, g - start))),
            pl.BlockSpec((3 * width + 128, LANES), place(lambda g, b: (g - start, 0))),
        ],
        out_shape=[
            jax.ShapeDtypeStruct((rows, count * 3 * LANES), BF16),
            jax.ShapeDtypeStruct((count * (3 * width + 128), LANES), BF16),
        ],
        scratch_shapes=[
            pltpu.VMEM((width, 3 * LANES), F32),
            pltpu.VMEM((8, 3 * LANES), F32),
            pltpu.VMEM(square, F32),
            pltpu.VMEM(square, F32),
            pltpu.VMEM(square, F32),
            pltpu.VMEM((LANES, BLOCK), F32),
            pltpu.VMEM((LANES, BLOCK), F32),
            pltpu.VMEM((2, BLOCK, BLOCK), BF16),
            pltpu.VMEM((2, 3, BLOCK, BLOCK), BF16),
            pltpu.VMEM((2, 3, BLOCK, LANES), F32),
            pltpu.VMEM((2, BLOCK, BLOCK), BF16),
            pltpu.VMEM((2, BLOCK, BLOCK), BF16),
        ],
        compiler_params=params(),
        cost_estimate=pl.CostEstimate(
            flops=count * 27_000_000_000,
            bytes_accessed=count * 16_000_000,
            transcendentals=count * 8_000_000,
        ),
        name=f"attention_backward_{start}",
    )(short_len, long_len, tokens, *acts, p_short, p_long)


def tokens_grad_kernel(dres, wq, wk, wv, *refs):
    out = refs[-1]
    grads = jnp.concatenate([ref[...] for ref in refs[:-1]], 1)
    weights = jnp.concatenate(
        [w[:, g * LANES : (g + 1) * LANES] for g in range(GROUPS) for w in (wq, wk, wv)], 1
    )
    out[...] = (dres[...] + dot_nt(grads, weights)).astype(BF16)


def tokens_gradient(dres, wq, wk, wv, parts):
    rows, width = dres.shape
    row_spec = pl.BlockSpec((BLOCK, width), lambda i: (i, 0))
    return pl.pallas_call(
        tokens_grad_kernel,
        grid=(rows // BLOCK,),
        in_specs=[row_spec]
        + [whole(wq.shape)] * 3
        + [pl.BlockSpec((BLOCK, part.shape[1]), lambda i: (i, 0)) for part in parts],
        out_specs=row_spec,
        out_shape=jax.ShapeDtypeStruct((rows, width), BF16),
        compiler_params=params(),
        cost_estimate=pl.CostEstimate(
            flops=2_000_000_000, bytes_accessed=10_000_000, transcendentals=0
        ),
        name="tokens_gradient",
    )(dres, wq, wk, wv, *parts)


def swap(value):
    return lax.ppermute(value, "tensor", [(0, 1), (1, 0)])


def spread(value):
    return lax.all_to_all(value, "dp", 0, 0, tiled=True)


def gather(value):
    return lax.all_gather(value, "dp", axis=0, tiled=True)


def add_low(first, *others):
    total = first.astype(F32)
    for other in others:
        total = total + other.astype(F32)
    return total.astype(BF16)


def halves(block):
    size = block.shape[0] // 2
    mine = lax.axis_index("tensor")
    keep = lax.dynamic_slice_in_dim(block, mine * size, size, 0)
    give = lax.dynamic_slice_in_dim(block, (1 - mine) * size, size, 0)
    return keep, give


def join(first, second):
    mine = lax.axis_index("tensor")
    low = jnp.where(mine == 0, first, second)
    high = jnp.where(mine == 0, second, first)
    return jnp.concatenate([low, high], 0)


def scatter_sum(block, count, span):
    rows, width = block.shape
    (got,) = yield span, [(spread, block.reshape(count, rows // count, width))]
    return jnp.sum(got.astype(F32), axis=0).astype(BF16)


def qkv_chain(summed, count):
    keep, give = halves(summed)
    (got,) = yield 1, [(swap, give)]
    part = yield from scatter_sum(add_low(keep, got), count, 1)
    every = jnp.broadcast_to(part[None], (count, *part.shape))
    (got,) = yield 1, [(spread, every)]
    total = got.reshape(keep.shape)
    (got,) = yield 1, [(swap, total)]
    return join(total, got)


def first_chain(ffn_mine, ffn_other, attn_sum, count):
    keep, give = halves(attn_sum)
    got_ffn, got_attn = yield 1, [(swap, ffn_other), (swap, give)]
    ffn_rows = ffn_mine.shape[0]
    both = jnp.concatenate([add_low(ffn_mine, got_ffn), add_low(keep, got_attn)], 0)
    part = yield from scatter_sum(both, count, 1)
    (total,) = yield 1, [(gather, part)]
    attn = total[ffn_rows:]
    (got,) = yield 1, [(swap, attn)]
    return total[:ffn_rows], join(attn, got)


class Flights:
    def __init__(self):
        self.asked = {}
        self.flying = {}
        self.done = {}

    def advance(self, name, generator, got=None):
        try:
            span, wants = next(generator) if got is None else generator.send(got)
            self.asked[name] = (generator, span, wants)
        except StopIteration as end:
            self.done[name] = end.value

    def busy(self):
        return bool(self.asked or self.flying)

    def step(self, token, work=None):
        asked, self.asked = self.asked, {}
        sends = [value for _, _, wants in asked.values() for _, value in wants]
        token, *sends = lax.optimization_barrier((token, *sends))
        sent = iter(sends)
        for name, (generator, span, wants) in asked.items():
            self.flying[name] = [generator, span, [move(next(sent)) for move, _ in wants]]
        result = None
        if work is not None:
            result, token = work(token)
        landed = []
        for name, flight in self.flying.items():
            flight[1] -= 1
            if flight[1] <= 0 or work is None:
                landed.append(name)
        for name in landed:
            generator, _, got = self.flying.pop(name)
            if work is not None:
                token, *got = lax.optimization_barrier((token, *got))
            self.advance(name, generator, got)
        return result, token


def per_device(
    dp_count,
    tokens,
    query_weight,
    query_bias,
    key_weight,
    value_weight,
    value_bias,
    proj_weight,
    proj_bias,
    first_gain,
    first_shift,
    up_weight,
    up_bias,
    down_weight,
    down_bias,
    second_gain,
    second_shift,
    teach_query,
    teach_key,
    teach_value,
    short_lengths,
    long_lengths,
    cotangent,
):
    width = tokens.shape[1]
    half = up_weight.shape[1]

    up_other, down_other, ub_other = (
        swap(value) for value in (up_weight, down_weight, up_bias.reshape(1, -1))
    )
    vectors = jnp.stack(
        [
            query_bias,
            value_bias,
            proj_bias,
            first_gain,
            first_shift,
            down_bias,
            second_gain,
            second_shift,
        ]
    ).astype(F32)
    q, k, v, ctx, p_short, p_long = attention_forward(
        tokens, query_weight, key_weight, value_weight, vectors, short_lengths, long_lengths
    )
    block_out, dres, dctx, ffn_mine, ffn_other, attn_sum = middle(
        tokens,
        ctx,
        cotangent,
        vectors,
        proj_weight,
        (up_weight, up_other),
        (up_bias.reshape(1, -1), ub_other),
        (down_weight, down_other),
    )
    flights = Flights()
    flights.advance("first", first_chain(ffn_mine, ffn_other, attn_sum, dp_count))
    flights.step(short_lengths)
    acts = (q, k, v, ctx, dctx, teach_query, teach_key, teach_value)
    parts = []
    sums = []
    token = short_lengths
    for start, stop in ((0, GROUPS - 1), (GROUPS - 1, GROUPS)):

        def work(lens):
            grads, summed = attention_backward(
                start, stop, lens, long_lengths, tokens, acts, p_short, p_long
            )
            return grads, summed

        grads, summed = flights.step(token, work)
        parts.append(grads)
        sums.append(summed)
        token, sums[-1] = lax.optimization_barrier((short_lengths, summed))
    flights.advance("qkv", qkv_chain(jnp.concatenate(sums, 0), dp_count))
    tokens_grad = tokens_gradient(dres, query_weight, key_weight, value_weight, parts)
    while flights.busy():
        flights.step(short_lengths)

    ffn, attn = flights.done["first"]
    ffn = ffn.astype(F32)
    attn = attn.astype(F32)
    count = half // width
    up_grad = jnp.concatenate([ffn[i * width : (i + 1) * width] for i in range(count)], 1)
    down_grad = ffn[half : 2 * half]
    up_bias_grad = ffn[2 * half : 2 * half + count].reshape(half)
    vectors = attn[width : width + 6]
    qkv = flights.done["qkv"].reshape(GROUPS, -1, LANES).astype(F32)

    def columns(start, stop):
        return jnp.concatenate([qkv[g, start:stop] for g in range(GROUPS)], 1)

    biases = columns(3 * width, 3 * width + 3)
    return (
        block_out,
        tokens_grad,
        columns(0, width),
        biases[0],
        columns(width, 2 * width),
        columns(2 * width, 3 * width),
        biases[2],
        attn[:width],
        vectors[0],
        vectors[1],
        vectors[2],
        up_grad,
        up_bias_grad,
        down_grad,
        vectors[3],
        vectors[4],
        vectors[5],
    )


def solution(mesh):
    in_specs = (
        P(("dp", "tensor"), None),
        P(),
        P(),
        P(),
        P(),
        P(),
        P(),
        P(),
        P(),
        P(),
        P(None, "tensor"),
        P("tensor"),
        P("tensor", None),
        P(),
        P(),
        P(),
        P(("dp", "tensor"), None),
        P(("dp", "tensor"), None),
        P(("dp", "tensor"), None),
        P(("dp", "tensor")),
        P(("dp", "tensor")),
        P(("dp", "tensor"), None),
    )
    out_specs = (
        P(("dp", "tensor"), None),
        P(("dp", "tensor"), None),
        P(),
        P(),
        P(),
        P(),
        P(),
        P(),
        P(),
        P(),
        P(),
        P(None, "tensor"),
        P("tensor"),
        P("tensor", None),
        P(),
        P(),
        P(),
    )
    return jax.shard_map(
        functools.partial(per_device, mesh.shape["dp"]),
        mesh=mesh,
        in_specs=in_specs,
        out_specs=out_specs,
        check_vma=False,
    )
```

```python
import functools

import jax
import jax.numpy as jnp
from jax import lax
from jax.experimental import pallas as pl
from jax.experimental.pallas import tpu as pltpu
from jax.sharding import PartitionSpec as P

HEADS = 12
HEAD_DIM = 32
TEACH_HD = 64
SHORT_LEN = 128
GROUP = 4
LANES = GROUP * HEAD_DIM
GROUPS = HEADS // GROUP
BLOCK = 512
MID_BLOCK = 512
PAD_ROWS = 96

MASKED = -1e30
LIMIT = 110.0
EPSILON = 1e-06
LOG2E = 1.4426950408889634
SCALE = HEAD_DIM**-0.5
EXP_SCALE = LOG2E * SCALE
TEACH_SCALE = LOG2E * TEACH_HD**-0.5
VMEM_BYTES = 56 * 2**20

F32 = jnp.float32
BF16 = jnp.bfloat16


def dot_nn(left, right):
    return lax.dot_general(left, right, (((1,), (0,)), ((), ())), preferred_element_type=F32)


def dot_nt(left, right):
    return lax.dot_general(left, right, (((1,), (1,)), ((), ())), preferred_element_type=F32)


def dot_tn(left, right):
    return lax.dot_general(left, right, (((0,), (0,)), ((), ())), preferred_element_type=F32)


def dot_tt(left, right):
    return lax.dot_general(left, right, (((0,), (1,)), ((), ())), preferred_element_type=F32)


def lane_row(condition, width=LANES):
    lane = lax.broadcasted_iota(jnp.int32, (1, width), 1)
    return condition(lane).astype(F32).astype(BF16)


def head_mask(block, head, width):
    return block * lane_row(lambda lane: lane // width == head, block.shape[1])


def scaled(block, factor):
    return (block.astype(F32) * factor).astype(BF16)


def peaks(block, width):
    size = block.shape[1]
    head = lax.broadcasted_iota(jnp.int32, (size, LANES), 0) // width
    own = (head == lax.broadcasted_iota(jnp.int32, (size, LANES), 1)).astype(F32).astype(BF16)
    return jnp.max(dot_nn(block * block, own), axis=0, keepdims=True)


def spare_lane(head, width):
    return LANES - width if head * width < LANES // 2 else 0


def with_bias(keys, lane, length):
    row = lax.broadcasted_iota(jnp.int32, keys.shape, 0)
    column = lax.broadcasted_iota(jnp.int32, keys.shape, 1)
    bias = jnp.where(row < length, 0.0, MASKED).astype(BF16)
    return jnp.where(column == lane, bias, keys)


def masked_sides(queries, keys, head, width):
    lane = spare_lane(head, width)
    one = lane_row(lambda index: index == lane)
    return head_mask(queries, head, width) + one, keys[lane]


def biased(keys, width, length):
    return {lane: with_bias(keys, lane, length) for lane in (LANES - width, 0)}


def query_flag(length, size):
    return (lax.broadcasted_iota(jnp.int32, (size, 1), 0) < length).astype(F32)


def weave(works):
    ticks = max(count for _, count in works)
    for tick in range(ticks):
        for work, count in works:
            if (tick + 1) * count // ticks > tick * count // ticks:
                next(work)
    for work, _ in works:
        for _ in work:
            pass


def exps(scores, axis, careful):
    if careful:
        scores = scores - jnp.max(scores, axis=axis, keepdims=True)
    heights = jnp.exp2(scores)
    return heights, jnp.sum(heights, axis=axis, keepdims=True)


def low_rows(column, size):
    block = jnp.broadcast_to(column, (column.shape[0], LANES)).astype(BF16)
    return jnp.concatenate([block] * (size // LANES), 1)


def short_bias(length):
    shape = (SHORT_LEN, GROUP * SHORT_LEN)
    return jnp.where(lax.broadcasted_iota(jnp.int32, shape, 0) < length, 0.0, MASKED)


def stack(block, width):
    return jnp.concatenate([head_mask(block, h, width) for h in range(GROUP)], 0)


def diagonal(block):
    return jnp.concatenate(
        [
            block[h * HEAD_DIM : (h + 1) * HEAD_DIM, h * SHORT_LEN : (h + 1) * SHORT_LEN]
            for h in range(GROUP)
        ],
        0,
    )


def params():
    return pltpu.CompilerParams(vmem_limit_bytes=VMEM_BYTES)


def whole(shape):
    return pl.BlockSpec(shape, lambda i: (0,) * len(shape))


def smem():
    return pl.BlockSpec(memory_space=pltpu.SMEM)


def forward_kernel(
    short_blocks,
    short_len,
    long_len,
    tokens,
    wq,
    wk,
    wv,
    bq,
    bv,
    q_out,
    k_out,
    v_out,
    ctx_out,
    ps_out,
    pl_out,
):
    step = pl.program_id(0)
    x = tokens[...]
    q_out[...] = (dot_nn(x, wq[...]) + row_of(bq)).astype(BF16)
    k_out[...] = dot_nn(x, wk[...]).astype(BF16)
    v_out[...] = (dot_nn(x, wv[...]) + row_of(bv)).astype(BF16)

    shift = EXP_SCALE * EXP_SCALE
    bound = jnp.max(peaks(q_out[...], HEAD_DIM) * peaks(k_out[...], HEAD_DIM)) * shift
    tame = bound < LIMIT * LIMIT

    def short_items(careful):
        items = BLOCK // SHORT_LEN

        @pl.loop(0, items)
        def _(item):
            rows = pl.ds(pl.multiple_of(item * SHORT_LEN, SHORT_LEN), SHORT_LEN)
            bias = short_bias(short_len[step * items + item])
            for g in range(GROUPS):
                cols = slice(g * LANES, (g + 1) * LANES)
                q, k, v = q_out[rows, cols], k_out[rows, cols], v_out[rows, cols]
                queries = stack(scaled(q, EXP_SCALE), HEAD_DIM)
                e, total = exps(dot_nt(k, queries) + bias, 0, careful)
                probs = e.astype(BF16) * (1.0 / total).astype(BF16)
                ps_out[g, rows, :] = probs
                ctx_out[rows, cols] = diagonal(dot_tn(v, probs)).T.astype(BF16)

    def long_item(careful):
        length = long_len[step - short_blocks]

        @pl.loop(0, GROUPS)
        def _(g):
            cols = pl.ds(pl.multiple_of(g * LANES, LANES), LANES)
            q = scaled(q_out[:, cols], EXP_SCALE)
            k = biased(k_out[:, cols], HEAD_DIM, length)
            v = v_out[:, cols]
            for h in range(GROUP):
                e, total = exps(dot_nt(*masked_sides(q, k, h, HEAD_DIM)), 1, careful)
                pl_out[g * GROUP + h] = e.astype(BF16) * low_rows(1.0 / total, BLOCK)
            probs = jnp.concatenate([pl_out[g * GROUP + h] for h in range(GROUP)], 1)
            ctx_out[:, cols] = dot_nn(probs, stack(v, HEAD_DIM)).astype(BF16)

    short = step < short_blocks
    for careful, chosen in ((False, tame), (True, jnp.logical_not(tame))):
        pl.when(jnp.logical_and(short, chosen))(functools.partial(short_items, careful))
        pl.when(jnp.logical_and(jnp.logical_not(short), chosen))(
            functools.partial(long_item, careful)
        )


def attention_forward(tokens, wq, wk, wv, bq, bv, short_len, long_len):
    rows, width = tokens.shape
    blocks = rows // BLOCK
    short_blocks = short_len.shape[0] * SHORT_LEN // BLOCK
    long_blocks = blocks - short_blocks
    row_spec = pl.BlockSpec((BLOCK, width), lambda i: (i, 0))
    act = jax.ShapeDtypeStruct((rows, width), BF16)
    return pl.pallas_call(
        functools.partial(forward_kernel, short_blocks),
        grid=(blocks,),
        in_specs=[smem(), smem(), row_spec]
        + [whole(a.shape) for a in (wq, wk, wv, bq, bv)],
        out_specs=[
            row_spec,
            row_spec,
            row_spec,
            row_spec,
            pl.BlockSpec((GROUPS, BLOCK, BLOCK), lambda i: (0, jnp.minimum(i, short_blocks - 1), 0)),
            pl.BlockSpec((HEADS, BLOCK, BLOCK), lambda i: (0, jnp.maximum(i - short_blocks, 0), 0)),
        ],
        out_shape=[
            act,
            act,
            act,
            act,
            jax.ShapeDtypeStruct((GROUPS, short_blocks * BLOCK, BLOCK), BF16),
            jax.ShapeDtypeStruct((HEADS, long_blocks * BLOCK, BLOCK), BF16),
        ],
        compiler_params=params(),
        cost_estimate=pl.CostEstimate(
            flops=12_000_000_000, bytes_accessed=24_000_000, transcendentals=8_000_000
        ),
        name="attention_forward",
    )(short_len, long_len, tokens, wq, wk, wv, bq, bv)


def norm_parts(resid):
    centred = resid - jnp.mean(resid, axis=-1, keepdims=True)
    spread = jnp.mean(centred * centred, axis=-1, keepdims=True)
    root = lax.rsqrt(spread + EPSILON)
    return centred * root, root


def norm_back(grad, y, root):
    return root * (
        grad
        - jnp.mean(grad, axis=-1, keepdims=True)
        - y * jnp.mean(grad * y, axis=-1, keepdims=True)
    )


def row_of(vector):
    return vector[...].astype(F32).reshape(1, vector.shape[0])


def column_sum(block):
    return jnp.sum(block.astype(F32), axis=0, keepdims=True)


def middle_kernel(
    core,
    tokens,
    ctx,
    cot,
    wo,
    up0,
    up1,
    dn0,
    dn1,
    ub0,
    ub1,
    bo_in,
    gain1_in,
    shift1_in,
    db_in,
    gain2_in,
    shift2_in,
    block_out,
    dres_out,
    dctx_out,
    keep_out,
    give_out,
    acc_up,
    acc_dn,
    acc_wo,
    acc_ub,
    acc_vec,
    slope,
    active,
):
    step = pl.program_id(0)
    half = up0.shape[1]
    width = up0.shape[0]

    @pl.when(step == 0)
    def _():
        for ref in (acc_up, acc_dn, acc_wo, acc_ub, acc_vec):
            ref[...] = jnp.zeros_like(ref)

    bo, gain1, shift1, db, gain2, shift2 = (
        row_of(ref) for ref in (bo_in, gain1_in, shift1_in, db_in, gain2_in, shift2_in)
    )
    ctx_low = ctx[...]
    resid = tokens[...].astype(F32) + dot_nn(ctx_low, wo[...]) + bo
    y1, root1 = norm_parts(resid)
    normed = y1 * gain1 + shift1
    normed_low = normed.astype(BF16)
    mid = normed + db
    for j, (up, ub, dn) in enumerate(((up0, ub0, dn0), (up1, ub1, dn1))):
        pre = dot_nn(normed_low, up[...]) + row_of(ub)
        phi = 0.5 + 0.5 * lax.erf(pre * (0.5**0.5))
        act = (pre * phi).astype(BF16)
        slope[j] = phi + pre * (jnp.exp2(pre * pre * (-0.5 * LOG2E)) * 0.3989422804014327)
        active[j] = act
        mid = mid + dot_nn(act, dn[...])
    y2, root2 = norm_parts(mid)
    block_out[...] = (y2 * gain2 + shift2).astype(BF16)
    cotangent = cot[...].astype(F32)
    dmid = norm_back(cotangent * gain2, y2, root2)
    dbranch = dmid.astype(BF16)
    acc_vec[3:4, :] += column_sum(dbranch)
    acc_vec[4:5, :] += column_sum(cotangent * y2)
    acc_vec[5:6, :] += column_sum(cotangent)
    dnormed = dmid
    for j, (up, dn) in enumerate(((up0, dn0), (up1, dn1))):
        acc_dn[j] += dot_tn(active[j], dbranch)
        dpre = (dot_nt(dbranch, dn[...]) * slope[j]).astype(BF16)
        acc_up[j] += dot_tn(normed_low, dpre)
        acc_ub[j : j + 1, :] += column_sum(dpre)
        dnormed = dnormed + dot_nt(dpre, up[...])
    acc_vec[1:2, :] += column_sum(dnormed * y1)
    acc_vec[2:3, :] += column_sum(dnormed)
    dres = norm_back(dnormed * gain1, y1, root1)
    dres_out[...] = dres
    dattn = dres.astype(BF16)
    acc_vec[0:1, :] += column_sum(dattn)
    acc_wo[...] += dot_tn(ctx_low, dattn)
    dctx_out[...] = dot_nt(dattn, wo[...]).astype(BF16)

    @pl.when(step == pl.num_programs(0) - 1)
    def _():
        for j, out in enumerate((keep_out, give_out)):
            for part in range(half // width):
                cols = slice(part * width, (part + 1) * width)
                out[part * width : (part + 1) * width, :] = acc_up[j, :, cols].astype(BF16)
            out[half : 2 * half, :] = acc_dn[j].astype(BF16)
            pads = [
                acc_ub[j : j + 1, part * width : (part + 1) * width]
                for part in range(half // width)
            ]
            pads.append(jnp.zeros((16 - len(pads), width), F32))
            out[2 * half : 2 * half + 16, :] = jnp.concatenate(pads, 0).astype(BF16)
        cut = (width + PAD_ROWS) // 2
        low = acc_wo[:cut, :].astype(BF16)
        pads = jnp.zeros((PAD_ROWS - 8, width), F32)
        high = jnp.concatenate([acc_wo[cut:, :], acc_vec[...], pads], 0).astype(BF16)
        first = core[0] == 0
        keep_out[2 * half + 16 :, :] = jnp.where(first, low, high)
        give_out[2 * half + 16 :, :] = jnp.where(first, high, low)


def middle(core, tokens, ctx, cot, wo, ups, dns, ubs, vectors):
    rows, width = tokens.shape
    half = ups[0].shape[1]
    row_spec = pl.BlockSpec((MID_BLOCK, width), lambda i: (i, 0))
    weights = (wo, *ups, *dns, *ubs, *vectors)
    act = jax.ShapeDtypeStruct((rows, width), BF16)
    sums = jax.ShapeDtypeStruct((2 * half + 16 + (width + PAD_ROWS) // 2, width), BF16)
    return pl.pallas_call(
        middle_kernel,
        grid=(rows // MID_BLOCK,),
        in_specs=[smem()] + [row_spec] * 3 + [whole(w.shape) for w in weights],
        out_specs=[row_spec] * 3 + [whole(sums.shape), whole(sums.shape)],
        out_shape=[act, jax.ShapeDtypeStruct((rows, width), F32), act, sums, sums],
        scratch_shapes=[
            pltpu.VMEM((2, width, half), F32),
            pltpu.VMEM((2, half, width), F32),
            pltpu.VMEM((width, width), F32),
            pltpu.VMEM((8, half), F32),
            pltpu.VMEM((8, width), F32),
            pltpu.VMEM((2, MID_BLOCK, half), F32),
            pltpu.VMEM((2, MID_BLOCK, half), BF16),
        ],
        compiler_params=params(),
        cost_estimate=pl.CostEstimate(
            flops=34_000_000_000, bytes_accessed=20_000_000, transcendentals=6_000_000
        ),
        name="middle",
    )(core, tokens, ctx, cot, *weights)


def backward_kernel(
    first,
    blocks,
    short_blocks,
    carried,
    short_len,
    long_len,
    core,
    tokens,
    q_in,
    k_in,
    v_in,
    ctx_in,
    dctx_in,
    tq_in,
    tk_in,
    tv_in,
    ps_in,
    pl_in,
    *refs,
):
    if carried:
        acc_in, bias_in, *refs = refs[:2] + refs[5:]
    (
        grad_out,
        keep_out,
        give_out,
        acc,
        bias_acc,
        dq_buf,
    dk_buf,
    dv_buf,
    dkt_buf,
    dvt_buf,
    dp_buf,
    exp_buf,
    total_buf,
    ds_buf,
    drel_buf,
    ) = refs
    block = lax.rem(first + pl.program_id(0), blocks)

    if carried:

        @pl.when(pl.program_id(0) == 0)
        def _():
            acc[...] = acc_in[...]
            bias_acc[...] = bias_in[...]

    @pl.when(block == 0)
    def _():
        acc[...] = jnp.zeros_like(acc)
        bias_acc[...] = jnp.zeros_like(bias_acc)

    teach_peak = peaks(tq_in[...], TEACH_HD) * peaks(tk_in[...], TEACH_HD)
    rel_peak = peaks(tv_in[...], TEACH_HD)
    own_peak = peaks(v_in[...], HEAD_DIM) * EXP_SCALE
    bound = jnp.maximum(teach_peak, rel_peak * rel_peak) * (TEACH_SCALE * TEACH_SCALE)
    tame = jnp.max(jnp.maximum(bound, own_peak * own_peak)) < LIMIT * LIMIT


    def teach_scores(keys, queries):
        queries = scaled(queries, TEACH_SCALE)
        parts = []
        for pair in range(GROUP // 2):
            cols = slice(pair * LANES, (pair + 1) * LANES)
            both = jnp.concatenate([head_mask(queries[:, cols], h, TEACH_HD) for h in range(2)], 0)
            parts.append(dot_nt(keys[:, cols], both))
        return jnp.concatenate(parts, 1)

    def short_item(careful, item):
        start = item * SHORT_LEN
        if careful:
            start = pl.multiple_of(start, SHORT_LEN)
        rows = pl.ds(start, SHORT_LEN)
        length = short_len[block * (BLOCK // SHORT_LEN) + item]
        bias = short_bias(length)
        lane = lax.broadcasted_iota(jnp.int32, (1, GROUP * SHORT_LEN), 1)
        flag = (lane % SHORT_LEN < length).astype(F32)
        q, k, v = q_in[rows, :], k_in[rows, :], v_in[rows, :]
        dctx, ctx = dctx_in[rows, :], ctx_in[rows, :]
        tq, tk, tv = tq_in[rows, :], tk_in[rows, :], tv_in[rows, :]
        q_all, v_all, dctx_all = (stack(part, HEAD_DIM) for part in (q, v, dctx))
        p = ps_in[0, rows, :]

        def soft(scores):
            e, total = exps(scores + bias, 0, careful)
            return e.astype(BF16) * (flag / total).astype(BF16)

        weighed = (dctx.astype(F32) * ctx.astype(F32)).T
        delta = jnp.concatenate(
            [
                jnp.sum(weighed[h * HEAD_DIM : (h + 1) * HEAD_DIM], axis=0, keepdims=True)
                for h in range(GROUP)
            ],
            1,
        )
        dp = (dot_nt(v, dctx_all) + (flag - delta)).astype(BF16)
        ds = p * dp - soft(teach_scores(tk, tq))
        dq_buf[rows, :] = diagonal(dot_tn(k, ds)).T * SCALE
        dk_buf[rows, :] = dot_nn(ds, q_all) * SCALE
        own = soft(dot_nt(v, stack(scaled(v, EXP_SCALE), HEAD_DIM)))
        drel = own - soft(teach_scores(tv, tv))
        rel = dot_nn(drel, v_all) + diagonal(dot_tn(v, drel)).T
        dv_buf[rows, :] = dot_nn(p, dctx_all) + SCALE * rel

    def short_items(careful):
        if careful:
            pl.loop(0, BLOCK // SHORT_LEN)(functools.partial(short_item, True))
        else:
            for item in range(BLOCK // SHORT_LEN):
                short_item(False, item)


    def long_item():
        length = long_len[block - short_blocks]
        q, k, v = q_in[...], k_in[...], v_in[...]
        dctx, ctx = dctx_in[...], ctx_in[...]
        qt, vt, dctxt = q.T, v.T, dctx.T
        weighed = -(dctx.astype(F32) * ctx.astype(F32)).astype(BF16)
        right = jnp.concatenate([v, jnp.ones_like(v)], 1)
        v_scaled = scaled(v, EXP_SCALE)
        v_keys = biased(v, HEAD_DIM, length)
        flag = query_flag(length, BLOCK)
        flags = jnp.broadcast_to(flag, v.shape).astype(BF16)
        teach = {}

        def teach_pair(source, pair):
            if (source, pair) not in teach:
                part = (tq_in, tk_in, tv_in)[source][:, pair * LANES : (pair + 1) * LANES]
                teach[source, pair] = (
                    biased(part, TEACH_HD, length) if source else None,
                    None if source == 1 else scaled(part, TEACH_SCALE),
                )
            return teach[source, pair]

        def sides(kind, h):
            if kind == 0:
                left, keys = teach_pair(0, h // 2)[1], teach_pair(1, h // 2)[0]
                return masked_sides(left, keys, h % 2, TEACH_HD)
            if kind == 1:
                return masked_sides(v_scaled, v_keys, h, HEAD_DIM)
            if kind == 2:
                keys, left = teach_pair(2, h // 2)
                return masked_sides(left, keys, h % 2, TEACH_HD)
            lane = spare_lane(h, HEAD_DIM)
            extra = head_mask(weighed, h, HEAD_DIM) + flags * lane_row(lambda i: i == lane)
            return jnp.concatenate([head_mask(dctx, h, HEAD_DIM), extra], 1), right

        halves = [slice(i * (BLOCK // 2), (i + 1) * (BLOCK // 2)) for i in range(2)]

        def score_items(h):
            for kind in range(4):
                left, keys = sides(kind, h)
                for j, cols in enumerate(halves):
                    scores = dot_nt(left, keys[cols])
                    if kind == 3:
                        dp_buf[h % 2, :, cols] = scores.astype(BF16)
                    else:
                        e = jnp.exp2(scores)
                        exp_buf[h % 2, kind, :, cols] = e.astype(BF16)
                        part = e[:, :LANES] + e[:, LANES:]
                        if j == 0:
                            total_buf[h % 2, kind] = part
                        else:
                            total_buf[h % 2, kind] += part
                    yield

        def product_items(h):
            dims = slice(h * HEAD_DIM, (h + 1) * HEAD_DIM)
            ds, drel = ds_buf.at[h % 2], drel_buf.at[h % 2]
            for cols in halves:
                dvt_buf[dims, cols] = dot_nn(dctxt[dims, :], pl_in[h, :, cols])
                yield
                dkt_buf[dims, cols] = dot_nn(qt[dims, :], ds[:, cols]) * SCALE
                yield
                dvt_buf[dims, cols] += SCALE * dot_nn(vt[dims, :], drel[:, cols])
                yield
            for buf, grads, keys in ((dq_buf, ds, k), (dv_buf, drel, v)):
                part = dot_nn(grads[...], head_mask(keys, h, HEAD_DIM))
                if h == 0:
                    buf[...] = part
                else:
                    buf[...] += part
                yield

        def row_items(h):
            count = BLOCK // 8
            for i in range(8):
                rows = slice(i * count, (i + 1) * count)

                def soft(kind):
                    total = jnp.sum(total_buf[h % 2, kind, rows, :], axis=1, keepdims=True)
                    return exp_buf[h % 2, kind, rows, :] * low_rows(flag[rows] / total, BLOCK)

                ds_buf[h % 2, rows, :] = pl_in[h, rows, :] * dp_buf[h % 2, rows, :] - soft(0)
                drel_buf[h % 2, rows, :] = soft(1) - soft(2)
                yield

        for h in range(-1, GROUP + 1):
            works = []
            if h + 1 < GROUP:
                works.append((score_items(h + 1), 8))
            if 0 <= h < GROUP:
                works.append((row_items(h), 8))
            if h >= 1:
                works.append((product_items(h - 1), 8))
            weave(works)
        dq_buf[...] *= SCALE
        dk_buf[...] = dkt_buf[...].T
        dv_buf[...] = dvt_buf[...].T + SCALE * dv_buf[...]

    def long_item_careful():
        length = long_len[block - short_blocks]
        flag = query_flag(length, BLOCK)
        bias = jnp.where(
            lax.broadcasted_iota(jnp.int32, (1, BLOCK), 1) < length, 0.0, MASKED
        )
        for buf in (dq_buf, dk_buf, dv_buf):
            buf[...] = jnp.zeros_like(buf)

        def soft(queries, keys, h, width, scale):
            scores = dot_nt(head_mask(scaled(queries, scale), h, width), keys)
            e, total = exps(scores + bias, 1, True)
            return e * (flag / total)

        @pl.loop(0, GROUP)
        def _(h):
            q, k, v, dctx = (
                head_mask(ref[...], h, HEAD_DIM) for ref in (q_in, k_in, v_in, dctx_in)
            )
            p = pl_in[h]
            delta = jnp.sum(dctx.astype(F32) * ctx_in[...].astype(F32), axis=1, keepdims=True)
            dp = dot_nt(dctx, v) + (flag - delta)
            teach = soft(tq_in[...], tk_in[...], h, TEACH_HD, TEACH_SCALE)
            ds = (p.astype(F32) * dp - teach).astype(BF16)
            own = soft(v, v, h, HEAD_DIM, EXP_SCALE)
            drel = (own - soft(tv_in[...], tv_in[...], h, TEACH_HD, TEACH_SCALE)).astype(BF16)
            dq_buf[...] += dot_nn(ds, k) * SCALE
            dk_buf[...] += dot_tn(ds, q) * SCALE
            dv_buf[...] += dot_tn(p, dctx) + SCALE * (dot_nn(drel, v) + dot_tn(drel, v))

    short = block < short_blocks
    long = jnp.logical_not(short)
    wild = jnp.logical_not(tame)
    pl.when(jnp.logical_and(short, tame))(functools.partial(short_items, False))
    pl.when(jnp.logical_and(short, wild))(functools.partial(short_items, True))
    pl.when(jnp.logical_and(long, tame))(long_item)
    pl.when(jnp.logical_and(long, wild))(long_item_careful)

    grads = jnp.concatenate([buf[...].astype(BF16) for buf in (dq_buf, dk_buf, dv_buf)], 1)
    grad_out[...] = grads
    acc[...] += dot_tn(tokens[...], grads)
    bias_acc[0:1, :] += column_sum(grads)

    @pl.when(block == blocks - 1)
    def _():
        width = tokens.shape[1]
        sides = [bias_acc[0:1, w * LANES : (w + 1) * LANES] for w in range(3)]
        full = [acc[:, w * LANES : (w + 1) * LANES] for w in range(3)]
        full = jnp.concatenate([*full, *sides, jnp.zeros((125, LANES), F32)], 0).astype(BF16)
        cut = full.shape[0] // 2
        is_first = core[0] == 0
        keep_out[...] = jnp.where(is_first, full[:cut], full[cut:])
        give_out[...] = jnp.where(is_first, full[cut:], full[:cut])


def attention_backward(steps, short_len, long_len, core, tokens, acts, p_short, p_long, carry):
    rows, width = tokens.shape
    blocks = rows // BLOCK
    short_blocks = short_len.shape[0] * SHORT_LEN // BLOCK
    start, stop = steps

    def place(pick):
        return lambda i: pick((start + i) // blocks, (start + i) % blocks)

    def group_spec(size):
        return pl.BlockSpec((BLOCK, size), place(lambda g, b: (b, g)))

    p_specs = [
        pl.BlockSpec(
            (1, BLOCK, BLOCK), place(lambda g, b: (g, jnp.minimum(b, short_blocks - 1), 0))
        ),
        pl.BlockSpec(
            (GROUP, BLOCK, BLOCK), place(lambda g, b: (g, jnp.maximum(b - short_blocks, 0), 0))
        ),
    ]
    cut = (3 * width + 128) // 2
    sums = jax.ShapeDtypeStruct((GROUPS * cut, LANES), BF16)
    acc = jax.ShapeDtypeStruct((width, 3 * LANES), F32)
    bias_acc = jax.ShapeDtypeStruct((8, 3 * LANES), F32)
    half_spec = pl.BlockSpec((cut, LANES), place(lambda g, b: (g, 0)))
    square = (BLOCK, LANES)
    ins = [short_len, long_len, core, tokens, *acts, p_short, p_long]
    carry_specs = []
    aliases = {}
    if carry is not None:
        grads, keep, give, acc_in, bias_in = carry
        aliases = {len(ins) + 2 + i: i for i in range(3)}
        ins += [acc_in, bias_in, grads, keep, give]
        carry_specs = [whole(acc.shape), whole(bias_acc.shape)]
        carry_specs += [pl.BlockSpec(memory_space=pl.ANY)] * 3
    return pl.pallas_call(
        functools.partial(backward_kernel, start, blocks, short_blocks, carry is not None),
        grid=(stop - start,),
        in_specs=[smem(), smem(), smem()]
        + [pl.BlockSpec((BLOCK, width), place(lambda g, b: (b, 0)))]
        + [group_spec(LANES)] * 5
        + [group_spec(GROUP * TEACH_HD)] * 3
        + p_specs
        + carry_specs,
        out_specs=[
            pl.BlockSpec((BLOCK, 3 * LANES), place(lambda g, b: (b, g))),
            half_spec,
            half_spec,
            whole(acc.shape),
            whole(bias_acc.shape),
        ],
        out_shape=[
            jax.ShapeDtypeStruct((rows, GROUPS * 3 * LANES), BF16),
            sums,
            sums,
            acc,
            bias_acc,
        ],
        scratch_shapes=[
            pltpu.VMEM(square, F32),
            pltpu.VMEM(square, F32),
            pltpu.VMEM(square, F32),
            pltpu.VMEM((LANES, BLOCK), F32),
            pltpu.VMEM((LANES, BLOCK), F32),
            pltpu.VMEM((2, BLOCK, BLOCK), BF16),
            pltpu.VMEM((2, 3, BLOCK, BLOCK), BF16),
            pltpu.VMEM((2, 3, BLOCK, LANES), F32),
            pltpu.VMEM((2, BLOCK, BLOCK), BF16),
            pltpu.VMEM((2, BLOCK, BLOCK), BF16),
        ],
        input_output_aliases=aliases,
        compiler_params=params(),
        cost_estimate=pl.CostEstimate(
            flops=(stop - start) * 7_000_000_000,
            bytes_accessed=(stop - start) * 4_000_000,
            transcendentals=(stop - start) * 2_000_000,
        ),
        name=f"attention_backward_{start}",
    )(*ins)


def tokens_grad_kernel(dres, wq, wk, wv, grads, out):
    weights = jnp.concatenate(
        [w[:, g * LANES : (g + 1) * LANES] for g in range(GROUPS) for w in (wq, wk, wv)], 1
    )
    out[...] = (dres[...] + dot_nt(grads[...], weights)).astype(BF16)


def tokens_gradient(dres, wq, wk, wv, grads):
    rows, width = dres.shape
    row_spec = pl.BlockSpec((BLOCK, width), lambda i: (i, 0))
    return pl.pallas_call(
        tokens_grad_kernel,
        grid=(rows // BLOCK,),
        in_specs=[row_spec]
        + [whole(wq.shape)] * 3
        + [pl.BlockSpec((BLOCK, grads.shape[1]), lambda i: (i, 0))],
        out_specs=row_spec,
        out_shape=jax.ShapeDtypeStruct((rows, width), BF16),
        compiler_params=params(),
        cost_estimate=pl.CostEstimate(
            flops=2_000_000_000, bytes_accessed=10_000_000, transcendentals=0
        ),
        name="tokens_gradient",
    )(dres, wq, wk, wv, grads)


def swap(value):
    return lax.ppermute(value, "tensor", [(0, 1), (1, 0)])


def spread(value):
    return lax.all_to_all(value, "dp", 0, 0, tiled=True)


def sum_chain(keep, give, count):
    (got,) = yield 0, [(swap, give)]
    both = (keep.astype(F32) + got.astype(F32)).astype(BF16)
    rows, width = both.shape
    (got,) = yield 1, [(spread, both.reshape(count, rows // count, width))]
    part = jnp.sum(got.astype(F32), axis=0).astype(BF16)
    (got,) = yield 1, [(spread, jnp.broadcast_to(part[None], got.shape))]
    return got.reshape(rows, width)


def ordered(core, mine, other):
    first = core[0] == 0
    return jnp.where(first, mine, other), jnp.where(first, other, mine)


def first_finish_kernel(core, total, other, up_out, ub_out, dn_out, wo_out, *vector_outs):
    width, half = up_out.shape
    count = half // width
    for part in range(count):
        cols = slice(part * width, (part + 1) * width)
        up_out[:, cols] = total[cols, :].astype(F32)
    dn_out[...] = total[half : 2 * half, :].astype(F32)
    biases = total[2 * half : 2 * half + 16, :].astype(F32)
    ub_out[...] = jnp.concatenate([biases[i : i + 1] for i in range(count)], 1).reshape(half)
    halves = ordered(core, total[2 * half + 16 :, :].astype(F32), other[...].astype(F32))
    both = jnp.concatenate(halves, 0)
    wo_out[...] = both[:width]
    for i, out in enumerate(vector_outs):
        out[...] = both[width + i : width + i + 1].reshape(width)


def first_finish(core, total, other, half):
    width = total.shape[1]
    shapes = [(width, half), (half,), (half, width), (width, width)] + [(width,)] * 6
    return pl.pallas_call(
        first_finish_kernel,
        in_specs=[smem()] + [pl.BlockSpec(memory_space=pltpu.VMEM)] * 2,
        out_shape=[jax.ShapeDtypeStruct(shape, F32) for shape in shapes],
        compiler_params=params(),
        name="first_finish",
    )(core, total, other)


def qkv_finish_kernel(core, total, other, wq_out, wk_out, wv_out, bq_out, bv_out):
    width = wq_out.shape[0]
    low, high = ordered(core, total[...].astype(F32), other[...].astype(F32))
    cut = low.shape[0] // GROUPS
    sides = []
    for g in range(GROUPS):
        rows = slice(g * cut, (g + 1) * cut)
        full = jnp.concatenate([low[rows], high[rows]], 0)
        cols = slice(g * LANES, (g + 1) * LANES)
        for w, out in enumerate((wq_out, wk_out, wv_out)):
            out[:, cols] = full[w * width : (w + 1) * width]
        sides.append(full[3 * width : 3 * width + 8])
    sides = jnp.concatenate(sides, 1)
    bq_out[...] = sides[0:1].reshape(width)
    bv_out[...] = sides[2:3].reshape(width)


def qkv_finish(core, total, other, width):
    shapes = [(width, width)] * 3 + [(width,)] * 2
    return pl.pallas_call(
        qkv_finish_kernel,
        in_specs=[smem()] + [pl.BlockSpec(memory_space=pltpu.VMEM)] * 2,
        out_shape=[jax.ShapeDtypeStruct(shape, F32) for shape in shapes],
        compiler_params=params(),
        name="qkv_finish",
    )(core, total, other)


class Flights:
    def __init__(self):
        self.asked = {}
        self.flying = {}
        self.done = {}

    def advance(self, name, generator, got=None):
        try:
            span, wants = next(generator) if got is None else generator.send(got)
            self.asked[name] = (generator, span, wants)
        except StopIteration as end:
            self.done[name] = end.value

    def step(self, token, work=None):
        asked, self.asked = self.asked, {}
        sends = [value for _, _, wants in asked.values() for _, value in wants]
        token, *sends = lax.optimization_barrier((token, *sends))
        sent = iter(sends)
        for name, (generator, span, wants) in asked.items():
            self.flying[name] = [generator, span, [move(next(sent)) for move, _ in wants]]
        result = None
        if work is not None:
            result, token = work(token)
        for name, (generator, span, got) in list(self.flying.items()):
            if work is not None:
                token, *got = lax.optimization_barrier((token, *got))
            del self.flying[name]
            self.advance(name, generator, got)
        return result, token


def per_device(
    dp_count,
    tokens,
    query_weight,
    query_bias,
    key_weight,
    value_weight,
    value_bias,
    proj_weight,
    proj_bias,
    first_gain,
    first_shift,
    up_weight,
    up_bias,
    down_weight,
    down_bias,
    second_gain,
    second_shift,
    teach_query,
    teach_key,
    teach_value,
    short_lengths,
    long_lengths,
    cotangent,
):
    width = tokens.shape[1]
    half = up_weight.shape[1]

    up_other, down_other, ub_other = (swap(value) for value in (up_weight, down_weight, up_bias))
    core = lax.axis_index("tensor").astype(jnp.int32).reshape(1)
    q, k, v, ctx, p_short, p_long = attention_forward(
        tokens,
        query_weight,
        key_weight,
        value_weight,
        query_bias,
        value_bias,
        short_lengths,
        long_lengths,
    )
    block_out, dres, dctx, keep, give = middle(
        core,
        tokens,
        ctx,
        cotangent,
        proj_weight,
        (up_weight, up_other),
        (down_weight, down_other),
        (up_bias, ub_other),
        (proj_bias, first_gain, first_shift, down_bias, second_gain, second_shift),
    )
    flights = Flights()
    flights.advance("first", sum_chain(keep, give, dp_count))
    flights.step(short_lengths)
    acts = (q, k, v, ctx, dctx, teach_query, teach_key, teach_value)
    steps = GROUPS * (tokens.shape[0] // BLOCK)
    token = short_lengths
    carry = None
    for piece in ((0, steps // 2), (steps // 2, steps)):

        def work(lens):
            out = attention_backward(
                piece, lens, long_lengths, core, tokens, acts, p_short, p_long, carry
            )
            return out[:1] + out[2:], out[1]

        (grads, give, *sums), keep = flights.step(token, work)
        token, keep = lax.optimization_barrier((short_lengths, keep))
        carry = [grads, keep, give, *sums]
    flights.advance("qkv", sum_chain(keep, give, dp_count))
    flights.step(short_lengths)

    def input_work(grads):
        return None, tokens_gradient(dres, query_weight, key_weight, value_weight, grads)

    _, tokens_grad = flights.step(grads, input_work)
    total = flights.done["first"]
    other = swap(total[2 * half + 16 :])

    def first_work(total):
        out = first_finish(core, total, other, half)
        return out[1:], out[0]

    first, up_grad = flights.step(total, first_work)
    total = flights.done["qkv"]
    qkv = qkv_finish(core, total, swap(total), width)
    up_bias_grad, down_grad, proj_grad, *vectors = first
    return (
        block_out,
        tokens_grad,
        qkv[0],
        qkv[3],
        qkv[1],
        qkv[2],
        qkv[4],
        proj_grad,
        vectors[0],
        vectors[1],
        vectors[2],
        up_grad,
        up_bias_grad,
        down_grad,
        vectors[3],
        vectors[4],
        vectors[5],
    )


def solution(mesh):
    in_specs = (
        P(("dp", "tensor"), None),
        P(),
        P(),
        P(),
        P(),
        P(),
        P(),
        P(),
        P(),
        P(),
        P(None, "tensor"),
        P("tensor"),
        P("tensor", None),
        P(),
        P(),
        P(),
        P(("dp", "tensor"), None),
        P(("dp", "tensor"), None),
        P(("dp", "tensor"), None),
        P(("dp", "tensor")),
        P(("dp", "tensor")),
        P(("dp", "tensor"), None),
    )
    out_specs = (
        P(("dp", "tensor"), None),
        P(("dp", "tensor"), None),
        P(),
        P(),
        P(),
        P(),
        P(),
        P(),
        P(),
        P(),
        P(),
        P(None, "tensor"),
        P("tensor"),
        P("tensor", None),
        P(),
        P(),
        P(),
    )
    return jax.shard_map(
        functools.partial(per_device, mesh.shape["dp"]),
        mesh=mesh,
        in_specs=in_specs,
        out_specs=out_specs,
        check_vma=False,
    )
```

```python
import functools

import jax
import jax.numpy as jnp
from jax import lax
from jax.experimental import pallas as pl
from jax.experimental.pallas import tpu as pltpu
from jax.sharding import PartitionSpec as P

HEADS = 12
HEAD_DIM = 32
TEACH_HD = 64
SHORT_LEN = 128
GROUP = 4
LANES = GROUP * HEAD_DIM
GROUPS = HEADS // GROUP
BLOCK = 512
MID_BLOCK = 1024
MID_PARTS = 2
PAD_ROWS = 96

MASKED = -1e30
LIMIT = 2.0**64
EPSILON = 1e-06
LOG2E = 1.4426950408889634
SCALE = HEAD_DIM**-0.5
EXP_SCALE = LOG2E * SCALE
TEACH_SCALE = LOG2E * TEACH_HD**-0.5
MIB = 2**20

F32 = jnp.float32
BF16 = jnp.bfloat16


def dot_nn(left, right):
    return lax.dot_general(left, right, (((1,), (0,)), ((), ())), preferred_element_type=F32)


def dot_nt(left, right):
    return lax.dot_general(left, right, (((1,), (1,)), ((), ())), preferred_element_type=F32)


def dot_tn(left, right):
    return lax.dot_general(left, right, (((0,), (0,)), ((), ())), preferred_element_type=F32)


def dot_tt(left, right):
    return lax.dot_general(left, right, (((0,), (1,)), ((), ())), preferred_element_type=F32)


def lane_row(condition, width=LANES):
    lane = lax.broadcasted_iota(jnp.int32, (1, width), 1)
    return condition(lane).astype(F32).astype(BF16)


def head_mask(block, head, width):
    return block * lane_row(lambda lane: lane // width == head, block.shape[1])


def scaled(block, factor):
    return (block.astype(F32) * factor).astype(BF16)


def spare_lane(head, width):
    return LANES - width if head * width < LANES // 2 else 0


def with_bias(keys, lane, length):
    row = lax.broadcasted_iota(jnp.int32, keys.shape, 0)
    column = lax.broadcasted_iota(jnp.int32, keys.shape, 1)
    bias = jnp.where(row < length, 0.0, MASKED).astype(BF16)
    return jnp.where(column == lane, bias, keys)


def masked_sides(queries, keys, head, width):
    lane = spare_lane(head, width)
    one = lane_row(lambda index: index == lane)
    return head_mask(queries, head, width) + one, keys[lane]


def biased(keys, width, length):
    return {lane: with_bias(keys, lane, length) for lane in (LANES - width, 0)}


def query_flag(length, size):
    return (lax.broadcasted_iota(jnp.int32, (size, 1), 0) < length).astype(F32)


def weave(works):
    ticks = max(count for _, count in works)
    for tick in range(ticks):
        for work, count in works:
            if (tick + 1) * count // ticks > tick * count // ticks:
                next(work)
    for work, _ in works:
        for _ in work:
            pass


def exps(scores, axis, careful):
    if careful:
        scores = scores - jnp.max(scores, axis=axis, keepdims=True)
    heights = jnp.exp2(scores)
    return heights, jnp.sum(heights, axis=axis, keepdims=True)


def low_rows(column, size):
    block = jnp.broadcast_to(column, (column.shape[0], LANES)).astype(BF16)
    return jnp.concatenate([block] * (size // LANES), 1)


def short_bias(length):
    shape = (SHORT_LEN, GROUP * SHORT_LEN)
    return jnp.where(lax.broadcasted_iota(jnp.int32, shape, 0) < length, 0.0, MASKED)


def stack(block, width):
    return jnp.concatenate([head_mask(block, h, width) for h in range(GROUP)], 0)


def diagonal(block):
    return jnp.concatenate(
        [
            block[h * HEAD_DIM : (h + 1) * HEAD_DIM, h * SHORT_LEN : (h + 1) * SHORT_LEN]
            for h in range(GROUP)
        ],
        0,
    )


def params(mebibytes):
    return pltpu.CompilerParams(vmem_limit_bytes=mebibytes * MIB)


def whole(shape):
    return pl.BlockSpec(shape, lambda i: (0,) * len(shape))


def smem():
    return pl.BlockSpec(memory_space=pltpu.SMEM)


def forward_kernel(
    short_blocks,
    short_len,
    long_len,
    tokens,
    wq,
    wk,
    wv,
    bq,
    bv,
    q_out,
    k_out,
    v_out,
    ctx_out,
    ps_out,
    pl_out,
    side_out,
    worst,
):
    step = pl.program_id(0)
    x = tokens[...]
    side_out[...] = x.T
    q_out[...] = (dot_nn(x, wq[...]) + row_of(bq)).astype(BF16)
    k_out[...] = dot_nn(x, wk[...]).astype(BF16)
    v_out[...] = (dot_nn(x, wv[...]) + row_of(bv)).astype(BF16)

    def note(total, inverse):
        high = jnp.maximum(total, inverse)
        rows = high.shape[0]
        for i in range(max(high.shape[1] // LANES, 1)):
            part = high[:, i * LANES : (i + 1) * LANES]
            worst[:rows, :] = jnp.maximum(worst[:rows, :], part)


    def short_scores(item, g, found):
        rows = slice(item * SHORT_LEN, (item + 1) * SHORT_LEN)
        cols = slice(g * LANES, (g + 1) * LANES)
        bias = short_bias(short_len[step * (BLOCK // SHORT_LEN) + item])[:, : 2 * SHORT_LEN]
        queries = stack(scaled(q_out[rows, cols], EXP_SCALE), HEAD_DIM)
        for pair in range(GROUP // 2):
            heads = slice(pair * 2 * SHORT_LEN, (pair + 1) * 2 * SHORT_LEN)
            e, total = exps(dot_nt(k_out[rows, cols], queries[heads]) + bias, 0, False)
            found[pair] = e.astype(BF16), total
            yield

    def short_rows(item, g, found):
        rows = slice(item * SHORT_LEN, (item + 1) * SHORT_LEN)
        for pair in range(GROUP // 2):
            heads = slice(pair * 2 * SHORT_LEN, (pair + 1) * 2 * SHORT_LEN)
            e, total = found[pair]
            inverse = 1.0 / total
            note(total, inverse)
            found[pair] = e * inverse.astype(BF16)
            ps_out[g, rows, heads] = found[pair]
            yield

    def short_products(item, g, found):
        rows = slice(item * SHORT_LEN, (item + 1) * SHORT_LEN)
        cols = slice(g * LANES, (g + 1) * LANES)
        probs = jnp.concatenate([found[pair] for pair in range(GROUP // 2)], 1)
        ctx_out[rows, cols] = diagonal(dot_tn(v_out[rows, cols], probs)).T.astype(BF16)
        yield

    def short_items():
        units = [(item, g, {}) for item in range(BLOCK // SHORT_LEN) for g in range(GROUPS)]
        for tick in range(len(units) + 2):
            works = []
            if tick < len(units):
                works.append((short_scores(*units[tick]), 2))
            if 0 <= tick - 1 < len(units):
                works.append((short_rows(*units[tick - 1]), 2))
            if 0 <= tick - 2:
                works.append((short_products(*units[tick - 2]), 1))
            weave(works)

    def long_item():
        length = long_len[step - short_blocks]
        halves = [slice(i * (BLOCK // 2), (i + 1) * (BLOCK // 2)) for i in range(2)]

        @pl.loop(0, GROUPS)
        def _(g):
            cols = pl.ds(pl.multiple_of(g * LANES, LANES), LANES)
            queries = scaled(q_out[:, cols], EXP_SCALE)
            keys = biased(k_out[:, cols], HEAD_DIM, length)
            values = v_out[:, cols]
            sums = []

            def scores(h, found):
                left, right = masked_sides(queries, keys, h, HEAD_DIM)
                for half in halves:
                    e = jnp.exp2(dot_nt(left, right[half]))
                    part = e[:, :LANES] + e[:, LANES:]
                    found["sum"] = found["sum"] + part if "sum" in found else part
                    found[half.start] = e.astype(BF16)
                    yield

            def normalise(h, found):
                count = BLOCK // 4
                for i in range(4):
                    rows = slice(i * count, (i + 1) * count)
                    total = jnp.sum(found["sum"][rows], axis=1, keepdims=True)
                    inverse = 1.0 / total
                    note(total, inverse)
                    e = jnp.concatenate([found[half.start][rows] for half in halves], 1)
                    pl_out[g * GROUP + h, rows, :] = e * low_rows(inverse, BLOCK)
                    yield

            def products(h):
                part = dot_nn(pl_out[g * GROUP + h], head_mask(values, h, HEAD_DIM))
                sums.append(part)
                yield

            found = [{} for _ in range(GROUP)]
            for tick in range(GROUP + 2):
                works = []
                if tick < GROUP:
                    works.append((scores(tick, found[tick]), 2))
                if 0 <= tick - 1 < GROUP:
                    works.append((normalise(tick - 1, found[tick - 1]), 4))
                if 0 <= tick - 2:
                    works.append((products(tick - 2), 1))
                weave(works)
            ctx_out[:, cols] = functools.reduce(jnp.add, sums).astype(BF16)


    def short_items_careful():
        items = BLOCK // SHORT_LEN

        @pl.loop(0, items)
        def _(item):
            rows = pl.ds(pl.multiple_of(item * SHORT_LEN, SHORT_LEN), SHORT_LEN)
            bias = short_bias(short_len[step * items + item])
            for g in range(GROUPS):
                cols = slice(g * LANES, (g + 1) * LANES)
                q, k, v = q_out[rows, cols], k_out[rows, cols], v_out[rows, cols]
                e, total = exps(dot_nt(k, stack(q, HEAD_DIM)) * EXP_SCALE + bias, 0, True)
                probs = (e * (1.0 / total)).astype(BF16)
                ps_out[g, rows, :] = probs
                ctx_out[rows, cols] = diagonal(dot_tn(v, probs)).T.astype(BF16)

    def long_item_careful():
        length = long_len[step - short_blocks]
        bias = jnp.where(lax.broadcasted_iota(jnp.int32, (1, BLOCK), 1) < length, 0.0, MASKED)

        @pl.loop(0, GROUPS)
        def _(g):
            cols = pl.ds(pl.multiple_of(g * LANES, LANES), LANES)
            q, k, v = q_out[:, cols], k_out[:, cols], v_out[:, cols]
            ctx = jnp.zeros((BLOCK, LANES), F32)
            for h in range(GROUP):
                scores = dot_nt(head_mask(q, h, HEAD_DIM), k) * EXP_SCALE + bias
                e, total = exps(scores, 1, True)
                probs = (e * (1.0 / total)).astype(BF16)
                pl_out[g * GROUP + h] = probs
                ctx = ctx + dot_nn(probs, head_mask(v, h, HEAD_DIM))
            ctx_out[:, cols] = ctx.astype(BF16)

    short = step < short_blocks
    long = jnp.logical_not(short)
    worst[...] = jnp.zeros_like(worst)
    pl.when(short)(short_items)
    pl.when(long)(long_item)
    wild = jnp.logical_not(jnp.max(worst[...]) < LIMIT)
    pl.when(jnp.logical_and(short, wild))(short_items_careful)
    pl.when(jnp.logical_and(long, wild))(long_item_careful)


def attention_forward(tokens, wq, wk, wv, bq, bv, short_len, long_len):
    rows, width = tokens.shape
    blocks = rows // BLOCK
    short_blocks = short_len.shape[0] * SHORT_LEN // BLOCK
    long_blocks = blocks - short_blocks
    row_spec = pl.BlockSpec((BLOCK, width), lambda i: (i, 0))
    act = jax.ShapeDtypeStruct((rows, width), BF16)
    return pl.pallas_call(
        functools.partial(forward_kernel, short_blocks),
        grid=(blocks,),
        in_specs=[smem(), smem(), row_spec]
        + [whole(a.shape) for a in (wq, wk, wv, bq, bv)],
        out_specs=[
            row_spec,
            row_spec,
            row_spec,
            row_spec,
            pl.BlockSpec((GROUPS, BLOCK, BLOCK), lambda i: (0, jnp.minimum(i, short_blocks - 1), 0)),
            pl.BlockSpec((HEADS, BLOCK, BLOCK), lambda i: (0, jnp.maximum(i - short_blocks, 0), 0)),
            pl.BlockSpec((width, BLOCK), lambda i: (0, i)),
        ],
        out_shape=[
            act,
            act,
            act,
            act,
            jax.ShapeDtypeStruct((GROUPS, short_blocks * BLOCK, BLOCK), BF16),
            jax.ShapeDtypeStruct((HEADS, long_blocks * BLOCK, BLOCK), BF16),
            jax.ShapeDtypeStruct((width, rows), BF16),
        ],
        scratch_shapes=[pltpu.VMEM((BLOCK // 4, LANES), F32)],
        compiler_params=params(56),
        cost_estimate=pl.CostEstimate(
            flops=12_000_000_000, bytes_accessed=24_000_000, transcendentals=8_000_000
        ),
        name="attention_forward",
    )(short_len, long_len, tokens, wq, wk, wv, bq, bv)


def norm_parts(resid):
    centred = resid - jnp.mean(resid, axis=-1, keepdims=True)
    spread = jnp.mean(centred * centred, axis=-1, keepdims=True)
    root = lax.rsqrt(spread + EPSILON)
    return centred * root, root


def norm_back(grad, y, root):
    return root * (
        grad
        - jnp.mean(grad, axis=-1, keepdims=True)
        - y * jnp.mean(grad * y, axis=-1, keepdims=True)
    )


def row_of(vector):
    return vector[...].astype(F32).reshape(1, vector.shape[0])


def column_sum(block):
    return jnp.sum(block.astype(F32), axis=0, keepdims=True)


def middle_kernel(
    core,
    tokens,
    ctx,
    cot,
    wo,
    up0,
    up1,
    dn0,
    dn1,
    ub0,
    ub1,
    bo_in,
    gain1_in,
    shift1_in,
    db_in,
    gain2_in,
    shift2_in,
    block_out,
    dres_out,
    dctx_out,
    keep_out,
    give_out,
    acc_up,
    acc_dn,
    acc_wo,
    acc_ub,
    acc_vec,
    slope,
    active,
    dpre,
    low_rows_buf,
    dbranch,
    dattn,
):
    step = pl.program_id(0)
    half = up0.shape[1]
    width = up0.shape[0]

    @pl.when(step == 0)
    def _():
        for ref in (acc_up, acc_dn, acc_wo, acc_ub, acc_vec):
            ref[...] = jnp.zeros_like(ref)

    bo, gain1, shift1, db, gain2, shift2 = (
        row_of(ref) for ref in (bo_in, gain1_in, shift1_in, db_in, gain2_in, shift2_in)
    )
    def gelu(j, pre, rows):
        pre = pre + row_of((ub0, ub1)[j])
        phi = 0.5 + 0.5 * lax.erf(pre * (0.5**0.5))
        slope[j, rows, :] = phi + pre * (jnp.exp2(pre * pre * (-0.5 * LOG2E)) * 0.3989422804014327)
        active[j, rows, :] = (pre * phi).astype(BF16)

    def back_gelu(j, dactive, rows):
        grad = (dactive * slope[j, rows, :]).astype(BF16)
        dpre[j, rows, :] = grad
        acc_ub[j : j + 1, :] += column_sum(grad)
        return grad

    def row_work(rows):
        resid = tokens[rows, :].astype(F32) + dot_nn(ctx[rows, :], wo[...]) + bo
        yield
        y1, root1 = norm_parts(resid)
        normed = y1 * gain1 + shift1
        normed_low = normed.astype(BF16)
        low_rows_buf[rows, :] = normed_low
        mid = normed + db
        yield
        pre0 = dot_nn(normed_low, up0[...])
        yield
        pre1 = dot_nn(normed_low, up1[...])
        gelu(0, pre0, rows)
        yield
        mid = mid + dot_nn(active[0, rows, :], dn0[...])
        gelu(1, pre1, rows)
        yield
        mid = mid + dot_nn(active[1, rows, :], dn1[...])
        yield
        y2, root2 = norm_parts(mid)
        block_out[rows, :] = (y2 * gain2 + shift2).astype(BF16)
        cotangent = cot[rows, :].astype(F32)
        dmid = norm_back(cotangent * gain2, y2, root2)
        dbranch_low = dmid.astype(BF16)
        dbranch[rows, :] = dbranch_low
        acc_vec[3:4, :] += column_sum(dbranch_low)
        acc_vec[4:5, :] += column_sum(cotangent * y2)
        acc_vec[5:6, :] += column_sum(cotangent)
        yield
        dactive0 = dot_nt(dbranch_low, dn0[...])
        yield
        dactive1 = dot_nt(dbranch_low, dn1[...])
        dpre0 = back_gelu(0, dactive0, rows)
        yield
        dnormed = dmid + dot_nt(dpre0, up0[...])
        dpre1 = back_gelu(1, dactive1, rows)
        yield
        dnormed = dnormed + dot_nt(dpre1, up1[...])
        yield
        acc_vec[1:2, :] += column_sum(dnormed * y1)
        acc_vec[2:3, :] += column_sum(dnormed)
        dres = norm_back(dnormed * gain1, y1, root1)
        dres_out[rows, :] = dres
        dattn_low = dres.astype(BF16)
        dattn[rows, :] = dattn_low
        acc_vec[0:1, :] += column_sum(dattn_low)
        yield
        dctx_out[rows, :] = dot_nt(dattn_low, wo[...]).astype(BF16)
        yield

    def weight_work():
        for j in range(2):
            acc_dn[j] += dot_tn(dbranch[...], active[j])
            yield
        for j in range(2):
            acc_up[j] += dot_tn(low_rows_buf[...], dpre[j])
            yield
        acc_wo[...] += dot_tn(ctx[...], dattn[...])
        yield

    stages = 13
    parts = MID_PARTS
    size = MID_BLOCK // parts
    works = [row_work(slice(i * size, (i + 1) * size)) for i in range(parts)]
    weights_now = weight_work()
    for tick in range(stages + parts - 1):
        for i, work in enumerate(works):
            if 0 <= tick - i < stages:
                next(work)
        if tick >= stages - 2:
            next(weights_now)
    for _ in weights_now:
        pass

    @pl.when(step == pl.num_programs(0) - 1)
    def _():
        for j, out in enumerate((keep_out, give_out)):
            for part in range(half // width):
                cols = slice(part * width, (part + 1) * width)
                out[cols, :] = acc_up[j, :, cols].astype(BF16)
                out[half + part * width : half + (part + 1) * width, :] = acc_dn[j, :, cols].astype(
                    BF16
                )
            pads = [
                acc_ub[j : j + 1, part * width : (part + 1) * width]
                for part in range(half // width)
            ]
            pads.append(jnp.zeros((16 - len(pads), width), F32))
            out[2 * half : 2 * half + 16, :] = jnp.concatenate(pads, 0).astype(BF16)
        cut = (width + PAD_ROWS) // 2
        low = acc_wo[:cut, :].astype(BF16)
        pads = jnp.zeros((PAD_ROWS - 8, width), F32)
        high = jnp.concatenate([acc_wo[cut:, :], acc_vec[...], pads], 0).astype(BF16)
        first = core[0] == 0
        keep_out[2 * half + 16 :, :] = jnp.where(first, low, high)
        give_out[2 * half + 16 :, :] = jnp.where(first, high, low)


def middle(core, tokens, ctx, cot, wo, ups, dns, ubs, vectors):
    rows, width = tokens.shape
    half = ups[0].shape[1]
    row_spec = pl.BlockSpec((MID_BLOCK, width), lambda i: (i, 0))
    weights = (wo, *ups, *dns, *ubs, *vectors)
    act = jax.ShapeDtypeStruct((rows, width), BF16)
    sums = jax.ShapeDtypeStruct((2 * half + 16 + (width + PAD_ROWS) // 2, width), BF16)
    return pl.pallas_call(
        middle_kernel,
        grid=(rows // MID_BLOCK,),
        in_specs=[smem()] + [row_spec] * 3 + [whole(w.shape) for w in weights],
        out_specs=[row_spec] * 3 + [whole(sums.shape), whole(sums.shape)],
        out_shape=[act, jax.ShapeDtypeStruct((rows, width), F32), act, sums, sums],
        scratch_shapes=[
            pltpu.VMEM((2, width, half), F32),
            pltpu.VMEM((2, width, half), F32),
            pltpu.VMEM((width, width), F32),
            pltpu.VMEM((8, half), F32),
            pltpu.VMEM((8, width), F32),
            pltpu.VMEM((2, MID_BLOCK, half), F32),
            pltpu.VMEM((2, MID_BLOCK, half), BF16),
            pltpu.VMEM((2, MID_BLOCK, half), BF16),
            pltpu.VMEM((MID_BLOCK, width), BF16),
            pltpu.VMEM((MID_BLOCK, width), BF16),
            pltpu.VMEM((MID_BLOCK, width), BF16),
        ],
        compiler_params=params(44),
        cost_estimate=pl.CostEstimate(
            flops=34_000_000_000, bytes_accessed=20_000_000, transcendentals=6_000_000
        ),
        name="middle",
    )(core, tokens, ctx, cot, *weights)


def backward_kernel(
    first,
    blocks,
    short_blocks,
    carried,
    short_len,
    long_len,
    core,
    side,
    q_in,
    k_in,
    v_in,
    ctx_in,
    dctx_in,
    tq_in,
    tk_in,
    tv_in,
    ps_in,
    pl_in,
    *refs,
):
    if carried:
        acc_in, bias_in, *refs = refs[:2] + refs[5:]
    (
        grad_out,
        keep_out,
        give_out,
        acc,
        bias_acc,
        dq_buf,
    dk_buf,
    dv_buf,
    dkt_buf,
    dvt_buf,
    dp_buf,
    exp_buf,
    total_buf,
    ds_buf,
    drel_buf,
    worst,
    ) = refs
    block = lax.rem(first + pl.program_id(0), blocks)

    if carried:

        @pl.when(pl.program_id(0) == 0)
        def _():
            acc[...] = acc_in[...]
            bias_acc[...] = bias_in[...]

    @pl.when(block == 0)
    def _():
        acc[...] = jnp.zeros_like(acc)
        bias_acc[...] = jnp.zeros_like(bias_acc)


    def short_scores(item, found):
        rows = slice(item * SHORT_LEN, (item + 1) * SHORT_LEN)
        length = short_len[block * (BLOCK // SHORT_LEN) + item]
        bias = short_bias(length)[:, : 2 * SHORT_LEN]
        lane = lax.broadcasted_iota(jnp.int32, (1, GROUP * SHORT_LEN), 1)
        flag = (lane % SHORT_LEN < length).astype(F32)
        v, dctx = v_in[rows, :], dctx_in[rows, :]
        found["v_all"], found["dctx_all"] = stack(v, HEAD_DIM), stack(dctx, HEAD_DIM)
        found["p"] = ps_in[0, rows, :]
        v_scaled = stack(scaled(v, EXP_SCALE), HEAD_DIM)
        weighed = (dctx.astype(F32) * ctx_in[rows, :].astype(F32)).T
        delta = [
            jnp.sum(weighed[h * HEAD_DIM : (h + 1) * HEAD_DIM], axis=0, keepdims=True)
            for h in range(GROUP)
        ]
        delta = flag - jnp.concatenate(delta, 1)
        for pair in range(GROUP // 2):
            cols = slice(pair * LANES, (pair + 1) * LANES)
            heads = slice(pair * 2 * SHORT_LEN, (pair + 1) * 2 * SHORT_LEN)
            for kind, (queries, keys) in enumerate(((tq_in, tk_in), (tv_in, tv_in))):
                part = scaled(queries[rows, cols], TEACH_SCALE)
                both = jnp.concatenate([head_mask(part, h, TEACH_HD) for h in range(2)], 0)
                scores = dot_nt(keys[rows, cols], both) + bias
                found[kind, pair] = measured(jnp.exp2(scores), flag[:, heads])
                yield
            scores = dot_nt(v, v_scaled[heads]) + bias
            found[2, pair] = measured(jnp.exp2(scores), flag[:, heads])
            yield
            dp = dot_nt(v, found["dctx_all"][heads]) + delta[:, heads]
            found[3, pair] = dp.astype(BF16)
            yield

    def measured(e, flag):
        total = jnp.sum(e, axis=0, keepdims=True)
        inverse = 1.0 / total
        width = total.shape[1]
        worst[0:1, :width] = jnp.maximum(worst[0:1, :width], jnp.maximum(total, inverse))
        return e.astype(BF16), (flag * inverse).astype(BF16)

    def short_rows(found):
        found["ds"], found["drel"] = [], []
        for pair in range(GROUP // 2):
            heads = slice(pair * 2 * SHORT_LEN, (pair + 1) * 2 * SHORT_LEN)
            teach, teach_rel, own = (found[kind, pair][0] * found[kind, pair][1] for kind in range(3))
            found["ds"].append(found["p"][:, heads] * found[3, pair] - teach)
            yield
            found["drel"].append(own - teach_rel)
            yield

    def short_products(item, found):
        rows = slice(item * SHORT_LEN, (item + 1) * SHORT_LEN)
        ds, drel = (jnp.concatenate(found[name], 1) for name in ("ds", "drel"))
        dq_buf[rows, :] = diagonal(dot_tn(k_in[rows, :], ds)).T * SCALE
        yield
        dk_buf[rows, :] = dot_nn(ds, stack(q_in[rows, :], HEAD_DIM)) * SCALE
        yield
        rel = diagonal(dot_tn(v_in[rows, :], drel)).T
        yield
        rel = rel + dot_nn(drel, found["v_all"])
        yield
        dv_buf[rows, :] = dot_nn(found["p"], found["dctx_all"]) + SCALE * rel
        yield

    def short_items():
        worst[...] = jnp.zeros_like(worst)
        items = BLOCK // SHORT_LEN
        found = [{} for _ in range(items)]
        for tick in range(items + 2):
            works = []
            if tick < items:
                works.append((short_scores(tick, found[tick]), 8))
            if 0 <= tick - 1 < items:
                works.append((short_rows(found[tick - 1]), 4))
            if 0 <= tick - 2:
                works.append((short_products(tick - 2, found[tick - 2]), 5))
            weave(works)

    def short_items_careful():
        @pl.loop(0, BLOCK // SHORT_LEN)
        def _(item):
            rows = pl.ds(pl.multiple_of(item * SHORT_LEN, SHORT_LEN), SHORT_LEN)
            length = short_len[block * (BLOCK // SHORT_LEN) + item]
            bias = short_bias(length)
            lane = lax.broadcasted_iota(jnp.int32, (1, GROUP * SHORT_LEN), 1)
            flag = (lane % SHORT_LEN < length).astype(F32)
            q, k, v = q_in[rows, :], k_in[rows, :], v_in[rows, :]
            dctx, ctx = dctx_in[rows, :], ctx_in[rows, :]
            tq, tk, tv = tq_in[rows, :], tk_in[rows, :], tv_in[rows, :]
            q_all, v_all, dctx_all = (stack(part, HEAD_DIM) for part in (q, v, dctx))
            p = ps_in[0, rows, :]

            def soft(scores, scale):
                e, total = exps(scores * scale + bias, 0, True)
                return e * (flag / total)

            def teach(keys, queries):
                parts = []
                for pair in range(GROUP // 2):
                    cols = slice(pair * LANES, (pair + 1) * LANES)
                    both = [head_mask(queries[:, cols], h, TEACH_HD) for h in range(2)]
                    parts.append(dot_nt(keys[:, cols], jnp.concatenate(both, 0)))
                return soft(jnp.concatenate(parts, 1), TEACH_SCALE)

            weighed = (dctx.astype(F32) * ctx.astype(F32)).T
            delta = [
                jnp.sum(weighed[h * HEAD_DIM : (h + 1) * HEAD_DIM], axis=0, keepdims=True)
                for h in range(GROUP)
            ]
            dp = dot_nt(v, dctx_all) + (flag - jnp.concatenate(delta, 1))
            ds = (p.astype(F32) * dp - teach(tk, tq)).astype(BF16)
            dq_buf[rows, :] = diagonal(dot_tn(k, ds)).T * SCALE
            dk_buf[rows, :] = dot_nn(ds, q_all) * SCALE
            drel = (soft(dot_nt(v, v_all), EXP_SCALE) - teach(tv, tv)).astype(BF16)
            rel = dot_nn(drel, v_all) + diagonal(dot_tn(v, drel)).T
            dv_buf[rows, :] = dot_nn(p, dctx_all) + SCALE * rel


    def long_item():
        worst[...] = jnp.zeros_like(worst)
        length = long_len[block - short_blocks]
        q, k, v = q_in[...], k_in[...], v_in[...]
        dctx, ctx = dctx_in[...], ctx_in[...]
        qt, vt, dctxt = q.T, v.T, dctx.T
        weighed = -(dctx.astype(F32) * ctx.astype(F32)).astype(BF16)
        right = jnp.concatenate([v, jnp.ones_like(v)], 1)
        v_scaled = scaled(v, EXP_SCALE)
        v_keys = biased(v, HEAD_DIM, length)
        flag = query_flag(length, BLOCK)
        flags = jnp.broadcast_to(flag, v.shape).astype(BF16)
        teach = {}

        def teach_pair(source, pair):
            if (source, pair) not in teach:
                part = (tq_in, tk_in, tv_in)[source][:, pair * LANES : (pair + 1) * LANES]
                teach[source, pair] = (
                    biased(part, TEACH_HD, length) if source else None,
                    None if source == 1 else scaled(part, TEACH_SCALE),
                )
            return teach[source, pair]

        def sides(kind, h):
            if kind == 0:
                left, keys = teach_pair(0, h // 2)[1], teach_pair(1, h // 2)[0]
                return masked_sides(left, keys, h % 2, TEACH_HD)
            if kind == 1:
                return masked_sides(v_scaled, v_keys, h, HEAD_DIM)
            if kind == 2:
                keys, left = teach_pair(2, h // 2)
                return masked_sides(left, keys, h % 2, TEACH_HD)
            lane = spare_lane(h, HEAD_DIM)
            extra = head_mask(weighed, h, HEAD_DIM) + flags * lane_row(lambda i: i == lane)
            return jnp.concatenate([head_mask(dctx, h, HEAD_DIM), extra], 1), right

        halves = [slice(i * (BLOCK // 2), (i + 1) * (BLOCK // 2)) for i in range(2)]

        def score_items(h):
            for kind in range(4):
                left, keys = sides(kind, h)
                for j, cols in enumerate(halves):
                    scores = dot_nt(left, keys[cols])
                    if kind == 3:
                        dp_buf[h % 2, :, cols] = scores.astype(BF16)
                    else:
                        e = jnp.exp2(scores)
                        exp_buf[h % 2, kind, :, cols] = e.astype(BF16)
                        part = e[:, :LANES] + e[:, LANES:]
                        if j == 0:
                            total_buf[h % 2, kind] = part
                        else:
                            total_buf[h % 2, kind] += part
                    yield

        def product_items(h):
            dims = slice(h * HEAD_DIM, (h + 1) * HEAD_DIM)
            ds, drel = ds_buf.at[h % 2], drel_buf.at[h % 2]
            for cols in halves:
                dvt_buf[dims, cols] = dot_nn(dctxt[dims, :], pl_in[h, :, cols])
                yield
                dkt_buf[dims, cols] = dot_nn(qt[dims, :], ds[:, cols]) * SCALE
                yield
                dvt_buf[dims, cols] += SCALE * dot_nn(vt[dims, :], drel[:, cols])
                yield
            for buf, grads, keys in ((dq_buf, ds, k), (dv_buf, drel, v)):
                part = dot_nn(grads[...], head_mask(keys, h, HEAD_DIM))
                if h == 0:
                    buf[...] = part
                else:
                    buf[...] += part
                yield

        def row_items(h):
            count = BLOCK // 8
            for i in range(8):
                rows = slice(i * count, (i + 1) * count)

                def soft(kind):
                    total = jnp.sum(total_buf[h % 2, kind, rows, :], axis=1, keepdims=True)
                    inverse = 1.0 / total
                    high = jnp.maximum(total, inverse)
                    worst[:, :LANES] = jnp.maximum(worst[:, :LANES], high)
                    return exp_buf[h % 2, kind, rows, :] * low_rows(flag[rows] * inverse, BLOCK)

                ds_buf[h % 2, rows, :] = pl_in[h, rows, :] * dp_buf[h % 2, rows, :] - soft(0)
                drel_buf[h % 2, rows, :] = soft(1) - soft(2)
                yield

        for h in range(-1, GROUP + 1):
            works = []
            if h + 1 < GROUP:
                works.append((score_items(h + 1), 8))
            if 0 <= h < GROUP:
                works.append((row_items(h), 8))
            if h >= 1:
                works.append((product_items(h - 1), 8))
            weave(works)
        dq_buf[...] *= SCALE
        dk_buf[...] = dkt_buf[...].astype(BF16).T.astype(F32)
        dv_buf[...] = dvt_buf[...].T + SCALE * dv_buf[...]

    def long_item_careful():
        length = long_len[block - short_blocks]
        flag = query_flag(length, BLOCK)
        bias = jnp.where(
            lax.broadcasted_iota(jnp.int32, (1, BLOCK), 1) < length, 0.0, MASKED
        )
        for buf in (dq_buf, dk_buf, dv_buf):
            buf[...] = jnp.zeros_like(buf)

        def soft(queries, keys, h, width, scale):
            scores = dot_nt(head_mask(queries, h, width), keys)
            e, total = exps(scores * scale + bias, 1, True)
            return e * (flag / total)

        @pl.loop(0, GROUP)
        def _(h):
            q, k, v, dctx = (
                head_mask(ref[...], h, HEAD_DIM) for ref in (q_in, k_in, v_in, dctx_in)
            )
            p = pl_in[h]
            delta = jnp.sum(dctx.astype(F32) * ctx_in[...].astype(F32), axis=1, keepdims=True)
            dp = dot_nt(dctx, v) + (flag - delta)
            teach = soft(tq_in[...], tk_in[...], h, TEACH_HD, TEACH_SCALE)
            ds = (p.astype(F32) * dp - teach).astype(BF16)
            own = soft(v, v, h, HEAD_DIM, EXP_SCALE)
            drel = (own - soft(tv_in[...], tv_in[...], h, TEACH_HD, TEACH_SCALE)).astype(BF16)
            dq_buf[...] += dot_nn(ds, k) * SCALE
            dk_buf[...] += dot_tn(ds, q) * SCALE
            dv_buf[...] += dot_tn(p, dctx) + SCALE * (dot_nn(drel, v) + dot_tn(drel, v))

    short = block < short_blocks
    pl.when(short)(short_items)
    pl.when(jnp.logical_not(short))(long_item)
    wild = jnp.logical_not(jnp.max(worst[...]) < LIMIT)
    pl.when(jnp.logical_and(short, wild))(short_items_careful)
    pl.when(jnp.logical_and(jnp.logical_not(short), wild))(long_item_careful)

    grads = jnp.concatenate([buf[...].astype(BF16) for buf in (dq_buf, dk_buf, dv_buf)], 1)
    grad_out[...] = grads
    acc[...] += dot_nn(side[...], grads)
    bias_acc[0:1, :] += column_sum(grads)

    @pl.when(block == blocks - 1)
    def _():
        width = side.shape[0]
        sides = [bias_acc[0:1, w * LANES : (w + 1) * LANES] for w in range(3)]
        full = [acc[:, w * LANES : (w + 1) * LANES] for w in range(3)]
        full = jnp.concatenate([*full, *sides, jnp.zeros((125, LANES), F32)], 0).astype(BF16)
        cut = full.shape[0] // 2
        is_first = core[0] == 0
        keep_out[...] = jnp.where(is_first, full[:cut], full[cut:])
        give_out[...] = jnp.where(is_first, full[cut:], full[:cut])


def attention_backward(steps, short_len, long_len, core, side, acts, p_short, p_long, carry):
    width, rows = side.shape
    blocks = rows // BLOCK
    short_blocks = short_len.shape[0] * SHORT_LEN // BLOCK
    start, stop = steps

    def place(pick):
        return lambda i: pick((start + i) // blocks, (start + i) % blocks)

    def group_spec(size):
        return pl.BlockSpec((BLOCK, size), place(lambda g, b: (b, g)))

    p_specs = [
        pl.BlockSpec(
            (1, BLOCK, BLOCK), place(lambda g, b: (g, jnp.minimum(b, short_blocks - 1), 0))
        ),
        pl.BlockSpec(
            (GROUP, BLOCK, BLOCK), place(lambda g, b: (g, jnp.maximum(b - short_blocks, 0), 0))
        ),
    ]
    cut = (3 * width + 128) // 2
    sums = jax.ShapeDtypeStruct((GROUPS * cut, LANES), BF16)
    acc = jax.ShapeDtypeStruct((width, 3 * LANES), F32)
    bias_acc = jax.ShapeDtypeStruct((8, 3 * LANES), F32)
    half_spec = pl.BlockSpec((cut, LANES), place(lambda g, b: (g, 0)))
    square = (BLOCK, LANES)
    ins = [short_len, long_len, core, side, *acts, p_short, p_long]
    carry_specs = []
    aliases = {}
    if carry is not None:
        grads, keep, give, acc_in, bias_in = carry
        aliases = {len(ins) + 2 + i: i for i in range(3)}
        ins += [acc_in, bias_in, grads, keep, give]
        carry_specs = [whole(acc.shape), whole(bias_acc.shape)]
        carry_specs += [pl.BlockSpec(memory_space=pl.ANY)] * 3
    return pl.pallas_call(
        functools.partial(backward_kernel, start, blocks, short_blocks, carry is not None),
        grid=(stop - start,),
        in_specs=[smem(), smem(), smem()]
        + [pl.BlockSpec((width, BLOCK), place(lambda g, b: (0, b)))]
        + [group_spec(LANES)] * 5
        + [group_spec(GROUP * TEACH_HD)] * 3
        + p_specs
        + carry_specs,
        out_specs=[
            pl.BlockSpec((BLOCK, 3 * LANES), place(lambda g, b: (b, g))),
            half_spec,
            half_spec,
            whole(acc.shape),
            whole(bias_acc.shape),
        ],
        out_shape=[
            jax.ShapeDtypeStruct((rows, GROUPS * 3 * LANES), BF16),
            sums,
            sums,
            acc,
            bias_acc,
        ],
        scratch_shapes=[
            pltpu.VMEM(square, F32),
            pltpu.VMEM(square, F32),
            pltpu.VMEM(square, F32),
            pltpu.VMEM((LANES, BLOCK), F32),
            pltpu.VMEM((LANES, BLOCK), F32),
            pltpu.VMEM((2, BLOCK, BLOCK), BF16),
            pltpu.VMEM((2, 3, BLOCK, BLOCK), BF16),
            pltpu.VMEM((2, 3, BLOCK, LANES), F32),
            pltpu.VMEM((2, BLOCK, BLOCK), BF16),
            pltpu.VMEM((2, BLOCK, BLOCK), BF16),
            pltpu.VMEM((BLOCK // 8, 2 * SHORT_LEN), F32),
        ],
        input_output_aliases=aliases,
        compiler_params=params(60),
        cost_estimate=pl.CostEstimate(
            flops=(stop - start) * 7_000_000_000,
            bytes_accessed=(stop - start) * 4_000_000,
            transcendentals=(stop - start) * 2_000_000,
        ),
        name=f"attention_backward_{start}",
    )(*ins)


def tokens_grad_kernel(dres, wq, wk, wv, grads, out):
    weights = jnp.concatenate(
        [w[:, g * LANES : (g + 1) * LANES] for g in range(GROUPS) for w in (wq, wk, wv)], 1
    )
    out[...] = (dres[...] + dot_nt(grads[...], weights)).astype(BF16)


def tokens_gradient(dres, wq, wk, wv, grads):
    rows, width = dres.shape
    row_spec = pl.BlockSpec((BLOCK, width), lambda i: (i, 0))
    return pl.pallas_call(
        tokens_grad_kernel,
        grid=(rows // BLOCK,),
        in_specs=[row_spec]
        + [whole(wq.shape)] * 3
        + [pl.BlockSpec((BLOCK, grads.shape[1]), lambda i: (i, 0))],
        out_specs=row_spec,
        out_shape=jax.ShapeDtypeStruct((rows, width), BF16),
        compiler_params=params(56),
        cost_estimate=pl.CostEstimate(
            flops=2_000_000_000, bytes_accessed=10_000_000, transcendentals=0
        ),
        name="tokens_gradient",
    )(dres, wq, wk, wv, grads)


def swap(value):
    return lax.ppermute(value, "tensor", [(0, 1), (1, 0)])


def spread(value):
    return lax.all_to_all(value, "dp", 0, 0, tiled=True)


def sum_chain(keep, give, count):
    (got,) = yield 0, [(swap, give)]
    both = (keep.astype(F32) + got.astype(F32)).astype(BF16)
    rows, width = both.shape
    (got,) = yield 1, [(spread, both.reshape(count, rows // count, width))]
    part = jnp.sum(got.astype(F32), axis=0).astype(BF16)
    (got,) = yield 1, [(spread, jnp.broadcast_to(part[None], got.shape))]
    return got.reshape(rows, width)


def ordered(core, mine, other):
    first = core[0] == 0
    return jnp.where(first, mine, other), jnp.where(first, other, mine)


def first_finish_kernel(core, total, other, up_out, ub_out, dn_out, wo_out, *vector_outs):
    width, half = up_out.shape
    count = half // width
    for part in range(count):
        cols = slice(part * width, (part + 1) * width)
        up_out[:, cols] = total[cols, :].astype(F32)
        dn_out[cols, :] = total[half + part * width : half + (part + 1) * width, :].astype(F32).T
    biases = total[2 * half : 2 * half + 16, :].astype(F32)
    ub_out[...] = jnp.concatenate([biases[i : i + 1] for i in range(count)], 1).reshape(half)
    halves = ordered(core, total[2 * half + 16 :, :].astype(F32), other[...].astype(F32))
    both = jnp.concatenate(halves, 0)
    wo_out[...] = both[:width]
    for i, out in enumerate(vector_outs):
        out[...] = both[width + i : width + i + 1].reshape(width)


def first_finish(core, total, other, half):
    width = total.shape[1]
    shapes = [(width, half), (half,), (half, width), (width, width)] + [(width,)] * 6
    return pl.pallas_call(
        first_finish_kernel,
        in_specs=[smem()] + [pl.BlockSpec(memory_space=pltpu.VMEM)] * 2,
        out_shape=[jax.ShapeDtypeStruct(shape, F32) for shape in shapes],
        compiler_params=params(16),
        name="first_finish",
    )(core, total, other)


def qkv_finish_kernel(core, total, other, wq_out, wk_out, wv_out, bq_out, bv_out):
    width = wq_out.shape[0]
    low, high = ordered(core, total[...].astype(F32), other[...].astype(F32))
    cut = low.shape[0] // GROUPS
    sides = []
    for g in range(GROUPS):
        rows = slice(g * cut, (g + 1) * cut)
        full = jnp.concatenate([low[rows], high[rows]], 0)
        cols = slice(g * LANES, (g + 1) * LANES)
        for w, out in enumerate((wq_out, wk_out, wv_out)):
            out[:, cols] = full[w * width : (w + 1) * width]
        sides.append(full[3 * width : 3 * width + 8])
    sides = jnp.concatenate(sides, 1)
    bq_out[...] = sides[0:1].reshape(width)
    bv_out[...] = sides[2:3].reshape(width)


def qkv_finish(core, total, other, width):
    shapes = [(width, width)] * 3 + [(width,)] * 2
    return pl.pallas_call(
        qkv_finish_kernel,
        in_specs=[smem()] + [pl.BlockSpec(memory_space=pltpu.VMEM)] * 2,
        out_shape=[jax.ShapeDtypeStruct(shape, F32) for shape in shapes],
        compiler_params=params(16),
        name="qkv_finish",
    )(core, total, other)


class Flights:
    def __init__(self):
        self.asked = {}
        self.flying = {}
        self.done = {}

    def advance(self, name, generator, got=None):
        try:
            span, wants = next(generator) if got is None else generator.send(got)
            self.asked[name] = (generator, span, wants)
        except StopIteration as end:
            self.done[name] = end.value

    def step(self, token, work=None):
        asked, self.asked = self.asked, {}
        sends = [value for _, _, wants in asked.values() for _, value in wants]
        token, *sends = lax.optimization_barrier((token, *sends))
        sent = iter(sends)
        for name, (generator, span, wants) in asked.items():
            self.flying[name] = [generator, span, [move(next(sent)) for move, _ in wants]]
        result = None
        if work is not None:
            result, token = work(token)
        for name, (generator, span, got) in list(self.flying.items()):
            if work is not None:
                token, *got = lax.optimization_barrier((token, *got))
            del self.flying[name]
            self.advance(name, generator, got)
        return result, token


def per_device(
    dp_count,
    tokens,
    query_weight,
    query_bias,
    key_weight,
    value_weight,
    value_bias,
    proj_weight,
    proj_bias,
    first_gain,
    first_shift,
    up_weight,
    up_bias,
    down_weight,
    down_bias,
    second_gain,
    second_shift,
    teach_query,
    teach_key,
    teach_value,
    short_lengths,
    long_lengths,
    cotangent,
):
    width = tokens.shape[1]
    half = up_weight.shape[1]

    up_other, down_other, ub_other = (swap(value) for value in (up_weight, down_weight, up_bias))
    core = lax.axis_index("tensor").astype(jnp.int32).reshape(1)
    q, k, v, ctx, p_short, p_long, side = attention_forward(
        tokens,
        query_weight,
        key_weight,
        value_weight,
        query_bias,
        value_bias,
        short_lengths,
        long_lengths,
    )
    block_out, dres, dctx, keep, give = middle(
        core,
        tokens,
        ctx,
        cotangent,
        proj_weight,
        (up_weight, up_other),
        (down_weight, down_other),
        (up_bias, ub_other),
        (proj_bias, first_gain, first_shift, down_bias, second_gain, second_shift),
    )
    flights = Flights()
    flights.advance("first", sum_chain(keep, give, dp_count))
    flights.step(short_lengths)
    acts = (q, k, v, ctx, dctx, teach_query, teach_key, teach_value)
    steps = GROUPS * (tokens.shape[0] // BLOCK)
    token = short_lengths
    carry = None
    for piece in ((0, steps // 2), (steps // 2, steps)):

        def work(lens):
            out = attention_backward(
                piece, lens, long_lengths, core, side, acts, p_short, p_long, carry
            )
            return out[:1] + out[2:], out[1]

        (grads, give, *sums), keep = flights.step(token, work)
        token, keep = lax.optimization_barrier((short_lengths, keep))
        carry = [grads, keep, give, *sums]
    flights.advance("qkv", sum_chain(keep, give, dp_count))
    flights.step(short_lengths)

    def input_work(grads):
        return None, tokens_gradient(dres, query_weight, key_weight, value_weight, grads)

    _, tokens_grad = flights.step(grads, input_work)
    total = flights.done["first"]
    other = swap(total[2 * half + 16 :])

    def first_work(total):
        out = first_finish(core, total, other, half)
        return out[1:], out[0]

    first, up_grad = flights.step(total, first_work)
    total = flights.done["qkv"]
    qkv = qkv_finish(core, total, swap(total), width)
    up_bias_grad, down_grad, proj_grad, *vectors = first
    return (
        block_out,
        tokens_grad,
        qkv[0],
        qkv[3],
        qkv[1],
        qkv[2],
        qkv[4],
        proj_grad,
        vectors[0],
        vectors[1],
        vectors[2],
        up_grad,
        up_bias_grad,
        down_grad,
        vectors[3],
        vectors[4],
        vectors[5],
    )


def solution(mesh):
    in_specs = (
        P(("dp", "tensor"), None),
        P(),
        P(),
        P(),
        P(),
        P(),
        P(),
        P(),
        P(),
        P(),
        P(None, "tensor"),
        P("tensor"),
        P("tensor", None),
        P(),
        P(),
        P(),
        P(("dp", "tensor"), None),
        P(("dp", "tensor"), None),
        P(("dp", "tensor"), None),
        P(("dp", "tensor")),
        P(("dp", "tensor")),
        P(("dp", "tensor"), None),
    )
    out_specs = (
        P(("dp", "tensor"), None),
        P(("dp", "tensor"), None),
        P(),
        P(),
        P(),
        P(),
        P(),
        P(),
        P(),
        P(),
        P(),
        P(None, "tensor"),
        P("tensor"),
        P("tensor", None),
        P(),
        P(),
        P(),
    )
    return jax.shard_map(
        functools.partial(per_device, mesh.shape["dp"]),
        mesh=mesh,
        in_specs=in_specs,
        out_specs=out_specs,
        check_vma=False,
    )
```

```python
import functools

import jax
import jax.numpy as jnp
from jax import lax
from jax.experimental import pallas as pl
from jax.experimental.pallas import tpu as pltpu
from jax.sharding import PartitionSpec as P

HEADS = 12
HEAD_DIM = 32
TEACH_HD = 64
SHORT_LEN = 128
GROUP = 4
LANES = GROUP * HEAD_DIM
GROUPS = HEADS // GROUP
BLOCK = 512
MID_BLOCK = 1024
MID_PARTS = 2
PAD_ROWS = 96
SPLIT = 7

MASKED = -1e30
LIMIT = 2.0**64
EPSILON = 1e-06
LOG2E = 1.4426950408889634
SCALE = HEAD_DIM**-0.5
EXP_SCALE = LOG2E * SCALE
TEACH_SCALE = LOG2E * TEACH_HD**-0.5
MIB = 2**20

F32 = jnp.float32
BF16 = jnp.bfloat16


def dot_nn(left, right):
    return lax.dot_general(left, right, (((1,), (0,)), ((), ())), preferred_element_type=F32)


def dot_nt(left, right):
    return lax.dot_general(left, right, (((1,), (1,)), ((), ())), preferred_element_type=F32)


def dot_tn(left, right):
    return lax.dot_general(left, right, (((0,), (0,)), ((), ())), preferred_element_type=F32)


def dot_tt(left, right):
    return lax.dot_general(left, right, (((0,), (1,)), ((), ())), preferred_element_type=F32)


def lane_row(condition, width=LANES):
    lane = lax.broadcasted_iota(jnp.int32, (1, width), 1)
    return condition(lane).astype(F32).astype(BF16)


def head_mask(block, head, width):
    return block * lane_row(lambda lane: lane // width == head, block.shape[1])


def scaled(block, factor):
    return (block.astype(F32) * factor).astype(BF16)


def spare_lane(head, width):
    return LANES - width if head * width < LANES // 2 else 0


def with_bias(keys, lane, length):
    row = lax.broadcasted_iota(jnp.int32, keys.shape, 0)
    column = lax.broadcasted_iota(jnp.int32, keys.shape, 1)
    bias = jnp.where(row < length, 0.0, MASKED).astype(BF16)
    return jnp.where(column == lane, bias, keys)


def masked_sides(queries, keys, head, width):
    lane = spare_lane(head, width)
    one = lane_row(lambda index: index == lane)
    return head_mask(queries, head, width) + one, keys[lane]


def biased(keys, width, length):
    return {lane: with_bias(keys, lane, length) for lane in (LANES - width, 0)}


def query_flag(length, size):
    return (lax.broadcasted_iota(jnp.int32, (size, 1), 0) < length).astype(F32)


def weave(works):
    ticks = max(count for _, count in works)
    for tick in range(ticks):
        for work, count in works:
            if (tick + 1) * count // ticks > tick * count // ticks:
                next(work)
    for work, _ in works:
        for _ in work:
            pass


def exps(scores, axis, careful):
    if careful:
        scores = scores - jnp.max(scores, axis=axis, keepdims=True)
    heights = jnp.exp2(scores)
    return heights, jnp.sum(heights, axis=axis, keepdims=True)


def low_rows(column, size):
    block = jnp.broadcast_to(column, (column.shape[0], LANES)).astype(BF16)
    return jnp.concatenate([block] * (size // LANES), 1)


def short_bias(length):
    shape = (SHORT_LEN, GROUP * SHORT_LEN)
    return jnp.where(lax.broadcasted_iota(jnp.int32, shape, 0) < length, 0.0, MASKED)


def stack(block, width):
    return jnp.concatenate([head_mask(block, h, width) for h in range(GROUP)], 0)


def diagonal(block):
    return jnp.concatenate(
        [
            block[h * HEAD_DIM : (h + 1) * HEAD_DIM, h * SHORT_LEN : (h + 1) * SHORT_LEN]
            for h in range(GROUP)
        ],
        0,
    )


def params(mebibytes):
    return pltpu.CompilerParams(vmem_limit_bytes=mebibytes * MIB)


def whole(shape):
    return pl.BlockSpec(shape, lambda i: (0,) * len(shape))


def smem():
    return pl.BlockSpec(memory_space=pltpu.SMEM)


def forward_kernel(
    short_blocks,
    short_len,
    long_len,
    tokens,
    wq,
    wk,
    wv,
    bq,
    bv,
    q_out,
    k_out,
    v_out,
    ctx_out,
    ps_out,
    pl_out,
    side_out,
    worst,
    p_buf,
    p_sems,
):
    step = pl.program_id(0)
    x = tokens[...]
    side_out[...] = x.T
    q_out[...] = (dot_nn(x, wq[...]) + row_of(bq)).astype(BF16)
    k_out[...] = dot_nn(x, wk[...]).astype(BF16)
    v_out[...] = (dot_nn(x, wv[...]) + row_of(bv)).astype(BF16)

    def note(total, inverse):
        high = jnp.maximum(total, inverse)
        rows = high.shape[0]
        for i in range(max(high.shape[1] // LANES, 1)):
            part = high[:, i * LANES : (i + 1) * LANES]
            worst[:rows, :] = jnp.maximum(worst[:rows, :], part)


    def short_scores(item, g, found):
        rows = slice(item * SHORT_LEN, (item + 1) * SHORT_LEN)
        cols = slice(g * LANES, (g + 1) * LANES)
        bias = short_bias(short_len[step * (BLOCK // SHORT_LEN) + item])[:, : 2 * SHORT_LEN]
        queries = stack(scaled(q_out[rows, cols], EXP_SCALE), HEAD_DIM)
        for pair in range(GROUP // 2):
            heads = slice(pair * 2 * SHORT_LEN, (pair + 1) * 2 * SHORT_LEN)
            e, total = exps(dot_nt(k_out[rows, cols], queries[heads]) + bias, 0, False)
            found[pair] = e.astype(BF16), total
            yield

    def short_rows(item, g, found):
        rows = slice(item * SHORT_LEN, (item + 1) * SHORT_LEN)
        for pair in range(GROUP // 2):
            heads = slice(pair * 2 * SHORT_LEN, (pair + 1) * 2 * SHORT_LEN)
            e, total = found[pair]
            inverse = 1.0 / total
            note(total, inverse)
            found[pair] = e * inverse.astype(BF16)
            ps_out[g, rows, heads] = found[pair]
            yield

    def short_products(item, g, found):
        rows = slice(item * SHORT_LEN, (item + 1) * SHORT_LEN)
        cols = slice(g * LANES, (g + 1) * LANES)
        probs = jnp.concatenate([found[pair] for pair in range(GROUP // 2)], 1)
        ctx_out[rows, cols] = diagonal(dot_tn(v_out[rows, cols], probs)).T.astype(BF16)
        yield

    def short_items():
        units = [(item, g, {}) for item in range(BLOCK // SHORT_LEN) for g in range(GROUPS)]
        for tick in range(len(units) + 2):
            works = []
            if tick < len(units):
                works.append((short_scores(*units[tick]), 2))
            if 0 <= tick - 1 < len(units):
                works.append((short_rows(*units[tick - 1]), 2))
            if 0 <= tick - 2:
                works.append((short_products(*units[tick - 2]), 1))
            weave(works)


    def p_copy(g):
        index = step - short_blocks
        slot = lax.rem(index * GROUPS + g, 2)
        heads = pl.ds(g * GROUP, GROUP)
        rows = pl.ds(index * BLOCK, BLOCK)
        return pltpu.make_async_copy(
            p_buf.at[slot], pl_out.at[heads, rows, :], p_sems.at[slot]
        )

    def p_slot(g):
        return p_buf.at[lax.rem((step - short_blocks) * GROUPS + g, 2)]

    def long_item():
        length = long_len[step - short_blocks]
        halves = [slice(i * (BLOCK // 2), (i + 1) * (BLOCK // 2)) for i in range(2)]

        @pl.loop(0, GROUPS)
        def _(g):
            p_now = p_slot(g)

            @pl.when((step - short_blocks) * GROUPS + g >= 2)
            def _():
                p_copy(g).wait()

            cols = pl.ds(pl.multiple_of(g * LANES, LANES), LANES)
            queries = scaled(q_out[:, cols], EXP_SCALE)
            keys = biased(k_out[:, cols], HEAD_DIM, length)
            values = v_out[:, cols]
            sums = []

            def scores(h, found):
                left, right = masked_sides(queries, keys, h, HEAD_DIM)
                for half in halves:
                    e = jnp.exp2(dot_nt(left, right[half]))
                    part = e[:, :LANES] + e[:, LANES:]
                    found["sum"] = found["sum"] + part if "sum" in found else part
                    found[half.start] = e.astype(BF16)
                    yield

            def normalise(h, found):
                count = BLOCK // 4
                for i in range(4):
                    rows = slice(i * count, (i + 1) * count)
                    total = jnp.sum(found["sum"][rows], axis=1, keepdims=True)
                    inverse = 1.0 / total
                    note(total, inverse)
                    e = jnp.concatenate([found[half.start][rows] for half in halves], 1)
                    p_now[h, rows, :] = e * low_rows(inverse, BLOCK)
                    yield

            def products(h):
                part = dot_nn(p_now[h], head_mask(values, h, HEAD_DIM))
                sums.append(part)
                yield

            found = [{} for _ in range(GROUP)]
            for tick in range(GROUP + 2):
                works = []
                if tick < GROUP:
                    works.append((scores(tick, found[tick]), 2))
                if 0 <= tick - 1 < GROUP:
                    works.append((normalise(tick - 1, found[tick - 1]), 4))
                if 0 <= tick - 2:
                    works.append((products(tick - 2), 1))
                weave(works)
            ctx_out[:, cols] = functools.reduce(jnp.add, sums).astype(BF16)
            p_copy(g).start()


    def short_items_careful():
        items = BLOCK // SHORT_LEN

        @pl.loop(0, items)
        def _(item):
            rows = pl.ds(pl.multiple_of(item * SHORT_LEN, SHORT_LEN), SHORT_LEN)
            bias = short_bias(short_len[step * items + item])
            for g in range(GROUPS):
                cols = slice(g * LANES, (g + 1) * LANES)
                q, k, v = q_out[rows, cols], k_out[rows, cols], v_out[rows, cols]
                e, total = exps(dot_nt(k, stack(q, HEAD_DIM)) * EXP_SCALE + bias, 0, True)
                probs = (e * (1.0 / total)).astype(BF16)
                ps_out[g, rows, :] = probs
                ctx_out[rows, cols] = diagonal(dot_tn(v, probs)).T.astype(BF16)

    def long_item_careful():
        length = long_len[step - short_blocks]
        bias = jnp.where(lax.broadcasted_iota(jnp.int32, (1, BLOCK), 1) < length, 0.0, MASKED)
        p_copy(1).wait()
        p_copy(2).wait()

        @pl.loop(0, GROUPS)
        def _(g):
            p_now = p_slot(g)
            cols = pl.ds(pl.multiple_of(g * LANES, LANES), LANES)
            q, k, v = q_out[:, cols], k_out[:, cols], v_out[:, cols]
            ctx = jnp.zeros((BLOCK, LANES), F32)
            for h in range(GROUP):
                scores = dot_nt(head_mask(q, h, HEAD_DIM), k) * EXP_SCALE + bias
                e, total = exps(scores, 1, True)
                probs = (e * (1.0 / total)).astype(BF16)
                p_now[h] = probs
                ctx = ctx + dot_nn(probs, head_mask(v, h, HEAD_DIM))
            ctx_out[:, cols] = ctx.astype(BF16)
            p_copy(g).start()

            @pl.when(g == 0)
            def _():
                p_copy(g).wait()

    short = step < short_blocks
    long = jnp.logical_not(short)
    worst[...] = jnp.zeros_like(worst)
    pl.when(short)(short_items)
    pl.when(long)(long_item)
    wild = jnp.logical_not(jnp.max(worst[...]) < LIMIT)
    pl.when(jnp.logical_and(short, wild))(short_items_careful)
    pl.when(jnp.logical_and(long, wild))(long_item_careful)

    @pl.when(step == pl.num_programs(0) - 1)
    def _():
        p_copy(1).wait()
        p_copy(2).wait()


def attention_forward(tokens, wq, wk, wv, bq, bv, short_len, long_len):
    rows, width = tokens.shape
    blocks = rows // BLOCK
    short_blocks = short_len.shape[0] * SHORT_LEN // BLOCK
    long_blocks = blocks - short_blocks
    row_spec = pl.BlockSpec((BLOCK, width), lambda i: (i, 0))
    act = jax.ShapeDtypeStruct((rows, width), BF16)
    return pl.pallas_call(
        functools.partial(forward_kernel, short_blocks),
        grid=(blocks,),
        in_specs=[smem(), smem(), row_spec]
        + [whole(a.shape) for a in (wq, wk, wv, bq, bv)],
        out_specs=[
            row_spec,
            row_spec,
            row_spec,
            row_spec,
            pl.BlockSpec((GROUPS, BLOCK, BLOCK), lambda i: (0, jnp.minimum(i, short_blocks - 1), 0)),
            pl.BlockSpec(memory_space=pl.ANY),
            pl.BlockSpec((width, BLOCK), lambda i: (0, i)),
        ],
        out_shape=[
            act,
            act,
            act,
            act,
            jax.ShapeDtypeStruct((GROUPS, short_blocks * BLOCK, BLOCK), BF16),
            jax.ShapeDtypeStruct((HEADS, long_blocks * BLOCK, BLOCK), BF16),
            jax.ShapeDtypeStruct((width, rows), BF16),
        ],
        scratch_shapes=[
            pltpu.VMEM((BLOCK // 4, LANES), F32),
            pltpu.VMEM((2, GROUP, BLOCK, BLOCK), BF16),
            pltpu.SemaphoreType.DMA((2,)),
        ],
        compiler_params=params(56),
        cost_estimate=pl.CostEstimate(
            flops=12_000_000_000, bytes_accessed=24_000_000, transcendentals=8_000_000
        ),
        name="attention_forward",
    )(short_len, long_len, tokens, wq, wk, wv, bq, bv)


def norm_parts(resid):
    centred = resid - jnp.mean(resid, axis=-1, keepdims=True)
    spread = jnp.mean(centred * centred, axis=-1, keepdims=True)
    root = lax.rsqrt(spread + EPSILON)
    return centred * root, root


def norm_back(grad, y, root):
    return root * (
        grad
        - jnp.mean(grad, axis=-1, keepdims=True)
        - y * jnp.mean(grad * y, axis=-1, keepdims=True)
    )


def row_of(vector):
    return vector[...].astype(F32).reshape(1, vector.shape[0])


def column_sum(block):
    return jnp.sum(block.astype(F32), axis=0, keepdims=True)


def middle_kernel(
    core,
    tokens,
    ctx,
    cot,
    wo,
    up0,
    up1,
    dn0,
    dn1,
    ub0,
    ub1,
    bo_in,
    gain1_in,
    shift1_in,
    db_in,
    gain2_in,
    shift2_in,
    block_out,
    dres_out,
    dctx_out,
    keep_out,
    give_out,
    acc_up,
    acc_dn,
    acc_wo,
    acc_ub,
    acc_vec,
    slope,
    active,
    dpre,
    low_rows_buf,
    dbranch,
    dattn,
):
    step = pl.program_id(0)
    half = up0.shape[1]
    width = up0.shape[0]

    @pl.when(step == 0)
    def _():
        for ref in (acc_up, acc_dn, acc_wo, acc_ub, acc_vec):
            ref[...] = jnp.zeros_like(ref)

    bo, gain1, shift1, db, gain2, shift2 = (
        row_of(ref) for ref in (bo_in, gain1_in, shift1_in, db_in, gain2_in, shift2_in)
    )
    def gelu(j, pre, rows):
        pre = pre + row_of((ub0, ub1)[j])
        phi = 0.5 + 0.5 * lax.erf(pre * (0.5**0.5))
        slope[j, rows, :] = phi + pre * (jnp.exp2(pre * pre * (-0.5 * LOG2E)) * 0.3989422804014327)
        active[j, rows, :] = (pre * phi).astype(BF16)

    def back_gelu(j, dactive, rows):
        grad = (dactive * slope[j, rows, :]).astype(BF16)
        dpre[j, rows, :] = grad
        acc_ub[j : j + 1, :] += column_sum(grad)
        return grad

    def row_work(rows):
        resid = tokens[rows, :].astype(F32) + dot_nn(ctx[rows, :], wo[...]) + bo
        yield
        y1, root1 = norm_parts(resid)
        normed = y1 * gain1 + shift1
        normed_low = normed.astype(BF16)
        low_rows_buf[rows, :] = normed_low
        mid = normed + db
        yield
        pre0 = dot_nn(normed_low, up0[...])
        yield
        pre1 = dot_nn(normed_low, up1[...])
        gelu(0, pre0, rows)
        yield
        mid = mid + dot_nn(active[0, rows, :], dn0[...])
        gelu(1, pre1, rows)
        yield
        mid = mid + dot_nn(active[1, rows, :], dn1[...])
        yield
        y2, root2 = norm_parts(mid)
        block_out[rows, :] = (y2 * gain2 + shift2).astype(BF16)
        cotangent = cot[rows, :].astype(F32)
        dmid = norm_back(cotangent * gain2, y2, root2)
        dbranch_low = dmid.astype(BF16)
        dbranch[rows, :] = dbranch_low
        acc_vec[3:4, :] += column_sum(dbranch_low)
        acc_vec[4:5, :] += column_sum(cotangent * y2)
        acc_vec[5:6, :] += column_sum(cotangent)
        yield
        dactive0 = dot_nt(dbranch_low, dn0[...])
        yield
        dactive1 = dot_nt(dbranch_low, dn1[...])
        dpre0 = back_gelu(0, dactive0, rows)
        yield
        dnormed = dmid + dot_nt(dpre0, up0[...])
        dpre1 = back_gelu(1, dactive1, rows)
        yield
        dnormed = dnormed + dot_nt(dpre1, up1[...])
        yield
        acc_vec[1:2, :] += column_sum(dnormed * y1)
        acc_vec[2:3, :] += column_sum(dnormed)
        dres = norm_back(dnormed * gain1, y1, root1)
        dres_out[rows, :] = dres
        dattn_low = dres.astype(BF16)
        dattn[rows, :] = dattn_low
        acc_vec[0:1, :] += column_sum(dattn_low)
        yield
        dctx_out[rows, :] = dot_nt(dattn_low, wo[...]).astype(BF16)
        yield

    def weight_work():
        for j in range(2):
            acc_dn[j] += dot_tn(dbranch[...], active[j])
            yield
        for j in range(2):
            acc_up[j] += dot_tn(low_rows_buf[...], dpre[j])
            yield
        acc_wo[...] += dot_tn(ctx[...], dattn[...])
        yield

    stages = 13
    parts = MID_PARTS
    size = MID_BLOCK // parts
    works = [row_work(slice(i * size, (i + 1) * size)) for i in range(parts)]
    weights_now = weight_work()
    for tick in range(stages + parts - 1):
        for i, work in enumerate(works):
            if 0 <= tick - i < stages:
                next(work)
        if tick >= stages - 2:
            next(weights_now)
    for _ in weights_now:
        pass

    @pl.when(step == pl.num_programs(0) - 1)
    def _():
        for j, out in enumerate((keep_out, give_out)):
            for part in range(half // width):
                cols = slice(part * width, (part + 1) * width)
                out[cols, :] = acc_up[j, :, cols].astype(BF16)
                out[half + part * width : half + (part + 1) * width, :] = acc_dn[j, :, cols].astype(
                    BF16
                )
            pads = [
                acc_ub[j : j + 1, part * width : (part + 1) * width]
                for part in range(half // width)
            ]
            pads.append(jnp.zeros((16 - len(pads), width), F32))
            out[2 * half : 2 * half + 16, :] = jnp.concatenate(pads, 0).astype(BF16)
        cut = (width + PAD_ROWS) // 2
        low = acc_wo[:cut, :].astype(BF16)
        pads = jnp.zeros((PAD_ROWS - 8, width), F32)
        high = jnp.concatenate([acc_wo[cut:, :], acc_vec[...], pads], 0).astype(BF16)
        first = core[0] == 0
        keep_out[2 * half + 16 :, :] = jnp.where(first, low, high)
        give_out[2 * half + 16 :, :] = jnp.where(first, high, low)


def middle(core, tokens, ctx, cot, wo, ups, dns, ubs, vectors):
    rows, width = tokens.shape
    half = ups[0].shape[1]
    row_spec = pl.BlockSpec((MID_BLOCK, width), lambda i: (i, 0))
    weights = (wo, *ups, *dns, *ubs, *vectors)
    act = jax.ShapeDtypeStruct((rows, width), BF16)
    sums = jax.ShapeDtypeStruct((2 * half + 16 + (width + PAD_ROWS) // 2, width), BF16)
    return pl.pallas_call(
        middle_kernel,
        grid=(rows // MID_BLOCK,),
        in_specs=[smem()] + [row_spec] * 3 + [whole(w.shape) for w in weights],
        out_specs=[row_spec] * 3 + [whole(sums.shape), whole(sums.shape)],
        out_shape=[act, jax.ShapeDtypeStruct((rows, width), F32), act, sums, sums],
        scratch_shapes=[
            pltpu.VMEM((2, width, half), F32),
            pltpu.VMEM((2, width, half), F32),
            pltpu.VMEM((width, width), F32),
            pltpu.VMEM((8, half), F32),
            pltpu.VMEM((8, width), F32),
            pltpu.VMEM((2, MID_BLOCK, half), F32),
            pltpu.VMEM((2, MID_BLOCK, half), BF16),
            pltpu.VMEM((2, MID_BLOCK, half), BF16),
            pltpu.VMEM((MID_BLOCK, width), BF16),
            pltpu.VMEM((MID_BLOCK, width), BF16),
            pltpu.VMEM((MID_BLOCK, width), BF16),
        ],
        compiler_params=params(44),
        cost_estimate=pl.CostEstimate(
            flops=34_000_000_000, bytes_accessed=20_000_000, transcendentals=6_000_000
        ),
        name="middle",
    )(core, tokens, ctx, cot, *weights)


def backward_kernel(
    first,
    blocks,
    short_blocks,
    carried,
    short_len,
    long_len,
    core,
    side,
    q_in,
    k_in,
    v_in,
    ctx_in,
    dctx_in,
    tq_in,
    tk_in,
    tv_in,
    ps_in,
    pl_in,
    *refs,
):
    if carried:
        acc_in, bias_in, *refs = refs[:2] + refs[5:]
    (
        grad_out,
        keep_out,
        give_out,
        acc,
        bias_acc,
        dq_buf,
    dk_buf,
    dv_buf,
    dkt_buf,
    dvt_buf,
    dp_buf,
    exp_buf,
    total_buf,
    ds_buf,
    drel_buf,
    worst,
    ) = refs
    block = lax.rem(first + pl.program_id(0), blocks)

    if carried:

        @pl.when(pl.program_id(0) == 0)
        def _():
            acc[...] = acc_in[...]
            bias_acc[...] = bias_in[...]

    @pl.when(block == 0)
    def _():
        acc[...] = jnp.zeros_like(acc)
        bias_acc[...] = jnp.zeros_like(bias_acc)


    def short_scores(item, found):
        rows = slice(item * SHORT_LEN, (item + 1) * SHORT_LEN)
        length = short_len[block * (BLOCK // SHORT_LEN) + item]
        bias = short_bias(length)[:, : 2 * SHORT_LEN]
        lane = lax.broadcasted_iota(jnp.int32, (1, GROUP * SHORT_LEN), 1)
        flag = (lane % SHORT_LEN < length).astype(F32)
        v, dctx = v_in[rows, :], dctx_in[rows, :]
        found["v_all"], found["dctx_all"] = stack(v, HEAD_DIM), stack(dctx, HEAD_DIM)
        found["p"] = ps_in[0, rows, :]
        v_scaled = stack(scaled(v, EXP_SCALE), HEAD_DIM)
        weighed = (dctx.astype(F32) * ctx_in[rows, :].astype(F32)).T
        delta = [
            jnp.sum(weighed[h * HEAD_DIM : (h + 1) * HEAD_DIM], axis=0, keepdims=True)
            for h in range(GROUP)
        ]
        delta = flag - jnp.concatenate(delta, 1)
        for pair in range(GROUP // 2):
            cols = slice(pair * LANES, (pair + 1) * LANES)
            heads = slice(pair * 2 * SHORT_LEN, (pair + 1) * 2 * SHORT_LEN)
            for kind, (queries, keys) in enumerate(((tq_in, tk_in), (tv_in, tv_in))):
                part = scaled(queries[rows, cols], TEACH_SCALE)
                both = jnp.concatenate([head_mask(part, h, TEACH_HD) for h in range(2)], 0)
                scores = dot_nt(keys[rows, cols], both) + bias
                found[kind, pair] = measured(jnp.exp2(scores), flag[:, heads])
                yield
            scores = dot_nt(v, v_scaled[heads]) + bias
            found[2, pair] = measured(jnp.exp2(scores), flag[:, heads])
            yield
            dp = dot_nt(v, found["dctx_all"][heads]) + delta[:, heads]
            found[3, pair] = dp.astype(BF16)
            yield

    def measured(e, flag):
        total = jnp.sum(e, axis=0, keepdims=True)
        inverse = 1.0 / total
        width = total.shape[1]
        worst[0:1, :width] = jnp.maximum(worst[0:1, :width], jnp.maximum(total, inverse))
        return e.astype(BF16), (flag * inverse).astype(BF16)

    def short_rows(found):
        found["ds"], found["drel"] = [], []
        for pair in range(GROUP // 2):
            heads = slice(pair * 2 * SHORT_LEN, (pair + 1) * 2 * SHORT_LEN)
            teach, teach_rel, own = (found[kind, pair][0] * found[kind, pair][1] for kind in range(3))
            found["ds"].append(found["p"][:, heads] * found[3, pair] - teach)
            yield
            found["drel"].append(own - teach_rel)
            yield

    def short_products(item, found):
        rows = slice(item * SHORT_LEN, (item + 1) * SHORT_LEN)
        ds, drel = (jnp.concatenate(found[name], 1) for name in ("ds", "drel"))
        dq_buf[rows, :] = diagonal(dot_tn(k_in[rows, :], ds)).T * SCALE
        yield
        dk_buf[rows, :] = dot_nn(ds, stack(q_in[rows, :], HEAD_DIM)) * SCALE
        yield
        rel = diagonal(dot_tn(v_in[rows, :], drel)).T
        yield
        rel = rel + dot_nn(drel, found["v_all"])
        yield
        dv_buf[rows, :] = dot_nn(found["p"], found["dctx_all"]) + SCALE * rel
        yield

    def short_items():
        worst[...] = jnp.zeros_like(worst)
        items = BLOCK // SHORT_LEN
        found = [{} for _ in range(items)]
        for tick in range(items + 2):
            works = []
            if tick < items:
                works.append((short_scores(tick, found[tick]), 8))
            if 0 <= tick - 1 < items:
                works.append((short_rows(found[tick - 1]), 4))
            if 0 <= tick - 2:
                works.append((short_products(tick - 2, found[tick - 2]), 5))
            weave(works)

    def short_items_careful():
        @pl.loop(0, BLOCK // SHORT_LEN)
        def _(item):
            rows = pl.ds(pl.multiple_of(item * SHORT_LEN, SHORT_LEN), SHORT_LEN)
            length = short_len[block * (BLOCK // SHORT_LEN) + item]
            bias = short_bias(length)
            lane = lax.broadcasted_iota(jnp.int32, (1, GROUP * SHORT_LEN), 1)
            flag = (lane % SHORT_LEN < length).astype(F32)
            q, k, v = q_in[rows, :], k_in[rows, :], v_in[rows, :]
            dctx, ctx = dctx_in[rows, :], ctx_in[rows, :]
            tq, tk, tv = tq_in[rows, :], tk_in[rows, :], tv_in[rows, :]
            q_all, v_all, dctx_all = (stack(part, HEAD_DIM) for part in (q, v, dctx))
            p = ps_in[0, rows, :]

            def soft(scores, scale):
                e, total = exps(scores * scale + bias, 0, True)
                return e * (flag / total)

            def teach(keys, queries):
                parts = []
                for pair in range(GROUP // 2):
                    cols = slice(pair * LANES, (pair + 1) * LANES)
                    both = [head_mask(queries[:, cols], h, TEACH_HD) for h in range(2)]
                    parts.append(dot_nt(keys[:, cols], jnp.concatenate(both, 0)))
                return soft(jnp.concatenate(parts, 1), TEACH_SCALE)

            weighed = (dctx.astype(F32) * ctx.astype(F32)).T
            delta = [
                jnp.sum(weighed[h * HEAD_DIM : (h + 1) * HEAD_DIM], axis=0, keepdims=True)
                for h in range(GROUP)
            ]
            dp = dot_nt(v, dctx_all) + (flag - jnp.concatenate(delta, 1))
            ds = (p.astype(F32) * dp - teach(tk, tq)).astype(BF16)
            dq_buf[rows, :] = diagonal(dot_tn(k, ds)).T * SCALE
            dk_buf[rows, :] = dot_nn(ds, q_all) * SCALE
            drel = (soft(dot_nt(v, v_all), EXP_SCALE) - teach(tv, tv)).astype(BF16)
            rel = dot_nn(drel, v_all) + diagonal(dot_tn(v, drel)).T
            dv_buf[rows, :] = dot_nn(p, dctx_all) + SCALE * rel


    def long_item():
        worst[...] = jnp.zeros_like(worst)
        length = long_len[block - short_blocks]
        q, k, v = q_in[...], k_in[...], v_in[...]
        dctx, ctx = dctx_in[...], ctx_in[...]
        qt, vt, dctxt = q.T, v.T, dctx.T
        weighed = -(dctx.astype(F32) * ctx.astype(F32)).astype(BF16)
        right = jnp.concatenate([v, jnp.ones_like(v)], 1)
        v_scaled = scaled(v, EXP_SCALE)
        v_keys = biased(v, HEAD_DIM, length)
        flag = query_flag(length, BLOCK)
        flags = jnp.broadcast_to(flag, v.shape).astype(BF16)
        teach = {}

        def teach_pair(source, pair):
            if (source, pair) not in teach:
                part = (tq_in, tk_in, tv_in)[source][:, pair * LANES : (pair + 1) * LANES]
                teach[source, pair] = (
                    biased(part, TEACH_HD, length) if source else None,
                    None if source == 1 else scaled(part, TEACH_SCALE),
                )
            return teach[source, pair]

        def sides(kind, h):
            if kind == 0:
                left, keys = teach_pair(0, h // 2)[1], teach_pair(1, h // 2)[0]
                return masked_sides(left, keys, h % 2, TEACH_HD)
            if kind == 1:
                return masked_sides(v_scaled, v_keys, h, HEAD_DIM)
            if kind == 2:
                keys, left = teach_pair(2, h // 2)
                return masked_sides(left, keys, h % 2, TEACH_HD)
            lane = spare_lane(h, HEAD_DIM)
            extra = head_mask(weighed, h, HEAD_DIM) + flags * lane_row(lambda i: i == lane)
            return jnp.concatenate([head_mask(dctx, h, HEAD_DIM), extra], 1), right

        halves = [slice(i * (BLOCK // 2), (i + 1) * (BLOCK // 2)) for i in range(2)]

        def score_items(h):
            for kind in range(4):
                left, keys = sides(kind, h)
                for j, cols in enumerate(halves):
                    scores = dot_nt(left, keys[cols])
                    if kind == 3:
                        dp_buf[h % 2, :, cols] = scores.astype(BF16)
                    else:
                        e = jnp.exp2(scores)
                        exp_buf[h % 2, kind, :, cols] = e.astype(BF16)
                        part = e[:, :LANES] + e[:, LANES:]
                        if j == 0:
                            total_buf[h % 2, kind] = part
                        else:
                            total_buf[h % 2, kind] += part
                    yield

        def product_items(h):
            dims = slice(h * HEAD_DIM, (h + 1) * HEAD_DIM)
            ds, drel = ds_buf.at[h % 2], drel_buf.at[h % 2]
            for cols in halves:
                dvt_buf[dims, cols] = dot_nn(dctxt[dims, :], pl_in[h, :, cols])
                yield
                dkt_buf[dims, cols] = dot_nn(qt[dims, :], ds[:, cols]) * SCALE
                yield
                dvt_buf[dims, cols] += SCALE * dot_nn(vt[dims, :], drel[:, cols])
                yield
            for buf, grads, keys in ((dq_buf, ds, k), (dv_buf, drel, v)):
                part = dot_nn(grads[...], head_mask(keys, h, HEAD_DIM))
                if h == 0:
                    buf[...] = part
                else:
                    buf[...] += part
                yield

        def row_items(h):
            count = BLOCK // 8
            for i in range(8):
                rows = slice(i * count, (i + 1) * count)

                def soft(kind):
                    total = jnp.sum(total_buf[h % 2, kind, rows, :], axis=1, keepdims=True)
                    inverse = 1.0 / total
                    high = jnp.maximum(total, inverse)
                    worst[:, :LANES] = jnp.maximum(worst[:, :LANES], high)
                    return exp_buf[h % 2, kind, rows, :] * low_rows(flag[rows] * inverse, BLOCK)

                ds_buf[h % 2, rows, :] = pl_in[h, rows, :] * dp_buf[h % 2, rows, :] - soft(0)
                drel_buf[h % 2, rows, :] = soft(1) - soft(2)
                yield

        for h in range(-1, GROUP + 1):
            works = []
            if h + 1 < GROUP:
                works.append((score_items(h + 1), 8))
            if 0 <= h < GROUP:
                works.append((row_items(h), 8))
            if h >= 1:
                works.append((product_items(h - 1), 8))
            weave(works)
        dq_buf[...] *= SCALE
        dk_buf[...] = dkt_buf[...].astype(BF16).T.astype(F32)
        dv_buf[...] = dvt_buf[...].T + SCALE * dv_buf[...]

    def long_item_careful():
        length = long_len[block - short_blocks]
        flag = query_flag(length, BLOCK)
        bias = jnp.where(
            lax.broadcasted_iota(jnp.int32, (1, BLOCK), 1) < length, 0.0, MASKED
        )
        for buf in (dq_buf, dk_buf, dv_buf):
            buf[...] = jnp.zeros_like(buf)

        def soft(queries, keys, h, width, scale):
            scores = dot_nt(head_mask(queries, h, width), keys)
            e, total = exps(scores * scale + bias, 1, True)
            return e * (flag / total)

        @pl.loop(0, GROUP)
        def _(h):
            q, k, v, dctx = (
                head_mask(ref[...], h, HEAD_DIM) for ref in (q_in, k_in, v_in, dctx_in)
            )
            p = pl_in[h]
            delta = jnp.sum(dctx.astype(F32) * ctx_in[...].astype(F32), axis=1, keepdims=True)
            dp = dot_nt(dctx, v) + (flag - delta)
            teach = soft(tq_in[...], tk_in[...], h, TEACH_HD, TEACH_SCALE)
            ds = (p.astype(F32) * dp - teach).astype(BF16)
            own = soft(v, v, h, HEAD_DIM, EXP_SCALE)
            drel = (own - soft(tv_in[...], tv_in[...], h, TEACH_HD, TEACH_SCALE)).astype(BF16)
            dq_buf[...] += dot_nn(ds, k) * SCALE
            dk_buf[...] += dot_tn(ds, q) * SCALE
            dv_buf[...] += dot_tn(p, dctx) + SCALE * (dot_nn(drel, v) + dot_tn(drel, v))

    short = block < short_blocks
    pl.when(short)(short_items)
    pl.when(jnp.logical_not(short))(long_item)
    wild = jnp.logical_not(jnp.max(worst[...]) < LIMIT)
    pl.when(jnp.logical_and(short, wild))(short_items_careful)
    pl.when(jnp.logical_and(jnp.logical_not(short), wild))(long_item_careful)

    grads = jnp.concatenate([buf[...].astype(BF16) for buf in (dq_buf, dk_buf, dv_buf)], 1)
    grad_out[...] = grads
    acc[...] += dot_nn(side[...], grads)
    bias_acc[0:1, :] += column_sum(grads)

    @pl.when(block == blocks - 1)
    def _():
        width = side.shape[0]
        sides = [bias_acc[0:1, w * LANES : (w + 1) * LANES] for w in range(3)]
        full = [acc[:, w * LANES : (w + 1) * LANES] for w in range(3)]
        full = jnp.concatenate([*full, *sides, jnp.zeros((125, LANES), F32)], 0).astype(BF16)
        cut = full.shape[0] // 2
        is_first = core[0] == 0
        keep_out[...] = jnp.where(is_first, full[:cut], full[cut:])
        give_out[...] = jnp.where(is_first, full[cut:], full[:cut])


def attention_backward(steps, short_len, long_len, core, side, acts, p_short, p_long, carry):
    width, rows = side.shape
    blocks = rows // BLOCK
    short_blocks = short_len.shape[0] * SHORT_LEN // BLOCK
    start, stop = steps

    def place(pick):
        return lambda i: pick((start + i) // blocks, (start + i) % blocks)

    def group_spec(size):
        return pl.BlockSpec((BLOCK, size), place(lambda g, b: (b, g)))

    p_specs = [
        pl.BlockSpec(
            (1, BLOCK, BLOCK), place(lambda g, b: (g, jnp.minimum(b, short_blocks - 1), 0))
        ),
        pl.BlockSpec(
            (GROUP, BLOCK, BLOCK), place(lambda g, b: (g, jnp.maximum(b - short_blocks, 0), 0))
        ),
    ]
    cut = (3 * width + 128) // 2
    sums = jax.ShapeDtypeStruct((GROUPS * cut, LANES), BF16)
    acc = jax.ShapeDtypeStruct((width, 3 * LANES), F32)
    bias_acc = jax.ShapeDtypeStruct((8, 3 * LANES), F32)
    half_spec = pl.BlockSpec((cut, LANES), place(lambda g, b: (g, 0)))
    square = (BLOCK, LANES)
    ins = [short_len, long_len, core, side, *acts, p_short, p_long]
    carry_specs = []
    aliases = {}
    if carry is not None:
        grads, keep, give, acc_in, bias_in = carry
        aliases = {len(ins) + 2 + i: i for i in range(3)}
        ins += [acc_in, bias_in, grads, keep, give]
        carry_specs = [whole(acc.shape), whole(bias_acc.shape)]
        carry_specs += [pl.BlockSpec(memory_space=pl.ANY)] * 3
    return pl.pallas_call(
        functools.partial(backward_kernel, start, blocks, short_blocks, carry is not None),
        grid=(stop - start,),
        in_specs=[smem(), smem(), smem()]
        + [pl.BlockSpec((width, BLOCK), place(lambda g, b: (0, b)))]
        + [group_spec(LANES)] * 5
        + [group_spec(GROUP * TEACH_HD)] * 3
        + p_specs
        + carry_specs,
        out_specs=[
            pl.BlockSpec((BLOCK, 3 * LANES), place(lambda g, b: (b, g))),
            half_spec,
            half_spec,
            whole(acc.shape),
            whole(bias_acc.shape),
        ],
        out_shape=[
            jax.ShapeDtypeStruct((rows, GROUPS * 3 * LANES), BF16),
            sums,
            sums,
            acc,
            bias_acc,
        ],
        scratch_shapes=[
            pltpu.VMEM(square, F32),
            pltpu.VMEM(square, F32),
            pltpu.VMEM(square, F32),
            pltpu.VMEM((LANES, BLOCK), F32),
            pltpu.VMEM((LANES, BLOCK), F32),
            pltpu.VMEM((2, BLOCK, BLOCK), BF16),
            pltpu.VMEM((2, 3, BLOCK, BLOCK), BF16),
            pltpu.VMEM((2, 3, BLOCK, LANES), F32),
            pltpu.VMEM((2, BLOCK, BLOCK), BF16),
            pltpu.VMEM((2, BLOCK, BLOCK), BF16),
            pltpu.VMEM((BLOCK // 8, 2 * SHORT_LEN), F32),
        ],
        input_output_aliases=aliases,
        compiler_params=params(60),
        cost_estimate=pl.CostEstimate(
            flops=(stop - start) * 7_000_000_000,
            bytes_accessed=(stop - start) * 4_000_000,
            transcendentals=(stop - start) * 2_000_000,
        ),
        name=f"attention_backward_{start}",
    )(*ins)


def tokens_grad_kernel(dres, wq, wk, wv, grads, out):
    weights = jnp.concatenate(
        [w[:, g * LANES : (g + 1) * LANES] for g in range(GROUPS) for w in (wq, wk, wv)], 1
    )
    out[...] = (dres[...] + dot_nt(grads[...], weights)).astype(BF16)


def tokens_gradient(dres, wq, wk, wv, grads):
    rows, width = dres.shape
    row_spec = pl.BlockSpec((BLOCK, width), lambda i: (i, 0))
    return pl.pallas_call(
        tokens_grad_kernel,
        grid=(rows // BLOCK,),
        in_specs=[row_spec]
        + [whole(wq.shape)] * 3
        + [pl.BlockSpec((BLOCK, grads.shape[1]), lambda i: (i, 0))],
        out_specs=row_spec,
        out_shape=jax.ShapeDtypeStruct((rows, width), BF16),
        compiler_params=params(56),
        cost_estimate=pl.CostEstimate(
            flops=2_000_000_000, bytes_accessed=10_000_000, transcendentals=0
        ),
        name="tokens_gradient",
    )(dres, wq, wk, wv, grads)


def swap(value):
    return lax.ppermute(value, "tensor", [(0, 1), (1, 0)])


def spread(value):
    return lax.all_to_all(value, "dp", 0, 0, tiled=True)


def sum_chain(keep, give, count):
    (got,) = yield [(swap, give)]
    both = (keep.astype(F32) + got.astype(F32)).astype(BF16)
    rows, width = both.shape
    (got,) = yield [(spread, both.reshape(count, rows // count, width))]
    part = jnp.sum(got.astype(F32), axis=0).astype(BF16)
    (got,) = yield [(spread, jnp.broadcast_to(part[None], got.shape))]
    return got.reshape(rows, width)


def stage_sizes(count):
    sizes = []
    while count > 1:
        sizes.append(4 if count % 4 == 0 else 2)
        count //= sizes[-1]
    return sizes


def offset_send(value, offset, count):
    return lax.ppermute(value, "dp", [(i, i ^ offset) for i in range(count)])


def pair_sum_kernel(place, keep, got, *outs):
    size = len(outs)
    for j, out in enumerate(outs):
        for i in range(out.shape[0]):
            chunk = place[0] ^ (i * size + j)
            out[i] = (keep[chunk].astype(F32) + got[chunk].astype(F32)).astype(BF16)


def pair_sum(place, keep, got, size):
    count, rows, width = keep.shape
    return pl.pallas_call(
        pair_sum_kernel,
        in_specs=[smem()] + [pl.BlockSpec(memory_space=pltpu.VMEM)] * 2,
        out_shape=[jax.ShapeDtypeStruct((count // size, rows, width), BF16)] * size,
        compiler_params=params(16),
        name="pair_sum",
    )(place, keep, got)


def direct_chain(place, keep, give, count):
    rows, width = keep.shape
    near, far = stage_sizes(count)
    (got,) = yield [(swap, give)]
    shape = (count, rows // count, width)
    own, *others = pair_sum(place, keep.reshape(shape), got.reshape(shape), near)

    def sends(values, shift):
        return [
            (functools.partial(offset_send, offset=(j + 1) << shift, count=count), value)
            for j, value in enumerate(values)
        ]

    def total(first, *rest):
        return sum((item.astype(F32) for item in rest), first.astype(F32)).astype(BF16)

    shift = near.bit_length() - 1
    got = yield sends(others, 0)
    part = total(own, *got)
    got = yield sends([part[j] for j in range(1, far)], shift)
    part = total(part[0], *got)
    got = yield sends([part] * (far - 1), shift)
    part = jnp.stack([part, *got])
    got = yield sends([part] * (near - 1), 0)
    mine = [part, *got]
    other = yield [(swap, value) for value in mine]
    return mine, other


def ordered(core, mine, other):
    first = core[0] == 0
    return jnp.where(first, mine, other), jnp.where(first, other, mine)


def first_finish_kernel(core, total, other, up_out, ub_out, dn_out, wo_out, *vector_outs):
    width, half = up_out.shape
    count = half // width
    for part in range(count):
        cols = slice(part * width, (part + 1) * width)
        up_out[:, cols] = total[cols, :].astype(F32)
        dn_out[cols, :] = total[half + part * width : half + (part + 1) * width, :].astype(F32).T
    biases = total[2 * half : 2 * half + 16, :].astype(F32)
    ub_out[...] = jnp.concatenate([biases[i : i + 1] for i in range(count)], 1).reshape(half)
    halves = ordered(core, total[2 * half + 16 :, :].astype(F32), other[...].astype(F32))
    both = jnp.concatenate(halves, 0)
    wo_out[...] = both[:width]
    for i, out in enumerate(vector_outs):
        out[...] = both[width + i : width + i + 1].reshape(width)


def first_finish(core, total, other, half):
    width = total.shape[1]
    shapes = [(width, half), (half,), (half, width), (width, width)] + [(width,)] * 6
    return pl.pallas_call(
        first_finish_kernel,
        in_specs=[smem()] + [pl.BlockSpec(memory_space=pltpu.VMEM)] * 2,
        out_shape=[jax.ShapeDtypeStruct(shape, F32) for shape in shapes],
        compiler_params=params(16),
        name="first_finish",
    )(core, total, other)


def qkv_finish_body(core, total, other, outs):
    wq_out, wk_out, wv_out, bq_out, bv_out = outs
    width = wq_out.shape[0]
    low, high = ordered(core, total, other)
    cut = low.shape[0] // GROUPS
    sides = []
    for g in range(GROUPS):
        rows = slice(g * cut, (g + 1) * cut)
        full = jnp.concatenate([low[rows], high[rows]], 0)
        cols = slice(g * LANES, (g + 1) * LANES)
        for w, out in enumerate((wq_out, wk_out, wv_out)):
            out[:, cols] = full[w * width : (w + 1) * width]
        sides.append(full[3 * width : 3 * width + 8])
    sides = jnp.concatenate(sides, 1)
    bq_out[...] = sides[0:1].reshape(width)
    bv_out[...] = sides[2:3].reshape(width)


def qkv_finish_kernel(core, total, other, *outs):
    qkv_finish_body(core, total[...].astype(F32), other[...].astype(F32), outs)


def qkv_direct_kernel(near, core, place, *refs):
    parts, outs, bufs = refs[: 2 * near], refs[2 * near : -2], refs[-2:]
    for buf, side in zip(bufs, (parts[:near], parts[near:])):
        for j, part in enumerate(side):
            for i in range(part.shape[0]):
                buf[place[0] ^ (i * near + j)] = part[i].astype(F32)
    rows = bufs[0].shape[0] * bufs[0].shape[1]
    total, other = (buf[...].reshape(rows, buf.shape[2]) for buf in bufs)
    qkv_finish_body(core, total, other, outs)


def qkv_shapes(width):
    return [jax.ShapeDtypeStruct(shape, F32) for shape in [(width, width)] * 3 + [(width,)] * 2]


def qkv_finish(core, total, other, width):
    return pl.pallas_call(
        qkv_finish_kernel,
        in_specs=[smem()] + [pl.BlockSpec(memory_space=pltpu.VMEM)] * 2,
        out_shape=qkv_shapes(width),
        compiler_params=params(16),
        name="qkv_finish",
    )(core, total, other)


def qkv_direct_finish(core, place, mine, other, width):
    near = len(mine)
    far, rows, lanes = mine[0].shape
    return pl.pallas_call(
        functools.partial(qkv_direct_kernel, near),
        in_specs=[smem()] * 2 + [pl.BlockSpec(memory_space=pltpu.VMEM)] * (2 * near),
        out_shape=qkv_shapes(width),
        scratch_shapes=[pltpu.VMEM((far * near, rows, lanes), F32)] * 2,
        compiler_params=params(16),
        name="qkv_direct_finish",
    )(core, place, *mine, *other)


class Flights:
    def __init__(self):
        self.asked = {}
        self.flying = {}
        self.done = {}

    def advance(self, name, generator, got=None):
        try:
            wants = next(generator) if got is None else generator.send(got)
            self.asked[name] = (generator, wants)
        except StopIteration as end:
            self.done[name] = end.value

    def step(self, token, work=None, stay=()):
        asked, self.asked = self.asked, {}
        sends = [value for _, wants in asked.values() for _, value in wants]
        token, *sends = lax.optimization_barrier((token, *sends))
        sent = iter(sends)
        for name, (generator, wants) in asked.items():
            self.flying[name] = generator, [move(next(sent)) for move, _ in wants]
        result = None
        if work is not None:
            result, token = work(token)
        for name in [name for name in self.flying if name not in stay]:
            generator, got = self.flying.pop(name)
            if work is not None:
                token, *got = lax.optimization_barrier((token, *got))
            self.advance(name, generator, got)
        return result, token


def per_device(
    dp_count,
    tokens,
    query_weight,
    query_bias,
    key_weight,
    value_weight,
    value_bias,
    proj_weight,
    proj_bias,
    first_gain,
    first_shift,
    up_weight,
    up_bias,
    down_weight,
    down_bias,
    second_gain,
    second_shift,
    teach_query,
    teach_key,
    teach_value,
    short_lengths,
    long_lengths,
    cotangent,
):
    width = tokens.shape[1]
    half = up_weight.shape[1]

    up_other, down_other, ub_other = (swap(value) for value in (up_weight, down_weight, up_bias))
    core = lax.axis_index("tensor").astype(jnp.int32).reshape(1)
    q, k, v, ctx, p_short, p_long, side = attention_forward(
        tokens,
        query_weight,
        key_weight,
        value_weight,
        query_bias,
        value_bias,
        short_lengths,
        long_lengths,
    )
    block_out, dres, dctx, keep, give = middle(
        core,
        tokens,
        ctx,
        cotangent,
        proj_weight,
        (up_weight, up_other),
        (down_weight, down_other),
        (up_bias, ub_other),
        (proj_bias, first_gain, first_shift, down_bias, second_gain, second_shift),
    )
    flights = Flights()
    flights.advance("first", sum_chain(keep, give, dp_count))
    flights.step(short_lengths)
    acts = (q, k, v, ctx, dctx, teach_query, teach_key, teach_value)
    steps = GROUPS * (tokens.shape[0] // BLOCK)
    token = short_lengths
    carry = None
    cut = steps * SPLIT // 12
    for piece in ((0, cut), (cut, steps)):

        def work(lens):
            out = attention_backward(
                piece, lens, long_lengths, core, side, acts, p_short, p_long, carry
            )
            return out[:1] + out[2:], out[1]

        stay = ("first",) if piece[1] == steps else ()
        (grads, give, *sums), keep = flights.step(token, work, stay)
        token, keep = lax.optimization_barrier((short_lengths, keep))
        carry = [grads, keep, give, *sums]

    def input_work(grads):
        return None, tokens_gradient(dres, query_weight, key_weight, value_weight, grads)

    def first_work(total):
        out = first_finish(core, total, other, half)
        return out[1:], out[0]

    direct = keep.shape[0] // dp_count % 8 == 0 and len(stage_sizes(dp_count)) == 2
    if direct:
        place = lax.axis_index("dp").astype(jnp.int32).reshape(1)
        flights.advance("qkv", direct_chain(place, keep, give, dp_count))
    else:
        flights.advance("qkv", sum_chain(keep, give, dp_count))
    flights.step(short_lengths, None, ("first",))
    _, tokens_grad = flights.step(grads, input_work)
    total = flights.done["first"]
    other = swap(total[2 * half + 16 :])
    if direct:
        flights.step(short_lengths)
        flights.step(short_lengths)
    first, up_grad = flights.step(total, first_work)
    if direct:
        flights.step(short_lengths)
        qkv = qkv_direct_finish(core, place, *flights.done["qkv"], width)
    else:
        total = flights.done["qkv"]
        qkv = qkv_finish(core, total, swap(total), width)
    up_bias_grad, down_grad, proj_grad, *vectors = first
    return (
        block_out,
        tokens_grad,
        qkv[0],
        qkv[3],
        qkv[1],
        qkv[2],
        qkv[4],
        proj_grad,
        vectors[0],
        vectors[1],
        vectors[2],
        up_grad,
        up_bias_grad,
        down_grad,
        vectors[3],
        vectors[4],
        vectors[5],
    )


def solution(mesh):
    in_specs = (
        P(("dp", "tensor"), None),
        P(),
        P(),
        P(),
        P(),
        P(),
        P(),
        P(),
        P(),
        P(),
        P(None, "tensor"),
        P("tensor"),
        P("tensor", None),
        P(),
        P(),
        P(),
        P(("dp", "tensor"), None),
        P(("dp", "tensor"), None),
        P(("dp", "tensor"), None),
        P(("dp", "tensor")),
        P(("dp", "tensor")),
        P(("dp", "tensor"), None),
    )
    out_specs = (
        P(("dp", "tensor"), None),
        P(("dp", "tensor"), None),
        P(),
        P(),
        P(),
        P(),
        P(),
        P(),
        P(),
        P(),
        P(),
        P(None, "tensor"),
        P("tensor"),
        P("tensor", None),
        P(),
        P(),
        P(),
    )
    return jax.shard_map(
        functools.partial(per_device, mesh.shape["dp"]),
        mesh=mesh,
        in_specs=in_specs,
        out_specs=out_specs,
        check_vma=False,
    )
```

```python
import functools

import jax
import jax.numpy as jnp
from jax import lax
from jax.experimental import pallas as pl
from jax.experimental.pallas import tpu as pltpu
from jax.sharding import PartitionSpec as P

HEADS = 12
HEAD_DIM = 32
TEACH_HD = 64
SHORT_LEN = 128
GROUP = 4
LANES = GROUP * HEAD_DIM
GROUPS = HEADS // GROUP
BLOCK = 512
MID_BLOCK = 1024
MID_PARTS = 2
PAD_ROWS = 96
SPLIT = 8

MASKED = -1e30
LIMIT = 2.0**64
EPSILON = 1e-06
LOG2E = 1.4426950408889634
SCALE = HEAD_DIM**-0.5
EXP_SCALE = LOG2E * SCALE
TEACH_SCALE = LOG2E * TEACH_HD**-0.5
MIB = 2**20

F32 = jnp.float32
BF16 = jnp.bfloat16


def dot_nn(left, right):
    return lax.dot_general(left, right, (((1,), (0,)), ((), ())), preferred_element_type=F32)


def dot_nt(left, right):
    return lax.dot_general(left, right, (((1,), (1,)), ((), ())), preferred_element_type=F32)


def dot_tn(left, right):
    return lax.dot_general(left, right, (((0,), (0,)), ((), ())), preferred_element_type=F32)


def dot_tt(left, right):
    return lax.dot_general(left, right, (((0,), (1,)), ((), ())), preferred_element_type=F32)


def lane_row(condition, width=LANES):
    lane = lax.broadcasted_iota(jnp.int32, (1, width), 1)
    return condition(lane).astype(F32).astype(BF16)


def head_mask(block, head, width):
    return block * lane_row(lambda lane: lane // width == head, block.shape[1])


def scaled(block, factor):
    return (block.astype(F32) * factor).astype(BF16)


def spare_lane(head, width):
    return LANES - width if head * width < LANES // 2 else 0


def with_bias(keys, lane, length):
    row = lax.broadcasted_iota(jnp.int32, keys.shape, 0)
    column = lax.broadcasted_iota(jnp.int32, keys.shape, 1)
    bias = jnp.where(row < length, 0.0, MASKED).astype(BF16)
    return jnp.where(column == lane, bias, keys)


def masked_sides(queries, keys, head, width):
    lane = spare_lane(head, width)
    one = lane_row(lambda index: index == lane)
    return head_mask(queries, head, width) + one, keys[lane]


def biased(keys, width, length):
    return {lane: with_bias(keys, lane, length) for lane in (LANES - width, 0)}


def query_flag(length, size):
    return (lax.broadcasted_iota(jnp.int32, (size, 1), 0) < length).astype(F32)


def weave(works):
    ticks = max(count for _, count in works)
    for tick in range(ticks):
        for work, count in works:
            if (tick + 1) * count // ticks > tick * count // ticks:
                next(work)
    for work, _ in works:
        for _ in work:
            pass


def exps(scores, axis, careful):
    if careful:
        scores = scores - jnp.max(scores, axis=axis, keepdims=True)
    heights = jnp.exp2(scores)
    return heights, jnp.sum(heights, axis=axis, keepdims=True)


def low_rows(column, size):
    block = jnp.broadcast_to(column, (column.shape[0], LANES)).astype(BF16)
    return jnp.concatenate([block] * (size // LANES), 1)


def short_bias(length):
    shape = (SHORT_LEN, GROUP * SHORT_LEN)
    return jnp.where(lax.broadcasted_iota(jnp.int32, shape, 0) < length, 0.0, MASKED)


def stack(block, width):
    return jnp.concatenate([head_mask(block, h, width) for h in range(GROUP)], 0)


def diagonal(block):
    return jnp.concatenate(
        [
            block[h * HEAD_DIM : (h + 1) * HEAD_DIM, h * SHORT_LEN : (h + 1) * SHORT_LEN]
            for h in range(GROUP)
        ],
        0,
    )


def params(mebibytes):
    return pltpu.CompilerParams(vmem_limit_bytes=mebibytes * MIB)


def whole(shape):
    return pl.BlockSpec(shape, lambda i: (0,) * len(shape))


def smem():
    return pl.BlockSpec(memory_space=pltpu.SMEM)


def forward_kernel(
    short_blocks,
    short_len,
    long_len,
    tokens,
    wq,
    wk,
    wv,
    bq,
    bv,
    q_out,
    k_out,
    v_out,
    ctx_out,
    ps_out,
    pl_out,
    side_out,
    worst,
    p_buf,
    p_sems,
):
    step = pl.program_id(0)
    x = tokens[...]
    side_out[...] = x.T
    q_out[...] = (dot_nn(x, wq[...]) + row_of(bq)).astype(BF16)
    k_out[...] = dot_nn(x, wk[...]).astype(BF16)
    v_out[...] = (dot_nn(x, wv[...]) + row_of(bv)).astype(BF16)

    def note(total, inverse):
        high = jnp.maximum(total, inverse)
        rows = high.shape[0]
        for i in range(max(high.shape[1] // LANES, 1)):
            part = high[:, i * LANES : (i + 1) * LANES]
            worst[:rows, :] = jnp.maximum(worst[:rows, :], part)


    def short_scores(item, g, found):
        rows = slice(item * SHORT_LEN, (item + 1) * SHORT_LEN)
        cols = slice(g * LANES, (g + 1) * LANES)
        bias = short_bias(short_len[step * (BLOCK // SHORT_LEN) + item])[:, : 2 * SHORT_LEN]
        queries = stack(scaled(q_out[rows, cols], EXP_SCALE), HEAD_DIM)
        for pair in range(GROUP // 2):
            heads = slice(pair * 2 * SHORT_LEN, (pair + 1) * 2 * SHORT_LEN)
            e, total = exps(dot_nt(k_out[rows, cols], queries[heads]) + bias, 0, False)
            found[pair] = e.astype(BF16), total
            yield

    def short_rows(item, g, found):
        rows = slice(item * SHORT_LEN, (item + 1) * SHORT_LEN)
        for pair in range(GROUP // 2):
            heads = slice(pair * 2 * SHORT_LEN, (pair + 1) * 2 * SHORT_LEN)
            e, total = found[pair]
            inverse = 1.0 / total
            note(total, inverse)
            found[pair] = e * inverse.astype(BF16)
            ps_out[g, rows, heads] = found[pair]
            yield

    def short_products(item, g, found):
        rows = slice(item * SHORT_LEN, (item + 1) * SHORT_LEN)
        cols = slice(g * LANES, (g + 1) * LANES)
        probs = jnp.concatenate([found[pair] for pair in range(GROUP // 2)], 1)
        ctx_out[rows, cols] = diagonal(dot_tn(v_out[rows, cols], probs)).T.astype(BF16)
        yield

    def short_items():
        units = [(item, g, {}) for item in range(BLOCK // SHORT_LEN) for g in range(GROUPS)]
        for tick in range(len(units) + 2):
            works = []
            if tick < len(units):
                works.append((short_scores(*units[tick]), 2))
            if 0 <= tick - 1 < len(units):
                works.append((short_rows(*units[tick - 1]), 2))
            if 0 <= tick - 2:
                works.append((short_products(*units[tick - 2]), 1))
            weave(works)


    def p_copy(g):
        index = step - short_blocks
        slot = lax.rem(index * GROUPS + g, 2)
        heads = pl.ds(g * GROUP, GROUP)
        rows = pl.ds(index * BLOCK, BLOCK)
        return pltpu.make_async_copy(
            p_buf.at[slot], pl_out.at[heads, rows, :], p_sems.at[slot]
        )

    def p_slot(g):
        return p_buf.at[lax.rem((step - short_blocks) * GROUPS + g, 2)]

    def long_item():
        length = long_len[step - short_blocks]
        halves = [slice(i * (BLOCK // 2), (i + 1) * (BLOCK // 2)) for i in range(2)]

        @pl.loop(0, GROUPS)
        def _(g):
            p_now = p_slot(g)

            @pl.when((step - short_blocks) * GROUPS + g >= 2)
            def _():
                p_copy(g).wait()

            cols = pl.ds(pl.multiple_of(g * LANES, LANES), LANES)
            queries = scaled(q_out[:, cols], EXP_SCALE)
            keys = biased(k_out[:, cols], HEAD_DIM, length)
            values = v_out[:, cols]
            sums = []

            def scores(h, found):
                left, right = masked_sides(queries, keys, h, HEAD_DIM)
                for half in halves:
                    e = jnp.exp2(dot_nt(left, right[half]))
                    part = e[:, :LANES] + e[:, LANES:]
                    found["sum"] = found["sum"] + part if "sum" in found else part
                    found[half.start] = e.astype(BF16)
                    yield

            def normalise(h, found):
                count = BLOCK // 4
                for i in range(4):
                    rows = slice(i * count, (i + 1) * count)
                    total = jnp.sum(found["sum"][rows], axis=1, keepdims=True)
                    inverse = 1.0 / total
                    note(total, inverse)
                    e = jnp.concatenate([found[half.start][rows] for half in halves], 1)
                    p_now[h, rows, :] = e * low_rows(inverse, BLOCK)
                    yield

            def products(h):
                part = dot_nn(p_now[h], head_mask(values, h, HEAD_DIM))
                sums.append(part)
                yield

            found = [{} for _ in range(GROUP)]
            for tick in range(GROUP + 2):
                works = []
                if tick < GROUP:
                    works.append((scores(tick, found[tick]), 2))
                if 0 <= tick - 1 < GROUP:
                    works.append((normalise(tick - 1, found[tick - 1]), 4))
                if 0 <= tick - 2:
                    works.append((products(tick - 2), 1))
                weave(works)
            ctx_out[:, cols] = functools.reduce(jnp.add, sums).astype(BF16)
            p_copy(g).start()


    def short_items_careful():
        items = BLOCK // SHORT_LEN

        @pl.loop(0, items)
        def _(item):
            rows = pl.ds(pl.multiple_of(item * SHORT_LEN, SHORT_LEN), SHORT_LEN)
            bias = short_bias(short_len[step * items + item])
            for g in range(GROUPS):
                cols = slice(g * LANES, (g + 1) * LANES)
                q, k, v = q_out[rows, cols], k_out[rows, cols], v_out[rows, cols]
                e, total = exps(dot_nt(k, stack(q, HEAD_DIM)) * EXP_SCALE + bias, 0, True)
                probs = (e * (1.0 / total)).astype(BF16)
                ps_out[g, rows, :] = probs
                ctx_out[rows, cols] = diagonal(dot_tn(v, probs)).T.astype(BF16)

    def long_item_careful():
        length = long_len[step - short_blocks]
        bias = jnp.where(lax.broadcasted_iota(jnp.int32, (1, BLOCK), 1) < length, 0.0, MASKED)
        p_copy(1).wait()
        p_copy(2).wait()

        @pl.loop(0, GROUPS)
        def _(g):
            p_now = p_slot(g)
            cols = pl.ds(pl.multiple_of(g * LANES, LANES), LANES)
            q, k, v = q_out[:, cols], k_out[:, cols], v_out[:, cols]
            ctx = jnp.zeros((BLOCK, LANES), F32)
            for h in range(GROUP):
                scores = dot_nt(head_mask(q, h, HEAD_DIM), k) * EXP_SCALE + bias
                e, total = exps(scores, 1, True)
                probs = (e * (1.0 / total)).astype(BF16)
                p_now[h] = probs
                ctx = ctx + dot_nn(probs, head_mask(v, h, HEAD_DIM))
            ctx_out[:, cols] = ctx.astype(BF16)
            p_copy(g).start()

            @pl.when(g == 0)
            def _():
                p_copy(g).wait()

    short = step < short_blocks
    long = jnp.logical_not(short)
    worst[...] = jnp.zeros_like(worst)
    pl.when(short)(short_items)
    pl.when(long)(long_item)
    wild = jnp.logical_not(jnp.max(worst[...]) < LIMIT)
    pl.when(jnp.logical_and(short, wild))(short_items_careful)
    pl.when(jnp.logical_and(long, wild))(long_item_careful)

    @pl.when(step == pl.num_programs(0) - 1)
    def _():
        p_copy(1).wait()
        p_copy(2).wait()


def attention_forward(tokens, wq, wk, wv, bq, bv, short_len, long_len):
    rows, width = tokens.shape
    blocks = rows // BLOCK
    short_blocks = short_len.shape[0] * SHORT_LEN // BLOCK
    long_blocks = blocks - short_blocks
    row_spec = pl.BlockSpec((BLOCK, width), lambda i: (i, 0))
    act = jax.ShapeDtypeStruct((rows, width), BF16)
    return pl.pallas_call(
        functools.partial(forward_kernel, short_blocks),
        grid=(blocks,),
        in_specs=[smem(), smem(), row_spec]
        + [whole(a.shape) for a in (wq, wk, wv, bq, bv)],
        out_specs=[
            row_spec,
            row_spec,
            row_spec,
            row_spec,
            pl.BlockSpec((GROUPS, BLOCK, BLOCK), lambda i: (0, jnp.minimum(i, short_blocks - 1), 0)),
            pl.BlockSpec(memory_space=pl.ANY),
            pl.BlockSpec((width, BLOCK), lambda i: (0, i)),
        ],
        out_shape=[
            act,
            act,
            act,
            act,
            jax.ShapeDtypeStruct((GROUPS, short_blocks * BLOCK, BLOCK), BF16),
            jax.ShapeDtypeStruct((HEADS, long_blocks * BLOCK, BLOCK), BF16),
            jax.ShapeDtypeStruct((width, rows), BF16),
        ],
        scratch_shapes=[
            pltpu.VMEM((BLOCK // 4, LANES), F32),
            pltpu.VMEM((2, GROUP, BLOCK, BLOCK), BF16),
            pltpu.SemaphoreType.DMA((2,)),
        ],
        compiler_params=params(56),
        cost_estimate=pl.CostEstimate(
            flops=12_000_000_000, bytes_accessed=24_000_000, transcendentals=8_000_000
        ),
        name="attention_forward",
    )(short_len, long_len, tokens, wq, wk, wv, bq, bv)


def norm_parts(resid):
    centred = resid - jnp.mean(resid, axis=-1, keepdims=True)
    spread = jnp.mean(centred * centred, axis=-1, keepdims=True)
    root = lax.rsqrt(spread + EPSILON)
    return centred * root, root


def norm_back(grad, y, root):
    return root * (
        grad
        - jnp.mean(grad, axis=-1, keepdims=True)
        - y * jnp.mean(grad * y, axis=-1, keepdims=True)
    )


def row_of(vector):
    return vector[...].astype(F32).reshape(1, vector.shape[0])


def column_sum(block):
    return jnp.sum(block.astype(F32), axis=0, keepdims=True)


def middle_kernel(
    core,
    tokens,
    ctx,
    cot,
    wo,
    up0,
    up1,
    dn0,
    dn1,
    ub0,
    ub1,
    bo_in,
    gain1_in,
    shift1_in,
    db_in,
    gain2_in,
    shift2_in,
    block_out,
    dres_out,
    dctx_out,
    keep_out,
    give_out,
    acc_up,
    acc_dn,
    acc_wo,
    acc_ub,
    acc_vec,
    slope,
    active,
    dpre,
    low_rows_buf,
    dbranch,
    dattn,
):
    step = pl.program_id(0)
    half = up0.shape[1]
    width = up0.shape[0]

    @pl.when(step == 0)
    def _():
        for ref in (acc_up, acc_dn, acc_wo, acc_ub, acc_vec):
            ref[...] = jnp.zeros_like(ref)

    bo, gain1, shift1, db, gain2, shift2 = (
        row_of(ref) for ref in (bo_in, gain1_in, shift1_in, db_in, gain2_in, shift2_in)
    )
    def gelu(j, pre, rows):
        pre = pre + row_of((ub0, ub1)[j])
        phi = 0.5 + 0.5 * lax.erf(pre * (0.5**0.5))
        slope[j, rows, :] = phi + pre * (jnp.exp2(pre * pre * (-0.5 * LOG2E)) * 0.3989422804014327)
        active[j, rows, :] = (pre * phi).astype(BF16)

    def back_gelu(j, dactive, rows):
        grad = (dactive * slope[j, rows, :]).astype(BF16)
        dpre[j, rows, :] = grad
        acc_ub[j : j + 1, :] += column_sum(grad)
        return grad

    def row_work(rows):
        resid = tokens[rows, :].astype(F32) + dot_nn(ctx[rows, :], wo[...]) + bo
        yield
        y1, root1 = norm_parts(resid)
        normed = y1 * gain1 + shift1
        normed_low = normed.astype(BF16)
        low_rows_buf[rows, :] = normed_low
        mid = normed + db
        yield
        pre0 = dot_nn(normed_low, up0[...])
        yield
        pre1 = dot_nn(normed_low, up1[...])
        gelu(0, pre0, rows)
        yield
        mid = mid + dot_nn(active[0, rows, :], dn0[...])
        gelu(1, pre1, rows)
        yield
        mid = mid + dot_nn(active[1, rows, :], dn1[...])
        yield
        y2, root2 = norm_parts(mid)
        block_out[rows, :] = (y2 * gain2 + shift2).astype(BF16)
        cotangent = cot[rows, :].astype(F32)
        dmid = norm_back(cotangent * gain2, y2, root2)
        dbranch_low = dmid.astype(BF16)
        dbranch[rows, :] = dbranch_low
        acc_vec[3:4, :] += column_sum(dbranch_low)
        acc_vec[4:5, :] += column_sum(cotangent * y2)
        acc_vec[5:6, :] += column_sum(cotangent)
        yield
        dactive0 = dot_nt(dbranch_low, dn0[...])
        yield
        dactive1 = dot_nt(dbranch_low, dn1[...])
        dpre0 = back_gelu(0, dactive0, rows)
        yield
        dnormed = dmid + dot_nt(dpre0, up0[...])
        dpre1 = back_gelu(1, dactive1, rows)
        yield
        dnormed = dnormed + dot_nt(dpre1, up1[...])
        yield
        acc_vec[1:2, :] += column_sum(dnormed * y1)
        acc_vec[2:3, :] += column_sum(dnormed)
        dres = norm_back(dnormed * gain1, y1, root1)
        dres_out[rows, :] = dres
        dattn_low = dres.astype(BF16)
        dattn[rows, :] = dattn_low
        acc_vec[0:1, :] += column_sum(dattn_low)
        yield
        dctx_out[rows, :] = dot_nt(dattn_low, wo[...]).astype(BF16)
        yield

    def weight_work():
        for j in range(2):
            acc_dn[j] += dot_tn(dbranch[...], active[j])
            yield
        for j in range(2):
            acc_up[j] += dot_tn(low_rows_buf[...], dpre[j])
            yield
        acc_wo[...] += dot_tn(ctx[...], dattn[...])
        yield

    stages = 13
    parts = MID_PARTS
    size = MID_BLOCK // parts
    works = [row_work(slice(i * size, (i + 1) * size)) for i in range(parts)]
    weights_now = weight_work()
    for tick in range(stages + parts - 1):
        for i, work in enumerate(works):
            if 0 <= tick - i < stages:
                next(work)
        if tick >= stages - 2:
            next(weights_now)
    for _ in weights_now:
        pass

    @pl.when(step == pl.num_programs(0) - 1)
    def _():
        for j, out in enumerate((keep_out, give_out)):
            for part in range(half // width):
                cols = slice(part * width, (part + 1) * width)
                out[cols, :] = acc_up[j, :, cols].astype(BF16)
                out[half + part * width : half + (part + 1) * width, :] = acc_dn[j, :, cols].astype(
                    BF16
                )
            pads = [
                acc_ub[j : j + 1, part * width : (part + 1) * width]
                for part in range(half // width)
            ]
            pads.append(jnp.zeros((16 - len(pads), width), F32))
            out[2 * half : 2 * half + 16, :] = jnp.concatenate(pads, 0).astype(BF16)
        cut = (width + PAD_ROWS) // 2
        low = acc_wo[:cut, :].astype(BF16)
        pads = jnp.zeros((PAD_ROWS - 8, width), F32)
        high = jnp.concatenate([acc_wo[cut:, :], acc_vec[...], pads], 0).astype(BF16)
        first = core[0] == 0
        keep_out[2 * half + 16 :, :] = jnp.where(first, low, high)
        give_out[2 * half + 16 :, :] = jnp.where(first, high, low)


def middle(core, tokens, ctx, cot, wo, ups, dns, ubs, vectors):
    rows, width = tokens.shape
    half = ups[0].shape[1]
    row_spec = pl.BlockSpec((MID_BLOCK, width), lambda i: (i, 0))
    weights = (wo, *ups, *dns, *ubs, *vectors)
    act = jax.ShapeDtypeStruct((rows, width), BF16)
    sums = jax.ShapeDtypeStruct((2 * half + 16 + (width + PAD_ROWS) // 2, width), BF16)
    return pl.pallas_call(
        middle_kernel,
        grid=(rows // MID_BLOCK,),
        in_specs=[smem()] + [row_spec] * 3 + [whole(w.shape) for w in weights],
        out_specs=[row_spec] * 3 + [whole(sums.shape), whole(sums.shape)],
        out_shape=[act, jax.ShapeDtypeStruct((rows, width), F32), act, sums, sums],
        scratch_shapes=[
            pltpu.VMEM((2, width, half), F32),
            pltpu.VMEM((2, width, half), F32),
            pltpu.VMEM((width, width), F32),
            pltpu.VMEM((8, half), F32),
            pltpu.VMEM((8, width), F32),
            pltpu.VMEM((2, MID_BLOCK, half), F32),
            pltpu.VMEM((2, MID_BLOCK, half), BF16),
            pltpu.VMEM((2, MID_BLOCK, half), BF16),
            pltpu.VMEM((MID_BLOCK, width), BF16),
            pltpu.VMEM((MID_BLOCK, width), BF16),
            pltpu.VMEM((MID_BLOCK, width), BF16),
        ],
        compiler_params=params(44),
        cost_estimate=pl.CostEstimate(
            flops=34_000_000_000, bytes_accessed=20_000_000, transcendentals=6_000_000
        ),
        name="middle",
    )(core, tokens, ctx, cot, *weights)


def backward_kernel(
    first,
    blocks,
    short_blocks,
    extended,
    carried,
    short_len,
    long_len,
    core,
    side,
    q_in,
    k_in,
    v_in,
    ctx_in,
    dctx_in,
    tq_in,
    tk_in,
    tv_in,
    ps_in,
    pl_in,
    *refs,
):
    if carried:
        acc_in, bias_in, *refs = refs
    if extended:
        refs = refs[3:]
    (
        grad_out,
        keep_out,
        give_out,
        acc,
        bias_acc,
        dq_buf,
        dk_buf,
        dv_buf,
        dkt_buf,
        dvt_buf,
        ds_buf,
        worst,
    ) = refs
    block = lax.rem(first + pl.program_id(0), blocks)

    if carried:

        @pl.when(pl.program_id(0) == 0)
        def _():
            acc[...] = acc_in[...]
            bias_acc[...] = bias_in[...]

    @pl.when(block == 0)
    def _():
        acc[...] = jnp.zeros_like(acc)
        bias_acc[...] = jnp.zeros_like(bias_acc)


    def short_scores(item, found):
        rows = slice(item * SHORT_LEN, (item + 1) * SHORT_LEN)
        length = short_len[block * (BLOCK // SHORT_LEN) + item]
        bias = short_bias(length)[:, : 2 * SHORT_LEN]
        lane = lax.broadcasted_iota(jnp.int32, (1, GROUP * SHORT_LEN), 1)
        flag = (lane % SHORT_LEN < length).astype(F32)
        v, dctx = v_in[rows, :], dctx_in[rows, :]
        found["v_all"], found["dctx_all"] = stack(v, HEAD_DIM), stack(dctx, HEAD_DIM)
        found["p"] = ps_in[0, rows, :]
        v_scaled = stack(scaled(v, EXP_SCALE), HEAD_DIM)
        weighed = (dctx.astype(F32) * ctx_in[rows, :].astype(F32)).T
        delta = [
            jnp.sum(weighed[h * HEAD_DIM : (h + 1) * HEAD_DIM], axis=0, keepdims=True)
            for h in range(GROUP)
        ]
        delta = flag - jnp.concatenate(delta, 1)
        for pair in range(GROUP // 2):
            cols = slice(pair * LANES, (pair + 1) * LANES)
            heads = slice(pair * 2 * SHORT_LEN, (pair + 1) * 2 * SHORT_LEN)
            for kind, (queries, keys) in enumerate(((tq_in, tk_in), (tv_in, tv_in))):
                part = scaled(queries[rows, cols], TEACH_SCALE)
                both = jnp.concatenate([head_mask(part, h, TEACH_HD) for h in range(2)], 0)
                scores = dot_nt(keys[rows, cols], both) + bias
                found[kind, pair] = measured(jnp.exp2(scores), flag[:, heads])
                yield
            scores = dot_nt(v, v_scaled[heads]) + bias
            found[2, pair] = measured(jnp.exp2(scores), flag[:, heads])
            yield
            dp = dot_nt(v, found["dctx_all"][heads]) + delta[:, heads]
            found[3, pair] = dp.astype(BF16)
            yield

    def measured(e, flag):
        total = jnp.sum(e, axis=0, keepdims=True)
        inverse = 1.0 / total
        width = total.shape[1]
        worst[0:1, :width] = jnp.maximum(worst[0:1, :width], jnp.maximum(total, inverse))
        return e.astype(BF16), (flag * inverse).astype(BF16)

    def short_rows(found):
        found["ds"], found["drel"] = [], []
        for pair in range(GROUP // 2):
            heads = slice(pair * 2 * SHORT_LEN, (pair + 1) * 2 * SHORT_LEN)
            teach, teach_rel, own = (found[kind, pair][0] * found[kind, pair][1] for kind in range(3))
            found["ds"].append(found["p"][:, heads] * found[3, pair] - teach)
            yield
            found["drel"].append(own - teach_rel)
            yield

    def short_products(item, found):
        rows = slice(item * SHORT_LEN, (item + 1) * SHORT_LEN)
        ds, drel = (jnp.concatenate(found[name], 1) for name in ("ds", "drel"))
        dq_buf[rows, :] = diagonal(dot_tn(k_in[rows, :], ds)).T * SCALE
        yield
        dk_buf[rows, :] = dot_nn(ds, stack(q_in[rows, :], HEAD_DIM)) * SCALE
        yield
        rel = diagonal(dot_tn(v_in[rows, :], drel)).T
        yield
        rel = rel + dot_nn(drel, found["v_all"])
        yield
        dv_buf[rows, :] = dot_nn(found["p"], found["dctx_all"]) + SCALE * rel
        yield

    def short_items():
        worst[...] = jnp.zeros_like(worst)
        items = BLOCK // SHORT_LEN
        found = [{} for _ in range(items)]
        for tick in range(items + 2):
            works = []
            if tick < items:
                works.append((short_scores(tick, found[tick]), 8))
            if 0 <= tick - 1 < items:
                works.append((short_rows(found[tick - 1]), 4))
            if 0 <= tick - 2:
                works.append((short_products(tick - 2, found[tick - 2]), 5))
            weave(works)

    def short_items_careful():
        @pl.loop(0, BLOCK // SHORT_LEN)
        def _(item):
            rows = pl.ds(pl.multiple_of(item * SHORT_LEN, SHORT_LEN), SHORT_LEN)
            length = short_len[block * (BLOCK // SHORT_LEN) + item]
            bias = short_bias(length)
            lane = lax.broadcasted_iota(jnp.int32, (1, GROUP * SHORT_LEN), 1)
            flag = (lane % SHORT_LEN < length).astype(F32)
            q, k, v = q_in[rows, :], k_in[rows, :], v_in[rows, :]
            dctx, ctx = dctx_in[rows, :], ctx_in[rows, :]
            tq, tk, tv = tq_in[rows, :], tk_in[rows, :], tv_in[rows, :]
            q_all, v_all, dctx_all = (stack(part, HEAD_DIM) for part in (q, v, dctx))
            p = ps_in[0, rows, :]

            def soft(scores, scale):
                e, total = exps(scores * scale + bias, 0, True)
                return e * (flag / total)

            def teach(keys, queries):
                parts = []
                for pair in range(GROUP // 2):
                    cols = slice(pair * LANES, (pair + 1) * LANES)
                    both = [head_mask(queries[:, cols], h, TEACH_HD) for h in range(2)]
                    parts.append(dot_nt(keys[:, cols], jnp.concatenate(both, 0)))
                return soft(jnp.concatenate(parts, 1), TEACH_SCALE)

            weighed = (dctx.astype(F32) * ctx.astype(F32)).T
            delta = [
                jnp.sum(weighed[h * HEAD_DIM : (h + 1) * HEAD_DIM], axis=0, keepdims=True)
                for h in range(GROUP)
            ]
            dp = dot_nt(v, dctx_all) + (flag - jnp.concatenate(delta, 1))
            ds = (p.astype(F32) * dp - teach(tk, tq)).astype(BF16)
            dq_buf[rows, :] = diagonal(dot_tn(k, ds)).T * SCALE
            dk_buf[rows, :] = dot_nn(ds, q_all) * SCALE
            drel = (soft(dot_nt(v, v_all), EXP_SCALE) - teach(tv, tv)).astype(BF16)
            rel = dot_nn(drel, v_all) + diagonal(dot_tn(v, drel)).T
            dv_buf[rows, :] = dot_nn(p, dctx_all) + SCALE * rel


    def long_item():
        worst[...] = jnp.zeros_like(worst)
        length = long_len[block - short_blocks]
        q, k, v = q_in[...], k_in[...], v_in[...]
        dctx, ctx = dctx_in[...], ctx_in[...]
        qt, vt, dctxt = q.T, v.T, dctx.T
        weighed = -(dctx.astype(F32) * ctx.astype(F32)).astype(BF16)
        right = jnp.concatenate([v, jnp.ones_like(v)], 1)
        flag = query_flag(length, BLOCK)
        flags = jnp.broadcast_to(flag, v.shape).astype(BF16)
        flag_row = lax.broadcasted_iota(jnp.int32, (1, BLOCK), 1) < length
        halves = [slice(i * (BLOCK // 2), (i + 1) * (BLOCK // 2)) for i in range(2)]
        teach = {}

        def teach_pair(source, pair):
            if (source, pair) not in teach:
                part = (tq_in, tk_in, tv_in)[source][:, pair * LANES : (pair + 1) * LANES]
                if source == 0:
                    teach[source, pair] = scaled(part, TEACH_SCALE)
                elif source == 1:
                    teach[source, pair] = biased(part, TEACH_HD, length)
                else:
                    teach[source, pair] = own_sides(part, TEACH_HD, TEACH_SCALE)
            return teach[source, pair]

        def own_sides(part, width, scale):
            queries = scaled(part, scale)
            sides = {}
            for lane in (LANES - width, 0):
                keys = with_bias(part, lane, length)
                column = lax.broadcasted_iota(jnp.int32, part.shape, 1)
                ones = jnp.ones_like(part)
                sides[lane] = queries, jnp.where(column == lane + 1, ones, keys)
            return sides

        bias = jnp.where(flags > 0, jnp.zeros_like(flags), jnp.full_like(flags, MASKED))

        def own_scores(sides, h, width):
            lane = spare_lane(h, width)
            queries, keys = sides[lane]
            left = head_mask(queries, h, width) + lane_row(lambda index: index == lane)
            return left + bias * lane_row(lambda index: index == lane + 1), keys

        v_sides = own_sides(v, HEAD_DIM, EXP_SCALE)

        def score_items(h, found):
            left, keys = masked_sides(
                teach_pair(0, h // 2), teach_pair(1, h // 2), h % 2, TEACH_HD
            )
            sums = []
            found["teach"] = []
            for cols in halves:
                e = jnp.exp2(dot_nt(left, keys[cols]))
                sums.append(e[:, :LANES] + e[:, LANES:])
                found["teach"].append(e.astype(BF16))
                yield
            found["sum"] = sums[0] + sums[1]
            lane = spare_lane(h, HEAD_DIM)
            extra = head_mask(weighed, h, HEAD_DIM) + flags * lane_row(lambda i: i == lane)
            left = jnp.concatenate([head_mask(dctx, h, HEAD_DIM), extra], 1)
            found["dp"] = []
            for cols in halves:
                found["dp"].append(dot_nt(left, right[cols]).astype(BF16))
                yield
            for kind in range(2):
                if kind == 0:
                    left, keys = own_scores(v_sides, h, HEAD_DIM)
                else:
                    left, keys = own_scores(teach_pair(2, h // 2), h % 2, TEACH_HD)
                totals = []
                found[kind] = []
                for i, j in ((0, 0), (0, 1), (1, 1)):
                    e = jnp.exp2(dot_nt(left[halves[i]], keys[halves[j]]))
                    found[kind].append(e.astype(BF16))
                    totals.append(jnp.sum(e, axis=0, keepdims=True))
                    if i != j:
                        across = jnp.sum(e, axis=1, keepdims=True)
                        across = jnp.broadcast_to(across, (BLOCK // 2, LANES)).T[0:1, :]
                    yield
                found["total", kind] = jnp.concatenate(
                    [totals[0] + across, totals[1] + totals[2]], 1
                )

        def row_items(h, found):
            dims = slice(h * HEAD_DIM, (h + 1) * HEAD_DIM)
            for kind in range(2):
                total = found["total", kind]
                inverse = 1.0 / total
                high = jnp.where(flag_row, jnp.maximum(total, inverse), 1.0)
                for cols in halves:
                    worst[0:1, :] = jnp.maximum(worst[0:1, :], high[:, cols])
                inverse = jnp.where(flag_row, inverse, 0.0)
                found["inverse", kind] = inverse
                rows = (vt[dims, :].astype(F32) * inverse).astype(BF16)
                found["rows", kind] = jnp.concatenate([vt[dims, :], rows], 0)
                yield
            count = BLOCK // 8
            for i in range(8):
                rows = slice(i * count, (i + 1) * count)
                total = jnp.sum(found["sum"][rows], axis=1, keepdims=True)
                inverse = 1.0 / total
                high = jnp.maximum(total, inverse)
                worst[:, :LANES] = jnp.maximum(worst[:, :LANES], high)
                factor = low_rows(flag[rows] * inverse, BLOCK // 2)
                for j, cols in enumerate(halves):
                    ds_buf[h % 2, rows, cols] = (
                        pl_in[h, rows, cols] * found["dp"][j][rows]
                        - found["teach"][j][rows] * factor
                    )
                yield

        def value_items(h, found):
            for _ in range(2):
                yield
            dims = slice(h * HEAD_DIM, (h + 1) * HEAD_DIM)
            rel = [None, None]
            for kind in range(2):
                near, across, far = found[kind]
                left = found["rows", kind]
                inverse = found["inverse", kind]
                for j in range(2):
                    if j == 0:
                        part = dot_nn(left[:, halves[0]], near)
                        yield
                        part = part + dot_nt(left[:, halves[1]], across)
                    else:
                        part = dot_nn(left[:, halves[0]], across)
                        yield
                        part = part + dot_nn(left[:, halves[1]], far)
                    part = inverse[:, halves[j]] * part[:HEAD_DIM] + part[HEAD_DIM:]
                    rel[j] = part if kind == 0 else rel[j] - part
                    yield
            for j, cols in enumerate(halves):
                dvt_buf[dims, cols] = dot_nn(dctxt[dims, :], pl_in[h, :, cols]) + SCALE * rel[j]
                yield

        def product_items(h):
            dims = slice(h * HEAD_DIM, (h + 1) * HEAD_DIM)
            ds = ds_buf.at[h % 2]
            for cols in halves:
                dkt_buf[dims, cols] = dot_nn(qt[dims, :], ds[:, cols]) * SCALE
                yield
            part = dot_nn(ds[...], head_mask(k, h, HEAD_DIM))
            if h == 0:
                dq_buf[...] = part
            else:
                dq_buf[...] += part
            yield

        found = [{} for _ in range(GROUP)]
        for h in range(-1, GROUP + 1):
            works = []
            if h + 1 < GROUP:
                works.append((score_items(h + 1, found[h + 1]), 10))
            if 0 <= h < GROUP:
                works.append((row_items(h, found[h]), 10))
                works.append((value_items(h, found[h]), 12))
            if h >= 1:
                works.append((product_items(h - 1), 3))
            weave(works)
        dq_buf[...] *= SCALE
        dk_buf[...] = dkt_buf[...].astype(BF16).T.astype(F32)
        dv_buf[...] = dvt_buf[...].T

    def long_item_careful():
        length = long_len[block - short_blocks]
        flag = query_flag(length, BLOCK)
        bias = jnp.where(
            lax.broadcasted_iota(jnp.int32, (1, BLOCK), 1) < length, 0.0, MASKED
        )
        for buf in (dq_buf, dk_buf, dv_buf):
            buf[...] = jnp.zeros_like(buf)

        def soft(queries, keys, h, width, scale):
            scores = dot_nt(head_mask(queries, h, width), keys)
            e, total = exps(scores * scale + bias, 1, True)
            return e * (flag / total)

        @pl.loop(0, GROUP)
        def _(h):
            q, k, v, dctx = (
                head_mask(ref[...], h, HEAD_DIM) for ref in (q_in, k_in, v_in, dctx_in)
            )
            p = pl_in[h]
            delta = jnp.sum(dctx.astype(F32) * ctx_in[...].astype(F32), axis=1, keepdims=True)
            dp = dot_nt(dctx, v) + (flag - delta)
            teach = soft(tq_in[...], tk_in[...], h, TEACH_HD, TEACH_SCALE)
            ds = (p.astype(F32) * dp - teach).astype(BF16)
            own = soft(v, v, h, HEAD_DIM, EXP_SCALE)
            drel = (own - soft(tv_in[...], tv_in[...], h, TEACH_HD, TEACH_SCALE)).astype(BF16)
            dq_buf[...] += dot_nn(ds, k) * SCALE
            dk_buf[...] += dot_tn(ds, q) * SCALE
            dv_buf[...] += dot_tn(p, dctx) + SCALE * (dot_nn(drel, v) + dot_tn(drel, v))

    short = block < short_blocks
    pl.when(short)(short_items)
    pl.when(jnp.logical_not(short))(long_item)
    wild = jnp.logical_not(jnp.max(worst[...]) < LIMIT)
    pl.when(jnp.logical_and(short, wild))(short_items_careful)
    pl.when(jnp.logical_and(jnp.logical_not(short), wild))(long_item_careful)

    grads = jnp.concatenate([buf[...].astype(BF16) for buf in (dq_buf, dk_buf, dv_buf)], 1)
    grad_out[...] = grads
    acc[...] += dot_nn(side[...], grads)
    bias_acc[0:1, :] += column_sum(grads)

    @pl.when(block == blocks - 1)
    def _():
        width = side.shape[0]
        sides = [bias_acc[0:1, w * LANES : (w + 1) * LANES] for w in range(3)]
        full = [acc[:, w * LANES : (w + 1) * LANES] for w in range(3)]
        full = jnp.concatenate([*full, *sides, jnp.zeros((125, LANES), F32)], 0).astype(BF16)
        cut = full.shape[0] // 2
        is_first = core[0] == 0
        keep_out[...] = jnp.where(is_first, full[:cut], full[cut:])
        give_out[...] = jnp.where(is_first, full[cut:], full[:cut])


def attention_backward(steps, short_len, long_len, core, side, acts, p_short, p_long, carry):
    width, rows = side.shape
    blocks = rows // BLOCK
    short_blocks = short_len.shape[0] * SHORT_LEN // BLOCK
    start, stop = steps

    def place(pick):
        return lambda i: pick((start + i) // blocks, (start + i) % blocks)

    def group_spec(size):
        return pl.BlockSpec((BLOCK, size), place(lambda g, b: (b, g)))

    p_specs = [
        pl.BlockSpec(
            (1, BLOCK, BLOCK), place(lambda g, b: (g, jnp.minimum(b, short_blocks - 1), 0))
        ),
        pl.BlockSpec(
            (GROUP, BLOCK, BLOCK), place(lambda g, b: (g, jnp.maximum(b - short_blocks, 0), 0))
        ),
    ]
    cut = (3 * width + 128) // 2
    sums = jax.ShapeDtypeStruct((GROUPS * cut, LANES), BF16)
    acc = jax.ShapeDtypeStruct((width, 3 * LANES), F32)
    bias_acc = jax.ShapeDtypeStruct((8, 3 * LANES), F32)
    half_spec = pl.BlockSpec((cut, LANES), place(lambda g, b: (g, 0)))
    square = (BLOCK, LANES)
    ins = [short_len, long_len, core, side, *acts, p_short, p_long]
    carried, handed = start % blocks != 0, stop % blocks != 0
    carry_specs = []
    aliases = {}
    if carry is not None:
        grads, keep, give, *sums_in = carry
        if carried:
            ins += sums_in
            carry_specs += [whole(acc.shape), whole(bias_acc.shape)]
        aliases = {len(ins) + i: i for i in range(3)}
        ins += [grads, keep, give]
        carry_specs += [pl.BlockSpec(memory_space=pl.ANY)] * 3
    out_specs = [
        pl.BlockSpec((BLOCK, 3 * LANES), place(lambda g, b: (b, g))),
        half_spec,
        half_spec,
    ]
    out_shape = [jax.ShapeDtypeStruct((rows, GROUPS * 3 * LANES), BF16), sums, sums]
    scratch = []
    if handed:
        out_specs += [whole(acc.shape), whole(bias_acc.shape)]
        out_shape += [acc, bias_acc]
    else:
        scratch = [pltpu.VMEM(acc.shape, F32), pltpu.VMEM(bias_acc.shape, F32)]
    return pl.pallas_call(
        functools.partial(
            backward_kernel, start, blocks, short_blocks, carry is not None, carried
        ),
        grid=(stop - start,),
        in_specs=[smem(), smem(), smem()]
        + [pl.BlockSpec((width, BLOCK), place(lambda g, b: (0, b)))]
        + [group_spec(LANES)] * 5
        + [group_spec(GROUP * TEACH_HD)] * 3
        + p_specs
        + carry_specs,
        out_specs=out_specs,
        out_shape=out_shape,
        scratch_shapes=scratch
        + [
            pltpu.VMEM(square, F32),
            pltpu.VMEM(square, F32),
            pltpu.VMEM(square, F32),
            pltpu.VMEM((LANES, BLOCK), F32),
            pltpu.VMEM((LANES, BLOCK), F32),
            pltpu.VMEM((2, BLOCK, BLOCK), BF16),
            pltpu.VMEM((BLOCK // 8, 2 * SHORT_LEN), F32),
        ],
        input_output_aliases=aliases,
        compiler_params=params(60),
        cost_estimate=pl.CostEstimate(
            flops=(stop - start) * 7_000_000_000,
            bytes_accessed=(stop - start) * 4_000_000,
            transcendentals=(stop - start) * 2_000_000,
        ),
        name=f"attention_backward_{start}",
    )(*ins)


def tokens_grad_kernel(dres, wq, wk, wv, grads, *refs):
    weights = jnp.concatenate(
        [w[:, g * LANES : (g + 1) * LANES] for g in range(GROUPS) for w in (wq, wk, wv)], 1
    )
    refs[-1][...] = (dres[...] + dot_nt(grads[...], weights)).astype(BF16)


def tokens_gradient(first, count, dres, wq, wk, wv, grads, before):
    rows, width = dres.shape
    row_spec = pl.BlockSpec((BLOCK, width), lambda i: (first + i, 0))
    ins = [dres, wq, wk, wv, grads]
    specs = [row_spec] + [whole(wq.shape)] * 3
    specs += [pl.BlockSpec((BLOCK, grads.shape[1]), lambda i: (first + i, 0))]
    aliases = {}
    if before is not None:
        aliases = {len(ins): 0}
        ins.append(before)
        specs.append(pl.BlockSpec(memory_space=pl.ANY))
    return pl.pallas_call(
        tokens_grad_kernel,
        grid=(count,),
        in_specs=specs,
        out_specs=row_spec,
        out_shape=jax.ShapeDtypeStruct((rows, width), BF16),
        input_output_aliases=aliases,
        compiler_params=params(56),
        cost_estimate=pl.CostEstimate(
            flops=count * 500_000_000, bytes_accessed=count * 2_500_000, transcendentals=0
        ),
        name=f"tokens_gradient_{first}",
    )(*ins)


def swap(value):
    return lax.ppermute(value, "tensor", [(0, 1), (1, 0)])


def spread(value):
    return lax.all_to_all(value, "dp", 0, 0, tiled=True)


def sum_chain(keep, give, count):
    (got,) = yield [(swap, give)]
    both = (keep.astype(F32) + got.astype(F32)).astype(BF16)
    rows, width = both.shape
    (got,) = yield [(spread, both.reshape(count, rows // count, width))]
    part = jnp.sum(got.astype(F32), axis=0).astype(BF16)
    (got,) = yield [(spread, jnp.broadcast_to(part[None], got.shape))]
    return got.reshape(rows, width)


def stage_sizes(count):
    sizes = []
    while count > 1:
        sizes.append(4 if count % 4 == 0 else 2)
        count //= sizes[-1]
    return sizes


def offset_send(value, offset, count):
    return lax.ppermute(value, "dp", [(i, i ^ offset) for i in range(count)])


def pair_sum_kernel(place, keep, got, *outs):
    size = len(outs)
    for j, out in enumerate(outs):
        for i in range(out.shape[0]):
            chunk = i * size + (place[0] % size ^ j)
            out[i] = (keep[chunk].astype(F32) + got[chunk].astype(F32)).astype(BF16)


def pair_sum(place, keep, got, size):
    count, rows, width = keep.shape
    return pl.pallas_call(
        pair_sum_kernel,
        in_specs=[smem()] + [pl.BlockSpec(memory_space=pltpu.VMEM)] * 2,
        out_shape=[jax.ShapeDtypeStruct((count // size, rows, width), BF16)] * size,
        compiler_params=params(16),
        name="pair_sum",
    )(place, keep, got)


def tree_sum(values):
    values = [value.astype(F32) for value in values]
    while len(values) > 1:
        values = [values[i] + values[i + 1] for i in range(0, len(values), 2)]
    return values[0].astype(BF16)


def direct_chain(place, keep, give, count):
    rows, width = keep.shape
    near, far = stage_sizes(count)
    (got,) = yield [(swap, give)]
    shape = (count, rows // count, width)
    own, *others = pair_sum(place, keep.reshape(shape), got.reshape(shape), near)

    def sends(values, shift):
        return [
            (functools.partial(offset_send, offset=(j + 1) << shift, count=count), value)
            for j, value in enumerate(values)
        ]

    shift = near.bit_length() - 1
    got = yield sends(others, 0)
    part = tree_sum([own, *got])
    got = yield sends([part] * (far - 1), shift)
    part = tree_sum([part, *got])
    got = yield sends([part] * (near - 1), 0)
    mine = [part, *got]
    other = yield [(swap, value) for value in mine]
    return mine, other


def ordered(core, mine, other):
    first = core[0] == 0
    return jnp.where(first, mine, other), jnp.where(first, other, mine)


def first_finish_kernel(core, total, other, up_out, ub_out, dn_out, wo_out, *vector_outs):
    width, half = up_out.shape
    count = half // width
    for part in range(count):
        cols = slice(part * width, (part + 1) * width)
        up_out[:, cols] = total[cols, :].astype(F32)
        dn_out[cols, :] = total[half + part * width : half + (part + 1) * width, :].astype(F32).T
    biases = total[2 * half : 2 * half + 16, :].astype(F32)
    ub_out[...] = jnp.concatenate([biases[i : i + 1] for i in range(count)], 1).reshape(half)
    halves = ordered(core, total[2 * half + 16 :, :].astype(F32), other[...].astype(F32))
    both = jnp.concatenate(halves, 0)
    wo_out[...] = both[:width]
    for i, out in enumerate(vector_outs):
        out[...] = both[width + i : width + i + 1].reshape(width)


def first_finish(core, total, other, half):
    width = total.shape[1]
    shapes = [(width, half), (half,), (half, width), (width, width)] + [(width,)] * 6
    return pl.pallas_call(
        first_finish_kernel,
        in_specs=[smem()] + [pl.BlockSpec(memory_space=pltpu.VMEM)] * 2,
        out_shape=[jax.ShapeDtypeStruct(shape, F32) for shape in shapes],
        compiler_params=params(16),
        name="first_finish",
    )(core, total, other)


def qkv_finish_body(core, total, other, outs):
    wq_out, wk_out, wv_out, bq_out, bv_out = outs
    width = wq_out.shape[0]
    low, high = ordered(core, total, other)
    cut = low.shape[0] // GROUPS
    sides = []
    for g in range(GROUPS):
        rows = slice(g * cut, (g + 1) * cut)
        full = jnp.concatenate([low[rows], high[rows]], 0)
        cols = slice(g * LANES, (g + 1) * LANES)
        for w, out in enumerate((wq_out, wk_out, wv_out)):
            out[:, cols] = full[w * width : (w + 1) * width]
        sides.append(full[3 * width : 3 * width + 8])
    sides = jnp.concatenate(sides, 1)
    bq_out[...] = sides[0:1].reshape(width)
    bv_out[...] = sides[2:3].reshape(width)


def qkv_finish_kernel(core, total, other, *outs):
    qkv_finish_body(core, total[...].astype(F32), other[...].astype(F32), outs)


def qkv_direct_kernel(near, core, place, *refs):
    parts, outs, bufs = refs[: 2 * near], refs[2 * near : -2], refs[-2:]
    for buf, side in zip(bufs, (parts[:near], parts[near:])):
        for j, part in enumerate(side):
            for i in range(part.shape[0]):
                buf[i * near + (place[0] % near ^ j)] = part[i].astype(F32)
    rows = bufs[0].shape[0] * bufs[0].shape[1]
    total, other = (buf[...].reshape(rows, buf.shape[2]) for buf in bufs)
    qkv_finish_body(core, total, other, outs)


def qkv_shapes(width):
    return [jax.ShapeDtypeStruct(shape, F32) for shape in [(width, width)] * 3 + [(width,)] * 2]


def qkv_finish(core, total, other, width):
    return pl.pallas_call(
        qkv_finish_kernel,
        in_specs=[smem()] + [pl.BlockSpec(memory_space=pltpu.VMEM)] * 2,
        out_shape=qkv_shapes(width),
        compiler_params=params(16),
        name="qkv_finish",
    )(core, total, other)


def qkv_direct_finish(core, place, mine, other, width):
    near = len(mine)
    far, rows, lanes = mine[0].shape
    return pl.pallas_call(
        functools.partial(qkv_direct_kernel, near),
        in_specs=[smem()] * 2 + [pl.BlockSpec(memory_space=pltpu.VMEM)] * (2 * near),
        out_shape=qkv_shapes(width),
        scratch_shapes=[pltpu.VMEM((far * near, rows, lanes), F32)] * 2,
        compiler_params=params(16),
        name="qkv_direct_finish",
    )(core, place, *mine, *other)


class Flights:
    def __init__(self):
        self.asked = {}
        self.flying = {}
        self.done = {}

    def advance(self, name, generator, got=None):
        try:
            wants = next(generator) if got is None else generator.send(got)
            self.asked[name] = (generator, wants)
        except StopIteration as end:
            self.done[name] = end.value

    def step(self, token, work=None, stay=()):
        asked, self.asked = self.asked, {}
        sends = [value for _, wants in asked.values() for _, value in wants]
        token, *sends = lax.optimization_barrier((token, *sends))
        sent = iter(sends)
        for name, (generator, wants) in asked.items():
            self.flying[name] = generator, [move(next(sent)) for move, _ in wants]
        result = None
        if work is not None:
            result, token = work(token)
        for name in [name for name in self.flying if name not in stay]:
            generator, got = self.flying.pop(name)
            if work is not None:
                token, *got = lax.optimization_barrier((token, *got))
            self.advance(name, generator, got)
        return result, token


def per_device(
    dp_count,
    tokens,
    query_weight,
    query_bias,
    key_weight,
    value_weight,
    value_bias,
    proj_weight,
    proj_bias,
    first_gain,
    first_shift,
    up_weight,
    up_bias,
    down_weight,
    down_bias,
    second_gain,
    second_shift,
    teach_query,
    teach_key,
    teach_value,
    short_lengths,
    long_lengths,
    cotangent,
):
    width = tokens.shape[1]
    half = up_weight.shape[1]

    up_other, down_other, ub_other = (swap(value) for value in (up_weight, down_weight, up_bias))
    core = lax.axis_index("tensor").astype(jnp.int32).reshape(1)
    q, k, v, ctx, p_short, p_long, side = attention_forward(
        tokens,
        query_weight,
        key_weight,
        value_weight,
        query_bias,
        value_bias,
        short_lengths,
        long_lengths,
    )
    block_out, dres, dctx, keep, give = middle(
        core,
        tokens,
        ctx,
        cotangent,
        proj_weight,
        (up_weight, up_other),
        (down_weight, down_other),
        (up_bias, ub_other),
        (proj_bias, first_gain, first_shift, down_bias, second_gain, second_shift),
    )
    flights = Flights()
    flights.advance("first", sum_chain(keep, give, dp_count))
    flights.step(short_lengths)
    acts = (q, k, v, ctx, dctx, teach_query, teach_key, teach_value)
    steps = GROUPS * (tokens.shape[0] // BLOCK)
    token = short_lengths
    carry = None
    cut = steps * SPLIT // 12
    for piece in ((0, cut), (cut, steps)):

        def work(lens):
            out = attention_backward(
                piece, lens, long_lengths, core, side, acts, p_short, p_long, carry
            )
            return out[:1] + out[2:], out[1]

        stay = ("first",) if piece[1] == steps else ()
        (grads, give, *sums), keep = flights.step(token, work, stay)
        token, keep = lax.optimization_barrier((short_lengths, keep))
        carry = [grads, keep, give, *sums]

    blocks = tokens.shape[0] // BLOCK
    weights = (query_weight, key_weight, value_weight)

    def input_work(first, count, before):
        def work(grads):
            return grads, tokens_gradient(first, count, dres, *weights, grads, before)

        return work

    def first_work(total):
        out = first_finish(core, total, other, half)
        return out[1:], out[0]

    direct = keep.shape[0] // dp_count % 8 == 0 and len(stage_sizes(dp_count)) == 2
    if direct:
        place = lax.axis_index("dp").astype(jnp.int32).reshape(1)
        flights.advance("qkv", direct_chain(place, keep, give, dp_count))
    else:
        flights.advance("qkv", sum_chain(keep, give, dp_count))
    flights.step(short_lengths, None, ("first",))
    if direct:
        grads, tokens_grad = flights.step(grads, input_work(0, blocks // 2, None))
        _, tokens_grad = flights.step(grads, input_work(blocks // 2, blocks // 2, tokens_grad))
    else:
        _, tokens_grad = flights.step(grads, input_work(0, blocks, None))
    total = flights.done["first"]
    other = swap(total[2 * half + 16 :])
    first, up_grad = flights.step(total, first_work)
    if direct:
        flights.step(short_lengths)
        qkv = qkv_direct_finish(core, place, *flights.done["qkv"], width)
    else:
        total = flights.done["qkv"]
        qkv = qkv_finish(core, total, swap(total), width)
    up_bias_grad, down_grad, proj_grad, *vectors = first
    return (
        block_out,
        tokens_grad,
        qkv[0],
        qkv[3],
        qkv[1],
        qkv[2],
        qkv[4],
        proj_grad,
        vectors[0],
        vectors[1],
        vectors[2],
        up_grad,
        up_bias_grad,
        down_grad,
        vectors[3],
        vectors[4],
        vectors[5],
    )


def solution(mesh):
    in_specs = (
        P(("dp", "tensor"), None),
        P(),
        P(),
        P(),
        P(),
        P(),
        P(),
        P(),
        P(),
        P(),
        P(None, "tensor"),
        P("tensor"),
        P("tensor", None),
        P(),
        P(),
        P(),
        P(("dp", "tensor"), None),
        P(("dp", "tensor"), None),
        P(("dp", "tensor"), None),
        P(("dp", "tensor")),
        P(("dp", "tensor")),
        P(("dp", "tensor"), None),
    )
    out_specs = (
        P(("dp", "tensor"), None),
        P(("dp", "tensor"), None),
        P(),
        P(),
        P(),
        P(),
        P(),
        P(),
        P(),
        P(),
        P(),
        P(None, "tensor"),
        P("tensor"),
        P("tensor", None),
        P(),
        P(),
        P(),
    )
    return jax.shard_map(
        functools.partial(per_device, mesh.shape["dp"]),
        mesh=mesh,
        in_specs=in_specs,
        out_specs=out_specs,
        check_vma=False,
    )
```

```python
import functools

import jax
import jax.numpy as jnp
from jax import lax
from jax.experimental import pallas as pl
from jax.experimental.pallas import tpu as pltpu
from jax.sharding import PartitionSpec as P

HEADS = 12
HEAD_DIM = 32
TEACH_HD = 64
SHORT_LEN = 128
GROUP = 4
LANES = GROUP * HEAD_DIM
GROUPS = HEADS // GROUP
BLOCK = 512
MID_BLOCK = 1024
MID_PARTS = 2
PAD_ROWS = 96
SPLIT = GROUPS - 1

MASKED = -1e30
LIMIT = 2.0**64
EPSILON = 1e-06
LOG2E = 1.4426950408889634
SCALE = HEAD_DIM**-0.5
EXP_SCALE = LOG2E * SCALE
TEACH_SCALE = LOG2E * TEACH_HD**-0.5
MIB = 2**20

F32 = jnp.float32
BF16 = jnp.bfloat16


def dot_nn(left, right):
    return lax.dot_general(left, right, (((1,), (0,)), ((), ())), preferred_element_type=F32)


def dot_nt(left, right):
    return lax.dot_general(left, right, (((1,), (1,)), ((), ())), preferred_element_type=F32)


def dot_tn(left, right):
    return lax.dot_general(left, right, (((0,), (0,)), ((), ())), preferred_element_type=F32)


def dot_tt(left, right):
    return lax.dot_general(left, right, (((0,), (1,)), ((), ())), preferred_element_type=F32)


def lane_row(condition, width=LANES):
    lane = lax.broadcasted_iota(jnp.int32, (1, width), 1)
    return condition(lane).astype(F32).astype(BF16)


def head_mask(block, head, width):
    return block * lane_row(lambda lane: lane // width == head, block.shape[1])


def scaled(block, factor):
    return (block.astype(F32) * factor).astype(BF16)


def spare_lane(head, width):
    return LANES - width if head * width < LANES // 2 else 0


def with_bias(keys, lane, length):
    row = lax.broadcasted_iota(jnp.int32, keys.shape, 0)
    column = lax.broadcasted_iota(jnp.int32, keys.shape, 1)
    bias = jnp.where(row < length, 0.0, MASKED).astype(BF16)
    return jnp.where(column == lane, bias, keys)


def masked_sides(queries, keys, head, width):
    lane = spare_lane(head, width)
    one = lane_row(lambda index: index == lane)
    return head_mask(queries, head, width) + one, keys[lane]


def biased(keys, width, length):
    return {lane: with_bias(keys, lane, length) for lane in (LANES - width, 0)}


def query_flag(length, size):
    return (lax.broadcasted_iota(jnp.int32, (size, 1), 0) < length).astype(F32)


def weave(works):
    ticks = max(count for _, count in works)
    for tick in range(ticks):
        for work, count in works:
            if (tick + 1) * count // ticks > tick * count // ticks:
                next(work)
    for work, _ in works:
        for _ in work:
            pass


def exps(scores, axis, careful):
    if careful:
        scores = scores - jnp.max(scores, axis=axis, keepdims=True)
    heights = jnp.exp2(scores)
    return heights, jnp.sum(heights, axis=axis, keepdims=True)


def low_rows(column, size):
    block = jnp.broadcast_to(column, (column.shape[0], LANES)).astype(BF16)
    return jnp.concatenate([block] * (size // LANES), 1)


def short_bias(length):
    shape = (SHORT_LEN, GROUP * SHORT_LEN)
    return jnp.where(lax.broadcasted_iota(jnp.int32, shape, 0) < length, 0.0, MASKED)


def stack(block, width):
    return jnp.concatenate([head_mask(block, h, width) for h in range(GROUP)], 0)


def diagonal(block):
    return jnp.concatenate(
        [
            block[h * HEAD_DIM : (h + 1) * HEAD_DIM, h * SHORT_LEN : (h + 1) * SHORT_LEN]
            for h in range(GROUP)
        ],
        0,
    )


def params(mebibytes):
    return pltpu.CompilerParams(vmem_limit_bytes=mebibytes * MIB)


def whole(shape):
    return pl.BlockSpec(shape, lambda i: (0,) * len(shape))


def smem():
    return pl.BlockSpec(memory_space=pltpu.SMEM)


def forward_kernel(
    short_blocks,
    short_len,
    long_len,
    tokens,
    wq,
    wk,
    wv,
    bq,
    bv,
    q_out,
    k_out,
    v_out,
    ctx_out,
    ps_out,
    pl_out,
    side_out,
    worst,
    p_buf,
    p_sems,
):
    step = pl.program_id(0)
    x = tokens[...]
    side_out[...] = x.T
    q_out[...] = (dot_nn(x, wq[...]) + row_of(bq)).astype(BF16)
    k_out[...] = dot_nn(x, wk[...]).astype(BF16)
    v_out[...] = (dot_nn(x, wv[...]) + row_of(bv)).astype(BF16)

    def note(total, inverse):
        high = jnp.maximum(total, inverse)
        rows = high.shape[0]
        for i in range(max(high.shape[1] // LANES, 1)):
            part = high[:, i * LANES : (i + 1) * LANES]
            worst[:rows, :] = jnp.maximum(worst[:rows, :], part)


    def short_scores(item, g, found):
        rows = slice(item * SHORT_LEN, (item + 1) * SHORT_LEN)
        cols = slice(g * LANES, (g + 1) * LANES)
        bias = short_bias(short_len[step * (BLOCK // SHORT_LEN) + item])[:, : 2 * SHORT_LEN]
        queries = stack(scaled(q_out[rows, cols], EXP_SCALE), HEAD_DIM)
        for pair in range(GROUP // 2):
            heads = slice(pair * 2 * SHORT_LEN, (pair + 1) * 2 * SHORT_LEN)
            e, total = exps(dot_nt(k_out[rows, cols], queries[heads]) + bias, 0, False)
            found[pair] = e.astype(BF16), total
            yield

    def short_rows(item, g, found):
        rows = slice(item * SHORT_LEN, (item + 1) * SHORT_LEN)
        for pair in range(GROUP // 2):
            heads = slice(pair * 2 * SHORT_LEN, (pair + 1) * 2 * SHORT_LEN)
            e, total = found[pair]
            inverse = 1.0 / total
            note(total, inverse)
            found[pair] = e * inverse.astype(BF16)
            ps_out[g, rows, heads] = found[pair]
            yield

    def short_products(item, g, found):
        rows = slice(item * SHORT_LEN, (item + 1) * SHORT_LEN)
        cols = slice(g * LANES, (g + 1) * LANES)
        probs = jnp.concatenate([found[pair] for pair in range(GROUP // 2)], 1)
        ctx_out[rows, cols] = diagonal(dot_tn(v_out[rows, cols], probs)).T.astype(BF16)
        yield

    def short_items():
        units = [(item, g, {}) for item in range(BLOCK // SHORT_LEN) for g in range(GROUPS)]
        for tick in range(len(units) + 2):
            works = []
            if tick < len(units):
                works.append((short_scores(*units[tick]), 2))
            if 0 <= tick - 1 < len(units):
                works.append((short_rows(*units[tick - 1]), 2))
            if 0 <= tick - 2:
                works.append((short_products(*units[tick - 2]), 1))
            weave(works)


    def p_copy(g):
        index = step - short_blocks
        slot = lax.rem(index * GROUPS + g, 2)
        heads = pl.ds(g * GROUP, GROUP)
        rows = pl.ds(index * BLOCK, BLOCK)
        return pltpu.make_async_copy(
            p_buf.at[slot], pl_out.at[heads, rows, :], p_sems.at[slot]
        )

    def p_slot(g):
        return p_buf.at[lax.rem((step - short_blocks) * GROUPS + g, 2)]

    def long_item():
        length = long_len[step - short_blocks]
        halves = [slice(i * (BLOCK // 2), (i + 1) * (BLOCK // 2)) for i in range(2)]

        sides = {}
        sums = [[] for _ in range(GROUPS)]

        def group_sides(g):
            if g not in sides:
                cols = slice(g * LANES, (g + 1) * LANES)
                keys = biased(k_out[:, cols], HEAD_DIM, length)
                sides[g] = scaled(q_out[:, cols], EXP_SCALE), keys
            return sides[g]

        def scores(head, found):
            left, right = masked_sides(*group_sides(head // GROUP), head % GROUP, HEAD_DIM)
            for half in halves:
                e = jnp.exp2(dot_nt(left, right[half]))
                part = e[:, :LANES] + e[:, LANES:]
                found["sum"] = found["sum"] + part if "sum" in found else part
                found[half.start] = e.astype(BF16)
                yield

        def normalise(head, found):
            g, h = head // GROUP, head % GROUP
            if h == 0:

                @pl.when((step - short_blocks) * GROUPS + g >= 2)
                def _():
                    p_copy(g).wait()

            count = BLOCK // 4
            for i in range(4):
                rows = slice(i * count, (i + 1) * count)
                total = jnp.sum(found["sum"][rows], axis=1, keepdims=True)
                inverse = 1.0 / total
                note(total, inverse)
                e = jnp.concatenate([found[half.start][rows] for half in halves], 1)
                p_slot(g)[h, rows, :] = e * low_rows(inverse, BLOCK)
                yield

        def products(head):
            g, h = head // GROUP, head % GROUP
            cols = slice(g * LANES, (g + 1) * LANES)
            sums[g].append(dot_nn(p_slot(g)[h], head_mask(v_out[:, cols], h, HEAD_DIM)))
            if h == GROUP - 1:
                ctx_out[:, cols] = functools.reduce(jnp.add, sums[g]).astype(BF16)
                p_copy(g).start()
            yield

        found = [{} for _ in range(HEADS)]
        for tick in range(HEADS + 2):
            works = []
            if tick < HEADS:
                works.append((scores(tick, found[tick]), 2))
            if 0 <= tick - 1 < HEADS:
                works.append((normalise(tick - 1, found[tick - 1]), 4))
            if 0 <= tick - 2:
                works.append((products(tick - 2), 1))
            weave(works)


    def short_items_careful():
        items = BLOCK // SHORT_LEN

        @pl.loop(0, items)
        def _(item):
            rows = pl.ds(pl.multiple_of(item * SHORT_LEN, SHORT_LEN), SHORT_LEN)
            bias = short_bias(short_len[step * items + item])
            for g in range(GROUPS):
                cols = slice(g * LANES, (g + 1) * LANES)
                q, k, v = q_out[rows, cols], k_out[rows, cols], v_out[rows, cols]
                e, total = exps(dot_nt(k, stack(q, HEAD_DIM)) * EXP_SCALE + bias, 0, True)
                probs = (e * (1.0 / total)).astype(BF16)
                ps_out[g, rows, :] = probs
                ctx_out[rows, cols] = diagonal(dot_tn(v, probs)).T.astype(BF16)

    def long_item_careful():
        length = long_len[step - short_blocks]
        bias = jnp.where(lax.broadcasted_iota(jnp.int32, (1, BLOCK), 1) < length, 0.0, MASKED)
        p_copy(1).wait()
        p_copy(2).wait()

        @pl.loop(0, GROUPS)
        def _(g):
            p_now = p_slot(g)
            cols = pl.ds(pl.multiple_of(g * LANES, LANES), LANES)
            q, k, v = q_out[:, cols], k_out[:, cols], v_out[:, cols]
            ctx = jnp.zeros((BLOCK, LANES), F32)
            for h in range(GROUP):
                scores = dot_nt(head_mask(q, h, HEAD_DIM), k) * EXP_SCALE + bias
                e, total = exps(scores, 1, True)
                probs = (e * (1.0 / total)).astype(BF16)
                p_now[h] = probs
                ctx = ctx + dot_nn(probs, head_mask(v, h, HEAD_DIM))
            ctx_out[:, cols] = ctx.astype(BF16)
            p_copy(g).start()

            @pl.when(g == 0)
            def _():
                p_copy(g).wait()

    short = step < short_blocks
    long = jnp.logical_not(short)
    worst[...] = jnp.zeros_like(worst)
    pl.when(short)(short_items)
    pl.when(long)(long_item)
    wild = jnp.logical_not(jnp.max(worst[...]) < LIMIT)
    pl.when(jnp.logical_and(short, wild))(short_items_careful)
    pl.when(jnp.logical_and(long, wild))(long_item_careful)

    @pl.when(step == pl.num_programs(0) - 1)
    def _():
        p_copy(1).wait()
        p_copy(2).wait()


def attention_forward(tokens, wq, wk, wv, bq, bv, short_len, long_len):
    rows, width = tokens.shape
    blocks = rows // BLOCK
    short_blocks = short_len.shape[0] * SHORT_LEN // BLOCK
    long_blocks = blocks - short_blocks
    row_spec = pl.BlockSpec((BLOCK, width), lambda i: (i, 0))
    act = jax.ShapeDtypeStruct((rows, width), BF16)
    return pl.pallas_call(
        functools.partial(forward_kernel, short_blocks),
        grid=(blocks,),
        in_specs=[smem(), smem(), row_spec]
        + [whole(a.shape) for a in (wq, wk, wv, bq, bv)],
        out_specs=[
            row_spec,
            row_spec,
            row_spec,
            row_spec,
            pl.BlockSpec((GROUPS, BLOCK, BLOCK), lambda i: (0, jnp.minimum(i, short_blocks - 1), 0)),
            pl.BlockSpec(memory_space=pl.ANY),
            pl.BlockSpec((width, BLOCK), lambda i: (0, i)),
        ],
        out_shape=[
            act,
            act,
            act,
            act,
            jax.ShapeDtypeStruct((GROUPS, short_blocks * BLOCK, BLOCK), BF16),
            jax.ShapeDtypeStruct((HEADS, long_blocks * BLOCK, BLOCK), BF16),
            jax.ShapeDtypeStruct((width, rows), BF16),
        ],
        scratch_shapes=[
            pltpu.VMEM((BLOCK // 4, LANES), F32),
            pltpu.VMEM((2, GROUP, BLOCK, BLOCK), BF16),
            pltpu.SemaphoreType.DMA((2,)),
        ],
        compiler_params=params(56),
        cost_estimate=pl.CostEstimate(
            flops=12_000_000_000, bytes_accessed=24_000_000, transcendentals=8_000_000
        ),
        name="attention_forward",
    )(short_len, long_len, tokens, wq, wk, wv, bq, bv)


def norm_parts(resid):
    centred = resid - jnp.mean(resid, axis=-1, keepdims=True)
    spread = jnp.mean(centred * centred, axis=-1, keepdims=True)
    root = lax.rsqrt(spread + EPSILON)
    return centred * root, root


def norm_back(grad, y, root):
    return root * (
        grad
        - jnp.mean(grad, axis=-1, keepdims=True)
        - y * jnp.mean(grad * y, axis=-1, keepdims=True)
    )


def row_of(vector):
    return vector[...].astype(F32).reshape(1, vector.shape[0])


def column_sum(block):
    return jnp.sum(block.astype(F32), axis=0, keepdims=True)


def middle_kernel(
    core,
    tokens,
    ctx,
    cot,
    wo,
    up0,
    up1,
    dn0,
    dn1,
    ub0,
    ub1,
    bo_in,
    gain1_in,
    shift1_in,
    db_in,
    gain2_in,
    shift2_in,
    block_out,
    dres_out,
    dctx_out,
    keep_out,
    give_out,
    acc_up,
    acc_dn,
    acc_wo,
    acc_ub,
    acc_vec,
    slope,
    active,
    dpre,
    low_rows_buf,
    dbranch,
    dattn,
):
    step = pl.program_id(0)
    half = up0.shape[1]
    width = up0.shape[0]

    @pl.when(step == 0)
    def _():
        for ref in (acc_up, acc_dn, acc_wo, acc_ub, acc_vec):
            ref[...] = jnp.zeros_like(ref)

    bo, gain1, shift1, db, gain2, shift2 = (
        row_of(ref) for ref in (bo_in, gain1_in, shift1_in, db_in, gain2_in, shift2_in)
    )
    def gelu(j, pre, rows):
        pre = pre + row_of((ub0, ub1)[j])
        phi = 0.5 + 0.5 * lax.erf(pre * (0.5**0.5))
        slope[j, rows, :] = phi + pre * (jnp.exp2(pre * pre * (-0.5 * LOG2E)) * 0.3989422804014327)
        active[j, rows, :] = (pre * phi).astype(BF16)

    def back_gelu(j, dactive, rows):
        grad = (dactive * slope[j, rows, :]).astype(BF16)
        dpre[j, rows, :] = grad
        acc_ub[j : j + 1, :] += column_sum(grad)
        return grad

    def row_work(rows):
        resid = tokens[rows, :].astype(F32) + dot_nn(ctx[rows, :], wo[...]) + bo
        yield
        y1, root1 = norm_parts(resid)
        normed = y1 * gain1 + shift1
        normed_low = normed.astype(BF16)
        low_rows_buf[rows, :] = normed_low
        mid = normed + db
        yield
        pre0 = dot_nn(normed_low, up0[...])
        yield
        pre1 = dot_nn(normed_low, up1[...])
        gelu(0, pre0, rows)
        yield
        mid = mid + dot_nn(active[0, rows, :], dn0[...])
        gelu(1, pre1, rows)
        yield
        mid = mid + dot_nn(active[1, rows, :], dn1[...])
        yield
        y2, root2 = norm_parts(mid)
        block_out[rows, :] = (y2 * gain2 + shift2).astype(BF16)
        cotangent = cot[rows, :].astype(F32)
        dmid = norm_back(cotangent * gain2, y2, root2)
        dbranch_low = dmid.astype(BF16)
        dbranch[rows, :] = dbranch_low
        acc_vec[3:4, :] += column_sum(dbranch_low)
        acc_vec[4:5, :] += column_sum(cotangent * y2)
        acc_vec[5:6, :] += column_sum(cotangent)
        yield
        dactive0 = dot_nt(dbranch_low, dn0[...])
        yield
        dactive1 = dot_nt(dbranch_low, dn1[...])
        dpre0 = back_gelu(0, dactive0, rows)
        yield
        dnormed = dmid + dot_nt(dpre0, up0[...])
        dpre1 = back_gelu(1, dactive1, rows)
        yield
        dnormed = dnormed + dot_nt(dpre1, up1[...])
        yield
        acc_vec[1:2, :] += column_sum(dnormed * y1)
        acc_vec[2:3, :] += column_sum(dnormed)
        dres = norm_back(dnormed * gain1, y1, root1)
        dres_out[rows, :] = dres
        dattn_low = dres.astype(BF16)
        dattn[rows, :] = dattn_low
        acc_vec[0:1, :] += column_sum(dattn_low)
        yield
        dctx_out[rows, :] = dot_nt(dattn_low, wo[...]).astype(BF16)
        yield

    def weight_work():
        for j in range(2):
            acc_dn[j] += dot_tn(dbranch[...], active[j])
            yield
        for j in range(2):
            acc_up[j] += dot_tn(low_rows_buf[...], dpre[j])
            yield
        acc_wo[...] += dot_tn(ctx[...], dattn[...])
        yield

    stages = 13
    parts = MID_PARTS
    size = MID_BLOCK // parts
    works = [row_work(slice(i * size, (i + 1) * size)) for i in range(parts)]
    weights_now = weight_work()
    for tick in range(stages + parts - 1):
        for i, work in enumerate(works):
            if 0 <= tick - i < stages:
                next(work)
        if tick >= stages - 2:
            next(weights_now)
    for _ in weights_now:
        pass

    @pl.when(step == pl.num_programs(0) - 1)
    def _():
        for j, out in enumerate((keep_out, give_out)):
            for part in range(half // width):
                cols = slice(part * width, (part + 1) * width)
                out[cols, :] = acc_up[j, :, cols].astype(BF16)
                out[half + part * width : half + (part + 1) * width, :] = acc_dn[j, :, cols].astype(
                    BF16
                )
            pads = [
                acc_ub[j : j + 1, part * width : (part + 1) * width]
                for part in range(half // width)
            ]
            pads.append(jnp.zeros((16 - len(pads), width), F32))
            out[2 * half : 2 * half + 16, :] = jnp.concatenate(pads, 0).astype(BF16)
        cut = (width + PAD_ROWS) // 2
        low = acc_wo[:cut, :].astype(BF16)
        pads = jnp.zeros((PAD_ROWS - 8, width), F32)
        high = jnp.concatenate([acc_wo[cut:, :], acc_vec[...], pads], 0).astype(BF16)
        first = core[0] == 0
        keep_out[2 * half + 16 :, :] = jnp.where(first, low, high)
        give_out[2 * half + 16 :, :] = jnp.where(first, high, low)


def middle(core, tokens, ctx, cot, wo, ups, dns, ubs, vectors):
    rows, width = tokens.shape
    half = ups[0].shape[1]
    row_spec = pl.BlockSpec((MID_BLOCK, width), lambda i: (i, 0))
    weights = (wo, *ups, *dns, *ubs, *vectors)
    act = jax.ShapeDtypeStruct((rows, width), BF16)
    sums = jax.ShapeDtypeStruct((2 * half + 16 + (width + PAD_ROWS) // 2, width), BF16)
    return pl.pallas_call(
        middle_kernel,
        grid=(rows // MID_BLOCK,),
        in_specs=[smem()] + [row_spec] * 3 + [whole(w.shape) for w in weights],
        out_specs=[row_spec] * 3 + [whole(sums.shape), whole(sums.shape)],
        out_shape=[act, jax.ShapeDtypeStruct((rows, width), F32), act, sums, sums],
        scratch_shapes=[
            pltpu.VMEM((2, width, half), F32),
            pltpu.VMEM((2, width, half), F32),
            pltpu.VMEM((width, width), F32),
            pltpu.VMEM((8, half), F32),
            pltpu.VMEM((8, width), F32),
            pltpu.VMEM((2, MID_BLOCK, half), F32),
            pltpu.VMEM((2, MID_BLOCK, half), BF16),
            pltpu.VMEM((2, MID_BLOCK, half), BF16),
            pltpu.VMEM((MID_BLOCK, width), BF16),
            pltpu.VMEM((MID_BLOCK, width), BF16),
            pltpu.VMEM((MID_BLOCK, width), BF16),
        ],
        compiler_params=params(44),
        cost_estimate=pl.CostEstimate(
            flops=34_000_000_000, bytes_accessed=20_000_000, transcendentals=6_000_000
        ),
        name="middle",
    )(core, tokens, ctx, cot, *weights)


def backward_kernel(
    first,
    blocks,
    short_blocks,
    extended,
    short_len,
    long_len,
    core,
    side,
    q_in,
    k_in,
    v_in,
    ctx_in,
    dctx_in,
    tq_in,
    tk_in,
    tv_in,
    ps_in,
    pl_in,
    *refs,
):
    if extended:
        refs = refs[1:]
    (
        grad_out,
        keep_out,
        give_out,
        grads_all,
        dq_buf,
        dk_buf,
        dv_buf,
        dkt_buf,
        dvt_buf,
        ds_buf,
        worst,
    ) = refs
    block = lax.rem(first + pl.program_id(0), blocks)


    def short_scores(item, found):
        rows = slice(item * SHORT_LEN, (item + 1) * SHORT_LEN)
        length = short_len[block * (BLOCK // SHORT_LEN) + item]
        bias = short_bias(length)[:, : 2 * SHORT_LEN]
        lane = lax.broadcasted_iota(jnp.int32, (1, GROUP * SHORT_LEN), 1)
        flag = (lane % SHORT_LEN < length).astype(F32)
        v, dctx = v_in[rows, :], dctx_in[rows, :]
        found["v_all"], found["dctx_all"] = stack(v, HEAD_DIM), stack(dctx, HEAD_DIM)
        found["p"] = ps_in[0, rows, :]
        v_scaled = stack(scaled(v, EXP_SCALE), HEAD_DIM)
        weighed = (dctx.astype(F32) * ctx_in[rows, :].astype(F32)).T
        delta = [
            jnp.sum(weighed[h * HEAD_DIM : (h + 1) * HEAD_DIM], axis=0, keepdims=True)
            for h in range(GROUP)
        ]
        delta = flag - jnp.concatenate(delta, 1)
        for pair in range(GROUP // 2):
            cols = slice(pair * LANES, (pair + 1) * LANES)
            heads = slice(pair * 2 * SHORT_LEN, (pair + 1) * 2 * SHORT_LEN)
            for kind, (queries, keys) in enumerate(((tq_in, tk_in), (tv_in, tv_in))):
                part = scaled(queries[rows, cols], TEACH_SCALE)
                both = jnp.concatenate([head_mask(part, h, TEACH_HD) for h in range(2)], 0)
                scores = dot_nt(keys[rows, cols], both) + bias
                found[kind, pair] = measured(jnp.exp2(scores), flag[:, heads])
                yield
            scores = dot_nt(v, v_scaled[heads]) + bias
            found[2, pair] = measured(jnp.exp2(scores), flag[:, heads])
            yield
            dp = dot_nt(v, found["dctx_all"][heads]) + delta[:, heads]
            found[3, pair] = dp.astype(BF16)
            yield

    def measured(e, flag):
        total = jnp.sum(e, axis=0, keepdims=True)
        inverse = 1.0 / total
        width = total.shape[1]
        worst[0:1, :width] = jnp.maximum(worst[0:1, :width], jnp.maximum(total, inverse))
        return e.astype(BF16), (flag * inverse).astype(BF16)

    def short_rows(found):
        found["ds"], found["drel"] = [], []
        for pair in range(GROUP // 2):
            heads = slice(pair * 2 * SHORT_LEN, (pair + 1) * 2 * SHORT_LEN)
            teach, teach_rel, own = (found[kind, pair][0] * found[kind, pair][1] for kind in range(3))
            found["ds"].append(found["p"][:, heads] * found[3, pair] - teach)
            yield
            found["drel"].append(own - teach_rel)
            yield

    def short_products(item, found):
        rows = slice(item * SHORT_LEN, (item + 1) * SHORT_LEN)
        ds, drel = (jnp.concatenate(found[name], 1) for name in ("ds", "drel"))
        dq_buf[rows, :] = diagonal(dot_tn(k_in[rows, :], ds)).T * SCALE
        yield
        dk_buf[rows, :] = dot_nn(ds, stack(q_in[rows, :], HEAD_DIM)) * SCALE
        yield
        rel = diagonal(dot_tn(v_in[rows, :], drel)).T
        yield
        rel = rel + dot_nn(drel, found["v_all"])
        yield
        dv_buf[rows, :] = dot_nn(found["p"], found["dctx_all"]) + SCALE * rel
        yield

    def short_items():
        worst[...] = jnp.zeros_like(worst)
        items = BLOCK // SHORT_LEN
        found = [{} for _ in range(items)]
        for tick in range(items + 2):
            works = []
            if tick < items:
                works.append((short_scores(tick, found[tick]), 8))
            if 0 <= tick - 1 < items:
                works.append((short_rows(found[tick - 1]), 4))
            if 0 <= tick - 2:
                works.append((short_products(tick - 2, found[tick - 2]), 5))
            weave(works)

    def short_items_careful():
        @pl.loop(0, BLOCK // SHORT_LEN)
        def _(item):
            rows = pl.ds(pl.multiple_of(item * SHORT_LEN, SHORT_LEN), SHORT_LEN)
            length = short_len[block * (BLOCK // SHORT_LEN) + item]
            bias = short_bias(length)
            lane = lax.broadcasted_iota(jnp.int32, (1, GROUP * SHORT_LEN), 1)
            flag = (lane % SHORT_LEN < length).astype(F32)
            q, k, v = q_in[rows, :], k_in[rows, :], v_in[rows, :]
            dctx, ctx = dctx_in[rows, :], ctx_in[rows, :]
            tq, tk, tv = tq_in[rows, :], tk_in[rows, :], tv_in[rows, :]
            q_all, v_all, dctx_all = (stack(part, HEAD_DIM) for part in (q, v, dctx))
            p = ps_in[0, rows, :]

            def soft(scores, scale):
                e, total = exps(scores * scale + bias, 0, True)
                return e * (flag / total)

            def teach(keys, queries):
                parts = []
                for pair in range(GROUP // 2):
                    cols = slice(pair * LANES, (pair + 1) * LANES)
                    both = [head_mask(queries[:, cols], h, TEACH_HD) for h in range(2)]
                    parts.append(dot_nt(keys[:, cols], jnp.concatenate(both, 0)))
                return soft(jnp.concatenate(parts, 1), TEACH_SCALE)

            weighed = (dctx.astype(F32) * ctx.astype(F32)).T
            delta = [
                jnp.sum(weighed[h * HEAD_DIM : (h + 1) * HEAD_DIM], axis=0, keepdims=True)
                for h in range(GROUP)
            ]
            dp = dot_nt(v, dctx_all) + (flag - jnp.concatenate(delta, 1))
            ds = (p.astype(F32) * dp - teach(tk, tq)).astype(BF16)
            dq_buf[rows, :] = diagonal(dot_tn(k, ds)).T * SCALE
            dk_buf[rows, :] = dot_nn(ds, q_all) * SCALE
            drel = (soft(dot_nt(v, v_all), EXP_SCALE) - teach(tv, tv)).astype(BF16)
            rel = dot_nn(drel, v_all) + diagonal(dot_tn(v, drel)).T
            dv_buf[rows, :] = dot_nn(p, dctx_all) + SCALE * rel


    def long_item():
        worst[...] = jnp.zeros_like(worst)
        length = long_len[block - short_blocks]
        q, k, v = q_in[...], k_in[...], v_in[...]
        dctx, ctx = dctx_in[...], ctx_in[...]
        qt, vt, dctxt = q.T, v.T, dctx.T
        weighed = -(dctx.astype(F32) * ctx.astype(F32)).astype(BF16)
        right = jnp.concatenate([v, jnp.ones_like(v)], 1)
        flag = query_flag(length, BLOCK)
        flags = jnp.broadcast_to(flag, v.shape).astype(BF16)
        flag_row = lax.broadcasted_iota(jnp.int32, (1, BLOCK), 1) < length
        halves = [slice(i * (BLOCK // 2), (i + 1) * (BLOCK // 2)) for i in range(2)]
        teach = {}

        def teach_pair(source, pair):
            if (source, pair) not in teach:
                part = (tq_in, tk_in, tv_in)[source][:, pair * LANES : (pair + 1) * LANES]
                if source == 0:
                    teach[source, pair] = scaled(part, TEACH_SCALE)
                elif source == 1:
                    teach[source, pair] = biased(part, TEACH_HD, length)
                else:
                    teach[source, pair] = own_sides(part, TEACH_HD, TEACH_SCALE)
            return teach[source, pair]

        def own_sides(part, width, scale):
            queries = scaled(part, scale)
            sides = {}
            for lane in (LANES - width, 0):
                keys = with_bias(part, lane, length)
                column = lax.broadcasted_iota(jnp.int32, part.shape, 1)
                ones = jnp.ones_like(part)
                sides[lane] = queries, jnp.where(column == lane + 1, ones, keys)
            return sides

        bias = jnp.where(flags > 0, jnp.zeros_like(flags), jnp.full_like(flags, MASKED))

        def own_scores(sides, h, width):
            lane = spare_lane(h, width)
            queries, keys = sides[lane]
            left = head_mask(queries, h, width) + lane_row(lambda index: index == lane)
            return left + bias * lane_row(lambda index: index == lane + 1), keys

        v_sides = own_sides(v, HEAD_DIM, EXP_SCALE)

        def score_items(h, found):
            left, keys = masked_sides(
                teach_pair(0, h // 2), teach_pair(1, h // 2), h % 2, TEACH_HD
            )
            sums = []
            found["teach"] = []
            for cols in halves:
                e = jnp.exp2(dot_nt(left, keys[cols]))
                sums.append(e[:, :LANES] + e[:, LANES:])
                found["teach"].append(e.astype(BF16))
                yield
            found["sum"] = sums[0] + sums[1]
            lane = spare_lane(h, HEAD_DIM)
            extra = head_mask(weighed, h, HEAD_DIM) + flags * lane_row(lambda i: i == lane)
            left = jnp.concatenate([head_mask(dctx, h, HEAD_DIM), extra], 1)
            found["dp"] = []
            for cols in halves:
                found["dp"].append(dot_nt(left, right[cols]).astype(BF16))
                yield
            for kind in range(2):
                if kind == 0:
                    left, keys = own_scores(v_sides, h, HEAD_DIM)
                else:
                    left, keys = own_scores(teach_pair(2, h // 2), h % 2, TEACH_HD)
                totals = []
                found[kind] = []
                for i, j in ((0, 0), (0, 1), (1, 1)):
                    e = jnp.exp2(dot_nt(left[halves[i]], keys[halves[j]]))
                    found[kind].append(e.astype(BF16))
                    totals.append(jnp.sum(e, axis=0, keepdims=True))
                    if i != j:
                        across = jnp.sum(e, axis=1, keepdims=True)
                        across = jnp.broadcast_to(across, (BLOCK // 2, LANES)).T[0:1, :]
                    yield
                found["total", kind] = jnp.concatenate(
                    [totals[0] + across, totals[1] + totals[2]], 1
                )

        def row_items(h, found):
            dims = slice(h * HEAD_DIM, (h + 1) * HEAD_DIM)
            for kind in range(2):
                total = found["total", kind]
                inverse = 1.0 / total
                high = jnp.where(flag_row, jnp.maximum(total, inverse), 1.0)
                for cols in halves:
                    worst[0:1, :] = jnp.maximum(worst[0:1, :], high[:, cols])
                inverse = jnp.where(flag_row, inverse, 0.0)
                found["inverse", kind] = inverse
                rows = (vt[dims, :].astype(F32) * inverse).astype(BF16)
                found["rows", kind] = jnp.concatenate([vt[dims, :], rows], 0)
                yield
            count = BLOCK // 8
            for i in range(8):
                rows = slice(i * count, (i + 1) * count)
                total = jnp.sum(found["sum"][rows], axis=1, keepdims=True)
                inverse = 1.0 / total
                high = jnp.maximum(total, inverse)
                worst[:, :LANES] = jnp.maximum(worst[:, :LANES], high)
                factor = low_rows(flag[rows] * inverse, BLOCK // 2)
                for j, cols in enumerate(halves):
                    ds_buf[h % 2, rows, cols] = (
                        pl_in[h, rows, cols] * found["dp"][j][rows]
                        - found["teach"][j][rows] * factor
                    )
                yield

        def value_items(h, found):
            for _ in range(2):
                yield
            dims = slice(h * HEAD_DIM, (h + 1) * HEAD_DIM)
            rel = [None, None]
            for kind in range(2):
                near, across, far = found[kind]
                left = found["rows", kind]
                inverse = found["inverse", kind]
                for j in range(2):
                    if j == 0:
                        part = dot_nn(left[:, halves[0]], near)
                        yield
                        part = part + dot_nt(left[:, halves[1]], across)
                    else:
                        part = dot_nn(left[:, halves[0]], across)
                        yield
                        part = part + dot_nn(left[:, halves[1]], far)
                    part = inverse[:, halves[j]] * part[:HEAD_DIM] + part[HEAD_DIM:]
                    rel[j] = part if kind == 0 else rel[j] - part
                    yield
            for j, cols in enumerate(halves):
                dvt_buf[dims, cols] = dot_nn(dctxt[dims, :], pl_in[h, :, cols]) + SCALE * rel[j]
                yield

        def product_items(h):
            dims = slice(h * HEAD_DIM, (h + 1) * HEAD_DIM)
            ds = ds_buf.at[h % 2]
            for cols in halves:
                dkt_buf[dims, cols] = dot_nn(qt[dims, :], ds[:, cols]) * SCALE
                yield
            part = dot_nn(ds[...], head_mask(k, h, HEAD_DIM))
            if h == 0:
                dq_buf[...] = part
            else:
                dq_buf[...] += part
            yield

        found = [{} for _ in range(GROUP)]
        for h in range(-1, GROUP + 1):
            works = []
            if h + 1 < GROUP:
                works.append((score_items(h + 1, found[h + 1]), 10))
            if 0 <= h < GROUP:
                works.append((row_items(h, found[h]), 10))
                works.append((value_items(h, found[h]), 12))
            if h >= 1:
                works.append((product_items(h - 1), 3))
            weave(works)
        dq_buf[...] *= SCALE
        dk_buf[...] = dkt_buf[...].astype(BF16).T.astype(F32)
        dv_buf[...] = dvt_buf[...].T

    def long_item_careful():
        length = long_len[block - short_blocks]
        flag = query_flag(length, BLOCK)
        bias = jnp.where(
            lax.broadcasted_iota(jnp.int32, (1, BLOCK), 1) < length, 0.0, MASKED
        )
        for buf in (dq_buf, dk_buf, dv_buf):
            buf[...] = jnp.zeros_like(buf)

        def soft(queries, keys, h, width, scale):
            scores = dot_nt(head_mask(queries, h, width), keys)
            e, total = exps(scores * scale + bias, 1, True)
            return e * (flag / total)

        @pl.loop(0, GROUP)
        def _(h):
            q, k, v, dctx = (
                head_mask(ref[...], h, HEAD_DIM) for ref in (q_in, k_in, v_in, dctx_in)
            )
            p = pl_in[h]
            delta = jnp.sum(dctx.astype(F32) * ctx_in[...].astype(F32), axis=1, keepdims=True)
            dp = dot_nt(dctx, v) + (flag - delta)
            teach = soft(tq_in[...], tk_in[...], h, TEACH_HD, TEACH_SCALE)
            ds = (p.astype(F32) * dp - teach).astype(BF16)
            own = soft(v, v, h, HEAD_DIM, EXP_SCALE)
            drel = (own - soft(tv_in[...], tv_in[...], h, TEACH_HD, TEACH_SCALE)).astype(BF16)
            dq_buf[...] += dot_nn(ds, k) * SCALE
            dk_buf[...] += dot_tn(ds, q) * SCALE
            dv_buf[...] += dot_tn(p, dctx) + SCALE * (dot_nn(drel, v) + dot_tn(drel, v))

    short = block < short_blocks
    pl.when(short)(short_items)
    pl.when(jnp.logical_not(short))(long_item)
    wild = jnp.logical_not(jnp.max(worst[...]) < LIMIT)
    pl.when(jnp.logical_and(short, wild))(short_items_careful)
    pl.when(jnp.logical_and(jnp.logical_not(short), wild))(long_item_careful)

    grads = jnp.concatenate([buf[...].astype(BF16) for buf in (dq_buf, dk_buf, dv_buf)], 1)
    grad_out[...] = grads
    grads_all[pl.ds(pl.multiple_of(block * BLOCK, BLOCK), BLOCK), :] = grads

    @pl.when(block == blocks - 1)
    def _():
        sums = dot_nn(side[...], grads_all[...])
        biases = column_sum(grads_all[...])
        full = [sums[:, w * LANES : (w + 1) * LANES] for w in range(3)]
        full += [biases[:, w * LANES : (w + 1) * LANES] for w in range(3)]
        full = jnp.concatenate([*full, jnp.zeros((125, LANES), F32)], 0).astype(BF16)
        cut = full.shape[0] // 2
        is_first = core[0] == 0
        keep_out[...] = jnp.where(is_first, full[:cut], full[cut:])
        give_out[...] = jnp.where(is_first, full[cut:], full[:cut])


def attention_backward(groups, short_len, long_len, core, side, acts, p_short, p_long, before):
    width, rows = side.shape
    blocks = rows // BLOCK
    short_blocks = short_len.shape[0] * SHORT_LEN // BLOCK
    start, stop = (group * blocks for group in groups)

    def place(pick):
        return lambda i: pick((start + i) // blocks, (start + i) % blocks)

    def group_spec(size):
        return pl.BlockSpec((BLOCK, size), place(lambda g, b: (b, g)))

    p_specs = [
        pl.BlockSpec(
            (1, BLOCK, BLOCK), place(lambda g, b: (g, jnp.minimum(b, short_blocks - 1), 0))
        ),
        pl.BlockSpec(
            (GROUP, BLOCK, BLOCK), place(lambda g, b: (g, jnp.maximum(b - short_blocks, 0), 0))
        ),
    ]
    cut = (3 * width + 128) // 2
    sums = jax.ShapeDtypeStruct(((groups[1] - groups[0]) * cut, LANES), BF16)
    half_spec = pl.BlockSpec((cut, LANES), place(lambda g, b: (g - groups[0], 0)))
    square = (BLOCK, LANES)
    ins = [short_len, long_len, core, side, *acts, p_short, p_long]
    before_specs = []
    aliases = {}
    if before is not None:
        aliases = {len(ins): 0}
        ins.append(before)
        before_specs = [pl.BlockSpec(memory_space=pl.ANY)]
    out_specs = [
        pl.BlockSpec((BLOCK, 3 * LANES), place(lambda g, b: (b, g))),
        half_spec,
        half_spec,
    ]
    out_shape = [jax.ShapeDtypeStruct((rows, GROUPS * 3 * LANES), BF16), sums, sums]
    return pl.pallas_call(
        functools.partial(backward_kernel, start, blocks, short_blocks, before is not None),
        grid=(stop - start,),
        in_specs=[smem(), smem(), smem()]
        + [whole(side.shape)]
        + [group_spec(LANES)] * 5
        + [group_spec(GROUP * TEACH_HD)] * 3
        + p_specs
        + before_specs,
        out_specs=out_specs,
        out_shape=out_shape,
        scratch_shapes=[
            pltpu.VMEM((rows, 3 * LANES), BF16),
            pltpu.VMEM(square, F32),
            pltpu.VMEM(square, F32),
            pltpu.VMEM(square, F32),
            pltpu.VMEM((LANES, BLOCK), F32),
            pltpu.VMEM((LANES, BLOCK), F32),
            pltpu.VMEM((2, BLOCK, BLOCK), BF16),
            pltpu.VMEM((BLOCK // 8, 2 * SHORT_LEN), F32),
        ],
        input_output_aliases=aliases,
        compiler_params=params(60),
        cost_estimate=pl.CostEstimate(
            flops=(stop - start) * 7_000_000_000,
            bytes_accessed=(stop - start) * 4_000_000,
            transcendentals=(stop - start) * 2_000_000,
        ),
        name=f"attention_backward_{start}",
    )(*ins)


def tokens_grad_kernel(dres, wq, wk, wv, grads, *refs):
    weights = jnp.concatenate(
        [w[:, g * LANES : (g + 1) * LANES] for g in range(GROUPS) for w in (wq, wk, wv)], 1
    )
    refs[-1][...] = (dres[...] + dot_nt(grads[...], weights)).astype(BF16)


def tokens_gradient(first, count, dres, wq, wk, wv, grads, before):
    rows, width = dres.shape
    row_spec = pl.BlockSpec((BLOCK, width), lambda i: (first + i, 0))
    ins = [dres, wq, wk, wv, grads]
    specs = [row_spec] + [whole(wq.shape)] * 3
    specs += [pl.BlockSpec((BLOCK, grads.shape[1]), lambda i: (first + i, 0))]
    aliases = {}
    if before is not None:
        aliases = {len(ins): 0}
        ins.append(before)
        specs.append(pl.BlockSpec(memory_space=pl.ANY))
    return pl.pallas_call(
        tokens_grad_kernel,
        grid=(count,),
        in_specs=specs,
        out_specs=row_spec,
        out_shape=jax.ShapeDtypeStruct((rows, width), BF16),
        input_output_aliases=aliases,
        compiler_params=params(56),
        cost_estimate=pl.CostEstimate(
            flops=count * 500_000_000, bytes_accessed=count * 2_500_000, transcendentals=0
        ),
        name=f"tokens_gradient_{first}",
    )(*ins)


def swap(value):
    return lax.ppermute(value, "tensor", [(0, 1), (1, 0)])


def spread(value):
    return lax.all_to_all(value, "dp", 0, 0, tiled=True)


def sum_chain(keep, give, count):
    (got,) = yield [(swap, give)]
    both = (keep.astype(F32) + got.astype(F32)).astype(BF16)
    rows, width = both.shape
    (got,) = yield [(spread, both.reshape(count, rows // count, width))]
    part = jnp.sum(got.astype(F32), axis=0).astype(BF16)
    (got,) = yield [(spread, jnp.broadcast_to(part[None], got.shape))]
    return got.reshape(rows, width)


def stage_sizes(count):
    sizes = []
    while count > 1:
        sizes.append(4 if count % 4 == 0 else 2)
        count //= sizes[-1]
    return sizes


def offset_send(value, offset, count):
    return lax.ppermute(value, "dp", [(i, i ^ offset) for i in range(count)])


def pair_sum_kernel(count, place, *refs):
    keeps, gots, outs = refs[:count], refs[count : 2 * count], refs[2 * count :]
    size = len(outs)
    for j, out in enumerate(outs):
        for i in range(out.shape[0]):
            chunk = i * size + (place[0] % size ^ j)
            start = 0
            for keep, got in zip(keeps, gots):
                stop = start + keep.shape[1]
                both = keep[chunk].astype(F32) + got[chunk].astype(F32)
                out[i, start:stop, :] = both.astype(BF16)
                start = stop


def pair_sum(place, keeps, gots, size):
    count, _, width = keeps[0].shape
    rows = sum(keep.shape[1] for keep in keeps)
    return pl.pallas_call(
        functools.partial(pair_sum_kernel, len(keeps)),
        in_specs=[smem()] + [pl.BlockSpec(memory_space=pltpu.VMEM)] * (2 * len(keeps)),
        out_shape=[jax.ShapeDtypeStruct((count // size, rows, width), BF16)] * size,
        compiler_params=params(16),
        name="pair_sum",
    )(place, *keeps, *gots)


def tree_sum(values):
    values = [value.astype(F32) for value in values]
    while len(values) > 1:
        values = [values[i] + values[i + 1] for i in range(0, len(values), 2)]
    return values[0].astype(BF16)


def direct_chain(place, keeps, got_first, give, count):
    near, far = stage_sizes(count)
    (got,) = yield [(swap, give)]

    def chunks(value):
        return value.reshape(count, value.shape[0] // count, value.shape[1])

    gots = [chunks(value) for value in (got_first, got)]
    own, *others = pair_sum(place, [chunks(keep) for keep in keeps], gots, near)

    def sends(values, shift):
        return [
            (functools.partial(offset_send, offset=(j + 1) << shift, count=count), value)
            for j, value in enumerate(values)
        ]

    shift = near.bit_length() - 1
    got = yield sends(others, 0)
    part = tree_sum([own, *got])
    got = yield sends([part] * (far - 1), shift)
    part = tree_sum([part, *got])
    got = yield sends([part] * (near - 1), 0)
    mine = [part, *got]
    other = yield [(swap, value) for value in mine]
    return mine, other


def ordered(core, mine, other):
    first = core[0] == 0
    return jnp.where(first, mine, other), jnp.where(first, other, mine)


def first_finish_kernel(core, total, other, up_out, ub_out, dn_out, wo_out, *vector_outs):
    width, half = up_out.shape
    count = half // width
    for part in range(count):
        cols = slice(part * width, (part + 1) * width)
        up_out[:, cols] = total[cols, :].astype(F32)
        dn_out[cols, :] = total[half + part * width : half + (part + 1) * width, :].astype(F32).T
    biases = total[2 * half : 2 * half + 16, :].astype(F32)
    ub_out[...] = jnp.concatenate([biases[i : i + 1] for i in range(count)], 1).reshape(half)
    halves = ordered(core, total[2 * half + 16 :, :].astype(F32), other[...].astype(F32))
    both = jnp.concatenate(halves, 0)
    wo_out[...] = both[:width]
    for i, out in enumerate(vector_outs):
        out[...] = both[width + i : width + i + 1].reshape(width)


def first_finish(core, total, other, half):
    width = total.shape[1]
    shapes = [(width, half), (half,), (half, width), (width, width)] + [(width,)] * 6
    return pl.pallas_call(
        first_finish_kernel,
        in_specs=[smem()] + [pl.BlockSpec(memory_space=pltpu.VMEM)] * 2,
        out_shape=[jax.ShapeDtypeStruct(shape, F32) for shape in shapes],
        compiler_params=params(16),
        name="first_finish",
    )(core, total, other)


def qkv_finish_body(core, total, other, outs):
    wq_out, wk_out, wv_out, bq_out, bv_out = outs
    width = wq_out.shape[0]
    low, high = ordered(core, total, other)
    cut = low.shape[0] // GROUPS
    sides = []
    for g in range(GROUPS):
        rows = slice(g * cut, (g + 1) * cut)
        full = jnp.concatenate([low[rows], high[rows]], 0)
        cols = slice(g * LANES, (g + 1) * LANES)
        for w, out in enumerate((wq_out, wk_out, wv_out)):
            out[:, cols] = full[w * width : (w + 1) * width]
        sides.append(full[3 * width : 3 * width + 8])
    sides = jnp.concatenate(sides, 1)
    bq_out[...] = sides[0:1].reshape(width)
    bv_out[...] = sides[2:3].reshape(width)


def qkv_finish_kernel(core, total, other, *outs):
    qkv_finish_body(core, total[...].astype(F32), other[...].astype(F32), outs)


def single_swap(value):
    (got,) = yield [(swap, value)]
    return got


def qkv_direct_kernel(near, cuts, core, place, *refs):
    parts, outs, bufs = refs[: 2 * near], refs[2 * near : -2], refs[-2:]
    for buf, side in zip(bufs, (parts[:near], parts[near:])):
        for j, part in enumerate(side):
            for i in range(part.shape[0]):
                buf[i * near + (place[0] % near ^ j)] = part[i].astype(F32)
    sides = []
    for buf in bufs:
        count, rows, lanes = buf.shape
        spans = zip((0, *cuts), (*cuts, rows))
        parts = [buf[:, a:b, :].reshape(count * (b - a), lanes) for a, b in spans]
        sides.append(jnp.concatenate(parts, 0))
    qkv_finish_body(core, *sides, outs)


def qkv_shapes(width):
    return [jax.ShapeDtypeStruct(shape, F32) for shape in [(width, width)] * 3 + [(width,)] * 2]


def qkv_finish(core, total, other, width):
    return pl.pallas_call(
        qkv_finish_kernel,
        in_specs=[smem()] + [pl.BlockSpec(memory_space=pltpu.VMEM)] * 2,
        out_shape=qkv_shapes(width),
        compiler_params=params(16),
        name="qkv_finish",
    )(core, total, other)


def qkv_direct_finish(core, place, cuts, mine, other, width):
    near = len(mine)
    far, rows, lanes = mine[0].shape
    return pl.pallas_call(
        functools.partial(qkv_direct_kernel, near, cuts),
        in_specs=[smem()] * 2 + [pl.BlockSpec(memory_space=pltpu.VMEM)] * (2 * near),
        out_shape=qkv_shapes(width),
        scratch_shapes=[pltpu.VMEM((far * near, rows, lanes), F32)] * 2,
        compiler_params=params(16),
        name="qkv_direct_finish",
    )(core, place, *mine, *other)


class Flights:
    def __init__(self):
        self.asked = {}
        self.flying = {}
        self.done = {}

    def advance(self, name, generator, got=None):
        try:
            wants = next(generator) if got is None else generator.send(got)
            self.asked[name] = (generator, wants)
        except StopIteration as end:
            self.done[name] = end.value

    def step(self, token, work=None, stay=()):
        asked, self.asked = self.asked, {}
        sends = [value for _, wants in asked.values() for _, value in wants]
        token, *sends = lax.optimization_barrier((token, *sends))
        sent = iter(sends)
        for name, (generator, wants) in asked.items():
            self.flying[name] = generator, [move(next(sent)) for move, _ in wants]
        result = None
        if work is not None:
            result, token = work(token)
        for name in [name for name in self.flying if name not in stay]:
            generator, got = self.flying.pop(name)
            if work is not None:
                token, *got = lax.optimization_barrier((token, *got))
            self.advance(name, generator, got)
        return result, token


def per_device(
    dp_count,
    tokens,
    query_weight,
    query_bias,
    key_weight,
    value_weight,
    value_bias,
    proj_weight,
    proj_bias,
    first_gain,
    first_shift,
    up_weight,
    up_bias,
    down_weight,
    down_bias,
    second_gain,
    second_shift,
    teach_query,
    teach_key,
    teach_value,
    short_lengths,
    long_lengths,
    cotangent,
):
    width = tokens.shape[1]
    half = up_weight.shape[1]

    up_other, down_other, ub_other = (swap(value) for value in (up_weight, down_weight, up_bias))
    core = lax.axis_index("tensor").astype(jnp.int32).reshape(1)
    q, k, v, ctx, p_short, p_long, side = attention_forward(
        tokens,
        query_weight,
        key_weight,
        value_weight,
        query_bias,
        value_bias,
        short_lengths,
        long_lengths,
    )
    block_out, dres, dctx, keep, give = middle(
        core,
        tokens,
        ctx,
        cotangent,
        proj_weight,
        (up_weight, up_other),
        (down_weight, down_other),
        (up_bias, ub_other),
        (proj_bias, first_gain, first_shift, down_bias, second_gain, second_shift),
    )
    flights = Flights()
    flights.advance("first", sum_chain(keep, give, dp_count))
    flights.step(short_lengths)
    acts = (q, k, v, ctx, dctx, teach_query, teach_key, teach_value)
    token = short_lengths
    grads = None
    keeps = []
    gives = []
    for groups in ((0, SPLIT), (SPLIT, GROUPS)):

        def work(lens):
            out = attention_backward(
                groups, lens, long_lengths, core, side, acts, p_short, p_long, grads
            )
            return out[:2], out[2]

        stay = ("first",) if groups[1] == GROUPS else ()
        (grads, keep), give = flights.step(token, work, stay)
        token, give = lax.optimization_barrier((short_lengths, give))
        keeps.append(keep)
        gives.append(give)
        if groups[1] < GROUPS:
            flights.advance("swap", single_swap(give))

    blocks = tokens.shape[0] // BLOCK
    weights = (query_weight, key_weight, value_weight)

    def input_work(first, count, before):
        def work(grads):
            return grads, tokens_gradient(first, count, dres, *weights, grads, before)

        return work

    def first_work(total):
        out = first_finish(core, total, other, half)
        return out[1:], out[0]

    sizes = [keep.shape[0] // dp_count for keep in keeps]
    direct = all(size % 8 == 0 for size in sizes) and len(stage_sizes(dp_count)) == 2
    if direct:
        place = lax.axis_index("dp").astype(jnp.int32).reshape(1)
        chain = direct_chain(place, keeps, flights.done["swap"], gives[1], dp_count)
    else:
        chain = sum_chain(jnp.concatenate(keeps, 0), jnp.concatenate(gives, 0), dp_count)
    flights.advance("qkv", chain)
    flights.step(short_lengths, None, ("first",))
    if direct:
        grads, tokens_grad = flights.step(grads, input_work(0, blocks // 2, None))
        _, tokens_grad = flights.step(grads, input_work(blocks // 2, blocks // 2, tokens_grad))
    else:
        _, tokens_grad = flights.step(grads, input_work(0, blocks, None))
    total = flights.done["first"]
    other = swap(total[2 * half + 16 :])
    first, up_grad = flights.step(total, first_work)
    if direct:
        flights.step(short_lengths)
        qkv = qkv_direct_finish(core, place, sizes[:1], *flights.done["qkv"], width)
    else:
        total = flights.done["qkv"]
        qkv = qkv_finish(core, total, swap(total), width)
    up_bias_grad, down_grad, proj_grad, *vectors = first
    return (
        block_out,
        tokens_grad,
        qkv[0],
        qkv[3],
        qkv[1],
        qkv[2],
        qkv[4],
        proj_grad,
        vectors[0],
        vectors[1],
        vectors[2],
        up_grad,
        up_bias_grad,
        down_grad,
        vectors[3],
        vectors[4],
        vectors[5],
    )


def solution(mesh):
    in_specs = (
        P(("dp", "tensor"), None),
        P(),
        P(),
        P(),
        P(),
        P(),
        P(),
        P(),
        P(),
        P(),
        P(None, "tensor"),
        P("tensor"),
        P("tensor", None),
        P(),
        P(),
        P(),
        P(("dp", "tensor"), None),
        P(("dp", "tensor"), None),
        P(("dp", "tensor"), None),
        P(("dp", "tensor")),
        P(("dp", "tensor")),
        P(("dp", "tensor"), None),
    )
    out_specs = (
        P(("dp", "tensor"), None),
        P(("dp", "tensor"), None),
        P(),
        P(),
        P(),
        P(),
        P(),
        P(),
        P(),
        P(),
        P(),
        P(None, "tensor"),
        P("tensor"),
        P("tensor", None),
        P(),
        P(),
        P(),
    )
    return jax.shard_map(
        functools.partial(per_device, mesh.shape["dp"]),
        mesh=mesh,
        in_specs=in_specs,
        out_specs=out_specs,
        check_vma=False,
    )
```

```python
import functools

import jax
import jax.numpy as jnp
from jax import lax
from jax.experimental import pallas as pl
from jax.experimental.pallas import tpu as pltpu
from jax.sharding import PartitionSpec as P

HEADS = 12
HEAD_DIM = 32
TEACH_HD = 64
SHORT_LEN = 128
GROUP = 4
LANES = GROUP * HEAD_DIM
GROUPS = HEADS // GROUP
BLOCK = 512
MID_BLOCK = 1024
MID_PARTS = 2
PAD_ROWS = 96
SPLIT = GROUPS - 1

MASKED = -1e30
LIMIT = 2.0**64
EPSILON = 1e-06
LOG2E = 1.4426950408889634
SCALE = HEAD_DIM**-0.5
EXP_SCALE = LOG2E * SCALE
TEACH_SCALE = LOG2E * TEACH_HD**-0.5
MIB = 2**20

F32 = jnp.float32
BF16 = jnp.bfloat16


def dot_nn(left, right):
    return lax.dot_general(left, right, (((1,), (0,)), ((), ())), preferred_element_type=F32)


def dot_nt(left, right):
    return lax.dot_general(left, right, (((1,), (1,)), ((), ())), preferred_element_type=F32)


def dot_tn(left, right):
    return lax.dot_general(left, right, (((0,), (0,)), ((), ())), preferred_element_type=F32)


def dot_tt(left, right):
    return lax.dot_general(left, right, (((0,), (1,)), ((), ())), preferred_element_type=F32)


def lane_row(condition, width=LANES):
    lane = lax.broadcasted_iota(jnp.int32, (1, width), 1)
    return condition(lane).astype(F32).astype(BF16)


def head_mask(block, head, width):
    return block * lane_row(lambda lane: lane // width == head, block.shape[1])


def scaled(block, factor):
    return (block.astype(F32) * factor).astype(BF16)


def spare_lane(head, width):
    return LANES - width if head * width < LANES // 2 else 0


def with_bias(keys, lane, length):
    row = lax.broadcasted_iota(jnp.int32, keys.shape, 0)
    column = lax.broadcasted_iota(jnp.int32, keys.shape, 1)
    bias = jnp.where(row < length, 0.0, MASKED).astype(BF16)
    return jnp.where(column == lane, bias, keys)


def masked_sides(queries, keys, head, width):
    lane = spare_lane(head, width)
    one = lane_row(lambda index: index == lane)
    return head_mask(queries, head, width) + one, keys[lane]


def biased(keys, width, length):
    return {lane: with_bias(keys, lane, length) for lane in (LANES - width, 0)}


def query_flag(length, size):
    return (lax.broadcasted_iota(jnp.int32, (size, 1), 0) < length).astype(F32)


def weave(works):
    ticks = max(count for _, count in works)
    for tick in range(ticks):
        for work, count in works:
            if (tick + 1) * count // ticks > tick * count // ticks:
                next(work)
    for work, _ in works:
        for _ in work:
            pass


def exps(scores, axis, careful):
    if careful:
        scores = scores - jnp.max(scores, axis=axis, keepdims=True)
    heights = jnp.exp2(scores)
    return heights, jnp.sum(heights, axis=axis, keepdims=True)


def low_rows(column, size):
    block = jnp.broadcast_to(column, (column.shape[0], LANES)).astype(BF16)
    return jnp.concatenate([block] * (size // LANES), 1)


def short_bias(length):
    shape = (SHORT_LEN, GROUP * SHORT_LEN)
    return jnp.where(lax.broadcasted_iota(jnp.int32, shape, 0) < length, 0.0, MASKED)


def stack(block, width):
    return jnp.concatenate([head_mask(block, h, width) for h in range(GROUP)], 0)


def diagonal(block):
    return jnp.concatenate(
        [
            block[h * HEAD_DIM : (h + 1) * HEAD_DIM, h * SHORT_LEN : (h + 1) * SHORT_LEN]
            for h in range(GROUP)
        ],
        0,
    )


def params(mebibytes):
    return pltpu.CompilerParams(vmem_limit_bytes=mebibytes * MIB)


def whole(shape):
    return pl.BlockSpec(shape, lambda i: (0,) * len(shape))


def smem():
    return pl.BlockSpec(memory_space=pltpu.SMEM)


def forward_kernel(
    short_blocks,
    short_len,
    long_len,
    tokens,
    wq,
    wk,
    wv,
    bq,
    bv,
    q_out,
    k_out,
    v_out,
    ctx_out,
    ps_out,
    pl_out,
    side_out,
    worst,
    p_buf,
    p_sems,
):
    step = pl.program_id(0)
    x = tokens[...]
    side_out[...] = x.T
    q_out[...] = (dot_nn(x, wq[...]) + row_of(bq)).astype(BF16)
    k_out[...] = dot_nn(x, wk[...]).astype(BF16)
    v_out[...] = (dot_nn(x, wv[...]) + row_of(bv)).astype(BF16)

    def note(total, inverse):
        high = jnp.maximum(total, inverse)
        rows = high.shape[0]
        for i in range(max(high.shape[1] // LANES, 1)):
            part = high[:, i * LANES : (i + 1) * LANES]
            worst[:rows, :] = jnp.maximum(worst[:rows, :], part)


    def short_scores(item, g, found):
        rows = slice(item * SHORT_LEN, (item + 1) * SHORT_LEN)
        cols = slice(g * LANES, (g + 1) * LANES)
        bias = short_bias(short_len[step * (BLOCK // SHORT_LEN) + item])[:, : 2 * SHORT_LEN]
        queries = stack(scaled(q_out[rows, cols], EXP_SCALE), HEAD_DIM)
        for pair in range(GROUP // 2):
            heads = slice(pair * 2 * SHORT_LEN, (pair + 1) * 2 * SHORT_LEN)
            e, total = exps(dot_nt(k_out[rows, cols], queries[heads]) + bias, 0, False)
            found[pair] = e.astype(BF16), total
            yield

    def short_rows(item, g, found):
        rows = slice(item * SHORT_LEN, (item + 1) * SHORT_LEN)
        for pair in range(GROUP // 2):
            heads = slice(pair * 2 * SHORT_LEN, (pair + 1) * 2 * SHORT_LEN)
            e, total = found[pair]
            inverse = 1.0 / total
            note(total, inverse)
            found[pair] = e * inverse.astype(BF16)
            ps_out[g, rows, heads] = found[pair]
            yield

    def short_products(item, g, found):
        rows = slice(item * SHORT_LEN, (item + 1) * SHORT_LEN)
        cols = slice(g * LANES, (g + 1) * LANES)
        probs = jnp.concatenate([found[pair] for pair in range(GROUP // 2)], 1)
        ctx_out[rows, cols] = diagonal(dot_tn(v_out[rows, cols], probs)).T.astype(BF16)
        yield

    def short_items():
        units = [(item, g, {}) for item in range(BLOCK // SHORT_LEN) for g in range(GROUPS)]
        for tick in range(len(units) + 2):
            works = []
            if tick < len(units):
                works.append((short_scores(*units[tick]), 2))
            if 0 <= tick - 1 < len(units):
                works.append((short_rows(*units[tick - 1]), 2))
            if 0 <= tick - 2:
                works.append((short_products(*units[tick - 2]), 1))
            weave(works)


    def p_copy(g):
        index = step - short_blocks
        slot = lax.rem(index * GROUPS + g, 2)
        heads = pl.ds(g * GROUP, GROUP)
        rows = pl.ds(index * BLOCK, BLOCK)
        return pltpu.make_async_copy(
            p_buf.at[slot], pl_out.at[heads, rows, :], p_sems.at[slot]
        )

    def p_slot(g):
        return p_buf.at[lax.rem((step - short_blocks) * GROUPS + g, 2)]

    def long_item():
        length = long_len[step - short_blocks]
        halves = [slice(i * (BLOCK // 2), (i + 1) * (BLOCK // 2)) for i in range(2)]

        sides = {}
        sums = [[] for _ in range(GROUPS)]

        def group_sides(g):
            if g not in sides:
                cols = slice(g * LANES, (g + 1) * LANES)
                keys = biased(k_out[:, cols], HEAD_DIM, length)
                sides[g] = scaled(q_out[:, cols], EXP_SCALE), keys
            return sides[g]

        def scores(head, found):
            left, right = masked_sides(*group_sides(head // GROUP), head % GROUP, HEAD_DIM)
            for half in halves:
                e = jnp.exp2(dot_nt(left, right[half]))
                part = e[:, :LANES] + e[:, LANES:]
                found["sum"] = found["sum"] + part if "sum" in found else part
                found[half.start] = e.astype(BF16)
                yield

        def normalise(head, found):
            g, h = head // GROUP, head % GROUP
            if h == 0:

                @pl.when((step - short_blocks) * GROUPS + g >= 2)
                def _():
                    p_copy(g).wait()

            count = BLOCK // 4
            for i in range(4):
                rows = slice(i * count, (i + 1) * count)
                total = jnp.sum(found["sum"][rows], axis=1, keepdims=True)
                inverse = 1.0 / total
                note(total, inverse)
                e = jnp.concatenate([found[half.start][rows] for half in halves], 1)
                p_slot(g)[h, rows, :] = e * low_rows(inverse, BLOCK)
                yield

        def products(head):
            g, h = head // GROUP, head % GROUP
            cols = slice(g * LANES, (g + 1) * LANES)
            sums[g].append(dot_nn(p_slot(g)[h], head_mask(v_out[:, cols], h, HEAD_DIM)))
            if h == GROUP - 1:
                ctx_out[:, cols] = functools.reduce(jnp.add, sums[g]).astype(BF16)
                p_copy(g).start()
            yield

        found = [{} for _ in range(HEADS)]
        for tick in range(HEADS + 2):
            works = []
            if tick < HEADS:
                works.append((scores(tick, found[tick]), 2))
            if 0 <= tick - 1 < HEADS:
                works.append((normalise(tick - 1, found[tick - 1]), 4))
            if 0 <= tick - 2:
                works.append((products(tick - 2), 1))
            weave(works)


    def short_items_careful():
        items = BLOCK // SHORT_LEN

        @pl.loop(0, items)
        def _(item):
            rows = pl.ds(pl.multiple_of(item * SHORT_LEN, SHORT_LEN), SHORT_LEN)
            bias = short_bias(short_len[step * items + item])
            for g in range(GROUPS):
                cols = slice(g * LANES, (g + 1) * LANES)
                q, k, v = q_out[rows, cols], k_out[rows, cols], v_out[rows, cols]
                e, total = exps(dot_nt(k, stack(q, HEAD_DIM)) * EXP_SCALE + bias, 0, True)
                probs = (e * (1.0 / total)).astype(BF16)
                ps_out[g, rows, :] = probs
                ctx_out[rows, cols] = diagonal(dot_tn(v, probs)).T.astype(BF16)

    def long_item_careful():
        length = long_len[step - short_blocks]
        bias = jnp.where(lax.broadcasted_iota(jnp.int32, (1, BLOCK), 1) < length, 0.0, MASKED)
        p_copy(1).wait()
        p_copy(2).wait()

        @pl.loop(0, GROUPS)
        def _(g):
            p_now = p_slot(g)
            cols = pl.ds(pl.multiple_of(g * LANES, LANES), LANES)
            q, k, v = q_out[:, cols], k_out[:, cols], v_out[:, cols]
            ctx = jnp.zeros((BLOCK, LANES), F32)
            for h in range(GROUP):
                scores = dot_nt(head_mask(q, h, HEAD_DIM), k) * EXP_SCALE + bias
                e, total = exps(scores, 1, True)
                probs = (e * (1.0 / total)).astype(BF16)
                p_now[h] = probs
                ctx = ctx + dot_nn(probs, head_mask(v, h, HEAD_DIM))
            ctx_out[:, cols] = ctx.astype(BF16)
            p_copy(g).start()

            @pl.when(g == 0)
            def _():
                p_copy(g).wait()

    short = step < short_blocks
    long = jnp.logical_not(short)
    worst[...] = jnp.zeros_like(worst)
    pl.when(short)(short_items)
    pl.when(long)(long_item)
    wild = jnp.logical_not(jnp.max(worst[...]) < LIMIT)
    pl.when(jnp.logical_and(short, wild))(short_items_careful)
    pl.when(jnp.logical_and(long, wild))(long_item_careful)

    @pl.when(step == pl.num_programs(0) - 1)
    def _():
        p_copy(1).wait()
        p_copy(2).wait()


def attention_forward(tokens, wq, wk, wv, bq, bv, short_len, long_len):
    rows, width = tokens.shape
    blocks = rows // BLOCK
    short_blocks = short_len.shape[0] * SHORT_LEN // BLOCK
    long_blocks = blocks - short_blocks
    row_spec = pl.BlockSpec((BLOCK, width), lambda i: (i, 0))
    act = jax.ShapeDtypeStruct((rows, width), BF16)
    return pl.pallas_call(
        functools.partial(forward_kernel, short_blocks),
        grid=(blocks,),
        in_specs=[smem(), smem(), row_spec]
        + [whole(a.shape) for a in (wq, wk, wv, bq, bv)],
        out_specs=[
            row_spec,
            row_spec,
            row_spec,
            row_spec,
            pl.BlockSpec((GROUPS, BLOCK, BLOCK), lambda i: (0, jnp.minimum(i, short_blocks - 1), 0)),
            pl.BlockSpec(memory_space=pl.ANY),
            pl.BlockSpec((width, BLOCK), lambda i: (0, i)),
        ],
        out_shape=[
            act,
            act,
            act,
            act,
            jax.ShapeDtypeStruct((GROUPS, short_blocks * BLOCK, BLOCK), BF16),
            jax.ShapeDtypeStruct((HEADS, long_blocks * BLOCK, BLOCK), BF16),
            jax.ShapeDtypeStruct((width, rows), BF16),
        ],
        scratch_shapes=[
            pltpu.VMEM((BLOCK // 4, LANES), F32),
            pltpu.VMEM((2, GROUP, BLOCK, BLOCK), BF16),
            pltpu.SemaphoreType.DMA((2,)),
        ],
        compiler_params=params(56),
        cost_estimate=pl.CostEstimate(
            flops=12_000_000_000, bytes_accessed=24_000_000, transcendentals=8_000_000
        ),
        name="attention_forward",
    )(short_len, long_len, tokens, wq, wk, wv, bq, bv)


def norm_parts(resid):
    centred = resid - jnp.mean(resid, axis=-1, keepdims=True)
    spread = jnp.mean(centred * centred, axis=-1, keepdims=True)
    root = lax.rsqrt(spread + EPSILON)
    return centred * root, root


def norm_back(grad, y, root):
    return root * (
        grad
        - jnp.mean(grad, axis=-1, keepdims=True)
        - y * jnp.mean(grad * y, axis=-1, keepdims=True)
    )


def row_of(vector):
    return vector[...].astype(F32).reshape(1, vector.shape[0])


def column_sum(block):
    return jnp.sum(block.astype(F32), axis=0, keepdims=True)


def middle_kernel(
    core,
    tokens,
    ctx,
    cot,
    wo,
    up0,
    up1,
    dn0,
    dn1,
    ub0,
    ub1,
    bo_in,
    gain1_in,
    shift1_in,
    db_in,
    gain2_in,
    shift2_in,
    block_out,
    dres_out,
    dctx_out,
    keep_out,
    give_out,
    acc_up,
    acc_dn,
    acc_wo,
    acc_ub,
    acc_vec,
    slope,
    active,
    dpre,
    low_rows_buf,
    dbranch,
    dattn,
):
    step = pl.program_id(0)
    half = up0.shape[1]
    width = up0.shape[0]

    @pl.when(step == 0)
    def _():
        for ref in (acc_up, acc_dn, acc_wo, acc_ub, acc_vec):
            ref[...] = jnp.zeros_like(ref)

    bo, gain1, shift1, db, gain2, shift2 = (
        row_of(ref) for ref in (bo_in, gain1_in, shift1_in, db_in, gain2_in, shift2_in)
    )
    def gelu(j, pre, rows):
        pre = pre + row_of((ub0, ub1)[j])
        phi = 0.5 + 0.5 * lax.erf(pre * (0.5**0.5))
        slope[j, rows, :] = phi + pre * (jnp.exp2(pre * pre * (-0.5 * LOG2E)) * 0.3989422804014327)
        active[j, rows, :] = (pre * phi).astype(BF16)

    def back_gelu(j, dactive, rows):
        grad = (dactive * slope[j, rows, :]).astype(BF16)
        dpre[j, rows, :] = grad
        acc_ub[j : j + 1, :] += column_sum(grad)
        return grad

    def row_work(rows):
        resid = tokens[rows, :].astype(F32) + dot_nn(ctx[rows, :], wo[...]) + bo
        yield
        y1, root1 = norm_parts(resid)
        normed = y1 * gain1 + shift1
        normed_low = normed.astype(BF16)
        low_rows_buf[rows, :] = normed_low
        mid = normed + db
        yield
        pre0 = dot_nn(normed_low, up0[...])
        yield
        pre1 = dot_nn(normed_low, up1[...])
        gelu(0, pre0, rows)
        yield
        mid = mid + dot_nn(active[0, rows, :], dn0[...])
        gelu(1, pre1, rows)
        yield
        mid = mid + dot_nn(active[1, rows, :], dn1[...])
        yield
        y2, root2 = norm_parts(mid)
        block_out[rows, :] = (y2 * gain2 + shift2).astype(BF16)
        cotangent = cot[rows, :].astype(F32)
        dmid = norm_back(cotangent * gain2, y2, root2)
        dbranch_low = dmid.astype(BF16)
        dbranch[rows, :] = dbranch_low
        acc_vec[3:4, :] += column_sum(dbranch_low)
        acc_vec[4:5, :] += column_sum(cotangent * y2)
        acc_vec[5:6, :] += column_sum(cotangent)
        yield
        dactive0 = dot_nt(dbranch_low, dn0[...])
        yield
        dactive1 = dot_nt(dbranch_low, dn1[...])
        dpre0 = back_gelu(0, dactive0, rows)
        yield
        dnormed = dmid + dot_nt(dpre0, up0[...])
        dpre1 = back_gelu(1, dactive1, rows)
        yield
        dnormed = dnormed + dot_nt(dpre1, up1[...])
        yield
        acc_vec[1:2, :] += column_sum(dnormed * y1)
        acc_vec[2:3, :] += column_sum(dnormed)
        dres = norm_back(dnormed * gain1, y1, root1)
        dres_out[rows, :] = dres
        dattn_low = dres.astype(BF16)
        dattn[rows, :] = dattn_low
        acc_vec[0:1, :] += column_sum(dattn_low)
        yield
        dctx_out[rows, :] = dot_nt(dattn_low, wo[...]).astype(BF16)
        yield

    def weight_work():
        for j in range(2):
            acc_dn[j] += dot_tn(dbranch[...], active[j])
            yield
        for j in range(2):
            acc_up[j] += dot_tn(low_rows_buf[...], dpre[j])
            yield
        acc_wo[...] += dot_tn(ctx[...], dattn[...])
        yield

    stages = 13
    parts = MID_PARTS
    size = MID_BLOCK // parts
    works = [row_work(slice(i * size, (i + 1) * size)) for i in range(parts)]
    weights_now = weight_work()
    for tick in range(stages + parts - 1):
        for i, work in enumerate(works):
            if 0 <= tick - i < stages:
                next(work)
        if tick >= stages - 2:
            next(weights_now)
    for _ in weights_now:
        pass

    @pl.when(step == pl.num_programs(0) - 1)
    def _():
        for j, out in enumerate((keep_out, give_out)):
            for part in range(half // width):
                cols = slice(part * width, (part + 1) * width)
                out[cols, :] = acc_up[j, :, cols].astype(BF16)
                out[half + part * width : half + (part + 1) * width, :] = acc_dn[j, :, cols].astype(
                    BF16
                )
            pads = [
                acc_ub[j : j + 1, part * width : (part + 1) * width]
                for part in range(half // width)
            ]
            pads.append(jnp.zeros((16 - len(pads), width), F32))
            out[2 * half : 2 * half + 16, :] = jnp.concatenate(pads, 0).astype(BF16)
        cut = (width + PAD_ROWS) // 2
        low = acc_wo[:cut, :].astype(BF16)
        pads = jnp.zeros((PAD_ROWS - 8, width), F32)
        high = jnp.concatenate([acc_wo[cut:, :], acc_vec[...], pads], 0).astype(BF16)
        first = core[0] == 0
        keep_out[2 * half + 16 :, :] = jnp.where(first, low, high)
        give_out[2 * half + 16 :, :] = jnp.where(first, high, low)


def middle(core, tokens, ctx, cot, wo, ups, dns, ubs, vectors):
    rows, width = tokens.shape
    half = ups[0].shape[1]
    row_spec = pl.BlockSpec((MID_BLOCK, width), lambda i: (i, 0))
    weights = (wo, *ups, *dns, *ubs, *vectors)
    act = jax.ShapeDtypeStruct((rows, width), BF16)
    sums = jax.ShapeDtypeStruct((2 * half + 16 + (width + PAD_ROWS) // 2, width), BF16)
    return pl.pallas_call(
        middle_kernel,
        grid=(rows // MID_BLOCK,),
        in_specs=[smem()] + [row_spec] * 3 + [whole(w.shape) for w in weights],
        out_specs=[row_spec] * 3 + [whole(sums.shape), whole(sums.shape)],
        out_shape=[act, jax.ShapeDtypeStruct((rows, width), F32), act, sums, sums],
        scratch_shapes=[
            pltpu.VMEM((2, width, half), F32),
            pltpu.VMEM((2, width, half), F32),
            pltpu.VMEM((width, width), F32),
            pltpu.VMEM((8, half), F32),
            pltpu.VMEM((8, width), F32),
            pltpu.VMEM((2, MID_BLOCK, half), F32),
            pltpu.VMEM((2, MID_BLOCK, half), BF16),
            pltpu.VMEM((2, MID_BLOCK, half), BF16),
            pltpu.VMEM((MID_BLOCK, width), BF16),
            pltpu.VMEM((MID_BLOCK, width), BF16),
            pltpu.VMEM((MID_BLOCK, width), BF16),
        ],
        compiler_params=params(44),
        cost_estimate=pl.CostEstimate(
            flops=34_000_000_000, bytes_accessed=20_000_000, transcendentals=6_000_000
        ),
        name="middle",
    )(core, tokens, ctx, cot, *weights)


def backward_kernel(
    first,
    blocks,
    short_blocks,
    extended,
    short_len,
    long_len,
    core,
    side_in,
    q_in,
    k_in,
    v_in,
    ctx_in,
    dctx_in,
    tq_in,
    tk_in,
    tv_in,
    ps_in,
    pl_in,
    *refs,
):
    if extended:
        refs = refs[1:]
    (
        grad_out,
        keep_out,
        give_out,
        grads_all,
        dq_buf,
        dk_buf,
        dv_buf,
        dkt_buf,
        dvt_buf,
        ds_buf,
        worst,
        side,
        side_sem,
    ) = refs
    block = lax.rem(first + pl.program_id(0), blocks)
    side_copy = pltpu.make_async_copy(side_in, side, side_sem.at[0])
    pl.when(pl.program_id(0) == 0)(side_copy.start)
    pl.when(pl.program_id(0) == blocks - 1)(side_copy.wait)


    def short_scores(item, found):
        rows = slice(item * SHORT_LEN, (item + 1) * SHORT_LEN)
        length = short_len[block * (BLOCK // SHORT_LEN) + item]
        bias = short_bias(length)[:, : 2 * SHORT_LEN]
        lane = lax.broadcasted_iota(jnp.int32, (1, GROUP * SHORT_LEN), 1)
        flag = (lane % SHORT_LEN < length).astype(F32)
        v, dctx = v_in[rows, :], dctx_in[rows, :]
        found["v_all"], found["dctx_all"] = stack(v, HEAD_DIM), stack(dctx, HEAD_DIM)
        found["p"] = ps_in[0, rows, :]
        v_scaled = stack(scaled(v, EXP_SCALE), HEAD_DIM)
        weighed = (dctx.astype(F32) * ctx_in[rows, :].astype(F32)).T
        delta = [
            jnp.sum(weighed[h * HEAD_DIM : (h + 1) * HEAD_DIM], axis=0, keepdims=True)
            for h in range(GROUP)
        ]
        delta = flag - jnp.concatenate(delta, 1)
        for pair in range(GROUP // 2):
            cols = slice(pair * LANES, (pair + 1) * LANES)
            heads = slice(pair * 2 * SHORT_LEN, (pair + 1) * 2 * SHORT_LEN)
            for kind, (queries, keys) in enumerate(((tq_in, tk_in), (tv_in, tv_in))):
                part = scaled(queries[rows, cols], TEACH_SCALE)
                both = jnp.concatenate([head_mask(part, h, TEACH_HD) for h in range(2)], 0)
                scores = dot_nt(keys[rows, cols], both) + bias
                found[kind, pair] = measured(jnp.exp2(scores), flag[:, heads])
                yield
            scores = dot_nt(v, v_scaled[heads]) + bias
            found[2, pair] = measured(jnp.exp2(scores), flag[:, heads])
            yield
            dp = dot_nt(v, found["dctx_all"][heads]) + delta[:, heads]
            found[3, pair] = dp.astype(BF16)
            yield

    def measured(e, flag):
        total = jnp.sum(e, axis=0, keepdims=True)
        inverse = 1.0 / total
        width = total.shape[1]
        worst[0:1, :width] = jnp.maximum(worst[0:1, :width], jnp.maximum(total, inverse))
        return e.astype(BF16), (flag * inverse).astype(BF16)

    def short_rows(found):
        found["ds"], found["drel"] = [], []
        for pair in range(GROUP // 2):
            heads = slice(pair * 2 * SHORT_LEN, (pair + 1) * 2 * SHORT_LEN)
            teach, teach_rel, own = (found[kind, pair][0] * found[kind, pair][1] for kind in range(3))
            found["ds"].append(found["p"][:, heads] * found[3, pair] - teach)
            yield
            found["drel"].append(own - teach_rel)
            yield

    def short_products(item, found):
        rows = slice(item * SHORT_LEN, (item + 1) * SHORT_LEN)
        ds, drel = (jnp.concatenate(found[name], 1) for name in ("ds", "drel"))
        dq_buf[rows, :] = diagonal(dot_tn(k_in[rows, :], ds)).T * SCALE
        yield
        dk_buf[rows, :] = dot_nn(ds, stack(q_in[rows, :], HEAD_DIM)) * SCALE
        yield
        rel = diagonal(dot_tn(v_in[rows, :], drel)).T
        yield
        rel = rel + dot_nn(drel, found["v_all"])
        yield
        dv_buf[rows, :] = dot_nn(found["p"], found["dctx_all"]) + SCALE * rel
        yield

    def short_items():
        worst[...] = jnp.zeros_like(worst)
        items = BLOCK // SHORT_LEN
        found = [{} for _ in range(items)]
        for tick in range(items + 2):
            works = []
            if tick < items:
                works.append((short_scores(tick, found[tick]), 8))
            if 0 <= tick - 1 < items:
                works.append((short_rows(found[tick - 1]), 4))
            if 0 <= tick - 2:
                works.append((short_products(tick - 2, found[tick - 2]), 5))
            weave(works)

    def short_items_careful():
        @pl.loop(0, BLOCK // SHORT_LEN)
        def _(item):
            rows = pl.ds(pl.multiple_of(item * SHORT_LEN, SHORT_LEN), SHORT_LEN)
            length = short_len[block * (BLOCK // SHORT_LEN) + item]
            bias = short_bias(length)
            lane = lax.broadcasted_iota(jnp.int32, (1, GROUP * SHORT_LEN), 1)
            flag = (lane % SHORT_LEN < length).astype(F32)
            q, k, v = q_in[rows, :], k_in[rows, :], v_in[rows, :]
            dctx, ctx = dctx_in[rows, :], ctx_in[rows, :]
            tq, tk, tv = tq_in[rows, :], tk_in[rows, :], tv_in[rows, :]
            q_all, v_all, dctx_all = (stack(part, HEAD_DIM) for part in (q, v, dctx))
            p = ps_in[0, rows, :]

            def soft(scores, scale):
                e, total = exps(scores * scale + bias, 0, True)
                return e * (flag / total)

            def teach(keys, queries):
                parts = []
                for pair in range(GROUP // 2):
                    cols = slice(pair * LANES, (pair + 1) * LANES)
                    both = [head_mask(queries[:, cols], h, TEACH_HD) for h in range(2)]
                    parts.append(dot_nt(keys[:, cols], jnp.concatenate(both, 0)))
                return soft(jnp.concatenate(parts, 1), TEACH_SCALE)

            weighed = (dctx.astype(F32) * ctx.astype(F32)).T
            delta = [
                jnp.sum(weighed[h * HEAD_DIM : (h + 1) * HEAD_DIM], axis=0, keepdims=True)
                for h in range(GROUP)
            ]
            dp = dot_nt(v, dctx_all) + (flag - jnp.concatenate(delta, 1))
            ds = (p.astype(F32) * dp - teach(tk, tq)).astype(BF16)
            dq_buf[rows, :] = diagonal(dot_tn(k, ds)).T * SCALE
            dk_buf[rows, :] = dot_nn(ds, q_all) * SCALE
            drel = (soft(dot_nt(v, v_all), EXP_SCALE) - teach(tv, tv)).astype(BF16)
            rel = dot_nn(drel, v_all) + diagonal(dot_tn(v, drel)).T
            dv_buf[rows, :] = dot_nn(p, dctx_all) + SCALE * rel


    def long_item():
        worst[...] = jnp.zeros_like(worst)
        length = long_len[block - short_blocks]
        q, k, v = q_in[...], k_in[...], v_in[...]
        dctx, ctx = dctx_in[...], ctx_in[...]
        qt, vt, dctxt = q.T, v.T, dctx.T
        weighed = -(dctx.astype(F32) * ctx.astype(F32)).astype(BF16)
        right = jnp.concatenate([v, jnp.ones_like(v)], 1)
        flag = query_flag(length, BLOCK)
        flags = jnp.broadcast_to(flag, v.shape).astype(BF16)
        flag_row = lax.broadcasted_iota(jnp.int32, (1, BLOCK), 1) < length
        halves = [slice(i * (BLOCK // 2), (i + 1) * (BLOCK // 2)) for i in range(2)]
        teach = {}

        def teach_pair(source, pair):
            if (source, pair) not in teach:
                part = (tq_in, tk_in, tv_in)[source][:, pair * LANES : (pair + 1) * LANES]
                if source == 0:
                    teach[source, pair] = scaled(part, TEACH_SCALE)
                elif source == 1:
                    teach[source, pair] = biased(part, TEACH_HD, length)
                else:
                    teach[source, pair] = own_sides(part, TEACH_HD, TEACH_SCALE)
            return teach[source, pair]

        def own_sides(part, width, scale):
            queries = scaled(part, scale)
            sides = {}
            for lane in (LANES - width, 0):
                keys = with_bias(part, lane, length)
                column = lax.broadcasted_iota(jnp.int32, part.shape, 1)
                ones = jnp.ones_like(part)
                sides[lane] = queries, jnp.where(column == lane + 1, ones, keys)
            return sides

        bias = jnp.where(flags > 0, jnp.zeros_like(flags), jnp.full_like(flags, MASKED))

        def own_scores(sides, h, width):
            lane = spare_lane(h, width)
            queries, keys = sides[lane]
            left = head_mask(queries, h, width) + lane_row(lambda index: index == lane)
            return left + bias * lane_row(lambda index: index == lane + 1), keys

        v_sides = own_sides(v, HEAD_DIM, EXP_SCALE)

        def score_items(h, found):
            left, keys = masked_sides(
                teach_pair(0, h // 2), teach_pair(1, h // 2), h % 2, TEACH_HD
            )
            sums = []
            found["teach"] = []
            for cols in halves:
                e = jnp.exp2(dot_nt(left, keys[cols]))
                sums.append(e[:, :LANES] + e[:, LANES:])
                found["teach"].append(e.astype(BF16))
                yield
            found["sum"] = sums[0] + sums[1]
            lane = spare_lane(h, HEAD_DIM)
            extra = head_mask(weighed, h, HEAD_DIM) + flags * lane_row(lambda i: i == lane)
            left = jnp.concatenate([head_mask(dctx, h, HEAD_DIM), extra], 1)
            found["dp"] = []
            for cols in halves:
                found["dp"].append(dot_nt(left, right[cols]).astype(BF16))
                yield
            for kind in range(2):
                if kind == 0:
                    left, keys = own_scores(v_sides, h, HEAD_DIM)
                else:
                    left, keys = own_scores(teach_pair(2, h // 2), h % 2, TEACH_HD)
                totals = []
                found[kind] = []
                for i, j in ((0, 0), (0, 1), (1, 1)):
                    e = jnp.exp2(dot_nt(left[halves[i]], keys[halves[j]]))
                    found[kind].append(e.astype(BF16))
                    totals.append(jnp.sum(e, axis=0, keepdims=True))
                    if i != j:
                        across = jnp.sum(e, axis=1, keepdims=True)
                        across = jnp.broadcast_to(across, (BLOCK // 2, LANES)).T[0:1, :]
                    yield
                found["total", kind] = jnp.concatenate(
                    [totals[0] + across, totals[1] + totals[2]], 1
                )

        def row_items(h, found):
            dims = slice(h * HEAD_DIM, (h + 1) * HEAD_DIM)
            for kind in range(2):
                total = found["total", kind]
                inverse = 1.0 / total
                high = jnp.where(flag_row, jnp.maximum(total, inverse), 1.0)
                for cols in halves:
                    worst[0:1, :] = jnp.maximum(worst[0:1, :], high[:, cols])
                inverse = jnp.where(flag_row, inverse, 0.0)
                found["inverse", kind] = inverse
                rows = (vt[dims, :].astype(F32) * inverse).astype(BF16)
                found["rows", kind] = jnp.concatenate([vt[dims, :], rows], 0)
                yield
            count = BLOCK // 8
            for i in range(8):
                rows = slice(i * count, (i + 1) * count)
                total = jnp.sum(found["sum"][rows], axis=1, keepdims=True)
                inverse = 1.0 / total
                high = jnp.maximum(total, inverse)
                worst[:, :LANES] = jnp.maximum(worst[:, :LANES], high)
                factor = low_rows(flag[rows] * inverse, BLOCK // 2)
                for j, cols in enumerate(halves):
                    ds_buf[h % 2, rows, cols] = (
                        pl_in[h, rows, cols] * found["dp"][j][rows]
                        - found["teach"][j][rows] * factor
                    )
                yield

        def value_items(h, found):
            for _ in range(2):
                yield
            dims = slice(h * HEAD_DIM, (h + 1) * HEAD_DIM)
            rel = [None, None]
            for kind in range(2):
                near, across, far = found[kind]
                left = found["rows", kind]
                inverse = found["inverse", kind]
                for j in range(2):
                    if j == 0:
                        part = dot_nn(left[:, halves[0]], near)
                        yield
                        part = part + dot_nt(left[:, halves[1]], across)
                    else:
                        part = dot_nn(left[:, halves[0]], across)
                        yield
                        part = part + dot_nn(left[:, halves[1]], far)
                    part = inverse[:, halves[j]] * part[:HEAD_DIM] + part[HEAD_DIM:]
                    rel[j] = part if kind == 0 else rel[j] - part
                    yield
            for j, cols in enumerate(halves):
                dvt_buf[dims, cols] = dot_nn(dctxt[dims, :], pl_in[h, :, cols]) + SCALE * rel[j]
                yield

        def product_items(h):
            dims = slice(h * HEAD_DIM, (h + 1) * HEAD_DIM)
            ds = ds_buf.at[h % 2]
            for cols in halves:
                dkt_buf[dims, cols] = dot_nn(qt[dims, :], ds[:, cols]) * SCALE
                yield
            part = dot_nn(ds[...], head_mask(k, h, HEAD_DIM))
            if h == 0:
                dq_buf[...] = part
            else:
                dq_buf[...] += part
            yield

        found = [{} for _ in range(GROUP)]
        for h in range(-1, GROUP + 1):
            works = []
            if h + 1 < GROUP:
                works.append((score_items(h + 1, found[h + 1]), 10))
            if 0 <= h < GROUP:
                works.append((row_items(h, found[h]), 10))
                works.append((value_items(h, found[h]), 12))
            if h >= 1:
                works.append((product_items(h - 1), 3))
            weave(works)
        dq_buf[...] *= SCALE
        dk_buf[...] = dkt_buf[...].astype(BF16).T.astype(F32)
        dv_buf[...] = dvt_buf[...].T

    def long_item_careful():
        length = long_len[block - short_blocks]
        flag = query_flag(length, BLOCK)
        bias = jnp.where(
            lax.broadcasted_iota(jnp.int32, (1, BLOCK), 1) < length, 0.0, MASKED
        )
        for buf in (dq_buf, dk_buf, dv_buf):
            buf[...] = jnp.zeros_like(buf)

        def soft(queries, keys, h, width, scale):
            scores = dot_nt(head_mask(queries, h, width), keys)
            e, total = exps(scores * scale + bias, 1, True)
            return e * (flag / total)

        @pl.loop(0, GROUP)
        def _(h):
            q, k, v, dctx = (
                head_mask(ref[...], h, HEAD_DIM) for ref in (q_in, k_in, v_in, dctx_in)
            )
            p = pl_in[h]
            delta = jnp.sum(dctx.astype(F32) * ctx_in[...].astype(F32), axis=1, keepdims=True)
            dp = dot_nt(dctx, v) + (flag - delta)
            teach = soft(tq_in[...], tk_in[...], h, TEACH_HD, TEACH_SCALE)
            ds = (p.astype(F32) * dp - teach).astype(BF16)
            own = soft(v, v, h, HEAD_DIM, EXP_SCALE)
            drel = (own - soft(tv_in[...], tv_in[...], h, TEACH_HD, TEACH_SCALE)).astype(BF16)
            dq_buf[...] += dot_nn(ds, k) * SCALE
            dk_buf[...] += dot_tn(ds, q) * SCALE
            dv_buf[...] += dot_tn(p, dctx) + SCALE * (dot_nn(drel, v) + dot_tn(drel, v))

    short = block < short_blocks
    pl.when(short)(short_items)
    pl.when(jnp.logical_not(short))(long_item)
    wild = jnp.logical_not(jnp.max(worst[...]) < LIMIT)
    pl.when(jnp.logical_and(short, wild))(short_items_careful)
    pl.when(jnp.logical_and(jnp.logical_not(short), wild))(long_item_careful)

    grads = jnp.concatenate([buf[...].astype(BF16) for buf in (dq_buf, dk_buf, dv_buf)], 1)
    grad_out[...] = grads
    grads_all[pl.ds(pl.multiple_of(block * BLOCK, BLOCK), BLOCK), :] = grads

    @pl.when(block == blocks - 1)
    def _():
        sums = dot_nn(side[...], grads_all[...])
        biases = column_sum(grads_all[...])
        full = [sums[:, w * LANES : (w + 1) * LANES] for w in range(3)]
        full += [biases[:, w * LANES : (w + 1) * LANES] for w in range(3)]
        full = jnp.concatenate([*full, jnp.zeros((125, LANES), F32)], 0).astype(BF16)
        cut = full.shape[0] // 2
        is_first = core[0] == 0
        keep_out[...] = jnp.where(is_first, full[:cut], full[cut:])
        give_out[...] = jnp.where(is_first, full[cut:], full[:cut])


def attention_backward(groups, short_len, long_len, core, side, acts, p_short, p_long, before):
    width, rows = side.shape
    blocks = rows // BLOCK
    short_blocks = short_len.shape[0] * SHORT_LEN // BLOCK
    start, stop = (group * blocks for group in groups)

    def place(pick):
        return lambda i: pick((start + i) // blocks, (start + i) % blocks)

    def group_spec(size):
        return pl.BlockSpec((BLOCK, size), place(lambda g, b: (b, g)))

    p_specs = [
        pl.BlockSpec(
            (1, BLOCK, BLOCK), place(lambda g, b: (g, jnp.minimum(b, short_blocks - 1), 0))
        ),
        pl.BlockSpec(
            (GROUP, BLOCK, BLOCK), place(lambda g, b: (g, jnp.maximum(b - short_blocks, 0), 0))
        ),
    ]
    cut = (3 * width + 128) // 2
    sums = jax.ShapeDtypeStruct(((groups[1] - groups[0]) * cut, LANES), BF16)
    half_spec = pl.BlockSpec((cut, LANES), place(lambda g, b: (g - groups[0], 0)))
    square = (BLOCK, LANES)
    ins = [short_len, long_len, core, side, *acts, p_short, p_long]
    before_specs = []
    aliases = {}
    if before is not None:
        aliases = {len(ins): 0}
        ins.append(before)
        before_specs = [pl.BlockSpec(memory_space=pl.ANY)]
    out_specs = [
        pl.BlockSpec((BLOCK, 3 * LANES), place(lambda g, b: (b, g))),
        half_spec,
        half_spec,
    ]
    out_shape = [jax.ShapeDtypeStruct((rows, GROUPS * 3 * LANES), BF16), sums, sums]
    return pl.pallas_call(
        functools.partial(backward_kernel, start, blocks, short_blocks, before is not None),
        grid=(stop - start,),
        in_specs=[smem(), smem(), smem()]
        + [pl.BlockSpec(memory_space=pl.ANY)]
        + [group_spec(LANES)] * 5
        + [group_spec(GROUP * TEACH_HD)] * 3
        + p_specs
        + before_specs,
        out_specs=out_specs,
        out_shape=out_shape,
        scratch_shapes=[
            pltpu.VMEM((rows, 3 * LANES), BF16),
            pltpu.VMEM(square, F32),
            pltpu.VMEM(square, F32),
            pltpu.VMEM(square, F32),
            pltpu.VMEM((LANES, BLOCK), F32),
            pltpu.VMEM((LANES, BLOCK), F32),
            pltpu.VMEM((2, BLOCK, BLOCK), BF16),
            pltpu.VMEM((BLOCK // 8, 2 * SHORT_LEN), F32),
            pltpu.VMEM(side.shape, BF16),
            pltpu.SemaphoreType.DMA((1,)),
        ],
        input_output_aliases=aliases,
        compiler_params=params(60),
        cost_estimate=pl.CostEstimate(
            flops=(stop - start) * 7_000_000_000,
            bytes_accessed=(stop - start) * 4_000_000,
            transcendentals=(stop - start) * 2_000_000,
        ),
        name=f"attention_backward_{start}",
    )(*ins)


def tokens_grad_kernel(dres, wq, wk, wv, grads, *refs):
    weights = jnp.concatenate(
        [w[:, g * LANES : (g + 1) * LANES] for g in range(GROUPS) for w in (wq, wk, wv)], 1
    )
    refs[-1][...] = (dres[...] + dot_nt(grads[...], weights)).astype(BF16)


def tokens_gradient(first, count, dres, wq, wk, wv, grads, before):
    rows, width = dres.shape
    row_spec = pl.BlockSpec((BLOCK, width), lambda i: (first + i, 0))
    ins = [dres, wq, wk, wv, grads]
    specs = [row_spec] + [whole(wq.shape)] * 3
    specs += [pl.BlockSpec((BLOCK, grads.shape[1]), lambda i: (first + i, 0))]
    aliases = {}
    if before is not None:
        aliases = {len(ins): 0}
        ins.append(before)
        specs.append(pl.BlockSpec(memory_space=pl.ANY))
    return pl.pallas_call(
        tokens_grad_kernel,
        grid=(count,),
        in_specs=specs,
        out_specs=row_spec,
        out_shape=jax.ShapeDtypeStruct((rows, width), BF16),
        input_output_aliases=aliases,
        compiler_params=params(56),
        cost_estimate=pl.CostEstimate(
            flops=count * 500_000_000, bytes_accessed=count * 2_500_000, transcendentals=0
        ),
        name=f"tokens_gradient_{first}",
    )(*ins)


def swap(value):
    return lax.ppermute(value, "tensor", [(0, 1), (1, 0)])


def spread(value):
    return lax.all_to_all(value, "dp", 0, 0, tiled=True)


def sum_chain(keep, give, count):
    (got,) = yield [(swap, give)]
    both = (keep.astype(F32) + got.astype(F32)).astype(BF16)
    rows, width = both.shape
    (got,) = yield [(spread, both.reshape(count, rows // count, width))]
    part = jnp.sum(got.astype(F32), axis=0).astype(BF16)
    (got,) = yield [(spread, jnp.broadcast_to(part[None], got.shape))]
    return got.reshape(rows, width)


def stage_sizes(count):
    sizes = []
    while count > 1:
        sizes.append(4 if count % 4 == 0 else 2)
        count //= sizes[-1]
    return sizes


def offset_send(value, offset, count):
    return lax.ppermute(value, "dp", [(i, i ^ offset) for i in range(count)])


def pair_sum_kernel(count, place, *refs):
    keeps, gots, outs = refs[:count], refs[count : 2 * count], refs[2 * count :]
    size = len(outs)
    for j, out in enumerate(outs):
        for i in range(out.shape[0]):
            chunk = i * size + (place[0] % size ^ j)
            start = 0
            for keep, got in zip(keeps, gots):
                stop = start + keep.shape[1]
                both = keep[chunk].astype(F32) + got[chunk].astype(F32)
                out[i, start:stop, :] = both.astype(BF16)
                start = stop


def pair_sum(place, keeps, gots, size):
    count, _, width = keeps[0].shape
    rows = sum(keep.shape[1] for keep in keeps)
    return pl.pallas_call(
        functools.partial(pair_sum_kernel, len(keeps)),
        in_specs=[smem()] + [pl.BlockSpec(memory_space=pltpu.VMEM)] * (2 * len(keeps)),
        out_shape=[jax.ShapeDtypeStruct((count // size, rows, width), BF16)] * size,
        compiler_params=params(16),
        name="pair_sum",
    )(place, *keeps, *gots)


def tree_sum(values):
    values = [value.astype(F32) for value in values]
    while len(values) > 1:
        values = [values[i] + values[i + 1] for i in range(0, len(values), 2)]
    return values[0].astype(BF16)


def direct_chain(place, keeps, got_first, give, count):
    near, far = stage_sizes(count)
    (got,) = yield [(swap, give)]

    def chunks(value):
        return value.reshape(count, value.shape[0] // count, value.shape[1])

    gots = [chunks(value) for value in (got_first, got)]
    own, *others = pair_sum(place, [chunks(keep) for keep in keeps], gots, near)

    def sends(values, shift):
        return [
            (functools.partial(offset_send, offset=(j + 1) << shift, count=count), value)
            for j, value in enumerate(values)
        ]

    shift = near.bit_length() - 1
    got = yield sends(others, 0)
    part = tree_sum([own, *got])
    got = yield sends([part] * (far - 1), shift)
    part = tree_sum([part, *got])
    got = yield sends([part] * (near - 1), 0)
    mine = [part, *got]
    other = yield [(swap, value) for value in mine]
    return mine, other


def ordered(core, mine, other):
    first = core[0] == 0
    return jnp.where(first, mine, other), jnp.where(first, other, mine)


def first_finish_kernel(core, total, other, up_out, ub_out, dn_out, wo_out, *vector_outs):
    width, half = up_out.shape
    count = half // width
    for part in range(count):
        cols = slice(part * width, (part + 1) * width)
        up_out[:, cols] = total[cols, :].astype(F32)
        dn_out[cols, :] = total[half + part * width : half + (part + 1) * width, :].astype(F32).T
    biases = total[2 * half : 2 * half + 16, :].astype(F32)
    ub_out[...] = jnp.concatenate([biases[i : i + 1] for i in range(count)], 1).reshape(half)
    halves = ordered(core, total[2 * half + 16 :, :].astype(F32), other[...].astype(F32))
    both = jnp.concatenate(halves, 0)
    wo_out[...] = both[:width]
    for i, out in enumerate(vector_outs):
        out[...] = both[width + i : width + i + 1].reshape(width)


def first_finish(core, total, other, half):
    width = total.shape[1]
    shapes = [(width, half), (half,), (half, width), (width, width)] + [(width,)] * 6
    return pl.pallas_call(
        first_finish_kernel,
        in_specs=[smem()] + [pl.BlockSpec(memory_space=pltpu.VMEM)] * 2,
        out_shape=[jax.ShapeDtypeStruct(shape, F32) for shape in shapes],
        compiler_params=params(16),
        name="first_finish",
    )(core, total, other)


def qkv_finish_body(core, total, other, outs):
    wq_out, wk_out, wv_out, bq_out, bv_out = outs
    width = wq_out.shape[0]
    low, high = ordered(core, total, other)
    cut = low.shape[0] // GROUPS
    sides = []
    for g in range(GROUPS):
        rows = slice(g * cut, (g + 1) * cut)
        full = jnp.concatenate([low[rows], high[rows]], 0)
        cols = slice(g * LANES, (g + 1) * LANES)
        for w, out in enumerate((wq_out, wk_out, wv_out)):
            out[:, cols] = full[w * width : (w + 1) * width]
        sides.append(full[3 * width : 3 * width + 8])
    sides = jnp.concatenate(sides, 1)
    bq_out[...] = sides[0:1].reshape(width)
    bv_out[...] = sides[2:3].reshape(width)


def qkv_finish_kernel(core, total, other, *outs):
    qkv_finish_body(core, total[...].astype(F32), other[...].astype(F32), outs)


def single_swap(value):
    (got,) = yield [(swap, value)]
    return got


def qkv_direct_kernel(near, cuts, core, place, *refs):
    parts, outs, bufs = refs[: 2 * near], refs[2 * near : -2], refs[-2:]
    for buf, side in zip(bufs, (parts[:near], parts[near:])):
        for j, part in enumerate(side):
            for i in range(part.shape[0]):
                buf[i * near + (place[0] % near ^ j)] = part[i].astype(F32)
    sides = []
    for buf in bufs:
        count, rows, lanes = buf.shape
        spans = zip((0, *cuts), (*cuts, rows))
        parts = [buf[:, a:b, :].reshape(count * (b - a), lanes) for a, b in spans]
        sides.append(jnp.concatenate(parts, 0))
    qkv_finish_body(core, *sides, outs)


def qkv_shapes(width):
    return [jax.ShapeDtypeStruct(shape, F32) for shape in [(width, width)] * 3 + [(width,)] * 2]


def qkv_finish(core, total, other, width):
    return pl.pallas_call(
        qkv_finish_kernel,
        in_specs=[smem()] + [pl.BlockSpec(memory_space=pltpu.VMEM)] * 2,
        out_shape=qkv_shapes(width),
        compiler_params=params(16),
        name="qkv_finish",
    )(core, total, other)


def qkv_direct_finish(core, place, cuts, mine, other, width):
    near = len(mine)
    far, rows, lanes = mine[0].shape
    return pl.pallas_call(
        functools.partial(qkv_direct_kernel, near, cuts),
        in_specs=[smem()] * 2 + [pl.BlockSpec(memory_space=pltpu.VMEM)] * (2 * near),
        out_shape=qkv_shapes(width),
        scratch_shapes=[pltpu.VMEM((far * near, rows, lanes), F32)] * 2,
        compiler_params=params(16),
        name="qkv_direct_finish",
    )(core, place, *mine, *other)


class Flights:
    def __init__(self):
        self.asked = {}
        self.flying = {}
        self.done = {}

    def advance(self, name, generator, got=None):
        try:
            wants = next(generator) if got is None else generator.send(got)
            self.asked[name] = (generator, wants)
        except StopIteration as end:
            self.done[name] = end.value

    def step(self, token, work=None, stay=()):
        asked, self.asked = self.asked, {}
        sends = [value for _, wants in asked.values() for _, value in wants]
        token, *sends = lax.optimization_barrier((token, *sends))
        sent = iter(sends)
        for name, (generator, wants) in asked.items():
            self.flying[name] = generator, [move(next(sent)) for move, _ in wants]
        result = None
        if work is not None:
            result, token = work(token)
        for name in [name for name in self.flying if name not in stay]:
            generator, got = self.flying.pop(name)
            if work is not None:
                token, *got = lax.optimization_barrier((token, *got))
            self.advance(name, generator, got)
        return result, token


def per_device(
    dp_count,
    tokens,
    query_weight,
    query_bias,
    key_weight,
    value_weight,
    value_bias,
    proj_weight,
    proj_bias,
    first_gain,
    first_shift,
    up_weight,
    up_bias,
    down_weight,
    down_bias,
    second_gain,
    second_shift,
    teach_query,
    teach_key,
    teach_value,
    short_lengths,
    long_lengths,
    cotangent,
):
    width = tokens.shape[1]
    half = up_weight.shape[1]

    up_other, down_other, ub_other = (swap(value) for value in (up_weight, down_weight, up_bias))
    core = lax.axis_index("tensor").astype(jnp.int32).reshape(1)
    q, k, v, ctx, p_short, p_long, side = attention_forward(
        tokens,
        query_weight,
        key_weight,
        value_weight,
        query_bias,
        value_bias,
        short_lengths,
        long_lengths,
    )
    block_out, dres, dctx, keep, give = middle(
        core,
        tokens,
        ctx,
        cotangent,
        proj_weight,
        (up_weight, up_other),
        (down_weight, down_other),
        (up_bias, ub_other),
        (proj_bias, first_gain, first_shift, down_bias, second_gain, second_shift),
    )
    flights = Flights()
    flights.advance("first", sum_chain(keep, give, dp_count))
    flights.step(short_lengths)
    acts = (q, k, v, ctx, dctx, teach_query, teach_key, teach_value)
    token = short_lengths
    grads = None
    keeps = []
    gives = []
    for groups in ((0, SPLIT), (SPLIT, GROUPS)):

        def work(lens):
            out = attention_backward(
                groups, lens, long_lengths, core, side, acts, p_short, p_long, grads
            )
            return out[:2], out[2]

        stay = ("first",) if groups[1] == GROUPS else ()
        (grads, keep), give = flights.step(token, work, stay)
        token, give = lax.optimization_barrier((short_lengths, give))
        keeps.append(keep)
        gives.append(give)
        if groups[1] < GROUPS:
            flights.advance("swap", single_swap(give))

    blocks = tokens.shape[0] // BLOCK
    weights = (query_weight, key_weight, value_weight)

    def input_work(first, count, before):
        def work(grads):
            return grads, tokens_gradient(first, count, dres, *weights, grads, before)

        return work

    def first_work(total):
        out = first_finish(core, total, other, half)
        return out[1:], out[0]

    sizes = [keep.shape[0] // dp_count for keep in keeps]
    direct = all(size % 8 == 0 for size in sizes) and len(stage_sizes(dp_count)) == 2
    if direct:
        place = lax.axis_index("dp").astype(jnp.int32).reshape(1)
        chain = direct_chain(place, keeps, flights.done["swap"], gives[1], dp_count)
    else:
        chain = sum_chain(jnp.concatenate(keeps, 0), jnp.concatenate(gives, 0), dp_count)
    flights.advance("qkv", chain)
    flights.step(short_lengths, None, ("first",))
    if direct:
        grads, tokens_grad = flights.step(grads, input_work(0, blocks // 2, None))
        _, tokens_grad = flights.step(grads, input_work(blocks // 2, blocks // 2, tokens_grad))
    else:
        _, tokens_grad = flights.step(grads, input_work(0, blocks, None))
    total = flights.done["first"]
    other = swap(total[2 * half + 16 :])
    first, up_grad = flights.step(total, first_work)
    if direct:
        flights.step(short_lengths)
        qkv = qkv_direct_finish(core, place, sizes[:1], *flights.done["qkv"], width)
    else:
        total = flights.done["qkv"]
        qkv = qkv_finish(core, total, swap(total), width)
    up_bias_grad, down_grad, proj_grad, *vectors = first
    return (
        block_out,
        tokens_grad,
        qkv[0],
        qkv[3],
        qkv[1],
        qkv[2],
        qkv[4],
        proj_grad,
        vectors[0],
        vectors[1],
        vectors[2],
        up_grad,
        up_bias_grad,
        down_grad,
        vectors[3],
        vectors[4],
        vectors[5],
    )


def solution(mesh):
    in_specs = (
        P(("dp", "tensor"), None),
        P(),
        P(),
        P(),
        P(),
        P(),
        P(),
        P(),
        P(),
        P(),
        P(None, "tensor"),
        P("tensor"),
        P("tensor", None),
        P(),
        P(),
        P(),
        P(("dp", "tensor"), None),
        P(("dp", "tensor"), None),
        P(("dp", "tensor"), None),
        P(("dp", "tensor")),
        P(("dp", "tensor")),
        P(("dp", "tensor"), None),
    )
    out_specs = (
        P(("dp", "tensor"), None),
        P(("dp", "tensor"), None),
        P(),
        P(),
        P(),
        P(),
        P(),
        P(),
        P(),
        P(),
        P(),
        P(None, "tensor"),
        P("tensor"),
        P("tensor", None),
        P(),
        P(),
        P(),
    )
    return jax.shard_map(
        functools.partial(per_device, mesh.shape["dp"]),
        mesh=mesh,
        in_specs=in_specs,
        out_specs=out_specs,
        check_vma=False,
    )
```
